32 devices in a mesh: groups: 2 (over y), tok: 4 (over z), ch: 2 (over x), sub: 2 (over core).
Axes of the slice: x: 2, y: 2, z: 4, core: 2. Of those that a mesh axis runs over, the one named last changes fastest.
Arguments:
- weather: float32 [128, 128, 128], P('groups', 'tok', ('ch', 'sub')), parts along dimension 0, may hold values from -6 to 6
- conv_first: float32 [9, 64, 64], replicated, may hold values from -0.25 to 0.25
- conv_second: float32 [9, 64, 64], replicated, may hold values from -0.25 to 0.25
- patch_embed: bfloat16 [256, 384], replicated, may hold values from -0.375 to 0.375
- token_mixing: bfloat16 [4096, 16384], P('tok', ('ch', 'sub')), may hold values from -0.09375 to 0.09375
Outputs:
- lifted: bfloat16 [768, 16384], P(('groups', 'tok'), ('ch', 'sub')), parts along dimension 0
The draws below stay inside these ranges and needn't reach their ends.
There are 2 independent parts, one for each index of `groups`. The reference program is written for one: setup_inputs(seed, part) draws one part's arguments, and reference() takes and returns one part's arrays. A program takes and returns all parts, laid end to end along the dimension named above; an argument that names none is the same for every part. Nothing has to cross between parts.
All inputs are finite; a program needn't handle non-finite values.
Results may differ from the reference program's by a relative error of at most 0.0058.
Values may be sent and summed in bfloat16 or wider, within the bound.
No kernel may reach another device: no remote copies, remote signals or barrier semaphores. Data moves between devices by JAX's collectives and lax.ppermute only.
A program may use at most 64 MiB of HBM per device.

```python
import jax
import jax.numpy as jnp
from jax import lax

CIN = 64
EMBED = 384
HIDDEN_SIZE = 16384
LON = 128
LAT = 128
TOKENS = 4096
BAND = 1024
N_TOK = 4


def block_levels(rng, dims, pieces, smallest, high):
    gain, own = 1.0, jax.random.fold_in(rng, 6)
    for position, blocks in pieces:
        draws = jnp.exp(jax.random.uniform(jax.random.fold_in(own, position), (blocks,), jnp.float32, smallest / len(pieces), high / len(pieces)))
        gain = gain * jnp.repeat(draws, dims[position] // blocks).reshape([-1 if axis == position else 1 for axis in range(len(dims))])
    return gain


def normal_values(own_key, shape, deviation, limit, cuts=(), held_as=jnp.bfloat16):
    entries = jax.random.normal(own_key, shape, jnp.float32) * deviation
    if len(cuts) > 0:
        entries = block_levels(own_key, shape, cuts, -0.22, 0.18) * entries
    return jnp.clip(entries, min=-limit, max=limit).astype(held_as)


def setup_inputs(seed: int = 0, part: int = 0) -> dict:
    key_list = jax.random.split(jax.random.key(seed), 6)
    part_splits = jax.random.split(jax.random.fold_in(key_list[5], part), 6)
    return {
        "weather": normal_values(part_splits[0], (CIN, LON, LAT), 1.0, 6.0, ((1, 4), (2, 4)), jnp.float32),
        "conv_first": normal_values(key_list[1], (9, CIN, CIN), (9 * CIN) ** -0.5, 0.25, (), jnp.float32),
        "conv_second": normal_values(key_list[2], (9, CIN, CIN), (9 * CIN) ** -0.5, 0.25, (), jnp.float32),
        "patch_embed": normal_values(key_list[3], (4 * CIN, EMBED), (4 * CIN) ** -0.5, 0.375),
        "token_mixing": normal_values(key_list[4], (TOKENS, HIDDEN_SIZE), TOKENS ** -0.5, 0.09375, ((0, 4), (1, 4))),
    }


def convolve(field_in, kernel):
    width_lon = field_in.shape[1]
    width_lat = field_in.shape[2]
    looped = jnp.concatenate([field_in[:, -1:, :], field_in, field_in[:, :1, :]], axis=1)
    padded = jnp.pad(looped, ((0, 0), (0, 0), (1, 1)))
    summed = jnp.zeros((kernel.shape[1], width_lon, width_lat), jnp.float32)
    for row_shift in range(3):
        for col_shift in range(3):
            window = padded[:, row_shift:row_shift + width_lon, col_shift:col_shift + width_lat]
            summed = summed + jnp.einsum("oi,ixy->oxy", kernel[3 * row_shift + col_shift], window, precision=lax.Precision.HIGHEST)
    return summed


def reference(weather, conv_first, conv_second, patch_embed, token_mixing):
    hidden_one = jax.nn.gelu(convolve(weather, conv_first), approximate=False)
    field_two = convolve(hidden_one, conv_second).astype(jnp.bfloat16)
    blocks = field_two.reshape(CIN, LON // 2, 2, LAT // 2, 2).astype(jnp.float32)
    embed_four = patch_embed.reshape(CIN, 2, 2, EMBED).astype(jnp.float32)
    tokens = jnp.einsum("cpaqb,cabo->pqo", blocks, embed_four).reshape(TOKENS, EMBED).astype(jnp.bfloat16)
    token_blocks = tokens.reshape(N_TOK, BAND, EMBED)
    weight_blocks = token_mixing.reshape(N_TOK, BAND, HIDDEN_SIZE)

    def add_block(carry, pair):
        product = lax.dot_general(pair[0].astype(jnp.float32), pair[1].astype(jnp.float32), (((0,), (0,)), ((), ())))
        return carry + product, None

    summed, unused = lax.scan(add_block, jnp.zeros((EMBED, HIDDEN_SIZE), jnp.float32), (token_blocks, weight_blocks))
    return jax.nn.gelu(summed, approximate=False).astype(jnp.bfloat16)
```

```python
import jax
import jax.numpy as jnp
from jax import lax
from jax.sharding import PartitionSpec as P


def padded_2(block, sides, width, periodic):
    for axis, dim in sides:
        count = lax.axis_size(axis)
        forward = [(i, i + 1) for i in range(count - 1)]
        if periodic:
            forward.append((count - 1, 0))
        backward = [(target, source) for source, target in forward]
        low = lax.ppermute(
            lax.slice_in_dim(block, block.shape[dim] - width, None, axis=dim), axis, forward
        )
        high = lax.ppermute(lax.slice_in_dim(block, 0, width, axis=dim), axis, backward)
        block = jnp.concatenate([low, block, high], axis=dim)
    return block


def valid_conv(padded, kernel):
    width_lon = padded.shape[1] - 2
    width_lat = padded.shape[2] - 2
    stacked = jnp.stack(
        [
            padded[:, row_shift : row_shift + width_lon, col_shift : col_shift + width_lat]
            for row_shift in range(3)
            for col_shift in range(3)
        ],
        0,
    )
    return jnp.einsum("toi,tixy->oxy", kernel, stacked, precision=lax.Precision.HIGHEST)


def embed_patches(field_in, patch_embed):
    chans, width_lon, width_lat = field_in.shape
    blocks = field_in.reshape(chans, width_lon // 2, 2, width_lat // 2, 2)
    embed_four = patch_embed.reshape(chans, 2, 2, patch_embed.shape[1])
    return jnp.einsum(
        "cpaqb,cabo->pqo", blocks, embed_four, preferred_element_type=jnp.float32
    ).astype(jnp.bfloat16)


def lift(tokens, token_mixing, pieces):
    count = lax.axis_size("tok")
    rows = tokens.shape[1] // count
    width = token_mixing.shape[1] // pieces
    down = [(i, (i - 1) % count) for i in range(count)]
    partials = []
    for piece in range(pieces):
        partials.append(
            lax.dot_general(
                tokens,
                token_mixing[:, piece * width : (piece + 1) * width],
                (((0,), (0,)), ((), ())),
                preferred_element_type=jnp.float32,
            )
        )
    travelling = [part[:rows].astype(jnp.bfloat16) for part in partials]
    for step in range(1, count):
        for piece in range(pieces):
            arrived = lax.ppermute(travelling[piece], "tok", down).astype(jnp.float32)
            summed = arrived + partials[piece][step * rows : (step + 1) * rows]
            if step == count - 1:
                summed = jax.nn.gelu(summed, approximate=False)
            travelling[piece] = summed.astype(jnp.bfloat16)
    return jnp.concatenate(travelling, axis=1)


def local(weather, conv_first, conv_second, patch_embed, token_mixing):
    count = lax.axis_size("tok")
    rows = patch_embed.shape[1] // count
    turn = ((lax.axis_index("tok") + 1) % count) * rows
    rolled = lax.dynamic_slice_in_dim(
        jnp.concatenate([patch_embed, patch_embed], axis=1), turn, patch_embed.shape[1], axis=1
    )
    widened = padded_2(weather, (("tok", 1),), 2, True)
    padded = padded_2(widened, ((("ch", "sub"), 2),), 2, False)
    hidden_one = jax.nn.gelu(valid_conv(padded, conv_first), approximate=False)
    width_lat = weather.shape[2]
    lat_index = (
        jnp.arange(width_lat + 2, dtype=jnp.int32) - 1 + lax.axis_index(("ch", "sub")) * width_lat
    )
    inside = (lat_index >= 0) & (lat_index < width_lat * lax.axis_size(("ch", "sub")))
    hidden_one = jnp.where(inside[None, None, :], hidden_one, jnp.float32(0.0))
    field_two = valid_conv(hidden_one, conv_second)
    field_two = field_two.astype(jnp.bfloat16)
    local_tokens = embed_patches(field_two, rolled)
    gathered = lax.all_gather(local_tokens, ("ch", "sub"), axis=1, tiled=True)
    tokens = gathered.reshape(-1, gathered.shape[2])
    return lift(tokens, token_mixing, 4)


def solution(mesh):
    placed = (P("groups", "tok", ("ch", "sub")), P(), P(), P(), P("tok", ("ch", "sub")))
    return jax.shard_map(
        local,
        mesh=mesh,
        in_specs=placed,
        out_specs=P(("groups", "tok"), ("ch", "sub")),
        check_vma=False,
    )
```

```python
import functools

import jax
import jax.numpy as jnp
from jax import lax
from jax.experimental import pallas as pl
from jax.experimental.pallas import tpu as pltpu
from jax.sharding import PartitionSpec as P

PIECES = 4
LANES = 128
VMEM_BYTES = 24 * 1024 * 1024
ROWS_AT_ONCE = 768


def pack_kernel(field_ref, low_ref, high_ref, packed_ref):
    lon, lat, chans = field_ref.shape
    pairs = field_ref[...].reshape(lon // 2, 2, lat, chans)
    joined = jnp.concatenate([pairs[:, 0], pairs[:, 1]], axis=-1).astype(packed_ref.dtype)
    packed_ref[pl.ds(1, lon // 2)] = joined
    low_ref[...] = joined[:1]
    high_ref[...] = joined[-1:]


def split_two(value):
    upper = value.astype(jnp.bfloat16)
    return upper, (value - upper.astype(jnp.float32)).astype(jnp.bfloat16)


def spread_taps(kernel_ref):
    chans = kernel_ref.shape[1]
    nothing = jnp.zeros((chans, kernel_ref.shape[2]), jnp.float32)
    rows = []
    for tap in range(3):
        taps = [kernel_ref[3 * turn + tap] for turn in range(3)]
        rows.append(jnp.concatenate([taps[1], taps[2], nothing, taps[0]], axis=-1))
        rows.append(jnp.concatenate([taps[0], taps[1], taps[2], nothing], axis=-1))
    return jnp.concatenate(rows, axis=0).T


def weights_kernel(first_ref, second_ref, embed_ref, taps_one_ref, taps_two_ref, embed_out_ref, scratch):
    for source, target in ((first_ref, taps_one_ref), (second_ref, taps_two_ref)):
        upper, lower = split_two(spread_taps(source))
        target[0] = upper
        target[1] = lower
    chans = embed_ref.shape[0] // 4
    for first in range(0, embed_ref.shape[1], LANES):
        scratch[...] = embed_ref[:, pl.ds(first, LANES)].astype(jnp.float32)
        ordered = [scratch[pl.ds(2 * a + b, chans, stride=4), :] for b in range(2) for a in range(2)]
        turned = jnp.concatenate(ordered, axis=0).T
        embed_out_ref[pl.ds(first, LANES), :] = turned.astype(embed_out_ref.dtype)


def pairs_at_once(pairs, lat):
    best = 1
    for size in range(1, pairs + 1):
        if pairs % size == 0 and size * lat <= ROWS_AT_ONCE:
            best = size
    return best


def window(pairs_of, first, size, last):
    rows = []
    for pair in range(first, first + size):
        here = pairs_of(pair)
        after = pairs_of(min(pair + 1, last))
        before = pairs_of(max(pair - 1, 0))
        lane = lax.broadcasted_iota(jnp.int32, here.shape, 1)
        rows.append(jnp.concatenate([here, jnp.where(lane < here.shape[1] // 2, after, before)], axis=-1))
    return jnp.concatenate(rows, axis=0)


def add_lat_taps(products, lat):
    wide = products.shape[1] // 3
    count = products.shape[0]
    row = lax.broadcasted_iota(jnp.int32, (count, wide), 0) % lat
    below = pltpu.roll(products[:, :wide], 1, axis=0)
    above = pltpu.roll(products[:, 2 * wide :], count - 1, axis=0)
    return (
        products[:, wide : 2 * wide]
        + jnp.where(row == 0, 0.0, below)
        + jnp.where(row == lat - 1, 0.0, above)
    )


def gelu(value):
    return 0.5 * value * (1.0 + lax.erf(value * (0.5**0.5)))


def encode_kernel(field_ref, taps_one_ref, taps_two_ref, embed_ref, tokens_ref, upper_ref, lower_ref, two_ref):
    parts, pairs, width, wide = field_ref.shape
    lat = parts * width
    last = pairs - 1

    def field_of(pair):
        return field_ref[:, pair].reshape(lat, wide)

    def dot(left, right):
        return jnp.dot(left, right, preferred_element_type=jnp.float32)

    size = pairs_at_once(pairs, lat)
    for first in range(0, pairs, size):
        rows = window(field_of, first, size, last)
        products = dot(rows, taps_one_ref[0]) + dot(rows, taps_one_ref[1])
        upper, lower = split_two(gelu(add_lat_taps(products, lat)))
        upper_ref[pl.ds(first, size)] = upper.reshape(size, lat, wide)
        lower_ref[pl.ds(first, size)] = lower.reshape(size, lat, wide)
    size = pairs_at_once(pairs - 2, lat)
    for first in range(1, pairs - 1, size):
        rows_upper = window(lambda pair: upper_ref[pair], first, size, last)
        rows_lower = window(lambda pair: lower_ref[pair], first, size, last)
        products = dot(rows_upper, taps_two_ref[0]) + dot(rows_upper, taps_two_ref[1])
        products = products + dot(rows_lower, taps_two_ref[0])
        rounded = add_lat_taps(products, lat).astype(jnp.bfloat16).astype(jnp.float32)
        two_ref[pl.ds((first - 1) * lat, size * lat), :] = rounded
    half = two_ref.shape[0] // 2
    patches = jnp.concatenate(
        [two_ref[pl.ds(b, half, stride=2), :].astype(jnp.bfloat16) for b in range(2)], axis=-1
    )
    tokens_ref[...] = lax.dot_general(
        embed_ref[...], patches, (((1,), (1,)), ((), ())), preferred_element_type=jnp.float32
    ).astype(tokens_ref.dtype)


def call(kernel, out_shape, inputs, scratch=(), flops=0, moved=0):
    return pl.pallas_call(
        kernel,
        out_shape=out_shape,
        in_specs=[pl.BlockSpec(memory_space=pltpu.VMEM)] * len(inputs),
        out_specs=jax.tree.map(lambda unused: pl.BlockSpec(memory_space=pltpu.VMEM), out_shape),
        scratch_shapes=list(scratch),
        compiler_params=pltpu.CompilerParams(vmem_limit_bytes=VMEM_BYTES),
        cost_estimate=pl.CostEstimate(flops=flops, bytes_accessed=moved, transcendentals=0),
    )(*inputs)


def encode(weather, conv_first, conv_second, patch_embed):
    chans, lon, lat = weather.shape
    pairs, wide = lon // 2, 2 * chans
    embed = patch_embed.shape[1]
    shape = functools.partial(jax.ShapeDtypeStruct, dtype=jnp.bfloat16)
    low, high, packed = call(
        pack_kernel,
        (shape((1, lat, wide)), shape((1, lat, wide)), shape((pairs + 2, lat, wide))),
        (jnp.transpose(weather, (1, 2, 0)),),
        moved=weather.size * 10,
    )
    count = lax.axis_size("tok")
    up = [(i, (i + 1) % count) for i in range(count)]
    down = [(target, source) for source, target in up]
    before = lax.ppermute(high, "tok", up)
    after = lax.ppermute(low, "tok", down)
    taps = shape((2, 4 * chans, 6 * chans))
    taps_one, taps_two, embed_rows = call(
        weights_kernel,
        (taps, taps, shape((embed, 4 * chans))),
        (conv_first, conv_second, patch_embed),
        scratch=[pltpu.VMEM((patch_embed.shape[0], LANES), jnp.float32)],
        moved=conv_first.size * 20,
    )
    packed = lax.dynamic_update_slice_in_dim(packed, before, 0, 0)
    packed = lax.dynamic_update_slice_in_dim(packed, after, pairs + 1, 0)
    gathered = lax.all_gather(packed, ("ch", "sub"), axis=0)
    full_lat = gathered.shape[0] * lat
    held = pltpu.VMEM((pairs + 2, full_lat, wide), jnp.bfloat16)
    return call(
        encode_kernel,
        shape((embed, pairs * full_lat // 2)),
        (gathered, taps_one, taps_two, embed_rows),
        scratch=[held, held, pltpu.VMEM((pairs * full_lat, wide), jnp.float32)],
        flops=2 * (pairs + 1) * full_lat * 4 * chans * 6 * chans * 5,
        moved=gathered.size * 2,
    )


def lift(tokens, token_mixing, pieces):
    count = lax.axis_size("tok")
    rows = tokens.shape[0] // count
    width = token_mixing.shape[1] // pieces
    down = [(i, (i - 1) % count) for i in range(count)]
    partials = [
        jnp.dot(
            tokens,
            token_mixing[:, piece * width : (piece + 1) * width],
            preferred_element_type=jnp.float32,
        )
        for piece in range(pieces)
    ]
    travelling = [part[:rows].astype(jnp.bfloat16) for part in partials]
    for step in range(1, count):
        for piece in range(pieces):
            arrived = lax.ppermute(travelling[piece], "tok", down).astype(jnp.float32)
            summed = arrived + partials[piece][step * rows : (step + 1) * rows]
            if step == count - 1:
                summed = jax.nn.gelu(summed, approximate=False)
            travelling[piece] = summed.astype(jnp.bfloat16)
    return jnp.concatenate(travelling, axis=1)


def local(weather, conv_first, conv_second, patch_embed, token_mixing):
    count = lax.axis_size("tok")
    embed = patch_embed.shape[1]
    turn = ((lax.axis_index("tok") + 1) % count) * (embed // count)
    rolled = lax.dynamic_slice_in_dim(
        jnp.concatenate([patch_embed, patch_embed], axis=1), turn, embed, axis=1
    )
    tokens = encode(weather, conv_first, conv_second, rolled)
    return lift(tokens, token_mixing, PIECES)


def solution(mesh):
    placed = (P("groups", "tok", ("ch", "sub")), P(), P(), P(), P("tok", ("ch", "sub")))
    return jax.shard_map(
        local,
        mesh=mesh,
        in_specs=placed,
        out_specs=P(("groups", "tok"), ("ch", "sub")),
        check_vma=False,
    )
```

```python
import functools

import jax
import jax.numpy as jnp
from jax import lax
from jax.experimental import pallas as pl
from jax.experimental.pallas import tpu as pltpu
from jax.sharding import PartitionSpec as P

PIECES = 4
STEP = 256
LANES = 128
VMEM_BYTES = 24 * 1024 * 1024
ROWS_AT_ONCE = 768


def pack_kernel(field_ref, low_ref, high_ref, packed_ref):
    lon, lat, chans = field_ref.shape
    pairs = field_ref[...].reshape(lon // 2, 2, lat, chans)
    joined = jnp.concatenate([pairs[:, 0], pairs[:, 1]], axis=-1).astype(packed_ref.dtype)
    packed_ref[pl.ds(1, lon // 2)] = joined
    low_ref[...] = joined[:1]
    high_ref[...] = joined[-1:]


def split_two(value):
    upper = value.astype(jnp.bfloat16)
    return upper, (value - upper.astype(jnp.float32)).astype(jnp.bfloat16)


def spread_taps(kernel_ref):
    chans = kernel_ref.shape[1]
    nothing = jnp.zeros((chans, kernel_ref.shape[2]), jnp.float32)
    rows = []
    for tap in range(3):
        taps = [kernel_ref[3 * turn + tap] for turn in range(3)]
        rows.append(jnp.concatenate([taps[1], taps[2], nothing, taps[0]], axis=-1))
        rows.append(jnp.concatenate([taps[0], taps[1], taps[2], nothing], axis=-1))
    return jnp.concatenate(rows, axis=0).T


def weights_kernel(first_ref, second_ref, embed_ref, taps_one_ref, taps_two_ref, embed_out_ref, scratch):
    for source, target in ((first_ref, taps_one_ref), (second_ref, taps_two_ref)):
        upper, lower = split_two(spread_taps(source))
        target[0] = upper
        target[1] = lower
    chans = embed_ref.shape[0] // 4
    for first in range(0, embed_ref.shape[1], LANES):
        scratch[...] = embed_ref[:, pl.ds(first, LANES)].astype(jnp.float32)
        ordered = [scratch[pl.ds(2 * a + b, chans, stride=4), :] for b in range(2) for a in range(2)]
        turned = jnp.concatenate(ordered, axis=0).T
        embed_out_ref[pl.ds(first, LANES), :] = turned.astype(embed_out_ref.dtype)


def pairs_at_once(pairs, lat):
    best = 1
    for size in range(1, pairs + 1):
        if pairs % size == 0 and size * lat <= ROWS_AT_ONCE:
            best = size
    return best


def window(pairs_of, first, size, last):
    rows = []
    for pair in range(first, first + size):
        here = pairs_of(pair)
        after = pairs_of(min(pair + 1, last))
        before = pairs_of(max(pair - 1, 0))
        lane = lax.broadcasted_iota(jnp.int32, here.shape, 1)
        rows.append(jnp.concatenate([here, jnp.where(lane < here.shape[1] // 2, after, before)], axis=-1))
    return jnp.concatenate(rows, axis=0)


def add_lat_taps(products, lat):
    wide = products.shape[1] // 3
    count = products.shape[0]
    row = lax.broadcasted_iota(jnp.int32, (count, wide), 0) % lat
    below = pltpu.roll(products[:, :wide], 1, axis=0)
    above = pltpu.roll(products[:, 2 * wide :], count - 1, axis=0)
    return (
        products[:, wide : 2 * wide]
        + jnp.where(row == 0, 0.0, below)
        + jnp.where(row == lat - 1, 0.0, above)
    )


def gelu(value):
    return 0.5 * value * (1.0 + lax.erf(value * (0.5**0.5)))


def encode_kernel(count_ch, count_sub, *refs):
    count = count_ch * count_sub
    blocks = refs[:count]
    taps_one_ref, taps_two_ref, embed_ref, tokens_ref, field_ref, upper_ref, lower_ref, two_ref = refs[count:]
    pairs, lat, wide = field_ref.shape
    width = lat // count
    last = pairs - 1
    for away_ch in range(count_ch):
        for away_sub in range(count_sub):
            at_ch = lax.rem(lax.axis_index("ch") + count_ch - away_ch, count_ch)
            at_sub = lax.rem(lax.axis_index("sub") + count_sub - away_sub, count_sub)
            start = pl.multiple_of((at_ch * count_sub + at_sub) * width, width)
            field_ref[:, pl.ds(start, width), :] = blocks[away_ch * count_sub + away_sub][...]

    def field_of(pair):
        return field_ref[pair]

    def dot(left, right):
        return jnp.dot(left, right, preferred_element_type=jnp.float32)

    size = pairs_at_once(pairs, lat)
    for first in range(0, pairs, size):
        rows = window(field_of, first, size, last)
        products = dot(rows, taps_one_ref[0]) + dot(rows, taps_one_ref[1])
        upper, lower = split_two(gelu(add_lat_taps(products, lat)))
        upper_ref[pl.ds(first, size)] = upper.reshape(size, lat, wide)
        lower_ref[pl.ds(first, size)] = lower.reshape(size, lat, wide)
    size = pairs_at_once(pairs - 2, lat)
    for first in range(1, pairs - 1, size):
        rows_upper = window(lambda pair: upper_ref[pair], first, size, last)
        rows_lower = window(lambda pair: lower_ref[pair], first, size, last)
        products = dot(rows_upper, taps_two_ref[0]) + dot(rows_upper, taps_two_ref[1])
        products = products + dot(rows_lower, taps_two_ref[0])
        rounded = add_lat_taps(products, lat).astype(jnp.bfloat16).astype(jnp.float32)
        two_ref[pl.ds((first - 1) * lat, size * lat), :] = rounded
    half = two_ref.shape[0] // 2
    patches = jnp.concatenate(
        [two_ref[pl.ds(b, half, stride=2), :].astype(jnp.bfloat16) for b in range(2)], axis=-1
    )
    tokens_ref[...] = lax.dot_general(
        embed_ref[...], patches, (((1,), (1,)), ((), ())), preferred_element_type=jnp.float32
    ).astype(tokens_ref.dtype)


def call(kernel, out_shape, inputs, scratch=(), flops=0, moved=0):
    return pl.pallas_call(
        kernel,
        out_shape=out_shape,
        in_specs=[pl.BlockSpec(memory_space=pltpu.VMEM)] * len(inputs),
        out_specs=jax.tree.map(lambda unused: pl.BlockSpec(memory_space=pltpu.VMEM), out_shape),
        scratch_shapes=list(scratch),
        compiler_params=pltpu.CompilerParams(vmem_limit_bytes=VMEM_BYTES),
        cost_estimate=pl.CostEstimate(flops=flops, bytes_accessed=moved, transcendentals=0),
    )(*inputs)


def turned(value, axis, away):
    count = lax.axis_size(axis)
    return lax.ppermute(value, axis, [(i, (i + away) % count) for i in range(count)])


def gather_blocks(block):
    rows = [block]
    for away in range(1, lax.axis_size("ch")):
        rows.append(turned(block, "ch", away))
    blocks = []
    for row in rows:
        blocks.append(row)
        for away in range(1, lax.axis_size("sub")):
            blocks.append(turned(row, "sub", away))
    return blocks


def encode(weather, conv_first, conv_second, patch_embed):
    chans, lon, lat = weather.shape
    pairs, wide = lon // 2, 2 * chans
    embed = patch_embed.shape[1]
    shape = functools.partial(jax.ShapeDtypeStruct, dtype=jnp.bfloat16)
    low, high, packed = call(
        pack_kernel,
        (shape((1, lat, wide)), shape((1, lat, wide)), shape((pairs + 2, lat, wide))),
        (jnp.transpose(weather, (1, 2, 0)),),
        moved=weather.size * 10,
    )
    before = turned(high, "tok", 1)
    after = turned(low, "tok", -1)
    taps = shape((2, 4 * chans, 6 * chans))
    taps_one, taps_two, embed_rows = call(
        weights_kernel,
        (taps, taps, shape((embed, 4 * chans))),
        (conv_first, conv_second, patch_embed),
        scratch=[pltpu.VMEM((patch_embed.shape[0], LANES), jnp.float32)],
        moved=conv_first.size * 20,
    )
    packed = lax.dynamic_update_slice_in_dim(packed, before, 0, 0)
    packed = lax.dynamic_update_slice_in_dim(packed, after, pairs + 1, 0)
    blocks = gather_blocks(packed)
    full_lat = len(blocks) * lat
    held = pltpu.VMEM((pairs + 2, full_lat, wide), jnp.bfloat16)
    return call(
        functools.partial(encode_kernel, lax.axis_size("ch"), lax.axis_size("sub")),
        shape((embed, pairs * full_lat // 2)),
        (*blocks, taps_one, taps_two, embed_rows),
        scratch=[held, held, held, pltpu.VMEM((pairs * full_lat, wide), jnp.float32)],
        flops=2 * (pairs + 1) * full_lat * 4 * chans * 6 * chans * 5,
        moved=packed.size * 2 * len(blocks),
    )


def partial_kernel(tokens_ref, mixing_ref, sent_ref, kept_ref):
    product = jnp.dot(tokens_ref[...], mixing_ref[...], preferred_element_type=jnp.float32)
    rows = sent_ref.shape[0]
    sent_ref[...] = product[:rows].astype(sent_ref.dtype)
    kept_ref[...] = product[rows:]


def partial(tokens, token_mixing, first, width, rows):
    embed, count = tokens.shape
    step = STEP if width % STEP == 0 else width
    return pl.pallas_call(
        partial_kernel,
        out_shape=(
            jax.ShapeDtypeStruct((rows, width), jnp.bfloat16),
            jax.ShapeDtypeStruct((embed - rows, width), jnp.float32),
        ),
        grid=(width // step,),
        in_specs=[
            pl.BlockSpec(memory_space=pltpu.VMEM),
            pl.BlockSpec((count, step), lambda i: (0, first // step + i)),
        ],
        out_specs=(
            pl.BlockSpec((rows, step), lambda i: (0, i)),
            pl.BlockSpec((embed - rows, step), lambda i: (0, i)),
        ),
        compiler_params=pltpu.CompilerParams(vmem_limit_bytes=VMEM_BYTES),
        cost_estimate=pl.CostEstimate(flops=0, bytes_accessed=0, transcendentals=0),
    )(tokens, token_mixing)


def lift(tokens, token_mixing, pieces):
    count = lax.axis_size("tok")
    rows = tokens.shape[0] // count
    width = token_mixing.shape[1] // pieces
    travelling, kept = [], []
    for piece in range(pieces):
        sent, others = partial(tokens, token_mixing, piece * width, width, rows)
        travelling.append(sent)
        kept.append(others)
    for step in range(1, count):
        for piece in range(pieces):
            arrived = turned(travelling[piece], "tok", -1).astype(jnp.float32)
            summed = arrived + kept[piece][(step - 1) * rows : step * rows]
            if step == count - 1:
                summed = gelu(summed)
            travelling[piece] = summed.astype(jnp.bfloat16)
    return jnp.concatenate(travelling, axis=1)


def local(weather, conv_first, conv_second, patch_embed, token_mixing):
    count = lax.axis_size("tok")
    embed = patch_embed.shape[1]
    turn = ((lax.axis_index("tok") + 1) % count) * (embed // count)
    rolled = lax.dynamic_slice_in_dim(
        jnp.concatenate([patch_embed, patch_embed], axis=1), turn, embed, axis=1
    )
    tokens = encode(weather, conv_first, conv_second, rolled)
    return lift(tokens, token_mixing, PIECES)


def solution(mesh):
    placed = (P("groups", "tok", ("ch", "sub")), P(), P(), P(), P("tok", ("ch", "sub")))
    return jax.shard_map(
        local,
        mesh=mesh,
        in_specs=placed,
        out_specs=P(("groups", "tok"), ("ch", "sub")),
        check_vma=False,
    )
```

```python
import functools
import itertools

import jax
import jax.numpy as jnp
from jax import lax
from jax.experimental import pallas as pl
from jax.experimental.pallas import tpu as pltpu
from jax.sharding import PartitionSpec as P

PIECES = 4
STEP = 256
LANES = 128
VMEM_BYTES = 24 * 1024 * 1024
ROWS_AT_ONCE = 768


def pack_kernel(field_ref, low_ref, high_ref, packed_ref):
    lon, lat, chans = field_ref.shape
    pairs = field_ref[...].reshape(lon // 2, 2, lat, chans)
    joined = jnp.concatenate([pairs[:, 0], pairs[:, 1]], axis=-1).astype(packed_ref.dtype)
    packed_ref[...] = joined
    low_ref[...] = joined[:1]
    high_ref[...] = joined[-1:]


def split_two(value):
    upper = value.astype(jnp.bfloat16)
    return upper, (value - upper.astype(jnp.float32)).astype(jnp.bfloat16)


def spread_taps(kernel_ref):
    chans = kernel_ref.shape[1]
    nothing = jnp.zeros((chans, kernel_ref.shape[2]), jnp.float32)
    rows = []
    for tap in range(3):
        taps = [kernel_ref[3 * turn + tap] for turn in range(3)]
        rows.append(jnp.concatenate([taps[1], taps[2], nothing, taps[0]], axis=-1))
        rows.append(jnp.concatenate([taps[0], taps[1], taps[2], nothing], axis=-1))
    return jnp.concatenate(rows, axis=0).T


def weights_kernel(first_ref, second_ref, embed_ref, taps_one_ref, taps_two_ref, embed_out_ref, scratch):
    for source, target in ((first_ref, taps_one_ref), (second_ref, taps_two_ref)):
        upper, lower = split_two(spread_taps(source))
        target[0] = upper
        target[1] = lower
    chans = embed_ref.shape[0] // 4
    embed = embed_ref.shape[1]
    count = lax.axis_size("tok")
    turn = lax.rem(lax.axis_index("tok") + 1, count) * (embed // count)
    turned_embed = pltpu.roll(embed_ref[...].astype(jnp.float32), lax.rem(embed - turn, embed), axis=1)
    for first in range(0, embed, LANES):
        scratch[...] = turned_embed[:, first : first + LANES]
        ordered = [scratch[pl.ds(2 * a + b, chans, stride=4), :] for b in range(2) for a in range(2)]
        rows = jnp.concatenate(ordered, axis=0).T
        embed_out_ref[pl.ds(first, LANES), :] = rows.astype(embed_out_ref.dtype)


def pairs_at_once(pairs, lat):
    best = 1
    for size in range(1, pairs + 1):
        if pairs % size == 0 and size * lat <= ROWS_AT_ONCE:
            best = size
    return best


def window(pairs_of, first, size, last):
    rows = []
    for pair in range(first, first + size):
        here = pairs_of(pair)
        after = pairs_of(min(pair + 1, last))
        before = pairs_of(max(pair - 1, 0))
        lane = lax.broadcasted_iota(jnp.int32, here.shape, 1)
        rows.append(jnp.concatenate([here, jnp.where(lane < here.shape[1] // 2, after, before)], axis=-1))
    return jnp.concatenate(rows, axis=0)


def add_lat_taps(products, lat):
    wide = products.shape[1] // 3
    count = products.shape[0]
    row = lax.broadcasted_iota(jnp.int32, (count, wide), 0) % lat
    below = pltpu.roll(products[:, :wide], 1, axis=0)
    above = pltpu.roll(products[:, 2 * wide :], count - 1, axis=0)
    return (
        products[:, wide : 2 * wide]
        + jnp.where(row == 0, 0.0, below)
        + jnp.where(row == lat - 1, 0.0, above)
    )


def gelu(value):
    return 0.5 * value * (1.0 + lax.erf(value * (0.5**0.5)))


def encode_kernel(count_ch, count_sub, *refs):
    count = count_ch * count_sub
    blocks, befores, afters = refs[:count], refs[count : 2 * count], refs[2 * count : 3 * count]
    taps_one_ref, taps_two_ref, embed_ref, tokens_ref, field_ref, upper_ref, lower_ref, two_ref = refs[3 * count :]
    pairs, lat, wide = field_ref.shape
    width = lat // count
    last = pairs - 1
    for away_ch in range(count_ch):
        for away_sub in range(count_sub):
            at_ch = lax.rem(lax.axis_index("ch") + count_ch - away_ch, count_ch)
            at_sub = lax.rem(lax.axis_index("sub") + count_sub - away_sub, count_sub)
            start = pl.multiple_of((at_ch * count_sub + at_sub) * width, width)
            away = away_ch * count_sub + away_sub
            field_ref[pl.ds(1, pairs - 2), pl.ds(start, width), :] = blocks[away][...]
            field_ref[pl.ds(0, 1), pl.ds(start, width), :] = befores[away][...]
            field_ref[pl.ds(pairs - 1, 1), pl.ds(start, width), :] = afters[away][...]

    def field_of(pair):
        return field_ref[pair]

    def dot(left, right):
        return jnp.dot(left, right, preferred_element_type=jnp.float32)

    size = pairs_at_once(pairs, lat)
    for first in range(0, pairs, size):
        rows = window(field_of, first, size, last)
        products = dot(rows, taps_one_ref[0]) + dot(rows, taps_one_ref[1])
        upper, lower = split_two(gelu(add_lat_taps(products, lat)))
        upper_ref[pl.ds(first, size)] = upper.reshape(size, lat, wide)
        lower_ref[pl.ds(first, size)] = lower.reshape(size, lat, wide)
    size = pairs_at_once(pairs - 2, lat)
    for first in range(1, pairs - 1, size):
        rows_upper = window(lambda pair: upper_ref[pair], first, size, last)
        rows_lower = window(lambda pair: lower_ref[pair], first, size, last)
        products = dot(rows_upper, taps_two_ref[0]) + dot(rows_upper, taps_two_ref[1])
        products = products + dot(rows_lower, taps_two_ref[0])
        rounded = add_lat_taps(products, lat).astype(jnp.bfloat16).astype(jnp.float32)
        two_ref[pl.ds((first - 1) * lat, size * lat), :] = rounded
    half = two_ref.shape[0] // 2
    patches = jnp.concatenate(
        [two_ref[pl.ds(b, half, stride=2), :].astype(jnp.bfloat16) for b in range(2)], axis=-1
    )
    tokens_ref[...] = lax.dot_general(
        embed_ref[...], patches, (((1,), (1,)), ((), ())), preferred_element_type=jnp.float32
    ).astype(tokens_ref.dtype)


def call(kernel, out_shape, inputs, scratch=(), flops=0, moved=0):
    return pl.pallas_call(
        kernel,
        out_shape=out_shape,
        in_specs=[pl.BlockSpec(memory_space=pltpu.VMEM)] * len(inputs),
        out_specs=jax.tree.map(lambda unused: pl.BlockSpec(memory_space=pltpu.VMEM), out_shape),
        scratch_shapes=list(scratch),
        compiler_params=pltpu.CompilerParams(vmem_limit_bytes=VMEM_BYTES),
        cost_estimate=pl.CostEstimate(flops=flops, bytes_accessed=moved, transcendentals=0),
    )(*inputs)


def turned(value, steps):
    axes = tuple(steps)
    sizes = [lax.axis_size(axis) for axis in axes]
    sources = list(itertools.product(*[range(size) for size in sizes]))
    place = {source: number for number, source in enumerate(sources)}
    route = []
    for source in sources:
        target = tuple((at + steps[axis]) % size for at, axis, size in zip(source, axes, sizes))
        route.append((place[source], place[target]))
    return lax.ppermute(value, axes, route)


def band_blocks(block, steps):
    blocks = []
    for away_ch in range(lax.axis_size("ch")):
        for away_sub in range(lax.axis_size("sub")):
            moves = dict(steps, ch=away_ch, sub=away_sub)
            moves = {axis: step for axis, step in moves.items() if step != 0}
            blocks.append(turned(block, moves) if moves else block)
    return blocks


def encode(weather, conv_first, conv_second, patch_embed):
    chans, lon, lat = weather.shape
    pairs, wide = lon // 2, 2 * chans
    embed = patch_embed.shape[1]
    shape = functools.partial(jax.ShapeDtypeStruct, dtype=jnp.bfloat16)
    low, high, packed = call(
        pack_kernel,
        (shape((1, lat, wide)), shape((1, lat, wide)), shape((pairs, lat, wide))),
        (jnp.transpose(weather, (1, 2, 0)),),
        moved=weather.size * 10,
    )
    taps = shape((2, 4 * chans, 6 * chans))
    taps_one, taps_two, embed_rows = call(
        weights_kernel,
        (taps, taps, shape((embed, 4 * chans))),
        (conv_first, conv_second, patch_embed),
        scratch=[pltpu.VMEM((patch_embed.shape[0], LANES), jnp.float32)],
        moved=conv_first.size * 20,
    )
    blocks = band_blocks(packed, {})
    befores = band_blocks(high, {"tok": 1})
    afters = band_blocks(low, {"tok": -1})
    full_lat = len(blocks) * lat
    held = pltpu.VMEM((pairs + 2, full_lat, wide), jnp.bfloat16)
    return call(
        functools.partial(encode_kernel, lax.axis_size("ch"), lax.axis_size("sub")),
        shape((embed, pairs * full_lat // 2)),
        (*blocks, *befores, *afters, taps_one, taps_two, embed_rows),
        scratch=[held, held, held, pltpu.VMEM((pairs * full_lat, wide), jnp.float32)],
        flops=2 * (pairs + 1) * full_lat * 4 * chans * 6 * chans * 5,
        moved=packed.size * 2 * len(blocks),
    )


def partial_kernel(first, tokens_ref, mixing_ref, sent_ref, kept_ref):
    rows, width = sent_ref.shape
    step = STEP if width % STEP == 0 else width
    tokens = tokens_ref[...]
    for at in range(0, width, step):
        product = jnp.dot(tokens, mixing_ref[:, pl.ds(first + at, step)], preferred_element_type=jnp.float32)
        sent_ref[:, pl.ds(at, step)] = product[:rows].astype(sent_ref.dtype)
        kept_ref[:, pl.ds(at, step)] = product[rows:]


def partial(tokens, token_mixing, first, width, rows):
    return call(
        functools.partial(partial_kernel, first),
        (
            jax.ShapeDtypeStruct((rows, width), jnp.bfloat16),
            jax.ShapeDtypeStruct((tokens.shape[0] - rows, width), jnp.float32),
        ),
        (tokens, token_mixing),
    )


def lift(tokens, token_mixing, pieces):
    count = lax.axis_size("tok")
    rows = tokens.shape[0] // count
    width = token_mixing.shape[1] // pieces
    travelling, kept = [], []
    for piece in range(pieces):
        sent, others = partial(tokens, token_mixing, piece * width, width, rows)
        travelling.append(sent)
        kept.append(others)
    for step in range(1, count):
        for piece in range(pieces):
            arrived = turned(travelling[piece], {"tok": -1}).astype(jnp.float32)
            summed = arrived + kept[piece][(step - 1) * rows : step * rows]
            if step == count - 1:
                summed = gelu(summed)
            travelling[piece] = summed.astype(jnp.bfloat16)
    return jnp.concatenate(travelling, axis=1)


def local(weather, conv_first, conv_second, patch_embed, token_mixing):
    tokens = encode(weather, conv_first, conv_second, patch_embed)
    return lift(tokens, token_mixing, PIECES)


def solution(mesh):
    placed = (P("groups", "tok", ("ch", "sub")), P(), P(), P(), P("tok", ("ch", "sub")))
    return jax.shard_map(
        local,
        mesh=mesh,
        in_specs=placed,
        out_specs=P(("groups", "tok"), ("ch", "sub")),
        check_vma=False,
    )
```

```python
import functools

import jax
import jax.numpy as jnp
from jax import lax
from jax.experimental import pallas as pl
from jax.experimental.pallas import tpu as pltpu
from jax.sharding import PartitionSpec as P

PIECES = 4
STEP = 256
LANES = 128
VMEM_BYTES = 24 * 1024 * 1024
ROWS_AT_ONCE = 768


def pack_kernel(field_ref, low_ref, high_ref, packed_ref):
    lon, lat, chans = field_ref.shape
    pairs = field_ref[...].reshape(lon // 2, 2, lat, chans)
    joined = jnp.concatenate([pairs[:, 0], pairs[:, 1]], axis=-1).astype(packed_ref.dtype)
    packed_ref[pl.ds(1, lon // 2)] = joined
    low_ref[...] = joined[:1]
    high_ref[...] = joined[-1:]


def split_two(value):
    upper = value.astype(jnp.bfloat16)
    return upper, (value - upper.astype(jnp.float32)).astype(jnp.bfloat16)


def spread_taps(kernel_ref):
    chans = kernel_ref.shape[1]
    nothing = jnp.zeros((chans, kernel_ref.shape[2]), jnp.float32)
    rows = []
    for tap in range(3):
        taps = [kernel_ref[3 * turn + tap] for turn in range(3)]
        rows.append(jnp.concatenate([taps[1], taps[2], nothing, taps[0]], axis=-1))
        rows.append(jnp.concatenate([taps[0], taps[1], taps[2], nothing], axis=-1))
    return jnp.concatenate(rows, axis=0).T


def weights_kernel(first_ref, second_ref, embed_ref, taps_one_ref, taps_two_ref, embed_out_ref, scratch):
    for source, target in ((first_ref, taps_one_ref), (second_ref, taps_two_ref)):
        upper, lower = split_two(spread_taps(source))
        target[0] = upper
        target[1] = lower
    chans = embed_ref.shape[0] // 4
    embed = embed_ref.shape[1]
    count = lax.axis_size("tok")
    turn = lax.rem(lax.axis_index("tok") + 1, count) * (embed // count)
    turned_embed = pltpu.roll(embed_ref[...].astype(jnp.float32), lax.rem(embed - turn, embed), axis=1)
    for first in range(0, embed, LANES):
        scratch[...] = turned_embed[:, first : first + LANES]
        ordered = [scratch[pl.ds(2 * a + b, chans, stride=4), :] for b in range(2) for a in range(2)]
        rows = jnp.concatenate(ordered, axis=0).T
        embed_out_ref[pl.ds(first, LANES), :] = rows.astype(embed_out_ref.dtype)


def pairs_at_once(pairs, lat):
    best = 1
    for size in range(1, pairs + 1):
        if pairs % size == 0 and size * lat <= ROWS_AT_ONCE:
            best = size
    return best


def window(pairs_of, first, size, last):
    rows = []
    for pair in range(first, first + size):
        here = pairs_of(pair)
        after = pairs_of(min(pair + 1, last))
        before = pairs_of(max(pair - 1, 0))
        lane = lax.broadcasted_iota(jnp.int32, here.shape, 1)
        rows.append(jnp.concatenate([here, jnp.where(lane < here.shape[1] // 2, after, before)], axis=-1))
    return jnp.concatenate(rows, axis=0)


def add_lat_taps(products, lat):
    wide = products.shape[1] // 3
    count = products.shape[0]
    row = lax.broadcasted_iota(jnp.int32, (count, wide), 0) % lat
    below = pltpu.roll(products[:, :wide], 1, axis=0)
    above = pltpu.roll(products[:, 2 * wide :], count - 1, axis=0)
    return (
        products[:, wide : 2 * wide]
        + jnp.where(row == 0, 0.0, below)
        + jnp.where(row == lat - 1, 0.0, above)
    )


def gelu(value):
    return 0.5 * value * (1.0 + lax.erf(value * (0.5**0.5)))


def encode_kernel(count_ch, count_sub, *refs):
    count = count_ch * count_sub
    blocks = refs[:count]
    taps_one_ref, taps_two_ref, embed_ref, tokens_ref, field_ref, upper_ref, lower_ref, two_ref = refs[count:]
    pairs, lat, wide = field_ref.shape
    width = lat // count
    last = pairs - 1
    for away_ch in range(count_ch):
        for away_sub in range(count_sub):
            at_ch = lax.rem(lax.axis_index("ch") + count_ch - away_ch, count_ch)
            at_sub = lax.rem(lax.axis_index("sub") + count_sub - away_sub, count_sub)
            start = pl.multiple_of((at_ch * count_sub + at_sub) * width, width)
            field_ref[:, pl.ds(start, width), :] = blocks[away_ch * count_sub + away_sub][...]

    def field_of(pair):
        return field_ref[pair]

    def dot(left, right):
        return jnp.dot(left, right, preferred_element_type=jnp.float32)

    size = pairs_at_once(pairs, lat)
    for first in range(0, pairs, size):
        rows = window(field_of, first, size, last)
        products = dot(rows, taps_one_ref[0]) + dot(rows, taps_one_ref[1])
        upper, lower = split_two(gelu(add_lat_taps(products, lat)))
        upper_ref[pl.ds(first, size)] = upper.reshape(size, lat, wide)
        lower_ref[pl.ds(first, size)] = lower.reshape(size, lat, wide)
    size = pairs_at_once(pairs - 2, lat)
    for first in range(1, pairs - 1, size):
        rows_upper = window(lambda pair: upper_ref[pair], first, size, last)
        rows_lower = window(lambda pair: lower_ref[pair], first, size, last)
        products = dot(rows_upper, taps_two_ref[0]) + dot(rows_upper, taps_two_ref[1])
        products = products + dot(rows_lower, taps_two_ref[0])
        rounded = add_lat_taps(products, lat).astype(jnp.bfloat16).astype(jnp.float32)
        two_ref[pl.ds((first - 1) * lat, size * lat), :] = rounded
    half = two_ref.shape[0] // 2
    patches = jnp.concatenate(
        [two_ref[pl.ds(b, half, stride=2), :].astype(jnp.bfloat16) for b in range(2)], axis=-1
    )
    tokens_ref[...] = lax.dot_general(
        embed_ref[...], patches, (((1,), (1,)), ((), ())), preferred_element_type=jnp.float32
    ).astype(tokens_ref.dtype)


def call(kernel, out_shape, inputs, scratch=(), flops=0, moved=0):
    return pl.pallas_call(
        kernel,
        out_shape=out_shape,
        in_specs=[pl.BlockSpec(memory_space=pltpu.VMEM)] * len(inputs),
        out_specs=jax.tree.map(lambda unused: pl.BlockSpec(memory_space=pltpu.VMEM), out_shape),
        scratch_shapes=list(scratch),
        compiler_params=pltpu.CompilerParams(vmem_limit_bytes=VMEM_BYTES),
        cost_estimate=pl.CostEstimate(flops=flops, bytes_accessed=moved, transcendentals=0),
    )(*inputs)


def turned(value, axis, away):
    count = lax.axis_size(axis)
    return lax.ppermute(value, axis, [(i, (i + away) % count) for i in range(count)])


def band_blocks(block, beside):
    rows = [block] + [turned(block, "ch", away) for away in range(1, lax.axis_size("ch"))]
    rows[1:], beside = lax.optimization_barrier((rows[1:], beside))
    blocks = []
    for row in rows:
        blocks.append(row)
        blocks.extend(turned(row, "sub", away) for away in range(1, lax.axis_size("sub")))
    return blocks, beside


def encode(weather, conv_first, conv_second, patch_embed):
    chans, lon, lat = weather.shape
    pairs, wide = lon // 2, 2 * chans
    embed = patch_embed.shape[1]
    shape = functools.partial(jax.ShapeDtypeStruct, dtype=jnp.bfloat16)
    low, high, packed = call(
        pack_kernel,
        (shape((1, lat, wide)), shape((1, lat, wide)), shape((pairs + 2, lat, wide))),
        (jnp.transpose(weather, (1, 2, 0)),),
        moved=weather.size * 10,
    )
    before = turned(high, "tok", 1)
    after = turned(low, "tok", -1)
    taps = shape((2, 4 * chans, 6 * chans))
    weights = call(
        weights_kernel,
        (taps, taps, shape((embed, 4 * chans))),
        (conv_first, conv_second, patch_embed),
        scratch=[pltpu.VMEM((patch_embed.shape[0], LANES), jnp.float32)],
        moved=conv_first.size * 20,
    )
    packed = lax.dynamic_update_slice_in_dim(packed, before, 0, 0)
    packed = lax.dynamic_update_slice_in_dim(packed, after, pairs + 1, 0)
    blocks, weights = band_blocks(packed, weights)
    full_lat = len(blocks) * lat
    held = pltpu.VMEM((pairs + 2, full_lat, wide), jnp.bfloat16)
    return call(
        functools.partial(encode_kernel, lax.axis_size("ch"), lax.axis_size("sub")),
        shape((embed, pairs * full_lat // 2)),
        (*blocks, *weights),
        scratch=[held, held, held, pltpu.VMEM((pairs * full_lat, wide), jnp.float32)],
        flops=2 * (pairs + 1) * full_lat * 4 * chans * 6 * chans * 5,
        moved=packed.size * 2 * len(blocks),
    )


def partial_kernel(first, tokens_ref, mixing_ref, sent_ref, kept_ref):
    rows, width = sent_ref.shape
    step = STEP if width % STEP == 0 else width
    tokens = tokens_ref[...]
    for at in range(0, width, step):
        product = jnp.dot(tokens, mixing_ref[:, pl.ds(first + at, step)], preferred_element_type=jnp.float32)
        sent_ref[:, pl.ds(at, step)] = product[:rows].astype(sent_ref.dtype)
        kept_ref[:, pl.ds(at, step)] = product[rows:]


def partial(tokens, token_mixing, first, width, rows):
    return call(
        functools.partial(partial_kernel, first),
        (
            jax.ShapeDtypeStruct((rows, width), jnp.bfloat16),
            jax.ShapeDtypeStruct((tokens.shape[0] - rows, width), jnp.float32),
        ),
        (tokens, token_mixing),
    )


def lift(tokens, token_mixing, pieces):
    count = lax.axis_size("tok")
    rows = tokens.shape[0] // count
    width = token_mixing.shape[1] // pieces
    travelling, kept = [], []
    for piece in range(pieces):
        sent, others = partial(tokens, token_mixing, piece * width, width, rows)
        travelling.append(sent)
        kept.append(others)
    for step in range(1, count):
        for piece in range(pieces):
            arrived = turned(travelling[piece], "tok", -1).astype(jnp.float32)
            summed = arrived + kept[piece][(step - 1) * rows : step * rows]
            if step == count - 1:
                summed = gelu(summed)
            travelling[piece] = summed.astype(jnp.bfloat16)
    return jnp.concatenate(travelling, axis=1)


def local(weather, conv_first, conv_second, patch_embed, token_mixing):
    tokens = encode(weather, conv_first, conv_second, patch_embed)
    return lift(tokens, token_mixing, PIECES)


def solution(mesh):
    placed = (P("groups", "tok", ("ch", "sub")), P(), P(), P(), P("tok", ("ch", "sub")))
    return jax.shard_map(
        local,
        mesh=mesh,
        in_specs=placed,
        out_specs=P(("groups", "tok"), ("ch", "sub")),
        check_vma=False,
    )
```

```python
import functools

import jax
import jax.numpy as jnp
from jax import lax
from jax.experimental import pallas as pl
from jax.experimental.pallas import tpu as pltpu
from jax.sharding import PartitionSpec as P

PIECES = 4
STEP = 256
LANES = 128
VMEM_BYTES = 24 * 1024 * 1024
ROWS_AT_ONCE = 768


def pack_kernel(field_ref, low_ref, high_ref, packed_ref):
    lon, lat, chans = field_ref.shape
    pairs = field_ref[...].reshape(lon // 2, 2, lat, chans)
    joined = jnp.concatenate([pairs[:, 0], pairs[:, 1]], axis=-1).astype(packed_ref.dtype)
    packed_ref[pl.ds(1, lon // 2)] = joined
    low_ref[...] = joined[:1]
    high_ref[...] = joined[-1:]


def split_two(value):
    upper = value.astype(jnp.bfloat16)
    return upper, (value - upper.astype(jnp.float32)).astype(jnp.bfloat16)


def spread_taps(kernel_ref):
    chans = kernel_ref.shape[1]
    nothing = jnp.zeros((chans, kernel_ref.shape[2]), jnp.float32)
    rows = []
    for tap in range(3):
        taps = [kernel_ref[3 * turn + tap] for turn in range(3)]
        rows.append(jnp.concatenate([taps[1], taps[2], nothing, taps[0]], axis=-1))
        rows.append(jnp.concatenate([taps[0], taps[1], taps[2], nothing], axis=-1))
    return jnp.concatenate(rows, axis=0).T


def weights_kernel(first_ref, second_ref, embed_ref, taps_one_ref, taps_two_ref, embed_out_ref, scratch):
    for source, target in ((first_ref, taps_one_ref), (second_ref, taps_two_ref)):
        upper, lower = split_two(spread_taps(source))
        target[0] = upper
        target[1] = lower
    chans = embed_ref.shape[0] // 4
    embed = embed_ref.shape[1]
    count = lax.axis_size("tok")
    turn = lax.axis_index("tok") * (embed // count)
    turned_embed = pltpu.roll(embed_ref[...].astype(jnp.float32), lax.rem(embed - turn, embed), axis=1)
    for first in range(0, embed, LANES):
        scratch[...] = turned_embed[:, first : first + LANES]
        ordered = [scratch[pl.ds(2 * a + b, chans, stride=4), :] for b in range(2) for a in range(2)]
        rows = jnp.concatenate(ordered, axis=0).T
        embed_out_ref[pl.ds(first, LANES), :] = rows.astype(embed_out_ref.dtype)


def pairs_at_once(pairs, lat):
    best = 1
    for size in range(1, pairs + 1):
        if pairs % size == 0 and size * lat <= ROWS_AT_ONCE:
            best = size
    return best


def window(pairs_of, first, size, last):
    rows = []
    for pair in range(first, first + size):
        here = pairs_of(pair)
        after = pairs_of(min(pair + 1, last))
        before = pairs_of(max(pair - 1, 0))
        lane = lax.broadcasted_iota(jnp.int32, here.shape, 1)
        rows.append(jnp.concatenate([here, jnp.where(lane < here.shape[1] // 2, after, before)], axis=-1))
    return jnp.concatenate(rows, axis=0)


def add_lat_taps(products, lat):
    wide = products.shape[1] // 3
    count = products.shape[0]
    row = lax.broadcasted_iota(jnp.int32, (count, wide), 0) % lat
    below = pltpu.roll(products[:, :wide], 1, axis=0)
    above = pltpu.roll(products[:, 2 * wide :], count - 1, axis=0)
    return (
        products[:, wide : 2 * wide]
        + jnp.where(row == 0, 0.0, below)
        + jnp.where(row == lat - 1, 0.0, above)
    )


def gelu(value):
    return 0.5 * value * (1.0 + lax.erf(value * (0.5**0.5)))


def encode_kernel(count_ch, count_sub, *refs):
    count = count_ch * count_sub
    blocks = refs[:count]
    taps_one_ref, taps_two_ref, embed_ref, tokens_ref, field_ref, upper_ref, lower_ref, two_ref = refs[count:]
    pairs, lat, wide = field_ref.shape
    width = lat // count
    last = pairs - 1
    for away_ch in range(count_ch):
        for away_sub in range(count_sub):
            at_ch = lax.rem(lax.axis_index("ch") + count_ch - away_ch, count_ch)
            at_sub = lax.rem(lax.axis_index("sub") + count_sub - away_sub, count_sub)
            start = pl.multiple_of((at_ch * count_sub + at_sub) * width, width)
            field_ref[:, pl.ds(start, width), :] = blocks[away_ch * count_sub + away_sub][...]

    def field_of(pair):
        return field_ref[pair]

    def dot(left, right):
        return jnp.dot(left, right, preferred_element_type=jnp.float32)

    size = pairs_at_once(pairs, lat)
    for first in range(0, pairs, size):
        rows = window(field_of, first, size, last)
        products = dot(rows, taps_one_ref[0]) + dot(rows, taps_one_ref[1])
        upper, lower = split_two(gelu(add_lat_taps(products, lat)))
        upper_ref[pl.ds(first, size)] = upper.reshape(size, lat, wide)
        lower_ref[pl.ds(first, size)] = lower.reshape(size, lat, wide)
    size = pairs_at_once(pairs - 2, lat)
    for first in range(1, pairs - 1, size):
        rows_upper = window(lambda pair: upper_ref[pair], first, size, last)
        rows_lower = window(lambda pair: lower_ref[pair], first, size, last)
        products = dot(rows_upper, taps_two_ref[0]) + dot(rows_upper, taps_two_ref[1])
        products = products + dot(rows_lower, taps_two_ref[0])
        rounded = add_lat_taps(products, lat).astype(jnp.bfloat16).astype(jnp.float32)
        two_ref[pl.ds((first - 1) * lat, size * lat), :] = rounded
    half = two_ref.shape[0] // 2
    patches = jnp.concatenate(
        [two_ref[pl.ds(b, half, stride=2), :].astype(jnp.bfloat16) for b in range(2)], axis=-1
    )
    tokens_ref[...] = lax.dot_general(
        embed_ref[...], patches, (((1,), (1,)), ((), ())), preferred_element_type=jnp.float32
    ).astype(tokens_ref.dtype)


def call(kernel, out_shape, inputs, scratch=(), flops=0, moved=0):
    return pl.pallas_call(
        kernel,
        out_shape=out_shape,
        in_specs=[pl.BlockSpec(memory_space=pltpu.VMEM)] * len(inputs),
        out_specs=jax.tree.map(lambda unused: pl.BlockSpec(memory_space=pltpu.VMEM), out_shape),
        scratch_shapes=list(scratch),
        compiler_params=pltpu.CompilerParams(vmem_limit_bytes=VMEM_BYTES),
        cost_estimate=pl.CostEstimate(flops=flops, bytes_accessed=moved, transcendentals=0),
    )(*inputs)


def turned(value, axis, away):
    count = lax.axis_size(axis)
    return lax.ppermute(value, axis, [(i, (i + away) % count) for i in range(count)])


def band_blocks(block, beside):
    rows = [block] + [turned(block, "ch", away) for away in range(1, lax.axis_size("ch"))]
    rows[1:], beside = lax.optimization_barrier((rows[1:], beside))
    blocks = []
    for row in rows:
        blocks.append(row)
        blocks.extend(turned(row, "sub", away) for away in range(1, lax.axis_size("sub")))
    return blocks, beside


def encode(weather, conv_first, conv_second, patch_embed):
    chans, lon, lat = weather.shape
    pairs, wide = lon // 2, 2 * chans
    embed = patch_embed.shape[1]
    shape = functools.partial(jax.ShapeDtypeStruct, dtype=jnp.bfloat16)
    low, high, packed = call(
        pack_kernel,
        (shape((1, lat, wide)), shape((1, lat, wide)), shape((pairs + 2, lat, wide))),
        (jnp.transpose(weather, (1, 2, 0)),),
        moved=weather.size * 10,
    )
    before = turned(high, "tok", 1)
    after = turned(low, "tok", -1)
    taps = shape((2, 4 * chans, 6 * chans))
    weights = call(
        weights_kernel,
        (taps, taps, shape((embed, 4 * chans))),
        (conv_first, conv_second, patch_embed),
        scratch=[pltpu.VMEM((patch_embed.shape[0], LANES), jnp.float32)],
        moved=conv_first.size * 20,
    )
    packed = lax.dynamic_update_slice_in_dim(packed, before, 0, 0)
    packed = lax.dynamic_update_slice_in_dim(packed, after, pairs + 1, 0)
    blocks, weights = band_blocks(packed, weights)
    full_lat = len(blocks) * lat
    held = pltpu.VMEM((pairs + 2, full_lat, wide), jnp.bfloat16)
    return call(
        functools.partial(encode_kernel, lax.axis_size("ch"), lax.axis_size("sub")),
        shape((embed, pairs * full_lat // 2)),
        (*blocks, *weights),
        scratch=[held, held, held, pltpu.VMEM((pairs * full_lat, wide), jnp.float32)],
        flops=2 * (pairs + 1) * full_lat * 4 * chans * 6 * chans * 5,
        moved=packed.size * 2 * len(blocks),
    )


def partial_kernel(first, tokens_ref, mixing_ref, sent_ref, kept_ref):
    width = sent_ref.shape[1]
    step = STEP if width % STEP == 0 else width
    tokens = tokens_ref[...]
    for at in range(0, width, step):
        product = jnp.dot(tokens, mixing_ref[:, pl.ds(first + at, step)], preferred_element_type=jnp.float32)
        kept_ref[:, pl.ds(at, step)] = product[: kept_ref.shape[0]]
        sent_ref[:, pl.ds(at, step)] = product[kept_ref.shape[0] :].astype(sent_ref.dtype)


def partial(tokens, token_mixing, first, width, rows):
    return call(
        functools.partial(partial_kernel, first),
        (
            jax.ShapeDtypeStruct((rows, width), jnp.bfloat16),
            jax.ShapeDtypeStruct((tokens.shape[0] - rows, width), jnp.float32),
        ),
        (tokens, token_mixing),
    )


def lift(tokens, token_mixing, pieces):
    count = lax.axis_size("tok")
    rows = tokens.shape[0] // count
    width = token_mixing.shape[1] // pieces
    travelling, kept = [], []
    for piece in range(pieces):
        sent, others = partial(tokens, token_mixing, piece * width, width, rows)
        travelling.append(sent)
        kept.append(others)
    for step in range(1, count):
        for piece in range(pieces):
            arrived = turned(travelling[piece], "tok", 1).astype(jnp.float32)
            at = (count - 1 - step) * rows
            summed = arrived + kept[piece][at : at + rows]
            if step == count - 1:
                summed = gelu(summed)
            travelling[piece] = summed.astype(jnp.bfloat16)
    return jnp.concatenate(travelling, axis=1)


def local(weather, conv_first, conv_second, patch_embed, token_mixing):
    tokens = encode(weather, conv_first, conv_second, patch_embed)
    return lift(tokens, token_mixing, PIECES)


def solution(mesh):
    placed = (P("groups", "tok", ("ch", "sub")), P(), P(), P(), P("tok", ("ch", "sub")))
    return jax.shard_map(
        local,
        mesh=mesh,
        in_specs=placed,
        out_specs=P(("groups", "tok"), ("ch", "sub")),
        check_vma=False,
    )
```

```python
import functools

import jax
import jax.numpy as jnp
from jax import lax
from jax.experimental import pallas as pl
from jax.experimental.pallas import tpu as pltpu
from jax.sharding import PartitionSpec as P

PIECES = 4
STEP = 256
LANES = 128
VMEM_BYTES = 24 * 1024 * 1024
ROWS_AT_ONCE = 1024


def pack_kernel(field_ref, packed_ref):
    lon, lat, chans = field_ref.shape
    pairs = field_ref[...].reshape(lon // 2, 2, lat, chans)
    packed_ref[...] = jnp.concatenate([pairs[:, 0], pairs[:, 1]], axis=-1).astype(packed_ref.dtype)


def join_kernel(count_ch, count_sub, *refs):
    blocks, (field_ref, low_ref, high_ref) = refs[:-3], refs[-3:]
    pairs, lat, wide = field_ref.shape
    width = lat // (count_ch * count_sub)
    for away_ch in range(count_ch):
        for away_sub in range(count_sub):
            at_ch = lax.rem(lax.axis_index("ch") + count_ch - away_ch, count_ch)
            at_sub = lax.rem(lax.axis_index("sub") + count_sub - away_sub, count_sub)
            here = pl.ds(pl.multiple_of((at_ch * count_sub + at_sub) * width, width), width)
            block = blocks[away_ch * count_sub + away_sub][...]
            field_ref[:, here, :] = block
            low_ref[:, here, :] = block[:1]
            high_ref[:, here, :] = block[pairs - 1 :]


def split_two(value):
    upper = value.astype(jnp.bfloat16)
    return upper, (value - upper.astype(jnp.float32)).astype(jnp.bfloat16)


def spread_taps(kernel_ref):
    chans = kernel_ref.shape[1]
    nothing = jnp.zeros((chans, kernel_ref.shape[2]), jnp.float32)
    rows = []
    for tap in range(3):
        taps = [kernel_ref[3 * turn + tap] for turn in range(3)]
        rows.append(jnp.concatenate([taps[1], taps[2], nothing, taps[0]], axis=-1))
        rows.append(jnp.concatenate([taps[0], taps[1], taps[2], nothing], axis=-1))
    return jnp.concatenate(rows, axis=0).T


def weights_kernel(first_ref, second_ref, embed_ref, taps_one_ref, taps_two_ref, embed_out_ref, scratch):
    for source, target in ((first_ref, taps_one_ref), (second_ref, taps_two_ref)):
        upper, lower = split_two(spread_taps(source))
        target[0] = upper
        target[1] = lower
    chans = embed_ref.shape[0] // 4
    embed = embed_ref.shape[1]
    count = lax.axis_size("tok")
    turn = lax.axis_index("tok") * (embed // count)
    turned_embed = pltpu.roll(embed_ref[...].astype(jnp.float32), lax.rem(embed - turn, embed), axis=1)
    for first in range(0, embed, LANES):
        scratch[...] = turned_embed[:, first : first + LANES]
        ordered = [scratch[pl.ds(2 * a + b, chans, stride=4), :] for b in range(2) for a in range(2)]
        rows = jnp.concatenate(ordered, axis=0).T
        embed_out_ref[pl.ds(first, LANES), :] = rows.astype(embed_out_ref.dtype)


def pairs_at_once(pairs, lat):
    best = 1
    for size in range(1, pairs + 1):
        if pairs % size == 0 and size * lat <= ROWS_AT_ONCE:
            best = size
    return best


def window(pair_at, pairs):
    rows = []
    for pair in pairs:
        here = pair_at(pair)
        lane = lax.broadcasted_iota(jnp.int32, here.shape, 1)
        beside = jnp.where(lane < here.shape[1] // 2, pair_at(pair + 1), pair_at(pair - 1))
        rows.append(jnp.concatenate([here, beside], axis=-1))
    return jnp.concatenate(rows, axis=0)


def add_lat_taps(products, lat):
    wide = products.shape[1] // 3
    count = products.shape[0]
    row = lax.broadcasted_iota(jnp.int32, (count, wide), 0) % lat
    below = pltpu.roll(products[:, :wide], 1, axis=0)
    above = pltpu.roll(products[:, 2 * wide :], count - 1, axis=0)
    return (
        products[:, wide : 2 * wide]
        + jnp.where(row == 0, 0.0, below)
        + jnp.where(row == lat - 1, 0.0, above)
    )


def gelu(value):
    return 0.5 * value * (1.0 + lax.erf(value * (0.5**0.5)))


def dot(left, right):
    return jnp.dot(left, right, preferred_element_type=jnp.float32)


def first_conv(field_at, pairs, taps_ref, lat):
    rows = window(field_at, pairs)
    products = dot(rows, taps_ref[0]) + dot(rows, taps_ref[1])
    parts = split_two(gelu(add_lat_taps(products, lat)))
    return [part.reshape(len(pairs), lat, part.shape[1]) for part in parts]


def second_conv(upper_at, lower_at, pairs, taps_ref, lat):
    upper, lower = window(upper_at, pairs), window(lower_at, pairs)
    products = dot(upper, taps_ref[0]) + dot(upper, taps_ref[1]) + dot(lower, taps_ref[0])
    return add_lat_taps(products, lat).astype(jnp.bfloat16).astype(jnp.float32)


def embed_patches(two_ref, embed_ref):
    half = two_ref.shape[0] // 2
    patches = jnp.concatenate(
        [two_ref[pl.ds(b, half, stride=2), :].astype(jnp.bfloat16) for b in range(2)], axis=-1
    )
    return lax.dot_general(
        embed_ref[...], patches, (((1,), (1,)), ((), ())), preferred_element_type=jnp.float32
    ).astype(jnp.bfloat16)


def runs(first, last, lat):
    size = pairs_at_once(last - first, lat)
    return [list(range(at, at + size)) for at in range(first, last, size)]


def inner_kernel(
    field_ref, taps_one_ref, taps_two_ref, embed_ref, tokens_ref, upper_edge_ref, lower_edge_ref, upper_ref, lower_ref, two_ref
):
    pairs, lat, wide = field_ref.shape
    for run in runs(1, pairs - 1, lat):
        upper, lower = first_conv(lambda pair: field_ref[pair], run, taps_one_ref, lat)
        upper_ref[pl.ds(run[0], len(run))] = upper
        lower_ref[pl.ds(run[0], len(run))] = lower
    for inside, edge in ((upper_ref, upper_edge_ref), (lower_ref, lower_edge_ref)):
        edge[pl.ds(0, 2)] = inside[pl.ds(1, 2)]
        edge[pl.ds(2, 2)] = inside[pl.ds(pairs - 3, 2)]
    for run in runs(2, pairs - 2, lat):
        two = second_conv(lambda pair: upper_ref[pair], lambda pair: lower_ref[pair], run, taps_two_ref, lat)
        two_ref[pl.ds((run[0] - 2) * lat, len(run) * lat), :] = two
    tokens_ref[...] = embed_patches(two_ref, embed_ref)


def outer_kernel(
    field_ref, before_ref, after_ref, upper_edge_ref, lower_edge_ref, taps_one_ref, taps_two_ref, embed_ref, inner_ref, tokens_ref, two_ref
):
    pairs, lat, wide = field_ref.shape

    def field_at(pair):
        if pair < 0:
            return before_ref[0]
        if pair >= pairs:
            return after_ref[0]
        return field_ref[pair]

    outermost = [-1, 0, pairs - 1, pairs]
    next_inside = [1, 2, pairs - 3, pairs - 2]
    upper, lower = first_conv(field_at, outermost, taps_one_ref, lat)

    def hidden_at(found, edge_ref):
        def at(pair):
            if pair in outermost:
                return found[outermost.index(pair)]
            return edge_ref[next_inside.index(pair)]

        return at

    two_ref[...] = second_conv(
        hidden_at(upper, upper_edge_ref), hidden_at(lower, lower_edge_ref), [0, 1, pairs - 2, pairs - 1], taps_two_ref, lat
    )
    outer = embed_patches(two_ref, embed_ref)
    inner = inner_ref.shape[1]
    tokens_ref[:, :lat] = outer[:, :lat]
    tokens_ref[:, pl.ds(lat, inner)] = inner_ref[...]
    tokens_ref[:, pl.ds(lat + inner, lat)] = outer[:, lat:]


def call(kernel, out_shape, inputs, scratch=(), flops=0, moved=0):
    return pl.pallas_call(
        kernel,
        out_shape=out_shape,
        in_specs=[pl.BlockSpec(memory_space=pltpu.VMEM)] * len(inputs),
        out_specs=jax.tree.map(lambda unused: pl.BlockSpec(memory_space=pltpu.VMEM), out_shape),
        scratch_shapes=list(scratch),
        compiler_params=pltpu.CompilerParams(vmem_limit_bytes=VMEM_BYTES),
        cost_estimate=pl.CostEstimate(flops=flops, bytes_accessed=moved, transcendentals=0),
    )(*inputs)


def turned(value, axis, away):
    count = lax.axis_size(axis)
    return lax.ppermute(value, axis, [(i, (i + away) % count) for i in range(count)])


def band_blocks(block, beside):
    rows = [block] + [turned(block, "ch", away) for away in range(1, lax.axis_size("ch"))]
    rows[1:], beside = lax.optimization_barrier((rows[1:], beside))
    blocks = []
    for row in rows:
        blocks.append(row)
        blocks.extend(turned(row, "sub", away) for away in range(1, lax.axis_size("sub")))
    return blocks, beside


def encode(weather, conv_first, conv_second, patch_embed):
    chans, lon, lat = weather.shape
    pairs, wide = lon // 2, 2 * chans
    embed = patch_embed.shape[1]
    shape = functools.partial(jax.ShapeDtypeStruct, dtype=jnp.bfloat16)
    packed = call(
        pack_kernel, shape((pairs, lat, wide)), (jnp.transpose(weather, (1, 2, 0)),), moved=weather.size * 10
    )
    taps = shape((2, 4 * chans, 6 * chans))
    weights = call(
        weights_kernel,
        (taps, taps, shape((embed, 4 * chans))),
        (conv_first, conv_second, patch_embed),
        scratch=[pltpu.VMEM((patch_embed.shape[0], LANES), jnp.float32)],
        moved=conv_first.size * 20,
    )
    blocks, weights = band_blocks(packed, weights)
    lat = len(blocks) * lat
    edge = shape((1, lat, wide))
    field, low, high = call(
        functools.partial(join_kernel, lax.axis_size("ch"), lax.axis_size("sub")),
        (shape((pairs, lat, wide)), edge, edge),
        blocks,
        moved=packed.size * 4 * len(blocks),
    )
    before = turned(high, "tok", 1)
    after = turned(low, "tok", -1)
    work = 2 * lat * 4 * chans * 6 * chans * 5
    held = shape((4, lat, wide))
    hidden = pltpu.VMEM((pairs, lat, wide), jnp.bfloat16)
    inner, upper_edge, lower_edge = call(
        inner_kernel,
        (shape((embed, (pairs - 4) * lat // 2)), held, held),
        (field, *weights),
        scratch=[hidden, hidden, pltpu.VMEM(((pairs - 4) * lat, wide), jnp.float32)],
        flops=work * (pairs - 3),
        moved=field.size * 2,
    )
    return call(
        outer_kernel,
        shape((embed, pairs * lat // 2)),
        (field, before, after, upper_edge, lower_edge, *weights, inner),
        scratch=[pltpu.VMEM((4 * lat, wide), jnp.float32)],
        flops=work * 4,
        moved=field.size * 2,
    )


def partial_kernel(first, tokens_ref, mixing_ref, sent_ref, kept_ref):
    width = sent_ref.shape[1]
    step = STEP if width % STEP == 0 else width
    tokens = tokens_ref[...]
    for at in range(0, width, step):
        product = jnp.dot(tokens, mixing_ref[:, pl.ds(first + at, step)], preferred_element_type=jnp.float32)
        kept_ref[:, pl.ds(at, step)] = product[: kept_ref.shape[0]]
        sent_ref[:, pl.ds(at, step)] = product[kept_ref.shape[0] :].astype(sent_ref.dtype)


def partial(tokens, token_mixing, first, width, rows):
    return call(
        functools.partial(partial_kernel, first),
        (
            jax.ShapeDtypeStruct((rows, width), jnp.bfloat16),
            jax.ShapeDtypeStruct((tokens.shape[0] - rows, width), jnp.float32),
        ),
        (tokens, token_mixing),
    )


def lift(tokens, token_mixing, pieces):
    count = lax.axis_size("tok")
    rows = tokens.shape[0] // count
    width = token_mixing.shape[1] // pieces
    travelling, kept = [], []
    for piece in range(pieces):
        sent, others = partial(tokens, token_mixing, piece * width, width, rows)
        travelling.append(sent)
        kept.append(others)
    for step in range(1, count):
        for piece in range(pieces):
            arrived = turned(travelling[piece], "tok", 1).astype(jnp.float32)
            at = (count - 1 - step) * rows
            summed = arrived + kept[piece][at : at + rows]
            if step == count - 1:
                summed = gelu(summed)
            travelling[piece] = summed.astype(jnp.bfloat16)
    return jnp.concatenate(travelling, axis=1)


def local(weather, conv_first, conv_second, patch_embed, token_mixing):
    tokens = encode(weather, conv_first, conv_second, patch_embed)
    return lift(tokens, token_mixing, PIECES)


def solution(mesh):
    placed = (P("groups", "tok", ("ch", "sub")), P(), P(), P(), P("tok", ("ch", "sub")))
    return jax.shard_map(
        local,
        mesh=mesh,
        in_specs=placed,
        out_specs=P(("groups", "tok"), ("ch", "sub")),
        check_vma=False,
    )
```

```python
import functools

import jax
import jax.numpy as jnp
from jax import lax
from jax.experimental import pallas as pl
from jax.experimental.pallas import tpu as pltpu
from jax.sharding import PartitionSpec as P

PIECES = 4
STEP = 256
LANES = 128
VMEM_BYTES = 24 * 1024 * 1024
ROWS_AT_ONCE = 1024


def pack_kernel(field_ref, packed_ref):
    lon, lat, chans = field_ref.shape
    pairs = field_ref[...].reshape(lon // 2, 2, lat, chans)
    packed_ref[...] = jnp.concatenate([pairs[:, 0], pairs[:, 1]], axis=-1).astype(packed_ref.dtype)


def join_kernel(count_ch, count_sub, *refs):
    blocks, (field_ref, low_ref, high_ref) = refs[:-3], refs[-3:]
    pairs, lat, wide = field_ref.shape
    width = lat // (count_ch * count_sub)
    for away_ch in range(count_ch):
        for away_sub in range(count_sub):
            at_ch = lax.rem(lax.axis_index("ch") + count_ch - away_ch, count_ch)
            at_sub = lax.rem(lax.axis_index("sub") + count_sub - away_sub, count_sub)
            here = pl.ds(pl.multiple_of((at_ch * count_sub + at_sub) * width, width), width)
            block = blocks[away_ch * count_sub + away_sub][...]
            field_ref[:, here, :] = block
            low_ref[:, here, :] = block[:1]
            high_ref[:, here, :] = block[pairs - 1 :]


def split_two(value):
    upper = value.astype(jnp.bfloat16)
    return upper, (value - upper.astype(jnp.float32)).astype(jnp.bfloat16)


def spread_taps(kernel_ref):
    chans = kernel_ref.shape[1]
    nothing = jnp.zeros((chans, kernel_ref.shape[2]), jnp.float32)
    rows = []
    for tap in range(3):
        taps = [kernel_ref[3 * turn + tap] for turn in range(3)]
        rows.append(jnp.concatenate([taps[1], taps[2], nothing, taps[0]], axis=-1))
        rows.append(jnp.concatenate([taps[0], taps[1], taps[2], nothing], axis=-1))
    return jnp.concatenate(rows, axis=0).T


def weights_kernel(first_ref, second_ref, embed_ref, taps_one_ref, taps_two_ref, embed_out_ref, scratch):
    for source, target in ((first_ref, taps_one_ref), (second_ref, taps_two_ref)):
        upper, lower = split_two(spread_taps(source))
        target[0] = upper
        target[1] = lower
    chans = embed_ref.shape[0] // 4
    embed = embed_ref.shape[1]
    count = lax.axis_size("tok")
    turn = lax.rem(lax.axis_index("tok") + 1, count) * (embed // count)
    turned_embed = pltpu.roll(embed_ref[...].astype(jnp.float32), lax.rem(embed - turn, embed), axis=1)
    for first in range(0, embed, LANES):
        scratch[...] = turned_embed[:, first : first + LANES]
        ordered = [scratch[pl.ds(2 * a + b, chans, stride=4), :] for b in range(2) for a in range(2)]
        rows = jnp.concatenate(ordered, axis=0).T
        embed_out_ref[pl.ds(first, LANES), :] = rows.astype(embed_out_ref.dtype)


def pairs_at_once(pairs, lat):
    best = 1
    for size in range(1, pairs + 1):
        if pairs % size == 0 and size * lat <= ROWS_AT_ONCE:
            best = size
    return best


def window(pair_at, pairs):
    rows = []
    for pair in pairs:
        here = pair_at(pair)
        lane = lax.broadcasted_iota(jnp.int32, here.shape, 1)
        beside = jnp.where(lane < here.shape[1] // 2, pair_at(pair + 1), pair_at(pair - 1))
        rows.append(jnp.concatenate([here, beside], axis=-1))
    return jnp.concatenate(rows, axis=0)


def add_lat_taps(products, lat):
    wide = products.shape[1] // 3
    count = products.shape[0]
    row = lax.broadcasted_iota(jnp.int32, (count, wide), 0) % lat
    below = pltpu.roll(products[:, :wide], 1, axis=0)
    above = pltpu.roll(products[:, 2 * wide :], count - 1, axis=0)
    return (
        products[:, wide : 2 * wide]
        + jnp.where(row == 0, 0.0, below)
        + jnp.where(row == lat - 1, 0.0, above)
    )


def gelu(value):
    return 0.5 * value * (1.0 + lax.erf(value * (0.5**0.5)))


def dot(left, right):
    return jnp.dot(left, right, preferred_element_type=jnp.float32)


def first_conv(field_at, pairs, taps_ref, lat):
    rows = window(field_at, pairs)
    products = dot(rows, taps_ref[0]) + dot(rows, taps_ref[1])
    parts = split_two(gelu(add_lat_taps(products, lat)))
    return [part.reshape(len(pairs), lat, part.shape[1]) for part in parts]


def second_conv(upper_at, lower_at, pairs, taps_ref, lat):
    upper, lower = window(upper_at, pairs), window(lower_at, pairs)
    products = dot(upper, taps_ref[0]) + dot(upper, taps_ref[1]) + dot(lower, taps_ref[0])
    return add_lat_taps(products, lat).astype(jnp.bfloat16).astype(jnp.float32)


def embed_patches(two_ref, embed_ref):
    half = two_ref.shape[0] // 2
    patches = jnp.concatenate(
        [two_ref[pl.ds(b, half, stride=2), :].astype(jnp.bfloat16) for b in range(2)], axis=-1
    )
    return lax.dot_general(
        embed_ref[...], patches, (((1,), (1,)), ((), ())), preferred_element_type=jnp.float32
    ).astype(jnp.bfloat16)


def runs(first, last, lat):
    size = pairs_at_once(last - first, lat)
    return [list(range(at, at + size)) for at in range(first, last, size)]


def inner_kernel(
    field_ref, taps_one_ref, taps_two_ref, embed_ref, tokens_ref, upper_edge_ref, lower_edge_ref, upper_ref, lower_ref, two_ref
):
    pairs, lat, wide = field_ref.shape
    for run in runs(1, pairs - 1, lat):
        upper, lower = first_conv(lambda pair: field_ref[pair], run, taps_one_ref, lat)
        upper_ref[pl.ds(run[0], len(run))] = upper
        lower_ref[pl.ds(run[0], len(run))] = lower
    for inside, edge in ((upper_ref, upper_edge_ref), (lower_ref, lower_edge_ref)):
        edge[pl.ds(0, 2)] = inside[pl.ds(1, 2)]
        edge[pl.ds(2, 2)] = inside[pl.ds(pairs - 3, 2)]
    for run in runs(2, pairs - 2, lat):
        two = second_conv(lambda pair: upper_ref[pair], lambda pair: lower_ref[pair], run, taps_two_ref, lat)
        two_ref[pl.ds((run[0] - 2) * lat, len(run) * lat), :] = two
    tokens_ref[...] = embed_patches(two_ref, embed_ref)


def outer_kernel(
    field_ref, before_ref, after_ref, upper_edge_ref, lower_edge_ref, taps_one_ref, taps_two_ref, embed_ref, inner_ref, tokens_ref, two_ref
):
    pairs, lat, wide = field_ref.shape

    def field_at(pair):
        if pair < 0:
            return before_ref[0]
        if pair >= pairs:
            return after_ref[0]
        return field_ref[pair]

    outermost = [-1, 0, pairs - 1, pairs]
    next_inside = [1, 2, pairs - 3, pairs - 2]
    upper, lower = first_conv(field_at, outermost, taps_one_ref, lat)

    def hidden_at(found, edge_ref):
        def at(pair):
            if pair in outermost:
                return found[outermost.index(pair)]
            return edge_ref[next_inside.index(pair)]

        return at

    two_ref[...] = second_conv(
        hidden_at(upper, upper_edge_ref), hidden_at(lower, lower_edge_ref), [0, 1, pairs - 2, pairs - 1], taps_two_ref, lat
    )
    outer = embed_patches(two_ref, embed_ref)
    inner = inner_ref.shape[1]
    tokens_ref[:, :lat] = outer[:, :lat]
    tokens_ref[:, pl.ds(lat, inner)] = inner_ref[...]
    tokens_ref[:, pl.ds(lat + inner, lat)] = outer[:, lat:]


def call(kernel, out_shape, inputs, scratch=(), flops=0, moved=0):
    return pl.pallas_call(
        kernel,
        out_shape=out_shape,
        in_specs=[pl.BlockSpec(memory_space=pltpu.VMEM)] * len(inputs),
        out_specs=jax.tree.map(lambda unused: pl.BlockSpec(memory_space=pltpu.VMEM), out_shape),
        scratch_shapes=list(scratch),
        compiler_params=pltpu.CompilerParams(vmem_limit_bytes=VMEM_BYTES),
        cost_estimate=pl.CostEstimate(flops=flops, bytes_accessed=moved, transcendentals=0),
    )(*inputs)


def turned(value, axis, away):
    count = lax.axis_size(axis)
    return lax.ppermute(value, axis, [(i, (i + away) % count) for i in range(count)])


def band_blocks(block, beside):
    rows = [block] + [turned(block, "ch", away) for away in range(1, lax.axis_size("ch"))]
    rows[1:], beside = lax.optimization_barrier((rows[1:], beside))
    blocks = []
    for row in rows:
        blocks.append(row)
        blocks.extend(turned(row, "sub", away) for away in range(1, lax.axis_size("sub")))
    return blocks, beside


def encode(weather, conv_first, conv_second, patch_embed):
    chans, lon, lat = weather.shape
    pairs, wide = lon // 2, 2 * chans
    embed = patch_embed.shape[1]
    shape = functools.partial(jax.ShapeDtypeStruct, dtype=jnp.bfloat16)
    packed = call(
        pack_kernel, shape((pairs, lat, wide)), (jnp.transpose(weather, (1, 2, 0)),), moved=weather.size * 10
    )
    taps = shape((2, 4 * chans, 6 * chans))
    weights = call(
        weights_kernel,
        (taps, taps, shape((embed, 4 * chans))),
        (conv_first, conv_second, patch_embed),
        scratch=[pltpu.VMEM((patch_embed.shape[0], LANES), jnp.float32)],
        moved=conv_first.size * 20,
    )
    blocks, weights = band_blocks(packed, weights)
    lat = len(blocks) * lat
    edge = shape((1, lat, wide))
    field, low, high = call(
        functools.partial(join_kernel, lax.axis_size("ch"), lax.axis_size("sub")),
        (shape((pairs, lat, wide)), edge, edge),
        blocks,
        moved=packed.size * 4 * len(blocks),
    )
    before = turned(high, "tok", 1)
    after = turned(low, "tok", -1)
    work = 2 * lat * 4 * chans * 6 * chans * 5
    held = shape((4, lat, wide))
    hidden = pltpu.VMEM((pairs, lat, wide), jnp.bfloat16)
    inner, upper_edge, lower_edge = call(
        inner_kernel,
        (shape((embed, (pairs - 4) * lat // 2)), held, held),
        (field, *weights),
        scratch=[hidden, hidden, pltpu.VMEM(((pairs - 4) * lat, wide), jnp.float32)],
        flops=work * (pairs - 3),
        moved=field.size * 2,
    )
    return call(
        outer_kernel,
        shape((embed, pairs * lat // 2)),
        (field, before, after, upper_edge, lower_edge, *weights, inner),
        scratch=[pltpu.VMEM((4 * lat, wide), jnp.float32)],
        flops=work * 4,
        moved=field.size * 2,
    )


def sent_kernel(tokens_ref, mixing_ref, *sent_refs):
    rows, width = sent_refs[0].shape
    step = STEP if width % STEP == 0 else width
    tokens = tokens_ref[:rows]
    for piece, sent_ref in enumerate(sent_refs):
        for at in range(0, width, step):
            product = dot(tokens, mixing_ref[:, pl.ds(piece * width + at, step)])
            sent_ref[:, pl.ds(at, step)] = product.astype(sent_ref.dtype)


def hop_kernel(first, arrived_ref, tokens_ref, mixing_ref, sent_ref, kept_ref):
    rows, width = sent_ref.shape
    step = STEP if width % STEP == 0 else width
    tokens = tokens_ref[rows:]
    for at in range(0, width, step):
        product = dot(tokens, mixing_ref[:, pl.ds(first + at, step)])
        arrived = arrived_ref[:, pl.ds(at, step)].astype(jnp.float32)
        sent_ref[:, pl.ds(at, step)] = (arrived + product[:rows]).astype(sent_ref.dtype)
        kept_ref[:, pl.ds(at, step)] = product[rows:]


def lift(tokens, token_mixing, pieces):
    count = lax.axis_size("tok")
    embed = tokens.shape[0]
    rows = embed // count
    width = token_mixing.shape[1] // pieces
    sent = jax.ShapeDtypeStruct((rows, width), jnp.bfloat16)
    travelling = list(call(sent_kernel, [sent] * pieces, (tokens, token_mixing)))
    kept = [None] * pieces
    for step in range(1, count):
        for piece in range(pieces):
            arrived = turned(travelling[piece], "tok", -1)
            if step == 1:
                travelling[piece], kept[piece] = call(
                    functools.partial(hop_kernel, piece * width),
                    [sent, jax.ShapeDtypeStruct((embed - 2 * rows, width), jnp.float32)],
                    (arrived, tokens, token_mixing),
                )
            else:
                at = (step - 2) * rows
                summed = arrived.astype(jnp.float32) + kept[piece][at : at + rows]
                if step == count - 1:
                    summed = gelu(summed)
                travelling[piece] = summed.astype(jnp.bfloat16)
    return jnp.concatenate(travelling, axis=1)


def local(weather, conv_first, conv_second, patch_embed, token_mixing):
    tokens = encode(weather, conv_first, conv_second, patch_embed)
    return lift(tokens, token_mixing, PIECES)


def solution(mesh):
    placed = (P("groups", "tok", ("ch", "sub")), P(), P(), P(), P("tok", ("ch", "sub")))
    return jax.shard_map(
        local,
        mesh=mesh,
        in_specs=placed,
        out_specs=P(("groups", "tok"), ("ch", "sub")),
        check_vma=False,
    )
```

```python
import functools

import jax
import jax.numpy as jnp
from jax import lax
from jax.experimental import pallas as pl
from jax.experimental.pallas import tpu as pltpu
from jax.sharding import PartitionSpec as P

PIECES = 2
STEP = 256
LANES = 128
VMEM_BYTES = 24 * 1024 * 1024
ROWS_AT_ONCE = 1024


def pack_kernel(field_ref, packed_ref):
    lon, lat, chans = field_ref.shape
    pairs = field_ref[...].reshape(lon // 2, 2, lat, chans)
    packed_ref[...] = jnp.concatenate([pairs[:, 0], pairs[:, 1]], axis=-1).astype(packed_ref.dtype)


def join_kernel(count_ch, count_sub, *refs):
    blocks, (field_ref, low_ref, high_ref) = refs[:-3], refs[-3:]
    pairs, lat, wide = field_ref.shape
    width = lat // (count_ch * count_sub)
    for away_ch in range(count_ch):
        for away_sub in range(count_sub):
            at_ch = lax.rem(lax.axis_index("ch") + count_ch - away_ch, count_ch)
            at_sub = lax.rem(lax.axis_index("sub") + count_sub - away_sub, count_sub)
            here = pl.ds(pl.multiple_of((at_ch * count_sub + at_sub) * width, width), width)
            block = blocks[away_ch * count_sub + away_sub][...]
            field_ref[:, here, :] = block
            low_ref[:, here, :] = block[:1]
            high_ref[:, here, :] = block[pairs - 1 :]


def split_two(value):
    upper = value.astype(jnp.bfloat16)
    return upper, (value - upper.astype(jnp.float32)).astype(jnp.bfloat16)


def spread_taps(kernel_ref):
    chans = kernel_ref.shape[1]
    nothing = jnp.zeros((chans, kernel_ref.shape[2]), jnp.float32)
    rows = []
    for tap in range(3):
        taps = [kernel_ref[3 * turn + tap] for turn in range(3)]
        rows.append(jnp.concatenate([taps[1], taps[2], nothing, taps[0]], axis=-1))
        rows.append(jnp.concatenate([taps[0], taps[1], taps[2], nothing], axis=-1))
    return jnp.concatenate(rows, axis=0).T


def weights_kernel(first_ref, second_ref, embed_ref, taps_one_ref, taps_two_ref, embed_out_ref, scratch):
    for source, target in ((first_ref, taps_one_ref), (second_ref, taps_two_ref)):
        upper, lower = split_two(spread_taps(source))
        target[0] = upper
        target[1] = lower
    chans = embed_ref.shape[0] // 4
    embed = embed_ref.shape[1]
    count = lax.axis_size("tok")
    turn = lax.rem(lax.axis_index("tok") + 1, count) * (embed // count)
    turned_embed = pltpu.roll(embed_ref[...].astype(jnp.float32), lax.rem(embed - turn, embed), axis=1)
    for first in range(0, embed, LANES):
        scratch[...] = turned_embed[:, first : first + LANES]
        ordered = [scratch[pl.ds(2 * a + b, chans, stride=4), :] for b in range(2) for a in range(2)]
        rows = jnp.concatenate(ordered, axis=0).T
        embed_out_ref[pl.ds(first, LANES), :] = rows.astype(embed_out_ref.dtype)


def pairs_at_once(pairs, lat):
    best = 1
    for size in range(1, pairs + 1):
        if pairs % size == 0 and size * lat <= ROWS_AT_ONCE:
            best = size
    return best


def window(pair_at, pairs):
    rows = []
    for pair in pairs:
        here = pair_at(pair)
        lane = lax.broadcasted_iota(jnp.int32, here.shape, 1)
        beside = jnp.where(lane < here.shape[1] // 2, pair_at(pair + 1), pair_at(pair - 1))
        rows.append(jnp.concatenate([here, beside], axis=-1))
    return jnp.concatenate(rows, axis=0)


def add_lat_taps(products, lat):
    wide = products.shape[1] // 3
    count = products.shape[0]
    row = lax.broadcasted_iota(jnp.int32, (count, wide), 0) % lat
    below = pltpu.roll(products[:, :wide], 1, axis=0)
    above = pltpu.roll(products[:, 2 * wide :], count - 1, axis=0)
    return (
        products[:, wide : 2 * wide]
        + jnp.where(row == 0, 0.0, below)
        + jnp.where(row == lat - 1, 0.0, above)
    )


def gelu(value):
    return 0.5 * value * (1.0 + lax.erf(value * (0.5**0.5)))


def dot(left, right):
    return jnp.dot(left, right, preferred_element_type=jnp.float32)


def first_conv(field_at, pairs, taps_ref, lat):
    rows = window(field_at, pairs)
    products = dot(rows, taps_ref[0]) + dot(rows, taps_ref[1])
    parts = split_two(gelu(add_lat_taps(products, lat)))
    return [part.reshape(len(pairs), lat, part.shape[1]) for part in parts]


def second_conv(upper_at, lower_at, pairs, taps_ref, lat):
    upper, lower = window(upper_at, pairs), window(lower_at, pairs)
    products = dot(upper, taps_ref[0]) + dot(upper, taps_ref[1]) + dot(lower, taps_ref[0])
    return add_lat_taps(products, lat).astype(jnp.bfloat16).astype(jnp.float32)


def embed_patches(two_ref, embed_ref):
    half = two_ref.shape[0] // 2
    patches = jnp.concatenate(
        [two_ref[pl.ds(b, half, stride=2), :].astype(jnp.bfloat16) for b in range(2)], axis=-1
    )
    return lax.dot_general(
        embed_ref[...], patches, (((1,), (1,)), ((), ())), preferred_element_type=jnp.float32
    ).astype(jnp.bfloat16)


def runs(first, last, lat):
    size = pairs_at_once(last - first, lat)
    return [list(range(at, at + size)) for at in range(first, last, size)]


def inner_kernel(
    field_ref, taps_one_ref, taps_two_ref, embed_ref, tokens_ref, upper_edge_ref, lower_edge_ref, upper_ref, lower_ref, two_ref
):
    pairs, lat, wide = field_ref.shape
    for run in runs(1, pairs - 1, lat):
        upper, lower = first_conv(lambda pair: field_ref[pair], run, taps_one_ref, lat)
        upper_ref[pl.ds(run[0], len(run))] = upper
        lower_ref[pl.ds(run[0], len(run))] = lower
    for inside, edge in ((upper_ref, upper_edge_ref), (lower_ref, lower_edge_ref)):
        edge[pl.ds(0, 2)] = inside[pl.ds(1, 2)]
        edge[pl.ds(2, 2)] = inside[pl.ds(pairs - 3, 2)]
    for run in runs(2, pairs - 2, lat):
        two = second_conv(lambda pair: upper_ref[pair], lambda pair: lower_ref[pair], run, taps_two_ref, lat)
        two_ref[pl.ds((run[0] - 2) * lat, len(run) * lat), :] = two
    tokens_ref[...] = embed_patches(two_ref, embed_ref)


def outer_kernel(
    field_ref, before_ref, after_ref, upper_edge_ref, lower_edge_ref, taps_one_ref, taps_two_ref, embed_ref, inner_ref, tokens_ref, two_ref
):
    pairs, lat, wide = field_ref.shape

    def field_at(pair):
        if pair < 0:
            return before_ref[0]
        if pair >= pairs:
            return after_ref[0]
        return field_ref[pair]

    outermost = [-1, 0, pairs - 1, pairs]
    next_inside = [1, 2, pairs - 3, pairs - 2]
    upper, lower = first_conv(field_at, outermost, taps_one_ref, lat)

    def hidden_at(found, edge_ref):
        def at(pair):
            if pair in outermost:
                return found[outermost.index(pair)]
            return edge_ref[next_inside.index(pair)]

        return at

    two_ref[...] = second_conv(
        hidden_at(upper, upper_edge_ref), hidden_at(lower, lower_edge_ref), [0, 1, pairs - 2, pairs - 1], taps_two_ref, lat
    )
    outer = embed_patches(two_ref, embed_ref)
    inner = inner_ref.shape[1]
    tokens_ref[:, :lat] = outer[:, :lat]
    tokens_ref[:, pl.ds(lat, inner)] = inner_ref[...]
    tokens_ref[:, pl.ds(lat + inner, lat)] = outer[:, lat:]


def call(kernel, out_shape, inputs, scratch=(), flops=0, moved=0):
    return pl.pallas_call(
        kernel,
        out_shape=out_shape,
        in_specs=[pl.BlockSpec(memory_space=pltpu.VMEM)] * len(inputs),
        out_specs=jax.tree.map(lambda unused: pl.BlockSpec(memory_space=pltpu.VMEM), out_shape),
        scratch_shapes=list(scratch),
        compiler_params=pltpu.CompilerParams(vmem_limit_bytes=VMEM_BYTES),
        cost_estimate=pl.CostEstimate(flops=flops, bytes_accessed=moved, transcendentals=0),
    )(*inputs)


def turned(value, axis, away):
    count = lax.axis_size(axis)
    return lax.ppermute(value, axis, [(i, (i + away) % count) for i in range(count)])


def band_blocks(block, beside):
    rows = [block] + [turned(block, "ch", away) for away in range(1, lax.axis_size("ch"))]
    rows[1:], beside = lax.optimization_barrier((rows[1:], beside))
    blocks = []
    for row in rows:
        blocks.append(row)
        blocks.extend(turned(row, "sub", away) for away in range(1, lax.axis_size("sub")))
    return blocks, beside


def encode(weather, conv_first, conv_second, patch_embed):
    chans, lon, lat = weather.shape
    pairs, wide = lon // 2, 2 * chans
    embed = patch_embed.shape[1]
    shape = functools.partial(jax.ShapeDtypeStruct, dtype=jnp.bfloat16)
    packed = call(
        pack_kernel, shape((pairs, lat, wide)), (jnp.transpose(weather, (1, 2, 0)),), moved=weather.size * 10
    )
    taps = shape((2, 4 * chans, 6 * chans))
    weights = call(
        weights_kernel,
        (taps, taps, shape((embed, 4 * chans))),
        (conv_first, conv_second, patch_embed),
        scratch=[pltpu.VMEM((patch_embed.shape[0], LANES), jnp.float32)],
        moved=conv_first.size * 20,
    )
    blocks, weights = band_blocks(packed, weights)
    lat = len(blocks) * lat
    edge = shape((1, lat, wide))
    field, low, high = call(
        functools.partial(join_kernel, lax.axis_size("ch"), lax.axis_size("sub")),
        (shape((pairs, lat, wide)), edge, edge),
        blocks,
        moved=packed.size * 4 * len(blocks),
    )
    before = turned(high, "tok", 1)
    after = turned(low, "tok", -1)
    work = 2 * lat * 4 * chans * 6 * chans * 5
    held = shape((4, lat, wide))
    hidden = pltpu.VMEM((pairs, lat, wide), jnp.bfloat16)
    inner, upper_edge, lower_edge = call(
        inner_kernel,
        (shape((embed, (pairs - 4) * lat // 2)), held, held),
        (field, *weights),
        scratch=[hidden, hidden, pltpu.VMEM(((pairs - 4) * lat, wide), jnp.float32)],
        flops=work * (pairs - 3),
        moved=field.size * 2,
    )
    return call(
        outer_kernel,
        shape((embed, pairs * lat // 2)),
        (field, before, after, upper_edge, lower_edge, *weights, inner),
        scratch=[pltpu.VMEM((4 * lat, wide), jnp.float32)],
        flops=work * 4,
        moved=field.size * 2,
    )


def sent_kernel(tokens_ref, mixing_ref, *sent_refs):
    rows, width = sent_refs[0].shape
    step = STEP if width % STEP == 0 else width
    tokens = tokens_ref[:rows]
    for piece, sent_ref in enumerate(sent_refs):
        for at in range(0, width, step):
            product = dot(tokens, mixing_ref[:, pl.ds(piece * width + at, step)])
            sent_ref[:, pl.ds(at, step)] = product.astype(sent_ref.dtype)


def hop_kernel(first, arrived_ref, tokens_ref, mixing_ref, sent_ref, kept_ref):
    rows, width = sent_ref.shape
    step = STEP if width % STEP == 0 else width
    tokens = tokens_ref[rows:]
    for at in range(0, width, step):
        product = dot(tokens, mixing_ref[:, pl.ds(first + at, step)])
        arrived = arrived_ref[:, pl.ds(at, step)].astype(jnp.float32)
        sent_ref[:, pl.ds(at, step)] = (arrived + product[:rows]).astype(sent_ref.dtype)
        kept_ref[:, pl.ds(at, step)] = product[rows:]


def lift(tokens, token_mixing, pieces):
    count = lax.axis_size("tok")
    embed = tokens.shape[0]
    rows = embed // count
    width = token_mixing.shape[1] // pieces
    sent = jax.ShapeDtypeStruct((rows, width), jnp.bfloat16)
    travelling = list(call(sent_kernel, [sent] * pieces, (tokens, token_mixing)))
    kept = [None] * pieces
    for step in range(1, count):
        for piece in range(pieces):
            arrived = turned(travelling[piece], "tok", -1)
            if step == 1:
                travelling[piece], kept[piece] = call(
                    functools.partial(hop_kernel, piece * width),
                    [sent, jax.ShapeDtypeStruct((embed - 2 * rows, width), jnp.float32)],
                    (arrived, tokens, token_mixing),
                )
            else:
                at = (step - 2) * rows
                summed = arrived.astype(jnp.float32) + kept[piece][at : at + rows]
                if step == count - 1:
                    summed = gelu(summed)
                travelling[piece] = summed.astype(jnp.bfloat16)
    return jnp.concatenate(travelling, axis=1)


def local(weather, conv_first, conv_second, patch_embed, token_mixing):
    tokens = encode(weather, conv_first, conv_second, patch_embed)
    return lift(tokens, token_mixing, PIECES)


def solution(mesh):
    placed = (P("groups", "tok", ("ch", "sub")), P(), P(), P(), P("tok", ("ch", "sub")))
    return jax.shard_map(
        local,
        mesh=mesh,
        in_specs=placed,
        out_specs=P(("groups", "tok"), ("ch", "sub")),
        check_vma=False,
    )
```

```python
import functools

import jax
import jax.numpy as jnp
from jax import lax
from jax.experimental import pallas as pl
from jax.experimental.pallas import tpu as pltpu
from jax.sharding import PartitionSpec as P

PIECES = 4
STEP = 256
LANES = 128
VMEM_BYTES = 24 * 1024 * 1024
ROWS_AT_ONCE = 1024


def pack_kernel(field_ref, packed_ref):
    lon, lat, chans = field_ref.shape
    pairs = field_ref[...].reshape(lon // 2, 2, lat, chans)
    packed_ref[...] = jnp.concatenate([pairs[:, 0], pairs[:, 1]], axis=-1).astype(packed_ref.dtype)


def join_kernel(count_ch, count_sub, *refs):
    blocks, (field_ref, low_ref, high_ref) = refs[:-3], refs[-3:]
    pairs, lat, wide = field_ref.shape
    width = lat // (count_ch * count_sub)
    for away_ch in range(count_ch):
        for away_sub in range(count_sub):
            at_ch = lax.rem(lax.axis_index("ch") + count_ch - away_ch, count_ch)
            at_sub = lax.rem(lax.axis_index("sub") + count_sub - away_sub, count_sub)
            here = pl.ds(pl.multiple_of((at_ch * count_sub + at_sub) * width, width), width)
            block = blocks[away_ch * count_sub + away_sub][...]
            field_ref[:, here, :] = block
            low_ref[:, here, :] = block[:1]
            high_ref[:, here, :] = block[pairs - 1 :]


def split_two(value):
    upper = value.astype(jnp.bfloat16)
    return upper, (value - upper.astype(jnp.float32)).astype(jnp.bfloat16)


def spread_taps(kernel_ref):
    chans = kernel_ref.shape[1]
    nothing = jnp.zeros((chans, kernel_ref.shape[2]), jnp.float32)
    rows = []
    for tap in range(3):
        taps = [kernel_ref[3 * turn + tap] for turn in range(3)]
        rows.append(jnp.concatenate([taps[1], taps[2], nothing, taps[0]], axis=-1))
        rows.append(jnp.concatenate([taps[0], taps[1], taps[2], nothing], axis=-1))
    return jnp.concatenate(rows, axis=0).T


def weights_kernel(first_ref, second_ref, embed_ref, taps_one_ref, taps_two_ref, embed_out_ref, scratch):
    for source, target in ((first_ref, taps_one_ref), (second_ref, taps_two_ref)):
        upper, lower = split_two(spread_taps(source))
        target[...] = jnp.concatenate([upper, lower, upper], axis=0)
    chans = embed_ref.shape[0] // 4
    embed = embed_ref.shape[1]
    count = lax.axis_size("tok")
    turn = lax.rem(lax.axis_index("tok") + 1, count) * (embed // count)
    turned_embed = pltpu.roll(embed_ref[...].astype(jnp.float32), lax.rem(embed - turn, embed), axis=1)
    for first in range(0, embed, LANES):
        scratch[...] = turned_embed[:, first : first + LANES]
        ordered = [scratch[pl.ds(2 * a + b, chans, stride=4), :] for b in range(2) for a in range(2)]
        rows = jnp.concatenate(ordered, axis=0).T
        embed_out_ref[pl.ds(first, LANES), :] = rows.astype(embed_out_ref.dtype)


def pairs_at_once(pairs, lat):
    best = 1
    for size in range(1, pairs + 1):
        if pairs % size == 0 and size * lat <= ROWS_AT_ONCE:
            best = size
    return best


def window(pair_at, pairs):
    rows = []
    for pair in pairs:
        here = pair_at(pair)
        lane = lax.broadcasted_iota(jnp.int32, here.shape, 1)
        beside = jnp.where(lane < here.shape[1] // 2, pair_at(pair + 1), pair_at(pair - 1))
        rows.append(jnp.concatenate([here, beside], axis=-1))
    return jnp.concatenate(rows, axis=0)


def add_lat_taps(products, lat):
    wide = products.shape[1] // 3
    count = products.shape[0]
    row = lax.broadcasted_iota(jnp.int32, (1, lat, wide), 1)
    below = pltpu.roll(products[:, :wide], 1, axis=0).reshape(-1, lat, wide)
    above = pltpu.roll(products[:, 2 * wide :], count - 1, axis=0).reshape(-1, lat, wide)
    here = products[:, wide : 2 * wide].reshape(-1, lat, wide)
    return here + jnp.where(row == 0, 0.0, below) + jnp.where(row == lat - 1, 0.0, above)


def gelu(value):
    return 0.5 * value * (1.0 + lax.erf(value * (0.5**0.5)))


def dot(left, right):
    return jnp.dot(left, right, preferred_element_type=jnp.float32)


def first_conv(field_at, pairs, taps_ref, lat):
    rows = window(field_at, pairs)
    products = dot(jnp.concatenate([rows, rows], axis=-1), taps_ref[: 2 * rows.shape[1]])
    return split_two(gelu(add_lat_taps(products, lat)))


def second_conv(upper_at, lower_at, pairs, taps_ref, lat):
    upper, lower = window(upper_at, pairs), window(lower_at, pairs)
    products = dot(jnp.concatenate([upper, upper, lower], axis=-1), taps_ref[...])
    rounded = add_lat_taps(products, lat).astype(jnp.bfloat16).astype(jnp.float32)
    return rounded.reshape(-1, rounded.shape[2])


def embed_patches(two_ref, embed_ref):
    half = two_ref.shape[0] // 2
    patches = jnp.concatenate(
        [two_ref[pl.ds(b, half, stride=2), :].astype(jnp.bfloat16) for b in range(2)], axis=-1
    )
    return lax.dot_general(
        embed_ref[...], patches, (((1,), (1,)), ((), ())), preferred_element_type=jnp.float32
    ).astype(jnp.bfloat16)


def runs(first, last, lat):
    size = pairs_at_once(last - first, lat)
    return [list(range(at, at + size)) for at in range(first, last, size)]


def inner_kernel(
    field_ref, taps_one_ref, taps_two_ref, embed_ref, tokens_ref, upper_edge_ref, lower_edge_ref, upper_ref, lower_ref, two_ref
):
    pairs, lat, wide = field_ref.shape
    for run in runs(1, pairs - 1, lat):
        upper, lower = first_conv(lambda pair: field_ref[pair], run, taps_one_ref, lat)
        upper_ref[pl.ds(run[0], len(run))] = upper
        lower_ref[pl.ds(run[0], len(run))] = lower
    for inside, edge in ((upper_ref, upper_edge_ref), (lower_ref, lower_edge_ref)):
        edge[pl.ds(0, 2)] = inside[pl.ds(1, 2)]
        edge[pl.ds(2, 2)] = inside[pl.ds(pairs - 3, 2)]
    for run in runs(2, pairs - 2, lat):
        two = second_conv(lambda pair: upper_ref[pair], lambda pair: lower_ref[pair], run, taps_two_ref, lat)
        two_ref[pl.ds((run[0] - 2) * lat, len(run) * lat), :] = two
    tokens_ref[...] = embed_patches(two_ref, embed_ref)


def outer_kernel(
    field_ref, before_ref, after_ref, upper_edge_ref, lower_edge_ref, taps_one_ref, taps_two_ref, embed_ref, inner_ref, tokens_ref, two_ref
):
    pairs, lat, wide = field_ref.shape

    def field_at(pair):
        if pair < 0:
            return before_ref[0]
        if pair >= pairs:
            return after_ref[0]
        return field_ref[pair]

    outermost = [-1, 0, pairs - 1, pairs]
    next_inside = [1, 2, pairs - 3, pairs - 2]
    upper, lower = first_conv(field_at, outermost, taps_one_ref, lat)

    def hidden_at(found, edge_ref):
        def at(pair):
            if pair in outermost:
                return found[outermost.index(pair)]
            return edge_ref[next_inside.index(pair)]

        return at

    two_ref[...] = second_conv(
        hidden_at(upper, upper_edge_ref), hidden_at(lower, lower_edge_ref), [0, 1, pairs - 2, pairs - 1], taps_two_ref, lat
    )
    outer = embed_patches(two_ref, embed_ref)
    inner = inner_ref.shape[1]
    tokens_ref[:, :lat] = outer[:, :lat]
    tokens_ref[:, pl.ds(lat, inner)] = inner_ref[...]
    tokens_ref[:, pl.ds(lat + inner, lat)] = outer[:, lat:]


def call(kernel, out_shape, inputs, scratch=(), flops=0, moved=0):
    return pl.pallas_call(
        kernel,
        out_shape=out_shape,
        in_specs=[pl.BlockSpec(memory_space=pltpu.VMEM)] * len(inputs),
        out_specs=jax.tree.map(lambda unused: pl.BlockSpec(memory_space=pltpu.VMEM), out_shape),
        scratch_shapes=list(scratch),
        compiler_params=pltpu.CompilerParams(vmem_limit_bytes=VMEM_BYTES),
        cost_estimate=pl.CostEstimate(flops=flops, bytes_accessed=moved, transcendentals=0),
    )(*inputs)


def turned(value, axis, away):
    count = lax.axis_size(axis)
    return lax.ppermute(value, axis, [(i, (i + away) % count) for i in range(count)])


def band_blocks(block, beside):
    rows = [block] + [turned(block, "ch", away) for away in range(1, lax.axis_size("ch"))]
    rows[1:], beside = lax.optimization_barrier((rows[1:], beside))
    blocks = []
    for row in rows:
        blocks.append(row)
        blocks.extend(turned(row, "sub", away) for away in range(1, lax.axis_size("sub")))
    return blocks, beside


def encode(weather, conv_first, conv_second, patch_embed):
    chans, lon, lat = weather.shape
    pairs, wide = lon // 2, 2 * chans
    embed = patch_embed.shape[1]
    shape = functools.partial(jax.ShapeDtypeStruct, dtype=jnp.bfloat16)
    packed = call(
        pack_kernel, shape((pairs, lat, wide)), (jnp.transpose(weather, (1, 2, 0)),), moved=weather.size * 10
    )
    taps = shape((12 * chans, 6 * chans))
    weights = call(
        weights_kernel,
        (taps, taps, shape((embed, 4 * chans))),
        (conv_first, conv_second, patch_embed),
        scratch=[pltpu.VMEM((patch_embed.shape[0], LANES), jnp.float32)],
        moved=conv_first.size * 20,
    )
    blocks, weights = band_blocks(packed, weights)
    lat = len(blocks) * lat
    edge = shape((1, lat, wide))
    field, low, high = call(
        functools.partial(join_kernel, lax.axis_size("ch"), lax.axis_size("sub")),
        (shape((pairs, lat, wide)), edge, edge),
        blocks,
        moved=packed.size * 4 * len(blocks),
    )
    before = turned(high, "tok", 1)
    after = turned(low, "tok", -1)
    work = 2 * lat * 4 * chans * 6 * chans * 5
    held = shape((4, lat, wide))
    hidden = pltpu.VMEM((pairs, lat, wide), jnp.bfloat16)
    inner, upper_edge, lower_edge = call(
        inner_kernel,
        (shape((embed, (pairs - 4) * lat // 2)), held, held),
        (field, *weights),
        scratch=[hidden, hidden, pltpu.VMEM(((pairs - 4) * lat, wide), jnp.float32)],
        flops=work * (pairs - 3),
        moved=field.size * 2,
    )
    return call(
        outer_kernel,
        shape((embed, pairs * lat // 2)),
        (field, before, after, upper_edge, lower_edge, *weights, inner),
        scratch=[pltpu.VMEM((4 * lat, wide), jnp.float32)],
        flops=work * 4,
        moved=field.size * 2,
    )


def sent_kernel(first, tokens_ref, mixing_ref, sent_ref):
    rows, width = sent_ref.shape
    step = STEP if width % STEP == 0 else width
    tokens = tokens_ref[:rows]
    for at in range(0, width, step):
        product = dot(tokens, mixing_ref[:, pl.ds(first + at, step)])
        sent_ref[:, pl.ds(at, step)] = product.astype(sent_ref.dtype)


def hop_kernel(first, arrived_ref, tokens_ref, mixing_ref, sent_ref, kept_ref):
    rows, width = sent_ref.shape
    step = STEP if width % STEP == 0 else width
    tokens = tokens_ref[rows:]
    for at in range(0, width, step):
        product = dot(tokens, mixing_ref[:, pl.ds(first + at, step)])
        arrived = arrived_ref[:, pl.ds(at, step)].astype(jnp.float32)
        sent_ref[:, pl.ds(at, step)] = (arrived + product[:rows]).astype(sent_ref.dtype)
        kept_ref[:, pl.ds(at, step)] = product[rows:]


def lift(tokens, token_mixing, pieces):
    count = lax.axis_size("tok")
    embed = tokens.shape[0]
    rows = embed // count
    width = token_mixing.shape[1] // pieces
    sent = jax.ShapeDtypeStruct((rows, width), jnp.bfloat16)
    travelling = [
        call(functools.partial(sent_kernel, piece * width), sent, (tokens, token_mixing)) for piece in range(pieces)
    ]
    kept = [None] * pieces
    for step in range(1, count):
        for piece in range(pieces):
            arrived = turned(travelling[piece], "tok", -1)
            if step == 1:
                travelling[piece], kept[piece] = call(
                    functools.partial(hop_kernel, piece * width),
                    [sent, jax.ShapeDtypeStruct((embed - 2 * rows, width), jnp.float32)],
                    (arrived, tokens, token_mixing),
                )
            else:
                at = (step - 2) * rows
                summed = arrived.astype(jnp.float32) + kept[piece][at : at + rows]
                if step == count - 1:
                    summed = gelu(summed)
                travelling[piece] = summed.astype(jnp.bfloat16)
    return jnp.concatenate(travelling, axis=1)


def local(weather, conv_first, conv_second, patch_embed, token_mixing):
    tokens = encode(weather, conv_first, conv_second, patch_embed)
    return lift(tokens, token_mixing, PIECES)


def solution(mesh):
    placed = (P("groups", "tok", ("ch", "sub")), P(), P(), P(), P("tok", ("ch", "sub")))
    return jax.shard_map(
        local,
        mesh=mesh,
        in_specs=placed,
        out_specs=P(("groups", "tok"), ("ch", "sub")),
        check_vma=False,
    )
```

```python
import functools

import jax
import jax.numpy as jnp
from jax import lax
from jax.experimental import pallas as pl
from jax.experimental.pallas import tpu as pltpu
from jax.sharding import PartitionSpec as P

PIECES = 4
STEP = 256
LANES = 128
VMEM_BYTES = 24 * 1024 * 1024
ROWS_AT_ONCE = 512


def pack_kernel(field_ref, packed_ref):
    lon, lat, chans = field_ref.shape
    pairs = field_ref[...].reshape(lon // 2, 2, lat, chans)
    packed_ref[...] = jnp.concatenate([pairs[:, 0], pairs[:, 1]], axis=-1).astype(packed_ref.dtype)


def join_kernel(count_ch, count_sub, *refs):
    blocks, (field_ref, low_ref, high_ref) = refs[:-3], refs[-3:]
    pairs, lat, wide = field_ref.shape
    width = lat // (count_ch * count_sub)
    for away_ch in range(count_ch):
        for away_sub in range(count_sub):
            at_ch = lax.rem(lax.axis_index("ch") + count_ch - away_ch, count_ch)
            at_sub = lax.rem(lax.axis_index("sub") + count_sub - away_sub, count_sub)
            here = pl.ds(pl.multiple_of((at_ch * count_sub + at_sub) * width, width), width)
            block = blocks[away_ch * count_sub + away_sub][...]
            field_ref[:, here, :] = block
            low_ref[:, here, :] = block[:1]
            high_ref[:, here, :] = block[pairs - 1 :]


def split_two(value):
    upper = value.astype(jnp.bfloat16)
    return upper, (value - upper.astype(jnp.float32)).astype(jnp.bfloat16)


def spread_taps(kernel_ref):
    chans = kernel_ref.shape[1]
    nothing = jnp.zeros((chans, kernel_ref.shape[2]), jnp.float32)
    rows = []
    for tap in range(3):
        taps = [kernel_ref[3 * turn + tap] for turn in range(3)]
        rows.append(jnp.concatenate([taps[1], taps[2], nothing, taps[0]], axis=-1))
        rows.append(jnp.concatenate([taps[0], taps[1], taps[2], nothing], axis=-1))
    return jnp.concatenate(rows, axis=0).T


def weights_kernel(first_ref, second_ref, embed_ref, taps_one_ref, taps_two_ref, embed_out_ref, scratch):
    for source, target in ((first_ref, taps_one_ref), (second_ref, taps_two_ref)):
        upper, lower = split_two(spread_taps(source))
        target[...] = jnp.concatenate([upper, lower, upper], axis=0)
    chans = embed_ref.shape[0] // 4
    embed = embed_ref.shape[1]
    count = lax.axis_size("tok")
    turn = lax.rem(lax.axis_index("tok") + 1, count) * (embed // count)
    turned_embed = pltpu.roll(embed_ref[...].astype(jnp.float32), lax.rem(embed - turn, embed), axis=1)
    for first in range(0, embed, LANES):
        scratch[...] = turned_embed[:, first : first + LANES]
        ordered = [scratch[pl.ds(2 * a + b, chans, stride=4), :] for b in range(2) for a in range(2)]
        rows = jnp.concatenate(ordered, axis=0).T
        embed_out_ref[pl.ds(first, LANES), :] = rows.astype(embed_out_ref.dtype)


def window(pair_at, pairs):
    rows = []
    for pair in pairs:
        here = pair_at(pair)
        lane = lax.broadcasted_iota(jnp.int32, here.shape, 1)
        beside = jnp.where(lane < here.shape[1] // 2, pair_at(pair + 1), pair_at(pair - 1))
        rows.append(jnp.concatenate([here, beside], axis=-1))
    return jnp.concatenate(rows, axis=0)


def add_lat_taps(products, lat):
    wide = products.shape[1] // 3
    count = products.shape[0]
    row = lax.broadcasted_iota(jnp.int32, (1, lat, wide), 1)
    below = pltpu.roll(products[:, :wide], 1, axis=0).reshape(-1, lat, wide)
    above = pltpu.roll(products[:, 2 * wide :], count - 1, axis=0).reshape(-1, lat, wide)
    here = products[:, wide : 2 * wide].reshape(-1, lat, wide)
    return here + jnp.where(row == 0, 0.0, below) + jnp.where(row == lat - 1, 0.0, above)


def gelu(value):
    return 0.5 * value * (1.0 + lax.erf(value * (0.5**0.5)))


def dot(left, right):
    return jnp.dot(left, right, preferred_element_type=jnp.float32)


def first_conv(rows, taps, lat):
    return gelu(add_lat_taps(dot(jnp.concatenate([rows, rows], axis=-1), taps), lat))


def second_conv(upper, lower, taps, lat):
    products = dot(jnp.concatenate([upper, upper, lower], axis=-1), taps)
    rounded = add_lat_taps(products, lat).astype(jnp.bfloat16).astype(jnp.float32)
    return rounded.reshape(-1, rounded.shape[2])


def reordered(taps_ref, parts, order):
    chans = taps_ref.shape[0] // 12
    rows = [taps_ref[pl.ds((4 * part + at) * chans, chans), :] for part in range(parts) for at in order]
    return jnp.concatenate(rows, axis=0)


def embed_patches(two_ref, embed_ref):
    half = two_ref.shape[0] // 2
    patches = jnp.concatenate(
        [two_ref[pl.ds(b, half, stride=2), :].astype(jnp.bfloat16) for b in range(2)], axis=-1
    )
    return lax.dot_general(
        embed_ref[...], patches, (((1,), (1,)), ((), ())), preferred_element_type=jnp.float32
    ).astype(jnp.bfloat16)


def runs(first, last, lat):
    count = -(-(last - first) * lat // max(ROWS_AT_ONCE, lat))
    cuts = [first + (last - first) * at // count for at in range(count + 1)]
    return [list(range(*cut)) for cut in zip(cuts[:-1], cuts[1:])]


def turned_half(value):
    turned_value = pltpu.roll(value.astype(jnp.float32), value.shape[1] // 2, axis=1)
    return turned_value.astype(value.dtype)


def inner_kernel(
    field_ref, taps_one_ref, taps_two_ref, embed_ref, tokens_ref, upper_edge_ref, lower_edge_ref, upper_ref, lower_ref, two_ref
):
    pairs, lat, wide = field_ref.shape
    first_runs, second_runs = runs(0, pairs, lat), runs(1, pairs - 1, lat)

    def field_at(pair):
        return field_ref[min(max(pair, 0), pairs - 1)]

    two_ref[pl.ds(0, lat), :] = jnp.zeros((lat, wide), jnp.float32)
    two_ref[pl.ds((pairs - 1) * lat, lat), :] = jnp.zeros((lat, wide), jnp.float32)
    for run in first_runs:
        rows = window(field_at, run)
        upper, lower = split_two(first_conv(rows, taps_one_ref[: 2 * rows.shape[1]], lat))
        upper_ref[pl.ds(run[0], len(run))] = upper
        lower_ref[pl.ds(run[0], len(run))] = lower
        while second_runs and (second_runs[0][-1] < run[-1]):
            ready = second_runs.pop(0)
            upper_rows = window(lambda pair: upper_ref[pair], ready)
            lower_rows = window(lambda pair: lower_ref[pair], ready)
            two = second_conv(upper_rows, lower_rows, taps_two_ref[...], lat)
            two_ref[pl.ds(ready[0] * lat, len(ready) * lat), :] = two
    lane = lax.broadcasted_iota(jnp.int32, (lat, wide), 1)
    for hidden, edge in ((upper_ref, upper_edge_ref), (lower_ref, lower_edge_ref)):
        edge[0] = jnp.where(lane < wide // 2, hidden[1], hidden[0])
        edge[1] = turned_half(jnp.where(lane < wide // 2, hidden[pairs - 1], hidden[pairs - 2]))
    tokens_ref[...] = embed_patches(two_ref, embed_ref)


def outer_kernel(
    field_ref, after_ref, before_ref, upper_edge_ref, lower_edge_ref, taps_one_ref, taps_two_ref, embed_ref, inner_ref, tokens_ref, two_ref
):
    pairs, lat, wide = field_ref.shape
    left = jnp.concatenate([before_ref[0], field_ref[0]], axis=-1)
    right = jnp.concatenate([field_ref[pairs - 1], after_ref[0]], axis=-1)
    rows = jnp.concatenate([left, right], axis=0)
    hidden = first_conv(rows, reordered(taps_one_ref, 2, (3, 0, 1, 2)), lat)
    parts = []
    for (at_left, at_right), edge in zip(
        zip(split_two(hidden[0]), split_two(turned_half(hidden[1]))), (upper_edge_ref, lower_edge_ref)
    ):
        left = jnp.concatenate([at_left, edge[0]], axis=-1)
        right = jnp.concatenate([edge[1], at_right], axis=-1)
        parts.append(jnp.concatenate([left, right], axis=0))
    two_ref[...] = second_conv(*parts, reordered(taps_two_ref, 3, (3, 0, 2, 1)), lat)
    outer = embed_patches(two_ref, embed_ref)
    column = lax.broadcasted_iota(jnp.int32, outer.shape, 1)
    rest = inner_ref.shape[1] - lat
    tokens_ref[...] = inner_ref[...]
    tokens_ref[:, :lat] = jnp.where(column < lat // 2, outer, inner_ref[:, :lat])
    tokens_ref[:, pl.ds(rest, lat)] = jnp.where(column < lat // 2, inner_ref[:, pl.ds(rest, lat)], outer)


def call(kernel, out_shape, inputs, scratch=(), flops=0, moved=0):
    return pl.pallas_call(
        kernel,
        out_shape=out_shape,
        in_specs=[pl.BlockSpec(memory_space=pltpu.VMEM)] * len(inputs),
        out_specs=jax.tree.map(lambda unused: pl.BlockSpec(memory_space=pltpu.VMEM), out_shape),
        scratch_shapes=list(scratch),
        compiler_params=pltpu.CompilerParams(vmem_limit_bytes=VMEM_BYTES),
        cost_estimate=pl.CostEstimate(flops=flops, bytes_accessed=moved, transcendentals=0),
    )(*inputs)


def turned(value, axis, away):
    count = lax.axis_size(axis)
    return lax.ppermute(value, axis, [(i, (i + away) % count) for i in range(count)])


def band_blocks(block, beside):
    rows = [block] + [turned(block, "ch", away) for away in range(1, lax.axis_size("ch"))]
    rows[1:], beside = lax.optimization_barrier((rows[1:], beside))
    blocks = []
    for row in rows:
        blocks.append(row)
        blocks.extend(turned(row, "sub", away) for away in range(1, lax.axis_size("sub")))
    return blocks, beside


def encode(weather, conv_first, conv_second, patch_embed):
    chans, lon, lat = weather.shape
    pairs, wide = lon // 2, 2 * chans
    embed = patch_embed.shape[1]
    shape = functools.partial(jax.ShapeDtypeStruct, dtype=jnp.bfloat16)
    packed = call(
        pack_kernel, shape((pairs, lat, wide)), (jnp.transpose(weather, (1, 2, 0)),), moved=weather.size * 10
    )
    taps = shape((12 * chans, 6 * chans))
    weights = call(
        weights_kernel,
        (taps, taps, shape((embed, 4 * chans))),
        (conv_first, conv_second, patch_embed),
        scratch=[pltpu.VMEM((patch_embed.shape[0], LANES), jnp.float32)],
        moved=conv_first.size * 20,
    )
    blocks, weights = band_blocks(packed, weights)
    lat = len(blocks) * lat
    edge = shape((1, lat, wide))
    field, low, high = call(
        functools.partial(join_kernel, lax.axis_size("ch"), lax.axis_size("sub")),
        (shape((pairs, lat, wide)), edge, edge),
        blocks,
        moved=packed.size * 4 * len(blocks),
    )
    after = turned(low, "tok", -1)
    before = turned(high, "tok", 1)
    work = 2 * lat * 4 * chans * 6 * chans * 5
    held = shape((2, lat, wide))
    hidden = pltpu.VMEM((pairs, lat, wide), jnp.bfloat16)
    inner, upper_edge, lower_edge = call(
        inner_kernel,
        (shape((embed, pairs * lat // 2)), held, held),
        (field, *weights),
        scratch=[hidden, hidden, pltpu.VMEM((pairs * lat, wide), jnp.float32)],
        flops=work * (pairs - 1),
        moved=field.size * 2,
    )
    return call(
        outer_kernel,
        shape((embed, pairs * lat // 2)),
        (field, after, before, upper_edge, lower_edge, *weights, inner),
        scratch=[pltpu.VMEM((2 * lat, wide), jnp.float32)],
        flops=work * 2,
        moved=field.size * 2,
    )


def sent_kernel(first, tokens_ref, mixing_ref, sent_ref):
    rows, width = sent_ref.shape
    step = STEP if width % STEP == 0 else width
    tokens = tokens_ref[:rows]
    for at in range(0, width, step):
        product = dot(tokens, mixing_ref[:, pl.ds(first + at, step)])
        sent_ref[:, pl.ds(at, step)] = product.astype(sent_ref.dtype)


def hop_kernel(first, arrived_ref, tokens_ref, mixing_ref, sent_ref, kept_ref):
    rows, width = sent_ref.shape
    step = STEP if width % STEP == 0 else width
    tokens = tokens_ref[rows:]
    for at in range(0, width, step):
        product = dot(tokens, mixing_ref[:, pl.ds(first + at, step)])
        arrived = arrived_ref[:, pl.ds(at, step)].astype(jnp.float32)
        sent_ref[:, pl.ds(at, step)] = (arrived + product[:rows]).astype(sent_ref.dtype)
        kept_ref[:, pl.ds(at, step)] = product[rows:]


def lift(tokens, token_mixing, pieces):
    count = lax.axis_size("tok")
    embed = tokens.shape[0]
    rows = embed // count
    width = token_mixing.shape[1] // pieces
    sent = jax.ShapeDtypeStruct((rows, width), jnp.bfloat16)
    travelling = [
        call(functools.partial(sent_kernel, piece * width), sent, (tokens, token_mixing)) for piece in range(pieces)
    ]
    kept = [None] * pieces
    for step in range(1, count):
        for piece in range(pieces):
            arrived = turned(travelling[piece], "tok", -1)
            if step == 1:
                travelling[piece], kept[piece] = call(
                    functools.partial(hop_kernel, piece * width),
                    [sent, jax.ShapeDtypeStruct((embed - 2 * rows, width), jnp.float32)],
                    (arrived, tokens, token_mixing),
                )
            else:
                at = (step - 2) * rows
                summed = arrived.astype(jnp.float32) + kept[piece][at : at + rows]
                if step == count - 1:
                    summed = gelu(summed)
                travelling[piece] = summed.astype(jnp.bfloat16)
    return jnp.concatenate(travelling, axis=1)


def local(weather, conv_first, conv_second, patch_embed, token_mixing):
    tokens = encode(weather, conv_first, conv_second, patch_embed)
    return lift(tokens, token_mixing, PIECES)


def solution(mesh):
    placed = (P("groups", "tok", ("ch", "sub")), P(), P(), P(), P("tok", ("ch", "sub")))
    return jax.shard_map(
        local,
        mesh=mesh,
        in_specs=placed,
        out_specs=P(("groups", "tok"), ("ch", "sub")),
        check_vma=False,
    )
```

```python
import functools

import jax
import jax.numpy as jnp
from jax import lax
from jax.experimental import pallas as pl
from jax.experimental.pallas import tpu as pltpu
from jax.sharding import PartitionSpec as P

PIECES = 4
STEP = 256
LANES = 128
VMEM_BYTES = 24 * 1024 * 1024
ROWS_AT_ONCE = 1024


def pack_kernel(field_ref, packed_ref):
    lon, lat, chans = field_ref.shape
    pairs = field_ref[...].reshape(lon // 2, 2, lat, chans)
    packed_ref[...] = jnp.concatenate([pairs[:, 0], pairs[:, 1]], axis=-1).astype(packed_ref.dtype)


def join_kernel(count_ch, count_sub, *refs):
    blocks, (field_ref, low_ref, high_ref) = refs[:-3], refs[-3:]
    pairs, lat, wide = field_ref.shape
    width = lat // (count_ch * count_sub)
    for away_ch in range(count_ch):
        for away_sub in range(count_sub):
            at_ch = lax.rem(lax.axis_index("ch") + count_ch - away_ch, count_ch)
            at_sub = lax.rem(lax.axis_index("sub") + count_sub - away_sub, count_sub)
            here = pl.ds(pl.multiple_of((at_ch * count_sub + at_sub) * width, width), width)
            block = blocks[away_ch * count_sub + away_sub][...]
            field_ref[:, here, :] = block
            low_ref[:, here, :] = block[:1]
            high_ref[:, here, :] = block[pairs - 1 :]


def split_two(value):
    upper = value.astype(jnp.bfloat16)
    return upper, (value - upper.astype(jnp.float32)).astype(jnp.bfloat16)


def spread_taps(kernel_ref):
    chans = kernel_ref.shape[1]
    nothing = jnp.zeros((chans, kernel_ref.shape[2]), jnp.float32)
    rows = []
    for tap in range(3):
        taps = [kernel_ref[3 * turn + tap] for turn in range(3)]
        rows.append(jnp.concatenate([taps[1], taps[2], nothing, taps[0]], axis=-1))
        rows.append(jnp.concatenate([taps[0], taps[1], taps[2], nothing], axis=-1))
    return jnp.concatenate(rows, axis=0).T


def weights_kernel(first_ref, second_ref, embed_ref, taps_one_ref, taps_two_ref, embed_out_ref, scratch):
    for source, target in ((first_ref, taps_one_ref), (second_ref, taps_two_ref)):
        upper, lower = split_two(spread_taps(source))
        target[...] = jnp.concatenate([upper, lower], axis=1)
    chans = embed_ref.shape[0] // 4
    embed = embed_ref.shape[1]
    count = lax.axis_size("tok")
    turn = lax.rem(lax.axis_index("tok") + 1, count) * (embed // count)
    turned_embed = pltpu.roll(embed_ref[...].astype(jnp.float32), lax.rem(embed - turn, embed), axis=1)
    for first in range(0, embed, LANES):
        scratch[...] = turned_embed[:, first : first + LANES]
        ordered = [scratch[pl.ds(2 * a + b, chans, stride=4), :] for b in range(2) for a in range(2)]
        rows = jnp.concatenate(ordered, axis=0).T
        embed_out_ref[pl.ds(first, LANES), :] = rows.astype(embed_out_ref.dtype)


def pairs_at_once(pairs, lat):
    best = 1
    for size in range(1, pairs + 1):
        if pairs % size == 0 and size * lat <= ROWS_AT_ONCE:
            best = size
    return best


def window(pair_at, pairs):
    rows = []
    for pair in pairs:
        here = pair_at(pair)
        lane = lax.broadcasted_iota(jnp.int32, here.shape, 1)
        beside = jnp.where(lane < here.shape[1] // 2, pair_at(pair + 1), pair_at(pair - 1))
        rows.append(jnp.concatenate([here, beside], axis=-1))
    return jnp.concatenate(rows, axis=0)


def add_lat_taps(products, lat):
    wide = products.shape[1] // 3
    count = products.shape[0]
    row = lax.broadcasted_iota(jnp.int32, (1, lat, wide), 1)
    below = pltpu.roll(products[:, :wide], 1, axis=0).reshape(-1, lat, wide)
    above = pltpu.roll(products[:, 2 * wide :], count - 1, axis=0).reshape(-1, lat, wide)
    here = products[:, wide : 2 * wide].reshape(-1, lat, wide)
    return here + jnp.where(row == 0, 0.0, below) + jnp.where(row == lat - 1, 0.0, above)


def gelu(value):
    return 0.5 * value * (1.0 + lax.erf(value * (0.5**0.5)))


def dot(left, right):
    return jnp.dot(left, right, preferred_element_type=jnp.float32)


def dot_both(rows, taps_ref):
    both = dot(rows, taps_ref[...])
    half = both.shape[1] // 2
    return both[:, :half] + both[:, half:]


def first_conv(field_at, pairs, taps_ref, lat):
    products = dot_both(window(field_at, pairs), taps_ref)
    return split_two(gelu(add_lat_taps(products, lat)))


def second_conv(upper_at, lower_at, pairs, taps_ref, lat):
    upper, lower = window(upper_at, pairs), window(lower_at, pairs)
    products = dot_both(upper, taps_ref) + dot(lower, taps_ref[:, : taps_ref.shape[1] // 2])
    rounded = add_lat_taps(products, lat).astype(jnp.bfloat16).astype(jnp.float32)
    return rounded.reshape(-1, rounded.shape[2])


def embed_patches(two_ref, embed_ref):
    half = two_ref.shape[0] // 2
    patches = jnp.concatenate(
        [two_ref[pl.ds(b, half, stride=2), :].astype(jnp.bfloat16) for b in range(2)], axis=-1
    )
    return lax.dot_general(
        embed_ref[...], patches, (((1,), (1,)), ((), ())), preferred_element_type=jnp.float32
    ).astype(jnp.bfloat16)


def runs(first, last, lat):
    size = pairs_at_once(last - first, lat)
    return [list(range(at, at + size)) for at in range(first, last, size)]


def inner_kernel(
    field_ref, taps_one_ref, taps_two_ref, embed_ref, tokens_ref, upper_edge_ref, lower_edge_ref, upper_ref, lower_ref, two_ref
):
    pairs, lat, wide = field_ref.shape
    for run in runs(1, pairs - 1, lat):
        upper, lower = first_conv(lambda pair: field_ref[pair], run, taps_one_ref, lat)
        upper_ref[pl.ds(run[0], len(run))] = upper
        lower_ref[pl.ds(run[0], len(run))] = lower
    for inside, edge in ((upper_ref, upper_edge_ref), (lower_ref, lower_edge_ref)):
        edge[pl.ds(0, 2)] = inside[pl.ds(1, 2)]
        edge[pl.ds(2, 2)] = inside[pl.ds(pairs - 3, 2)]
    for run in runs(2, pairs - 2, lat):
        two = second_conv(lambda pair: upper_ref[pair], lambda pair: lower_ref[pair], run, taps_two_ref, lat)
        two_ref[pl.ds((run[0] - 2) * lat, len(run) * lat), :] = two
    tokens_ref[...] = embed_patches(two_ref, embed_ref)


def outer_kernel(
    field_ref, before_ref, after_ref, upper_edge_ref, lower_edge_ref, taps_one_ref, taps_two_ref, embed_ref, inner_ref, tokens_ref, two_ref
):
    pairs, lat, wide = field_ref.shape

    def field_at(pair):
        if pair < 0:
            return before_ref[0]
        if pair >= pairs:
            return after_ref[0]
        return field_ref[pair]

    outermost = [-1, 0, pairs - 1, pairs]
    next_inside = [1, 2, pairs - 3, pairs - 2]
    upper, lower = first_conv(field_at, outermost, taps_one_ref, lat)

    def hidden_at(found, edge_ref):
        def at(pair):
            if pair in outermost:
                return found[outermost.index(pair)]
            return edge_ref[next_inside.index(pair)]

        return at

    two_ref[...] = second_conv(
        hidden_at(upper, upper_edge_ref), hidden_at(lower, lower_edge_ref), [0, 1, pairs - 2, pairs - 1], taps_two_ref, lat
    )
    outer = embed_patches(two_ref, embed_ref)
    inner = inner_ref.shape[1]
    tokens_ref[:, :lat] = outer[:, :lat]
    tokens_ref[:, pl.ds(lat, inner)] = inner_ref[...]
    tokens_ref[:, pl.ds(lat + inner, lat)] = outer[:, lat:]


def call(kernel, out_shape, inputs, scratch=(), flops=0, moved=0):
    return pl.pallas_call(
        kernel,
        out_shape=out_shape,
        in_specs=[pl.BlockSpec(memory_space=pltpu.VMEM)] * len(inputs),
        out_specs=jax.tree.map(lambda unused: pl.BlockSpec(memory_space=pltpu.VMEM), out_shape),
        scratch_shapes=list(scratch),
        compiler_params=pltpu.CompilerParams(vmem_limit_bytes=VMEM_BYTES),
        cost_estimate=pl.CostEstimate(flops=flops, bytes_accessed=moved, transcendentals=0),
    )(*inputs)


def turned(value, axis, away):
    count = lax.axis_size(axis)
    return lax.ppermute(value, axis, [(i, (i + away) % count) for i in range(count)])


def band_blocks(block, beside):
    rows = [block] + [turned(block, "ch", away) for away in range(1, lax.axis_size("ch"))]
    rows[1:], beside = lax.optimization_barrier((rows[1:], beside))
    blocks = []
    for row in rows:
        blocks.append(row)
        blocks.extend(turned(row, "sub", away) for away in range(1, lax.axis_size("sub")))
    return blocks, beside


def encode(weather, conv_first, conv_second, patch_embed):
    chans, lon, lat = weather.shape
    pairs, wide = lon // 2, 2 * chans
    embed = patch_embed.shape[1]
    shape = functools.partial(jax.ShapeDtypeStruct, dtype=jnp.bfloat16)
    packed = call(
        pack_kernel, shape((pairs, lat, wide)), (jnp.transpose(weather, (1, 2, 0)),), moved=weather.size * 10
    )
    taps = shape((4 * chans, 12 * chans))
    weights = call(
        weights_kernel,
        (taps, taps, shape((embed, 4 * chans))),
        (conv_first, conv_second, patch_embed),
        scratch=[pltpu.VMEM((patch_embed.shape[0], LANES), jnp.float32)],
        moved=conv_first.size * 20,
    )
    blocks, weights = band_blocks(packed, weights)
    lat = len(blocks) * lat
    edge = shape((1, lat, wide))
    field, low, high = call(
        functools.partial(join_kernel, lax.axis_size("ch"), lax.axis_size("sub")),
        (shape((pairs, lat, wide)), edge, edge),
        blocks,
        moved=packed.size * 4 * len(blocks),
    )
    before = turned(high, "tok", 1)
    after = turned(low, "tok", -1)
    work = 2 * lat * 4 * chans * 6 * chans * 5
    held = shape((4, lat, wide))
    hidden = pltpu.VMEM((pairs, lat, wide), jnp.bfloat16)
    inner, upper_edge, lower_edge = call(
        inner_kernel,
        (shape((embed, (pairs - 4) * lat // 2)), held, held),
        (field, *weights),
        scratch=[hidden, hidden, pltpu.VMEM(((pairs - 4) * lat, wide), jnp.float32)],
        flops=work * (pairs - 3),
        moved=field.size * 2,
    )
    return call(
        outer_kernel,
        shape((embed, pairs * lat // 2)),
        (field, before, after, upper_edge, lower_edge, *weights, inner),
        scratch=[pltpu.VMEM((4 * lat, wide), jnp.float32)],
        flops=work * 4,
        moved=field.size * 2,
    )


def sent_kernel(first, tokens_ref, mixing_ref, sent_ref):
    rows, width = sent_ref.shape
    step = STEP if width % STEP == 0 else width
    tokens = tokens_ref[:rows]
    for at in range(0, width, step):
        product = dot(tokens, mixing_ref[:, pl.ds(first + at, step)])
        sent_ref[:, pl.ds(at, step)] = product.astype(sent_ref.dtype)


def hop_kernel(first, arrived_ref, tokens_ref, mixing_ref, sent_ref, kept_ref):
    rows, width = sent_ref.shape
    step = STEP if width % STEP == 0 else width
    tokens = tokens_ref[rows:]
    for at in range(0, width, step):
        product = dot(tokens, mixing_ref[:, pl.ds(first + at, step)])
        arrived = arrived_ref[:, pl.ds(at, step)].astype(jnp.float32)
        sent_ref[:, pl.ds(at, step)] = (arrived + product[:rows]).astype(sent_ref.dtype)
        kept_ref[:, pl.ds(at, step)] = product[rows:]


def lift(tokens, token_mixing, pieces):
    count = lax.axis_size("tok")
    embed = tokens.shape[0]
    rows = embed // count
    width = token_mixing.shape[1] // pieces
    sent = jax.ShapeDtypeStruct((rows, width), jnp.bfloat16)
    travelling = [
        call(functools.partial(sent_kernel, piece * width), sent, (tokens, token_mixing)) for piece in range(pieces)
    ]
    kept = [None] * pieces
    for step in range(1, count):
        for piece in range(pieces):
            arrived = turned(travelling[piece], "tok", -1)
            if step == 1:
                travelling[piece], kept[piece] = call(
                    functools.partial(hop_kernel, piece * width),
                    [sent, jax.ShapeDtypeStruct((embed - 2 * rows, width), jnp.float32)],
                    (arrived, tokens, token_mixing),
                )
            else:
                at = (step - 2) * rows
                summed = arrived.astype(jnp.float32) + kept[piece][at : at + rows]
                if step == count - 1:
                    summed = gelu(summed)
                travelling[piece] = summed.astype(jnp.bfloat16)
    return jnp.concatenate(travelling, axis=1)


def local(weather, conv_first, conv_second, patch_embed, token_mixing):
    tokens = encode(weather, conv_first, conv_second, patch_embed)
    return lift(tokens, token_mixing, PIECES)


def solution(mesh):
    placed = (P("groups", "tok", ("ch", "sub")), P(), P(), P(), P("tok", ("ch", "sub")))
    return jax.shard_map(
        local,
        mesh=mesh,
        in_specs=placed,
        out_specs=P(("groups", "tok"), ("ch", "sub")),
        check_vma=False,
    )
```

```python
import functools

import jax
import jax.numpy as jnp
from jax import lax
from jax.experimental import pallas as pl
from jax.experimental.pallas import tpu as pltpu
from jax.sharding import PartitionSpec as P

PIECES = 4
STEP = 256
LANES = 128
VMEM_BYTES = 24 * 1024 * 1024
ROWS_AT_ONCE = 1024


def pack_kernel(field_ref, packed_ref):
    lon, lat, chans = field_ref.shape
    pairs = field_ref[...].reshape(lon // 2, 2, lat, chans)
    packed_ref[...] = jnp.concatenate([pairs[:, 0], pairs[:, 1]], axis=-1).astype(packed_ref.dtype)


def join_kernel(count_ch, count_sub, *refs):
    blocks, (field_ref, low_ref, high_ref) = refs[:-3], refs[-3:]
    pairs, lat, wide = field_ref.shape
    width = lat // (count_ch * count_sub)
    for away_ch in range(count_ch):
        for away_sub in range(count_sub):
            at_ch = lax.rem(lax.axis_index("ch") + count_ch - away_ch, count_ch)
            at_sub = lax.rem(lax.axis_index("sub") + count_sub - away_sub, count_sub)
            here = pl.ds(pl.multiple_of((at_ch * count_sub + at_sub) * width, width), width)
            block = blocks[away_ch * count_sub + away_sub][...]
            field_ref[:, here, :] = block
            low_ref[:, here, :] = block[:1]
            high_ref[:, here, :] = block[pairs - 1 :]


def split_two(value):
    upper = value.astype(jnp.bfloat16)
    return upper, (value - upper.astype(jnp.float32)).astype(jnp.bfloat16)


def spread_taps(kernel_ref):
    chans = kernel_ref.shape[1]
    nothing = jnp.zeros((chans, kernel_ref.shape[2]), jnp.float32)
    rows = []
    for tap in range(3):
        taps = [kernel_ref[3 * turn + tap] for turn in range(3)]
        rows.append(jnp.concatenate([taps[1], taps[2], nothing, taps[0]], axis=-1))
        rows.append(jnp.concatenate([taps[0], taps[1], taps[2], nothing], axis=-1))
    return jnp.concatenate(rows, axis=0).T


def weights_kernel(first_ref, second_ref, embed_ref, taps_one_ref, taps_two_ref, embed_out_ref, scratch):
    for source, target in ((first_ref, taps_one_ref), (second_ref, taps_two_ref)):
        upper, lower = split_two(spread_taps(source))
        target[...] = jnp.concatenate([upper, lower], axis=1)
    chans = embed_ref.shape[0] // 4
    embed = embed_ref.shape[1]
    count = lax.axis_size("tok")
    turn = lax.rem(lax.axis_index("tok") + 1, count) * (embed // count)
    turned_embed = pltpu.roll(embed_ref[...].astype(jnp.float32), lax.rem(embed - turn, embed), axis=1)
    for first in range(0, embed, LANES):
        scratch[...] = turned_embed[:, first : first + LANES]
        ordered = [scratch[pl.ds(2 * a + b, chans, stride=4), :] for b in range(2) for a in range(2)]
        rows = jnp.concatenate(ordered, axis=0).T
        embed_out_ref[pl.ds(first, LANES), :] = rows.astype(embed_out_ref.dtype)


def pairs_at_once(pairs, lat):
    best = 1
    for size in range(1, pairs + 1):
        if pairs % size == 0 and size * lat <= ROWS_AT_ONCE:
            best = size
    return best


def window(pair_at, pairs):
    rows = []
    for pair in pairs:
        here = pair_at(pair)
        lane = lax.broadcasted_iota(jnp.int32, here.shape, 1)
        beside = jnp.where(lane < here.shape[1] // 2, pair_at(pair + 1), pair_at(pair - 1))
        rows.append(jnp.concatenate([here, beside], axis=-1))
    return jnp.concatenate(rows, axis=0)


def add_lat_taps(products, lat):
    wide = products.shape[1] // 3
    count = products.shape[0]
    row = lax.broadcasted_iota(jnp.int32, (1, lat, wide), 1)
    below = pltpu.roll(products[:, :wide], 1, axis=0).reshape(-1, lat, wide)
    above = pltpu.roll(products[:, 2 * wide :], count - 1, axis=0).reshape(-1, lat, wide)
    here = products[:, wide : 2 * wide].reshape(-1, lat, wide)
    return here + jnp.where(row == 0, 0.0, below) + jnp.where(row == lat - 1, 0.0, above)


def gelu(value):
    return 0.5 * value * (1.0 + lax.erf(value * (0.5**0.5)))


def dot(left, right):
    return jnp.dot(left, right, preferred_element_type=jnp.float32)


def dot_both(rows, taps_ref):
    both = dot(rows, taps_ref[...])
    half = both.shape[1] // 2
    return both[:, :half] + both[:, half:]


def first_conv(field_at, pairs, taps_ref, lat):
    products = dot_both(window(field_at, pairs), taps_ref)
    return split_two(gelu(add_lat_taps(products, lat)))


def second_conv(upper_at, lower_at, pairs, taps_ref, lat):
    upper, lower = window(upper_at, pairs), window(lower_at, pairs)
    products = dot_both(upper, taps_ref) + dot(lower, taps_ref[:, : taps_ref.shape[1] // 2])
    rounded = add_lat_taps(products, lat).astype(jnp.bfloat16).astype(jnp.float32)
    return rounded.reshape(-1, rounded.shape[2])


def embed_patches(two_ref, embed_ref):
    half = two_ref.shape[0] // 2
    patches = jnp.concatenate(
        [two_ref[pl.ds(b, half, stride=2), :].astype(jnp.bfloat16) for b in range(2)], axis=-1
    )
    return lax.dot_general(
        embed_ref[...], patches, (((1,), (1,)), ((), ())), preferred_element_type=jnp.float32
    ).astype(jnp.bfloat16)


def runs(first, last, lat):
    size = pairs_at_once(last - first, lat)
    return [list(range(at, at + size)) for at in range(first, last, size)]


def inner_kernel(
    field_ref, taps_one_ref, taps_two_ref, embed_ref, tokens_ref, upper_edge_ref, lower_edge_ref, upper_ref, lower_ref, two_ref
):
    pairs, lat, wide = field_ref.shape
    for run in runs(1, pairs - 1, lat):
        upper, lower = first_conv(lambda pair: field_ref[pair], run, taps_one_ref, lat)
        upper_ref[pl.ds(run[0], len(run))] = upper
        lower_ref[pl.ds(run[0], len(run))] = lower
    for inside, edge in ((upper_ref, upper_edge_ref), (lower_ref, lower_edge_ref)):
        edge[pl.ds(0, 2)] = inside[pl.ds(1, 2)]
        edge[pl.ds(2, 2)] = inside[pl.ds(pairs - 3, 2)]
    for run in runs(2, pairs - 2, lat):
        two = second_conv(lambda pair: upper_ref[pair], lambda pair: lower_ref[pair], run, taps_two_ref, lat)
        two_ref[pl.ds((run[0] - 2) * lat, len(run) * lat), :] = two
    tokens_ref[...] = embed_patches(two_ref, embed_ref)


def outer_kernel(
    field_ref, before_ref, after_ref, upper_edge_ref, lower_edge_ref, taps_one_ref, taps_two_ref, embed_ref, inner_ref, tokens_ref, two_ref
):
    pairs, lat, wide = field_ref.shape

    def field_at(pair):
        if pair < 0:
            return before_ref[0]
        if pair >= pairs:
            return after_ref[0]
        return field_ref[pair]

    outermost = [-1, 0, pairs - 1, pairs]
    next_inside = [1, 2, pairs - 3, pairs - 2]
    upper, lower = first_conv(field_at, outermost, taps_one_ref, lat)

    def hidden_at(found, edge_ref):
        def at(pair):
            if pair in outermost:
                return found[outermost.index(pair)]
            return edge_ref[next_inside.index(pair)]

        return at

    two_ref[...] = second_conv(
        hidden_at(upper, upper_edge_ref), hidden_at(lower, lower_edge_ref), [0, 1, pairs - 2, pairs - 1], taps_two_ref, lat
    )
    outer = embed_patches(two_ref, embed_ref)
    inner = inner_ref.shape[1]
    tokens_ref[:, :lat] = outer[:, :lat]
    tokens_ref[:, pl.ds(lat, inner)] = inner_ref[...]
    tokens_ref[:, pl.ds(lat + inner, lat)] = outer[:, lat:]


def call(kernel, out_shape, inputs, scratch=(), flops=0, moved=0):
    return pl.pallas_call(
        kernel,
        out_shape=out_shape,
        in_specs=[pl.BlockSpec(memory_space=pltpu.VMEM)] * len(inputs),
        out_specs=jax.tree.map(lambda unused: pl.BlockSpec(memory_space=pltpu.VMEM), out_shape),
        scratch_shapes=list(scratch),
        compiler_params=pltpu.CompilerParams(vmem_limit_bytes=VMEM_BYTES),
        cost_estimate=pl.CostEstimate(flops=flops, bytes_accessed=moved, transcendentals=0),
    )(*inputs)


def turned(value, axis, away):
    count = lax.axis_size(axis)
    return lax.ppermute(value, axis, [(i, (i + away) % count) for i in range(count)])


def band_blocks(block, beside):
    rows = [block] + [turned(block, "ch", away) for away in range(1, lax.axis_size("ch"))]
    rows[1:], beside = lax.optimization_barrier((rows[1:], beside))
    blocks = []
    for row in rows:
        blocks.append(row)
        blocks.extend(turned(row, "sub", away) for away in range(1, lax.axis_size("sub")))
    return blocks, beside


def encode(weather, conv_first, conv_second, patch_embed):
    chans, lon, lat = weather.shape
    pairs, wide = lon // 2, 2 * chans
    embed = patch_embed.shape[1]
    shape = functools.partial(jax.ShapeDtypeStruct, dtype=jnp.bfloat16)
    packed = call(
        pack_kernel, shape((pairs, lat, wide)), (jnp.transpose(weather, (1, 2, 0)),), moved=weather.size * 10
    )
    taps = shape((4 * chans, 12 * chans))
    weights = call(
        weights_kernel,
        (taps, taps, shape((embed, 4 * chans))),
        (conv_first, conv_second, patch_embed),
        scratch=[pltpu.VMEM((patch_embed.shape[0], LANES), jnp.float32)],
        moved=conv_first.size * 20,
    )
    blocks, weights = band_blocks(packed, weights)
    lat = len(blocks) * lat
    edge = shape((1, lat, wide))
    field, low, high = call(
        functools.partial(join_kernel, lax.axis_size("ch"), lax.axis_size("sub")),
        (shape((pairs, lat, wide)), edge, edge),
        blocks,
        moved=packed.size * 4 * len(blocks),
    )
    before = turned(high, "tok", 1)
    after = turned(low, "tok", -1)
    work = 2 * lat * 4 * chans * 6 * chans * 5
    held = shape((4, lat, wide))
    hidden = pltpu.VMEM((pairs, lat, wide), jnp.bfloat16)
    inner, upper_edge, lower_edge = call(
        inner_kernel,
        (shape((embed, (pairs - 4) * lat // 2)), held, held),
        (field, *weights),
        scratch=[hidden, hidden, pltpu.VMEM(((pairs - 4) * lat, wide), jnp.float32)],
        flops=work * (pairs - 3),
        moved=field.size * 2,
    )
    return call(
        outer_kernel,
        shape((embed, pairs * lat // 2)),
        (field, before, after, upper_edge, lower_edge, *weights, inner),
        scratch=[pltpu.VMEM((4 * lat, wide), jnp.float32)],
        flops=work * 4,
        moved=field.size * 2,
    )


def sent_kernel(first, block, tokens_ref, mixing_ref, sent_ref):
    rows, width = sent_ref.shape
    step = STEP if width % STEP == 0 else width
    tokens = tokens_ref[pl.ds(block * rows, rows), :]
    for at in range(0, width, step):
        product = dot(tokens, mixing_ref[:, pl.ds(first + at, step)])
        sent_ref[:, pl.ds(at, step)] = product.astype(sent_ref.dtype)


def hop_kernel(first, blocks, arrived_ref, tokens_ref, mixing_ref, sent_ref, kept_ref):
    rows, width = sent_ref.shape
    step = STEP if width % STEP == 0 else width
    tokens = jnp.concatenate([tokens_ref[pl.ds(block * rows, rows), :] for block in blocks], axis=0)
    for at in range(0, width, step):
        product = dot(tokens, mixing_ref[:, pl.ds(first + at, step)])
        arrived = arrived_ref[:, pl.ds(at, step)].astype(jnp.float32)
        sent_ref[:, pl.ds(at, step)] = (arrived + product[:rows]).astype(sent_ref.dtype)
        kept_ref[:, pl.ds(at, step)] = product[rows:]


def lift(tokens, token_mixing, pieces):
    count = lax.axis_size("tok")
    embed = tokens.shape[0]
    rows = embed // count
    width = token_mixing.shape[1] // pieces
    sent = jax.ShapeDtypeStruct((rows, width), jnp.bfloat16)
    ways = [1 if piece % 2 == 0 else -1 for piece in range(pieces)]
    blocks = [list(range(count - 2, -1, -1)) if way == 1 else list(range(count - 1)) for way in ways]
    travelling = [
        call(functools.partial(sent_kernel, piece * width, blocks[piece][0]), sent, (tokens, token_mixing))
        for piece in range(pieces)
    ]
    kept = [None] * pieces
    for step in range(1, count):
        for piece in range(pieces):
            arrived = turned(travelling[piece], "tok", ways[piece])
            if step == 1:
                travelling[piece], kept[piece] = call(
                    functools.partial(hop_kernel, piece * width, blocks[piece][1:] + [count - 1]),
                    [sent, jax.ShapeDtypeStruct((embed - 2 * rows, width), jnp.float32)],
                    (arrived, tokens, token_mixing),
                )
            else:
                at = (step - 2) * rows
                summed = arrived.astype(jnp.float32) + kept[piece][at : at + rows]
                if step == count - 1:
                    summed = gelu(summed)
                travelling[piece] = summed.astype(jnp.bfloat16)
    return jnp.concatenate(travelling, axis=1)


def local(weather, conv_first, conv_second, patch_embed, token_mixing):
    tokens = encode(weather, conv_first, conv_second, patch_embed)
    return lift(tokens, token_mixing, PIECES)


def solution(mesh):
    placed = (P("groups", "tok", ("ch", "sub")), P(), P(), P(), P("tok", ("ch", "sub")))
    return jax.shard_map(
        local,
        mesh=mesh,
        in_specs=placed,
        out_specs=P(("groups", "tok"), ("ch", "sub")),
        check_vma=False,
    )
```

```python
import functools

import jax
import jax.numpy as jnp
from jax import lax
from jax.experimental import pallas as pl
from jax.experimental.pallas import tpu as pltpu
from jax.sharding import PartitionSpec as P

PIECES = 4
STEP = 256
LANES = 128
WRITES = 4
VMEM_BYTES = 24 * 1024 * 1024
ROWS_AT_ONCE = 1024


def pack_kernel(field_ref, packed_ref):
    lon, lat, chans = field_ref.shape
    pairs = field_ref[...].reshape(lon // 2, 2, lat, chans)
    packed_ref[...] = jnp.concatenate([pairs[:, 0], pairs[:, 1]], axis=-1).astype(packed_ref.dtype)


def join_kernel(count_ch, count_sub, *refs):
    blocks, (field_ref, low_ref, high_ref) = refs[:-3], refs[-3:]
    pairs, lat, wide = field_ref.shape
    width = lat // (count_ch * count_sub)
    for away_ch in range(count_ch):
        for away_sub in range(count_sub):
            at_ch = lax.rem(lax.axis_index("ch") + count_ch - away_ch, count_ch)
            at_sub = lax.rem(lax.axis_index("sub") + count_sub - away_sub, count_sub)
            here = pl.ds(pl.multiple_of((at_ch * count_sub + at_sub) * width, width), width)
            block = blocks[away_ch * count_sub + away_sub][...]
            field_ref[:, here, :] = block
            low_ref[:, here, :] = block[:1]
            high_ref[:, here, :] = block[pairs - 1 :]


def split_two(value):
    upper = value.astype(jnp.bfloat16)
    return upper, (value - upper.astype(jnp.float32)).astype(jnp.bfloat16)


def spread_taps(kernel_ref):
    chans = kernel_ref.shape[1]
    nothing = jnp.zeros((chans, kernel_ref.shape[2]), jnp.float32)
    rows = []
    for tap in range(3):
        taps = [kernel_ref[3 * turn + tap] for turn in range(3)]
        rows.append(jnp.concatenate([taps[1], taps[2], nothing, taps[0]], axis=-1))
        rows.append(jnp.concatenate([taps[0], taps[1], taps[2], nothing], axis=-1))
    return jnp.concatenate(rows, axis=0).T


def weights_kernel(first_ref, second_ref, embed_ref, taps_one_ref, taps_two_ref, embed_out_ref, scratch):
    for source, target in ((first_ref, taps_one_ref), (second_ref, taps_two_ref)):
        upper, lower = split_two(spread_taps(source))
        target[...] = jnp.concatenate([upper, lower], axis=1)
    chans = embed_ref.shape[0] // 4
    embed = embed_ref.shape[1]
    count = lax.axis_size("tok")
    turn = lax.rem(lax.axis_index("tok") + 1, count) * (embed // count)
    turned_embed = pltpu.roll(embed_ref[...].astype(jnp.float32), lax.rem(embed - turn, embed), axis=1)
    for first in range(0, embed, LANES):
        scratch[...] = turned_embed[:, first : first + LANES]
        ordered = [scratch[pl.ds(2 * a + b, chans, stride=4), :] for b in range(2) for a in range(2)]
        rows = jnp.concatenate(ordered, axis=0).T
        embed_out_ref[pl.ds(first, LANES), :] = rows.astype(embed_out_ref.dtype)


def pairs_at_once(pairs, lat):
    best = 1
    for size in range(1, pairs + 1):
        if pairs % size == 0 and size * lat <= ROWS_AT_ONCE:
            best = size
    return best


def window(pair_at, pairs):
    rows = []
    for pair in pairs:
        here = pair_at(pair)
        lane = lax.broadcasted_iota(jnp.int32, here.shape, 1)
        beside = jnp.where(lane < here.shape[1] // 2, pair_at(pair + 1), pair_at(pair - 1))
        rows.append(jnp.concatenate([here, beside], axis=-1))
    return jnp.concatenate(rows, axis=0)


def add_lat_taps(products, lat):
    wide = products.shape[1] // 3
    count = products.shape[0]
    row = lax.broadcasted_iota(jnp.int32, (1, lat, wide), 1)
    below = pltpu.roll(products[:, :wide], 1, axis=0).reshape(-1, lat, wide)
    above = pltpu.roll(products[:, 2 * wide :], count - 1, axis=0).reshape(-1, lat, wide)
    here = products[:, wide : 2 * wide].reshape(-1, lat, wide)
    return here + jnp.where(row == 0, 0.0, below) + jnp.where(row == lat - 1, 0.0, above)


def gelu(value):
    return 0.5 * value * (1.0 + lax.erf(value * (0.5**0.5)))


def dot(left, right):
    return jnp.dot(left, right, preferred_element_type=jnp.float32)


def dot_both(rows, taps_ref):
    both = dot(rows, taps_ref[...])
    half = both.shape[1] // 2
    return both[:, :half] + both[:, half:]


def first_conv(field_at, pairs, taps_ref, lat):
    products = dot_both(window(field_at, pairs), taps_ref)
    return split_two(gelu(add_lat_taps(products, lat)))


def second_conv(upper_at, lower_at, pairs, taps_ref, lat):
    upper, lower = window(upper_at, pairs), window(lower_at, pairs)
    products = dot_both(upper, taps_ref) + dot(lower, taps_ref[:, : taps_ref.shape[1] // 2])
    rounded = add_lat_taps(products, lat).astype(jnp.bfloat16).astype(jnp.float32)
    return rounded.reshape(-1, rounded.shape[2])


def embed_patches(two_ref, embed_ref):
    half = two_ref.shape[0] // 2
    patches = jnp.concatenate(
        [two_ref[pl.ds(b, half, stride=2), :].astype(jnp.bfloat16) for b in range(2)], axis=-1
    )
    return lax.dot_general(
        embed_ref[...], patches, (((1,), (1,)), ((), ())), preferred_element_type=jnp.float32
    ).astype(jnp.bfloat16)


def runs(first, last, lat):
    size = pairs_at_once(last - first, lat)
    return [list(range(at, at + size)) for at in range(first, last, size)]


def inner_kernel(
    field_ref, taps_one_ref, taps_two_ref, embed_ref, tokens_ref, upper_edge_ref, lower_edge_ref, upper_ref, lower_ref, two_ref
):
    pairs, lat, wide = field_ref.shape
    for run in runs(1, pairs - 1, lat):
        upper, lower = first_conv(lambda pair: field_ref[pair], run, taps_one_ref, lat)
        upper_ref[pl.ds(run[0], len(run))] = upper
        lower_ref[pl.ds(run[0], len(run))] = lower
    for inside, edge in ((upper_ref, upper_edge_ref), (lower_ref, lower_edge_ref)):
        edge[pl.ds(0, 2)] = inside[pl.ds(1, 2)]
        edge[pl.ds(2, 2)] = inside[pl.ds(pairs - 3, 2)]
    for run in runs(2, pairs - 2, lat):
        two = second_conv(lambda pair: upper_ref[pair], lambda pair: lower_ref[pair], run, taps_two_ref, lat)
        two_ref[pl.ds((run[0] - 2) * lat, len(run) * lat), :] = two
    tokens_ref[...] = embed_patches(two_ref, embed_ref)


def outer_kernel(
    field_ref, before_ref, after_ref, upper_edge_ref, lower_edge_ref, taps_one_ref, taps_two_ref, embed_ref, inner_ref, tokens_ref, two_ref
):
    pairs, lat, wide = field_ref.shape

    def field_at(pair):
        if pair < 0:
            return before_ref[0]
        if pair >= pairs:
            return after_ref[0]
        return field_ref[pair]

    outermost = [-1, 0, pairs - 1, pairs]
    next_inside = [1, 2, pairs - 3, pairs - 2]
    upper, lower = first_conv(field_at, outermost, taps_one_ref, lat)

    def hidden_at(found, edge_ref):
        def at(pair):
            if pair in outermost:
                return found[outermost.index(pair)]
            return edge_ref[next_inside.index(pair)]

        return at

    two_ref[...] = second_conv(
        hidden_at(upper, upper_edge_ref), hidden_at(lower, lower_edge_ref), [0, 1, pairs - 2, pairs - 1], taps_two_ref, lat
    )
    outer = embed_patches(two_ref, embed_ref)
    inner = inner_ref.shape[1]
    tokens_ref[:, :lat] = outer[:, :lat]
    tokens_ref[:, pl.ds(lat, inner)] = inner_ref[...]
    tokens_ref[:, pl.ds(lat + inner, lat)] = outer[:, lat:]


def call(kernel, out_shape, inputs, scratch=(), flops=0, moved=0):
    return pl.pallas_call(
        kernel,
        out_shape=out_shape,
        in_specs=[pl.BlockSpec(memory_space=pltpu.VMEM)] * len(inputs),
        out_specs=jax.tree.map(lambda unused: pl.BlockSpec(memory_space=pltpu.VMEM), out_shape),
        scratch_shapes=list(scratch),
        compiler_params=pltpu.CompilerParams(vmem_limit_bytes=VMEM_BYTES),
        cost_estimate=pl.CostEstimate(flops=flops, bytes_accessed=moved, transcendentals=0),
    )(*inputs)


def turned(value, axis, away):
    count = lax.axis_size(axis)
    return lax.ppermute(value, axis, [(i, (i + away) % count) for i in range(count)])


def band_blocks(block, beside):
    rows = [block] + [turned(block, "ch", away) for away in range(1, lax.axis_size("ch"))]
    rows[1:], beside = lax.optimization_barrier((rows[1:], beside))
    blocks = []
    for row in rows:
        blocks.append(row)
        blocks.extend(turned(row, "sub", away) for away in range(1, lax.axis_size("sub")))
    return blocks, beside


def encode(weather, conv_first, conv_second, patch_embed):
    chans, lon, lat = weather.shape
    pairs, wide = lon // 2, 2 * chans
    embed = patch_embed.shape[1]
    shape = functools.partial(jax.ShapeDtypeStruct, dtype=jnp.bfloat16)
    packed = call(
        pack_kernel, shape((pairs, lat, wide)), (jnp.transpose(weather, (1, 2, 0)),), moved=weather.size * 10
    )
    taps = shape((4 * chans, 12 * chans))
    weights = call(
        weights_kernel,
        (taps, taps, shape((embed, 4 * chans))),
        (conv_first, conv_second, patch_embed),
        scratch=[pltpu.VMEM((patch_embed.shape[0], LANES), jnp.float32)],
        moved=conv_first.size * 20,
    )
    blocks, weights = band_blocks(packed, weights)
    lat = len(blocks) * lat
    edge = shape((1, lat, wide))
    field, low, high = call(
        functools.partial(join_kernel, lax.axis_size("ch"), lax.axis_size("sub")),
        (shape((pairs, lat, wide)), edge, edge),
        blocks,
        moved=packed.size * 4 * len(blocks),
    )
    before = turned(high, "tok", 1)
    after = turned(low, "tok", -1)
    work = 2 * lat * 4 * chans * 6 * chans * 5
    held = shape((4, lat, wide))
    hidden = pltpu.VMEM((pairs, lat, wide), jnp.bfloat16)
    inner, upper_edge, lower_edge = call(
        inner_kernel,
        (shape((embed, (pairs - 4) * lat // 2)), held, held),
        (field, *weights),
        scratch=[hidden, hidden, pltpu.VMEM(((pairs - 4) * lat, wide), jnp.float32)],
        flops=work * (pairs - 3),
        moved=field.size * 2,
    )
    return call(
        outer_kernel,
        shape((embed, pairs * lat // 2)),
        (field, before, after, upper_edge, lower_edge, *weights, inner),
        scratch=[pltpu.VMEM((4 * lat, wide), jnp.float32)],
        flops=work * 4,
        moved=field.size * 2,
    )


def sent_kernel(first, block, tokens_ref, mixing_ref, sent_ref):
    rows, width = sent_ref.shape
    step = STEP if width % STEP == 0 else width
    tokens = tokens_ref[pl.ds(block * rows, rows), :]
    for at in range(0, width, step):
        product = dot(tokens, mixing_ref[:, pl.ds(first + at, step)])
        sent_ref[:, pl.ds(at, step)] = product.astype(sent_ref.dtype)


def hop_kernel(first, blocks, arrived_ref, tokens_ref, mixing_ref, sent_ref, kept_ref):
    rows, width = sent_ref.shape
    step = STEP if width % STEP == 0 else width
    tokens = jnp.concatenate([tokens_ref[pl.ds(block * rows, rows), :] for block in blocks], axis=0)
    for at in range(0, width, step):
        product = dot(tokens, mixing_ref[:, pl.ds(first + at, step)])
        arrived = arrived_ref[:, pl.ds(at, step)].astype(jnp.float32)
        sent_ref[:, pl.ds(at, step)] = (arrived + product[:rows]).astype(sent_ref.dtype)
        kept_ref[:, pl.ds(at, step)] = product[rows:]


def last_kernel(first, arrived_ref, kept_ref, *refs):
    result_ref, held_ref, written = refs[-3:]
    rows, width = arrived_ref.shape
    part = width // written.shape[0]
    copies = []
    for at in range(written.shape[0]):
        here = pl.ds(at * part, part)
        own = kept_ref[kept_ref.shape[0] - rows :, at * part : (at + 1) * part]
        held_ref[:, here] = gelu(arrived_ref[:, here].astype(jnp.float32) + own).astype(held_ref.dtype)
        target = result_ref.at[:, pl.ds(first + at * part, part)]
        copies.append(pltpu.make_async_copy(held_ref.at[:, here], target, written.at[at]))
        copies[-1].start()
    for copy in copies:
        copy.wait()


def finish(first, arrived, kept, result, columns):
    rows, width = arrived.shape
    near, far = pl.BlockSpec(memory_space=pltpu.VMEM), pl.BlockSpec(memory_space=pl.ANY)
    earlier = [] if result is None else [result]
    return pl.pallas_call(
        functools.partial(last_kernel, first),
        out_shape=jax.ShapeDtypeStruct((rows, columns), jnp.bfloat16),
        in_specs=[near, near] + [far] * len(earlier),
        out_specs=far,
        input_output_aliases={2: 0} if earlier else {},
        scratch_shapes=[
            pltpu.VMEM((rows, width), jnp.bfloat16),
            pltpu.SemaphoreType.DMA((WRITES if width % (WRITES * LANES) == 0 else 1,)),
        ],
        compiler_params=pltpu.CompilerParams(vmem_limit_bytes=VMEM_BYTES),
        cost_estimate=pl.CostEstimate(flops=0, bytes_accessed=0, transcendentals=0),
    )(arrived, kept, *earlier)


def lift(tokens, token_mixing, pieces):
    count = lax.axis_size("tok")
    embed = tokens.shape[0]
    rows = embed // count
    width = token_mixing.shape[1] // pieces
    sent = jax.ShapeDtypeStruct((rows, width), jnp.bfloat16)
    ways = [1 if piece % 2 == 0 else -1 for piece in range(pieces)]
    blocks = [list(range(count - 2, -1, -1)) if way == 1 else list(range(count - 1)) for way in ways]
    travelling = [
        call(functools.partial(sent_kernel, piece * width, blocks[piece][0]), sent, (tokens, token_mixing))
        for piece in range(pieces)
    ]
    kept = [None] * pieces
    result = None
    for step in range(1, count):
        for piece in range(pieces):
            arrived = turned(travelling[piece], "tok", ways[piece])
            if step == 1:
                travelling[piece], kept[piece] = call(
                    functools.partial(hop_kernel, piece * width, blocks[piece][1:] + [count - 1]),
                    [sent, jax.ShapeDtypeStruct((embed - 2 * rows, width), jnp.float32)],
                    (arrived, tokens, token_mixing),
                )
            elif step < count - 1:
                at = (step - 2) * rows
                summed = arrived.astype(jnp.float32) + kept[piece][at : at + rows]
                travelling[piece] = summed.astype(jnp.bfloat16)
            else:
                result = finish(piece * width, arrived, kept[piece], result, pieces * width)
    return result


def local(weather, conv_first, conv_second, patch_embed, token_mixing):
    tokens = encode(weather, conv_first, conv_second, patch_embed)
    return lift(tokens, token_mixing, PIECES)


def solution(mesh):
    placed = (P("groups", "tok", ("ch", "sub")), P(), P(), P(), P("tok", ("ch", "sub")))
    return jax.shard_map(
        local,
        mesh=mesh,
        in_specs=placed,
        out_specs=P(("groups", "tok"), ("ch", "sub")),
        check_vma=False,
    )
```

```python
import functools

import jax
import jax.numpy as jnp
from jax import lax
from jax.experimental import pallas as pl
from jax.experimental.pallas import tpu as pltpu
from jax.sharding import PartitionSpec as P

PIECES = 4
STEP = 256
LANES = 128
WRITES = 4
VMEM_BYTES = 24 * 1024 * 1024
ROWS_AT_ONCE = 1024


def pack_kernel(field_ref, packed_ref, low_ref, high_ref):
    lon, lat, chans = field_ref.shape
    pairs = field_ref[...].reshape(lon // 2, 2, lat, chans)
    joined = jnp.concatenate([pairs[:, 0], pairs[:, 1]], axis=-1).astype(packed_ref.dtype)
    packed_ref[...] = joined
    low_ref[...] = joined[:1]
    high_ref[...] = joined[-1:]


def place(away, count_ch, count_sub, width):
    away_ch, away_sub = away // count_sub, away % count_sub
    at_ch = lax.rem(lax.axis_index("ch") + count_ch - away_ch, count_ch)
    at_sub = lax.rem(lax.axis_index("sub") + count_sub - away_sub, count_sub)
    return pl.ds(pl.multiple_of((at_ch * count_sub + at_sub) * width, width), width)


def join_kernel(count_ch, count_sub, *refs):
    blocks, field_ref = refs[:-1], refs[-1]
    width = field_ref.shape[1] // len(blocks)
    for away, block in enumerate(blocks):
        field_ref[:, place(away, count_ch, count_sub, width), :] = block[...]


def split_two(value):
    upper = value.astype(jnp.bfloat16)
    return upper, (value - upper.astype(jnp.float32)).astype(jnp.bfloat16)


def spread_taps(kernel_ref):
    chans = kernel_ref.shape[1]
    nothing = jnp.zeros((chans, kernel_ref.shape[2]), jnp.float32)
    rows = []
    for tap in range(3):
        taps = [kernel_ref[3 * turn + tap] for turn in range(3)]
        rows.append(jnp.concatenate([taps[1], taps[2], nothing, taps[0]], axis=-1))
        rows.append(jnp.concatenate([taps[0], taps[1], taps[2], nothing], axis=-1))
    return jnp.concatenate(rows, axis=0).T


def weights_kernel(first_ref, second_ref, embed_ref, taps_one_ref, taps_two_ref, embed_out_ref, scratch):
    for source, target in ((first_ref, taps_one_ref), (second_ref, taps_two_ref)):
        upper, lower = split_two(spread_taps(source))
        target[...] = jnp.concatenate([upper, lower], axis=1)
    chans = embed_ref.shape[0] // 4
    embed = embed_ref.shape[1]
    count = lax.axis_size("tok")
    turn = lax.rem(lax.axis_index("tok") + 1, count) * (embed // count)
    turned_embed = pltpu.roll(embed_ref[...].astype(jnp.float32), lax.rem(embed - turn, embed), axis=1)
    for first in range(0, embed, LANES):
        scratch[...] = turned_embed[:, first : first + LANES]
        ordered = [scratch[pl.ds(2 * a + b, chans, stride=4), :] for b in range(2) for a in range(2)]
        rows = jnp.concatenate(ordered, axis=0).T
        embed_out_ref[pl.ds(first, LANES), :] = rows.astype(embed_out_ref.dtype)


def pairs_at_once(pairs, lat):
    best = 1
    for size in range(1, pairs + 1):
        if pairs % size == 0 and size * lat <= ROWS_AT_ONCE:
            best = size
    return best


def window(pair_at, pairs):
    rows = []
    for pair in pairs:
        here = pair_at(pair)
        lane = lax.broadcasted_iota(jnp.int32, here.shape, 1)
        beside = jnp.where(lane < here.shape[1] // 2, pair_at(pair + 1), pair_at(pair - 1))
        rows.append(jnp.concatenate([here, beside], axis=-1))
    return jnp.concatenate(rows, axis=0)


def add_lat_taps(products, lat):
    wide = products.shape[1] // 3
    count = products.shape[0]
    row = lax.broadcasted_iota(jnp.int32, (1, lat, wide), 1)
    below = pltpu.roll(products[:, :wide], 1, axis=0).reshape(-1, lat, wide)
    above = pltpu.roll(products[:, 2 * wide :], count - 1, axis=0).reshape(-1, lat, wide)
    here = products[:, wide : 2 * wide].reshape(-1, lat, wide)
    return here + jnp.where(row == 0, 0.0, below) + jnp.where(row == lat - 1, 0.0, above)


def gelu(value):
    return 0.5 * value * (1.0 + lax.erf(value * (0.5**0.5)))


def dot(left, right):
    return jnp.dot(left, right, preferred_element_type=jnp.float32)


def dot_both(rows, taps_ref):
    both = dot(rows, taps_ref[...])
    half = both.shape[1] // 2
    return both[:, :half] + both[:, half:]


def first_conv(field_at, pairs, taps_ref, lat):
    products = dot_both(window(field_at, pairs), taps_ref)
    return split_two(gelu(add_lat_taps(products, lat)))


def second_conv(upper_at, lower_at, pairs, taps_ref, lat):
    upper, lower = window(upper_at, pairs), window(lower_at, pairs)
    products = dot_both(upper, taps_ref) + dot(lower, taps_ref[:, : taps_ref.shape[1] // 2])
    rounded = add_lat_taps(products, lat).astype(jnp.bfloat16).astype(jnp.float32)
    return rounded.reshape(-1, rounded.shape[2])


def embed_patches(two_ref, embed_ref):
    half = two_ref.shape[0] // 2
    patches = jnp.concatenate(
        [two_ref[pl.ds(b, half, stride=2), :].astype(jnp.bfloat16) for b in range(2)], axis=-1
    )
    return lax.dot_general(
        embed_ref[...], patches, (((1,), (1,)), ((), ())), preferred_element_type=jnp.float32
    ).astype(jnp.bfloat16)


def runs(first, last, lat):
    size = pairs_at_once(last - first, lat)
    return [list(range(at, at + size)) for at in range(first, last, size)]


def inner_kernel(
    field_ref, taps_one_ref, taps_two_ref, embed_ref, tokens_ref, upper_edge_ref, lower_edge_ref, upper_ref, lower_ref, two_ref
):
    pairs, lat, wide = field_ref.shape
    for run in runs(1, pairs - 1, lat):
        upper, lower = first_conv(lambda pair: field_ref[pair], run, taps_one_ref, lat)
        upper_ref[pl.ds(run[0], len(run))] = upper
        lower_ref[pl.ds(run[0], len(run))] = lower
    for inside, edge in ((upper_ref, upper_edge_ref), (lower_ref, lower_edge_ref)):
        edge[pl.ds(0, 2)] = inside[pl.ds(1, 2)]
        edge[pl.ds(2, 2)] = inside[pl.ds(pairs - 3, 2)]
    for run in runs(2, pairs - 2, lat):
        two = second_conv(lambda pair: upper_ref[pair], lambda pair: lower_ref[pair], run, taps_two_ref, lat)
        two_ref[pl.ds((run[0] - 2) * lat, len(run) * lat), :] = two
    tokens_ref[...] = embed_patches(two_ref, embed_ref)


def outer_kernel(count_ch, count_sub, field_ref, *refs):
    count = count_ch * count_sub
    sides, refs = refs[:count], refs[count:]
    upper_edge_ref, lower_edge_ref, taps_one_ref, taps_two_ref, embed_ref, inner_ref, tokens_ref, two_ref, sides_ref = refs
    pairs, lat, wide = field_ref.shape
    for away, block in enumerate(sides):
        sides_ref[:, place(away, count_ch, count_sub, lat // count), :] = block[...]

    def field_at(pair):
        if pair < 0:
            return sides_ref[0]
        if pair >= pairs:
            return sides_ref[1]
        return field_ref[pair]

    outermost = [-1, 0, pairs - 1, pairs]
    next_inside = [1, 2, pairs - 3, pairs - 2]
    upper, lower = first_conv(field_at, outermost, taps_one_ref, lat)

    def hidden_at(found, edge_ref):
        def at(pair):
            if pair in outermost:
                return found[outermost.index(pair)]
            return edge_ref[next_inside.index(pair)]

        return at

    two_ref[...] = second_conv(
        hidden_at(upper, upper_edge_ref), hidden_at(lower, lower_edge_ref), [0, 1, pairs - 2, pairs - 1], taps_two_ref, lat
    )
    outer = embed_patches(two_ref, embed_ref)
    inner = inner_ref.shape[1]
    tokens_ref[:, :lat] = outer[:, :lat]
    tokens_ref[:, pl.ds(lat, inner)] = inner_ref[...]
    tokens_ref[:, pl.ds(lat + inner, lat)] = outer[:, lat:]


def call(kernel, out_shape, inputs, scratch=(), flops=0, moved=0):
    return pl.pallas_call(
        kernel,
        out_shape=out_shape,
        in_specs=[pl.BlockSpec(memory_space=pltpu.VMEM)] * len(inputs),
        out_specs=jax.tree.map(lambda unused: pl.BlockSpec(memory_space=pltpu.VMEM), out_shape),
        scratch_shapes=list(scratch),
        compiler_params=pltpu.CompilerParams(vmem_limit_bytes=VMEM_BYTES),
        cost_estimate=pl.CostEstimate(flops=flops, bytes_accessed=moved, transcendentals=0),
    )(*inputs)


def turned(value, axis, away):
    count = lax.axis_size(axis)
    return lax.ppermute(value, axis, [(i, (i + away) % count) for i in range(count)])


def band_blocks(block):
    rows = [block] + [turned(block, "ch", away) for away in range(1, lax.axis_size("ch"))]
    blocks = []
    for row in rows:
        blocks.append(row)
        blocks.extend(turned(row, "sub", away) for away in range(1, lax.axis_size("sub")))
    return blocks


def direct_blocks(block):
    sizes = lax.axis_size("ch"), lax.axis_size("sub")
    devices = [(at_ch, at_sub) for at_ch in range(sizes[0]) for at_sub in range(sizes[1])]
    blocks = [block]
    for away in devices[1:]:
        targets = [tuple((at + step) % size for at, step, size in zip(device, away, sizes)) for device in devices]
        route = [(number, devices.index(target)) for number, target in enumerate(targets)]
        blocks.append(lax.ppermute(block, ("ch", "sub"), route))
    return blocks


def encode(weather, conv_first, conv_second, patch_embed):
    chans, lon, lat = weather.shape
    pairs, wide = lon // 2, 2 * chans
    embed = patch_embed.shape[1]
    shape = functools.partial(jax.ShapeDtypeStruct, dtype=jnp.bfloat16)
    edge = shape((1, lat, wide))
    packed, low, high = call(
        pack_kernel,
        (shape((pairs, lat, wide)), edge, edge),
        (jnp.transpose(weather, (1, 2, 0)),),
        moved=weather.size * 10,
    )
    before = turned(high, "tok", 1)
    after = turned(low, "tok", -1)
    blocks = band_blocks(packed)
    taps = shape((4 * chans, 12 * chans))
    weights = call(
        weights_kernel,
        (taps, taps, shape((embed, 4 * chans))),
        (conv_first, conv_second, patch_embed),
        scratch=[pltpu.VMEM((patch_embed.shape[0], LANES), jnp.float32)],
        moved=conv_first.size * 20,
    )
    sides = direct_blocks(jnp.concatenate([before, after], axis=0))
    counts = lax.axis_size("ch"), lax.axis_size("sub")
    lat = len(blocks) * lat
    field = call(
        functools.partial(join_kernel, *counts),
        shape((pairs, lat, wide)),
        blocks,
        moved=packed.size * 4 * len(blocks),
    )
    work = 2 * lat * 4 * chans * 6 * chans * 5
    held = shape((4, lat, wide))
    hidden = pltpu.VMEM((pairs, lat, wide), jnp.bfloat16)
    inner, upper_edge, lower_edge = call(
        inner_kernel,
        (shape((embed, (pairs - 4) * lat // 2)), held, held),
        (field, *weights),
        scratch=[hidden, hidden, pltpu.VMEM(((pairs - 4) * lat, wide), jnp.float32)],
        flops=work * (pairs - 3),
        moved=field.size * 2,
    )
    return call(
        functools.partial(outer_kernel, *counts),
        shape((embed, pairs * lat // 2)),
        (field, *sides, upper_edge, lower_edge, *weights, inner),
        scratch=[pltpu.VMEM((4 * lat, wide), jnp.float32), pltpu.VMEM((2, lat, wide), jnp.bfloat16)],
        flops=work * 4,
        moved=field.size * 2,
    )


def sent_kernel(first, block, tokens_ref, mixing_ref, sent_ref):
    rows, width = sent_ref.shape
    step = STEP if width % STEP == 0 else width
    tokens = tokens_ref[pl.ds(block * rows, rows), :]
    for at in range(0, width, step):
        product = dot(tokens, mixing_ref[:, pl.ds(first + at, step)])
        sent_ref[:, pl.ds(at, step)] = product.astype(sent_ref.dtype)


def hop_kernel(first, blocks, arrived_ref, tokens_ref, mixing_ref, sent_ref, kept_ref):
    rows, width = sent_ref.shape
    step = STEP if width % STEP == 0 else width
    tokens = jnp.concatenate([tokens_ref[pl.ds(block * rows, rows), :] for block in blocks], axis=0)
    for at in range(0, width, step):
        product = dot(tokens, mixing_ref[:, pl.ds(first + at, step)])
        arrived = arrived_ref[:, pl.ds(at, step)].astype(jnp.float32)
        sent_ref[:, pl.ds(at, step)] = (arrived + product[:rows]).astype(sent_ref.dtype)
        kept_ref[:, pl.ds(at, step)] = product[rows:]


def last_kernel(first, arrived_ref, kept_ref, *refs):
    result_ref, held_ref, written = refs[-3:]
    rows, width = arrived_ref.shape
    part = width // written.shape[0]
    copies = []
    for at in range(written.shape[0]):
        here = pl.ds(at * part, part)
        own = kept_ref[kept_ref.shape[0] - rows :, at * part : (at + 1) * part]
        held_ref[:, here] = gelu(arrived_ref[:, here].astype(jnp.float32) + own).astype(held_ref.dtype)
        target = result_ref.at[:, pl.ds(first + at * part, part)]
        copies.append(pltpu.make_async_copy(held_ref.at[:, here], target, written.at[at]))
        copies[-1].start()
    for copy in copies:
        copy.wait()


def finish(first, arrived, kept, result, columns):
    rows, width = arrived.shape
    near, far = pl.BlockSpec(memory_space=pltpu.VMEM), pl.BlockSpec(memory_space=pl.ANY)
    earlier = [] if result is None else [result]
    return pl.pallas_call(
        functools.partial(last_kernel, first),
        out_shape=jax.ShapeDtypeStruct((rows, columns), jnp.bfloat16),
        in_specs=[near, near] + [far] * len(earlier),
        out_specs=far,
        input_output_aliases={2: 0} if earlier else {},
        scratch_shapes=[
            pltpu.VMEM((rows, width), jnp.bfloat16),
            pltpu.SemaphoreType.DMA((WRITES if width % (WRITES * LANES) == 0 else 1,)),
        ],
        compiler_params=pltpu.CompilerParams(vmem_limit_bytes=VMEM_BYTES),
        cost_estimate=pl.CostEstimate(flops=0, bytes_accessed=0, transcendentals=0),
    )(arrived, kept, *earlier)


def lift(tokens, token_mixing, pieces):
    count = lax.axis_size("tok")
    embed = tokens.shape[0]
    rows = embed // count
    width = token_mixing.shape[1] // pieces
    sent = jax.ShapeDtypeStruct((rows, width), jnp.bfloat16)
    ways = [1 if piece % 2 == 0 else -1 for piece in range(pieces)]
    blocks = [list(range(count - 2, -1, -1)) if way == 1 else list(range(count - 1)) for way in ways]
    travelling = [
        call(functools.partial(sent_kernel, piece * width, blocks[piece][0]), sent, (tokens, token_mixing))
        for piece in range(pieces)
    ]
    kept = [None] * pieces
    result = None
    for step in range(1, count):
        for piece in range(pieces):
            arrived = turned(travelling[piece], "tok", ways[piece])
            if step == 1:
                travelling[piece], kept[piece] = call(
                    functools.partial(hop_kernel, piece * width, blocks[piece][1:] + [count - 1]),
                    [sent, jax.ShapeDtypeStruct((embed - 2 * rows, width), jnp.float32)],
                    (arrived, tokens, token_mixing),
                )
            elif step < count - 1:
                at = (step - 2) * rows
                summed = arrived.astype(jnp.float32) + kept[piece][at : at + rows]
                travelling[piece] = summed.astype(jnp.bfloat16)
            else:
                result = finish(piece * width, arrived, kept[piece], result, pieces * width)
    return result


def local(weather, conv_first, conv_second, patch_embed, token_mixing):
    tokens = encode(weather, conv_first, conv_second, patch_embed)
    return lift(tokens, token_mixing, PIECES)


def solution(mesh):
    placed = (P("groups", "tok", ("ch", "sub")), P(), P(), P(), P("tok", ("ch", "sub")))
    return jax.shard_map(
        local,
        mesh=mesh,
        in_specs=placed,
        out_specs=P(("groups", "tok"), ("ch", "sub")),
        check_vma=False,
    )
```

```python
import functools

import jax
import jax.numpy as jnp
from jax import lax
from jax.experimental import pallas as pl
from jax.experimental.pallas import tpu as pltpu
from jax.sharding import PartitionSpec as P

PIECES = 4
STEP = 256
LANES = 128
PACK_COST = 20 * 10**9
WRITES = 4
VMEM_BYTES = 24 * 1024 * 1024
ROWS_AT_ONCE = 1024


def pack_kernel(field_ref, packed_ref, low_ref, high_ref):
    lon, lat, chans = field_ref.shape
    pairs = field_ref[...].reshape(lon // 2, 2, lat, chans)
    joined = jnp.concatenate([pairs[:, 0], pairs[:, 1]], axis=-1).astype(packed_ref.dtype)
    packed_ref[...] = joined
    low_ref[...] = joined[:1]
    high_ref[...] = joined[-1:]


def place(away, count_ch, count_sub, width):
    away_ch, away_sub = away // count_sub, away % count_sub
    at_ch = lax.rem(lax.axis_index("ch") + count_ch - away_ch, count_ch)
    at_sub = lax.rem(lax.axis_index("sub") + count_sub - away_sub, count_sub)
    return pl.ds(pl.multiple_of((at_ch * count_sub + at_sub) * width, width), width)


def join_kernel(count_ch, count_sub, *refs):
    blocks, field_ref = refs[:-1], refs[-1]
    width = field_ref.shape[1] // len(blocks)
    for away, block in enumerate(blocks):
        field_ref[:, place(away, count_ch, count_sub, width), :] = block[...]


def split_two(value):
    upper = value.astype(jnp.bfloat16)
    return upper, (value - upper.astype(jnp.float32)).astype(jnp.bfloat16)


def spread_taps(kernel_ref):
    chans = kernel_ref.shape[1]
    nothing = jnp.zeros((chans, kernel_ref.shape[2]), jnp.float32)
    rows = []
    for tap in range(3):
        taps = [kernel_ref[3 * turn + tap] for turn in range(3)]
        rows.append(jnp.concatenate([taps[1], taps[2], nothing, taps[0]], axis=-1))
        rows.append(jnp.concatenate([taps[0], taps[1], taps[2], nothing], axis=-1))
    return jnp.concatenate(rows, axis=0).T


def weights_kernel(first_ref, second_ref, embed_ref, taps_one_ref, taps_two_ref, embed_out_ref, scratch):
    for source, target in ((first_ref, taps_one_ref), (second_ref, taps_two_ref)):
        upper, lower = split_two(spread_taps(source))
        target[...] = jnp.concatenate([upper, lower], axis=1)
    chans = embed_ref.shape[0] // 4
    embed = embed_ref.shape[1]
    count = lax.axis_size("tok")
    turn = lax.rem(lax.axis_index("tok") + 1, count) * (embed // count)
    turned_embed = pltpu.roll(embed_ref[...].astype(jnp.float32), lax.rem(embed - turn, embed), axis=1)
    for first in range(0, embed, LANES):
        scratch[...] = turned_embed[:, first : first + LANES]
        ordered = [scratch[pl.ds(2 * a + b, chans, stride=4), :] for b in range(2) for a in range(2)]
        rows = jnp.concatenate(ordered, axis=0).T
        embed_out_ref[pl.ds(first, LANES), :] = rows.astype(embed_out_ref.dtype)


def pairs_at_once(pairs, lat):
    best = 1
    for size in range(1, pairs + 1):
        if pairs % size == 0 and size * lat <= ROWS_AT_ONCE:
            best = size
    return best


def window(pair_at, pairs):
    rows = []
    for pair in pairs:
        here = pair_at(pair)
        lane = lax.broadcasted_iota(jnp.int32, here.shape, 1)
        beside = jnp.where(lane < here.shape[1] // 2, pair_at(pair + 1), pair_at(pair - 1))
        rows.append(jnp.concatenate([here, beside], axis=-1))
    return jnp.concatenate(rows, axis=0)


def add_lat_taps(products, lat):
    wide = products.shape[1] // 3
    count = products.shape[0]
    row = lax.broadcasted_iota(jnp.int32, (1, lat, wide), 1)
    below = pltpu.roll(products[:, :wide], 1, axis=0).reshape(-1, lat, wide)
    above = pltpu.roll(products[:, 2 * wide :], count - 1, axis=0).reshape(-1, lat, wide)
    here = products[:, wide : 2 * wide].reshape(-1, lat, wide)
    return here + jnp.where(row == 0, 0.0, below) + jnp.where(row == lat - 1, 0.0, above)


def gelu(value):
    return 0.5 * value * (1.0 + lax.erf(value * (0.5**0.5)))


def dot(left, right):
    return jnp.dot(left, right, preferred_element_type=jnp.float32)


def dot_both(rows, taps_ref):
    both = dot(rows, taps_ref[...])
    half = both.shape[1] // 2
    return both[:, :half] + both[:, half:]


def first_conv(field_at, pairs, taps_ref, lat):
    products = dot_both(window(field_at, pairs), taps_ref)
    return split_two(gelu(add_lat_taps(products, lat)))


def second_conv(upper_at, lower_at, pairs, taps_ref, lat):
    upper, lower = window(upper_at, pairs), window(lower_at, pairs)
    products = dot_both(upper, taps_ref) + dot(lower, taps_ref[:, : taps_ref.shape[1] // 2])
    rounded = add_lat_taps(products, lat).astype(jnp.bfloat16).astype(jnp.float32)
    return rounded.reshape(-1, rounded.shape[2])


def embed_patches(two_ref, embed_ref):
    half = two_ref.shape[0] // 2
    patches = jnp.concatenate(
        [two_ref[pl.ds(b, half, stride=2), :].astype(jnp.bfloat16) for b in range(2)], axis=-1
    )
    return lax.dot_general(
        embed_ref[...], patches, (((1,), (1,)), ((), ())), preferred_element_type=jnp.float32
    ).astype(jnp.bfloat16)


def runs(first, last, lat):
    size = pairs_at_once(last - first, lat)
    return [list(range(at, at + size)) for at in range(first, last, size)]


def inner_kernel(
    field_ref, taps_one_ref, taps_two_ref, embed_ref, tokens_ref, upper_edge_ref, lower_edge_ref, upper_ref, lower_ref, two_ref
):
    pairs, lat, wide = field_ref.shape
    for run in runs(1, pairs - 1, lat):
        upper, lower = first_conv(lambda pair: field_ref[pair], run, taps_one_ref, lat)
        upper_ref[pl.ds(run[0], len(run))] = upper
        lower_ref[pl.ds(run[0], len(run))] = lower
    for inside, edge in ((upper_ref, upper_edge_ref), (lower_ref, lower_edge_ref)):
        edge[pl.ds(0, 2)] = inside[pl.ds(1, 2)]
        edge[pl.ds(2, 2)] = inside[pl.ds(pairs - 3, 2)]
    for run in runs(2, pairs - 2, lat):
        two = second_conv(lambda pair: upper_ref[pair], lambda pair: lower_ref[pair], run, taps_two_ref, lat)
        two_ref[pl.ds((run[0] - 2) * lat, len(run) * lat), :] = two
    tokens_ref[...] = embed_patches(two_ref, embed_ref)


def outer_kernel(count_ch, count_sub, field_ref, *refs):
    count = count_ch * count_sub
    sides, refs = refs[:count], refs[count:]
    upper_edge_ref, lower_edge_ref, taps_one_ref, taps_two_ref, embed_ref, inner_ref, tokens_ref, two_ref, sides_ref = refs
    pairs, lat, wide = field_ref.shape
    for away, block in enumerate(sides):
        sides_ref[:, place(away, count_ch, count_sub, lat // count), :] = block[...]

    def field_at(pair):
        if pair < 0:
            return sides_ref[0]
        if pair >= pairs:
            return sides_ref[1]
        return field_ref[pair]

    outermost = [-1, 0, pairs - 1, pairs]
    next_inside = [1, 2, pairs - 3, pairs - 2]
    upper, lower = first_conv(field_at, outermost, taps_one_ref, lat)

    def hidden_at(found, edge_ref):
        def at(pair):
            if pair in outermost:
                return found[outermost.index(pair)]
            return edge_ref[next_inside.index(pair)]

        return at

    two_ref[...] = second_conv(
        hidden_at(upper, upper_edge_ref), hidden_at(lower, lower_edge_ref), [0, 1, pairs - 2, pairs - 1], taps_two_ref, lat
    )
    outer = embed_patches(two_ref, embed_ref)
    inner = inner_ref.shape[1]
    tokens_ref[:, :lat] = outer[:, :lat]
    tokens_ref[:, pl.ds(lat, inner)] = inner_ref[...]
    tokens_ref[:, pl.ds(lat + inner, lat)] = outer[:, lat:]


def call(kernel, out_shape, inputs, scratch=(), flops=0, moved=0):
    return pl.pallas_call(
        kernel,
        out_shape=out_shape,
        in_specs=[pl.BlockSpec(memory_space=pltpu.VMEM)] * len(inputs),
        out_specs=jax.tree.map(lambda unused: pl.BlockSpec(memory_space=pltpu.VMEM), out_shape),
        scratch_shapes=list(scratch),
        compiler_params=pltpu.CompilerParams(vmem_limit_bytes=VMEM_BYTES),
        cost_estimate=pl.CostEstimate(flops=flops, bytes_accessed=moved, transcendentals=0),
    )(*inputs)


def turned(value, axis, away):
    count = lax.axis_size(axis)
    return lax.ppermute(value, axis, [(i, (i + away) % count) for i in range(count)])


def band_blocks(block):
    rows = [block] + [turned(block, "ch", away) for away in range(1, lax.axis_size("ch"))]
    blocks = []
    for row in rows:
        blocks.append(row)
        blocks.extend(turned(row, "sub", away) for away in range(1, lax.axis_size("sub")))
    return blocks


def direct_blocks(block):
    sizes = lax.axis_size("ch"), lax.axis_size("sub")
    devices = [(at_ch, at_sub) for at_ch in range(sizes[0]) for at_sub in range(sizes[1])]
    blocks = [block]
    for away in devices[1:]:
        targets = [tuple((at + step) % size for at, step, size in zip(device, away, sizes)) for device in devices]
        route = [(number, devices.index(target)) for number, target in enumerate(targets)]
        blocks.append(lax.ppermute(block, ("ch", "sub"), route))
    return blocks


def encode(weather, conv_first, conv_second, patch_embed):
    chans, lon, lat = weather.shape
    pairs, wide = lon // 2, 2 * chans
    embed = patch_embed.shape[1]
    shape = functools.partial(jax.ShapeDtypeStruct, dtype=jnp.bfloat16)
    edge = shape((1, lat, wide))
    packed, low, high = call(
        pack_kernel,
        (shape((pairs, lat, wide)), edge, edge),
        (jnp.transpose(weather, (1, 2, 0)),),
        moved=weather.size * 10,
        flops=PACK_COST,
    )
    before = turned(high, "tok", 1)
    after = turned(low, "tok", -1)
    blocks = band_blocks(packed)
    taps = shape((4 * chans, 12 * chans))
    weights = call(
        weights_kernel,
        (taps, taps, shape((embed, 4 * chans))),
        (conv_first, conv_second, patch_embed),
        scratch=[pltpu.VMEM((patch_embed.shape[0], LANES), jnp.float32)],
        moved=conv_first.size * 20,
    )
    sides = direct_blocks(jnp.concatenate([before, after], axis=0))
    counts = lax.axis_size("ch"), lax.axis_size("sub")
    lat = len(blocks) * lat
    field = call(
        functools.partial(join_kernel, *counts),
        shape((pairs, lat, wide)),
        blocks,
        moved=packed.size * 4 * len(blocks),
    )
    work = 2 * lat * 4 * chans * 6 * chans * 5
    held = shape((4, lat, wide))
    hidden = pltpu.VMEM((pairs, lat, wide), jnp.bfloat16)
    inner, upper_edge, lower_edge = call(
        inner_kernel,
        (shape((embed, (pairs - 4) * lat // 2)), held, held),
        (field, *weights),
        scratch=[hidden, hidden, pltpu.VMEM(((pairs - 4) * lat, wide), jnp.float32)],
        flops=work * (pairs - 3),
        moved=field.size * 2,
    )
    return call(
        functools.partial(outer_kernel, *counts),
        shape((embed, pairs * lat // 2)),
        (field, *sides, upper_edge, lower_edge, *weights, inner),
        scratch=[pltpu.VMEM((4 * lat, wide), jnp.float32), pltpu.VMEM((2, lat, wide), jnp.bfloat16)],
        flops=work * 4,
        moved=field.size * 2,
    )


def sent_kernel(first, block, tokens_ref, mixing_ref, sent_ref):
    rows, width = sent_ref.shape
    step = STEP if width % STEP == 0 else width
    tokens = tokens_ref[pl.ds(block * rows, rows), :]
    for at in range(0, width, step):
        product = dot(tokens, mixing_ref[:, pl.ds(first + at, step)])
        sent_ref[:, pl.ds(at, step)] = product.astype(sent_ref.dtype)


def hop_kernel(first, blocks, arrived_ref, tokens_ref, mixing_ref, sent_ref, kept_ref):
    rows, width = sent_ref.shape
    step = STEP if width % STEP == 0 else width
    tokens = jnp.concatenate([tokens_ref[pl.ds(block * rows, rows), :] for block in blocks], axis=0)
    for at in range(0, width, step):
        product = dot(tokens, mixing_ref[:, pl.ds(first + at, step)])
        arrived = arrived_ref[:, pl.ds(at, step)].astype(jnp.float32)
        sent_ref[:, pl.ds(at, step)] = (arrived + product[:rows]).astype(sent_ref.dtype)
        kept_ref[:, pl.ds(at, step)] = product[rows:]


def last_kernel(first, arrived_ref, kept_ref, *refs):
    result_ref, held_ref, written = refs[-3:]
    rows, width = arrived_ref.shape
    part = width // written.shape[0]
    copies = []
    for at in range(written.shape[0]):
        here = pl.ds(at * part, part)
        own = kept_ref[kept_ref.shape[0] - rows :, at * part : (at + 1) * part]
        held_ref[:, here] = gelu(arrived_ref[:, here].astype(jnp.float32) + own).astype(held_ref.dtype)
        target = result_ref.at[:, pl.ds(first + at * part, part)]
        copies.append(pltpu.make_async_copy(held_ref.at[:, here], target, written.at[at]))
        copies[-1].start()
    for copy in copies:
        copy.wait()


def finish(first, arrived, kept, result, columns):
    rows, width = arrived.shape
    near, far = pl.BlockSpec(memory_space=pltpu.VMEM), pl.BlockSpec(memory_space=pl.ANY)
    earlier = [] if result is None else [result]
    return pl.pallas_call(
        functools.partial(last_kernel, first),
        out_shape=jax.ShapeDtypeStruct((rows, columns), jnp.bfloat16),
        in_specs=[near, near] + [far] * len(earlier),
        out_specs=far,
        input_output_aliases={2: 0} if earlier else {},
        scratch_shapes=[
            pltpu.VMEM((rows, width), jnp.bfloat16),
            pltpu.SemaphoreType.DMA((WRITES if width % (WRITES * LANES) == 0 else 1,)),
        ],
        compiler_params=pltpu.CompilerParams(vmem_limit_bytes=VMEM_BYTES),
        cost_estimate=pl.CostEstimate(flops=0, bytes_accessed=0, transcendentals=0),
    )(arrived, kept, *earlier)


def lift(tokens, token_mixing, pieces):
    count = lax.axis_size("tok")
    embed = tokens.shape[0]
    rows = embed // count
    width = token_mixing.shape[1] // pieces
    sent = jax.ShapeDtypeStruct((rows, width), jnp.bfloat16)
    ways = [1 if piece % 2 == 0 else -1 for piece in range(pieces)]
    blocks = [list(range(count - 2, -1, -1)) if way == 1 else list(range(count - 1)) for way in ways]
    travelling = [
        call(functools.partial(sent_kernel, piece * width, blocks[piece][0]), sent, (tokens, token_mixing))
        for piece in range(pieces)
    ]
    kept = [None] * pieces
    result = None
    for step in range(1, count):
        for piece in range(pieces):
            arrived = turned(travelling[piece], "tok", ways[piece])
            if step == 1:
                travelling[piece], kept[piece] = call(
                    functools.partial(hop_kernel, piece * width, blocks[piece][1:] + [count - 1]),
                    [sent, jax.ShapeDtypeStruct((embed - 2 * rows, width), jnp.float32)],
                    (arrived, tokens, token_mixing),
                )
            elif step < count - 1:
                at = (step - 2) * rows
                summed = arrived.astype(jnp.float32) + kept[piece][at : at + rows]
                travelling[piece] = summed.astype(jnp.bfloat16)
            else:
                result = finish(piece * width, arrived, kept[piece], result, pieces * width)
    return result


def local(weather, conv_first, conv_second, patch_embed, token_mixing):
    tokens = encode(weather, conv_first, conv_second, patch_embed)
    return lift(tokens, token_mixing, PIECES)


def solution(mesh):
    placed = (P("groups", "tok", ("ch", "sub")), P(), P(), P(), P("tok", ("ch", "sub")))
    return jax.shard_map(
        local,
        mesh=mesh,
        in_specs=placed,
        out_specs=P(("groups", "tok"), ("ch", "sub")),
        check_vma=False,
    )
```

```python
import functools

import jax
import jax.numpy as jnp
from jax import lax
from jax.experimental import pallas as pl
from jax.experimental.pallas import tpu as pltpu
from jax.sharding import PartitionSpec as P

PIECES = 4
STEP = 256
LANES = 128
PACK_COST = 20 * 10**9
WRITES = 4
VMEM_BYTES = 24 * 1024 * 1024
ROWS_AT_ONCE = 1024


def pack_kernel(field_ref, packed_ref, low_ref, high_ref):
    lon, lat, chans = field_ref.shape
    pairs = field_ref[...].reshape(lon // 2, 2, lat, chans)
    joined = jnp.concatenate([pairs[:, 0], pairs[:, 1]], axis=-1).astype(packed_ref.dtype)
    packed_ref[...] = joined
    low_ref[...] = joined[:1]
    high_ref[...] = joined[-1:]


def place(away, count_ch, count_sub, width):
    away_ch, away_sub = away // count_sub, away % count_sub
    at_ch = lax.rem(lax.axis_index("ch") + count_ch - away_ch, count_ch)
    at_sub = lax.rem(lax.axis_index("sub") + count_sub - away_sub, count_sub)
    return pl.ds(pl.multiple_of((at_ch * count_sub + at_sub) * width, width), width)


def join_kernel(count_ch, count_sub, *refs):
    blocks, field_ref = refs[:-1], refs[-1]
    width = field_ref.shape[1] // len(blocks)
    for away, block in enumerate(blocks):
        field_ref[:, place(away, count_ch, count_sub, width), :] = block[...]


def split_two(value):
    upper = value.astype(jnp.bfloat16)
    return upper, (value - upper.astype(jnp.float32)).astype(jnp.bfloat16)


def spread_taps(kernel_ref):
    chans = kernel_ref.shape[1]
    nothing = jnp.zeros((chans, kernel_ref.shape[2]), jnp.float32)
    rows = []
    for tap in range(3):
        taps = [kernel_ref[3 * turn + tap] for turn in range(3)]
        rows.append(jnp.concatenate([taps[1], taps[2], nothing, taps[0]], axis=-1))
        rows.append(jnp.concatenate([taps[0], taps[1], taps[2], nothing], axis=-1))
    return jnp.concatenate(rows, axis=0).T


def weights_kernel(first_ref, second_ref, embed_ref, taps_one_ref, taps_two_ref, embed_out_ref, scratch):
    for source, target in ((first_ref, taps_one_ref), (second_ref, taps_two_ref)):
        upper, lower = split_two(spread_taps(source))
        target[...] = jnp.concatenate([upper, lower], axis=1)
    chans = embed_ref.shape[0] // 4
    embed = embed_ref.shape[1]
    count = lax.axis_size("tok")
    turn = lax.rem(lax.axis_index("tok") + 1, count) * (embed // count)
    turned_embed = pltpu.roll(embed_ref[...].astype(jnp.float32), lax.rem(embed - turn, embed), axis=1)
    for first in range(0, embed, LANES):
        scratch[...] = turned_embed[:, first : first + LANES]
        ordered = [scratch[pl.ds(2 * a + b, chans, stride=4), :] for b in range(2) for a in range(2)]
        rows = jnp.concatenate(ordered, axis=0).T
        embed_out_ref[pl.ds(first, LANES), :] = rows.astype(embed_out_ref.dtype)


def pairs_at_once(pairs, lat):
    best = 1
    for size in range(1, pairs + 1):
        if pairs % size == 0 and size * lat <= ROWS_AT_ONCE:
            best = size
    return best


def window(pair_at, pairs):
    rows = []
    for pair in pairs:
        here = pair_at(pair)
        lane = lax.broadcasted_iota(jnp.int32, here.shape, 1)
        beside = jnp.where(lane < here.shape[1] // 2, pair_at(pair + 1), pair_at(pair - 1))
        rows.append(jnp.concatenate([here, beside], axis=-1))
    return jnp.concatenate(rows, axis=0)


def add_lat_taps(products, lat):
    wide = products.shape[1] // 3
    count = products.shape[0]
    row = lax.broadcasted_iota(jnp.int32, (1, lat, wide), 1)
    below = pltpu.roll(products[:, :wide], 1, axis=0).reshape(-1, lat, wide)
    above = pltpu.roll(products[:, 2 * wide :], count - 1, axis=0).reshape(-1, lat, wide)
    here = products[:, wide : 2 * wide].reshape(-1, lat, wide)
    return here + jnp.where(row == 0, 0.0, below) + jnp.where(row == lat - 1, 0.0, above)


def gelu(value):
    return 0.5 * value * (1.0 + lax.erf(value * (0.5**0.5)))


def dot(left, right):
    return jnp.dot(left, right, preferred_element_type=jnp.float32)


def dot_both(rows, taps_ref):
    both = dot(rows, taps_ref[...])
    half = both.shape[1] // 2
    return both[:, :half] + both[:, half:]


def first_conv(field_at, pairs, taps_ref, lat):
    products = dot_both(window(field_at, pairs), taps_ref)
    return split_two(gelu(add_lat_taps(products, lat)))


def second_conv(upper_at, lower_at, pairs, taps_ref, lat):
    upper, lower = window(upper_at, pairs), window(lower_at, pairs)
    products = dot_both(upper, taps_ref) + dot(lower, taps_ref[:, : taps_ref.shape[1] // 2])
    rounded = add_lat_taps(products, lat).astype(jnp.bfloat16).astype(jnp.float32)
    return rounded.reshape(-1, rounded.shape[2])


def embed_patches(two_ref, embed_ref):
    half = two_ref.shape[0] // 2
    patches = jnp.concatenate(
        [two_ref[pl.ds(b, half, stride=2), :].astype(jnp.bfloat16) for b in range(2)], axis=-1
    )
    return lax.dot_general(
        embed_ref[...], patches, (((1,), (1,)), ((), ())), preferred_element_type=jnp.float32
    ).astype(jnp.bfloat16)


def runs(first, last, lat):
    size = pairs_at_once(last - first, lat)
    return [list(range(at, at + size)) for at in range(first, last, size)]


def inner_kernel(
    field_ref, taps_one_ref, taps_two_ref, embed_ref, tokens_ref, upper_edge_ref, lower_edge_ref, upper_ref, lower_ref, two_ref
):
    pairs, lat, wide = field_ref.shape
    for run in runs(1, pairs - 1, lat):
        upper, lower = first_conv(lambda pair: field_ref[pair], run, taps_one_ref, lat)
        upper_ref[pl.ds(run[0], len(run))] = upper
        lower_ref[pl.ds(run[0], len(run))] = lower
    for inside, edge in ((upper_ref, upper_edge_ref), (lower_ref, lower_edge_ref)):
        edge[pl.ds(0, 2)] = inside[pl.ds(1, 2)]
        edge[pl.ds(2, 2)] = inside[pl.ds(pairs - 3, 2)]
    for run in runs(2, pairs - 2, lat):
        two = second_conv(lambda pair: upper_ref[pair], lambda pair: lower_ref[pair], run, taps_two_ref, lat)
        two_ref[pl.ds((run[0] - 2) * lat, len(run) * lat), :] = two
    tokens_ref[...] = embed_patches(two_ref, embed_ref)


def outer_kernel(count_ch, count_sub, field_ref, *refs):
    count = count_ch * count_sub
    sides, refs = refs[:count], refs[count:]
    upper_edge_ref, lower_edge_ref, taps_one_ref, taps_two_ref, embed_ref, inner_ref, tokens_ref, two_ref, sides_ref = refs
    pairs, lat, wide = field_ref.shape
    for away, block in enumerate(sides):
        sides_ref[:, place(away, count_ch, count_sub, lat // count), :] = block[...]

    def field_at(pair):
        if pair < 0:
            return sides_ref[0]
        if pair >= pairs:
            return sides_ref[1]
        return field_ref[pair]

    outermost = [-1, 0, pairs - 1, pairs]
    next_inside = [1, 2, pairs - 3, pairs - 2]
    upper, lower = first_conv(field_at, outermost, taps_one_ref, lat)

    def hidden_at(found, edge_ref):
        def at(pair):
            if pair in outermost:
                return found[outermost.index(pair)]
            return edge_ref[next_inside.index(pair)]

        return at

    two_ref[...] = second_conv(
        hidden_at(upper, upper_edge_ref), hidden_at(lower, lower_edge_ref), [0, 1, pairs - 2, pairs - 1], taps_two_ref, lat
    )
    outer = embed_patches(two_ref, embed_ref)
    inner = inner_ref.shape[1]
    tokens_ref[:, :lat] = outer[:, :lat]
    tokens_ref[:, pl.ds(lat, inner)] = inner_ref[...]
    tokens_ref[:, pl.ds(lat + inner, lat)] = outer[:, lat:]


def call(kernel, out_shape, inputs, scratch=(), flops=0, moved=0):
    return pl.pallas_call(
        kernel,
        out_shape=out_shape,
        in_specs=[pl.BlockSpec(memory_space=pltpu.VMEM)] * len(inputs),
        out_specs=jax.tree.map(lambda unused: pl.BlockSpec(memory_space=pltpu.VMEM), out_shape),
        scratch_shapes=list(scratch),
        compiler_params=pltpu.CompilerParams(vmem_limit_bytes=VMEM_BYTES),
        cost_estimate=pl.CostEstimate(flops=flops, bytes_accessed=moved, transcendentals=0),
    )(*inputs)


def turned(value, axis, away):
    count = lax.axis_size(axis)
    return lax.ppermute(value, axis, [(i, (i + away) % count) for i in range(count)])


def band_blocks(block):
    rows = [block] + [turned(block, "ch", away) for away in range(1, lax.axis_size("ch"))]
    blocks = []
    for row in rows:
        blocks.append(row)
        blocks.extend(turned(row, "sub", away) for away in range(1, lax.axis_size("sub")))
    return blocks


def direct_blocks(block):
    sizes = lax.axis_size("ch"), lax.axis_size("sub")
    devices = [(at_ch, at_sub) for at_ch in range(sizes[0]) for at_sub in range(sizes[1])]
    blocks = [block]
    for away in devices[1:]:
        targets = [tuple((at + step) % size for at, step, size in zip(device, away, sizes)) for device in devices]
        route = [(number, devices.index(target)) for number, target in enumerate(targets)]
        blocks.append(lax.ppermute(block, ("ch", "sub"), route))
    return blocks


def encode(weather, conv_first, conv_second, patch_embed):
    chans, lon, lat = weather.shape
    pairs, wide = lon // 2, 2 * chans
    embed = patch_embed.shape[1]
    shape = functools.partial(jax.ShapeDtypeStruct, dtype=jnp.bfloat16)
    edge = shape((1, lat, wide))
    packed, low, high = call(
        pack_kernel,
        (shape((pairs, lat, wide)), edge, edge),
        (jnp.transpose(weather, (1, 2, 0)),),
        moved=weather.size * 10,
        flops=PACK_COST,
    )
    before = turned(high, "tok", 1)
    after = turned(low, "tok", -1)
    blocks = band_blocks(packed)
    taps = shape((4 * chans, 12 * chans))
    weights = call(
        weights_kernel,
        (taps, taps, shape((embed, 4 * chans))),
        (conv_first, conv_second, patch_embed),
        scratch=[pltpu.VMEM((patch_embed.shape[0], LANES), jnp.float32)],
        moved=conv_first.size * 20,
    )
    sides = direct_blocks(jnp.concatenate([before, after], axis=0))
    counts = lax.axis_size("ch"), lax.axis_size("sub")
    lat = len(blocks) * lat
    field = call(
        functools.partial(join_kernel, *counts),
        shape((pairs, lat, wide)),
        blocks,
        moved=packed.size * 4 * len(blocks),
    )
    work = 2 * lat * 4 * chans * 6 * chans * 5
    held = shape((4, lat, wide))
    hidden = pltpu.VMEM((pairs, lat, wide), jnp.bfloat16)
    inner, upper_edge, lower_edge = call(
        inner_kernel,
        (shape((embed, (pairs - 4) * lat // 2)), held, held),
        (field, *weights),
        scratch=[hidden, hidden, pltpu.VMEM(((pairs - 4) * lat, wide), jnp.float32)],
        flops=work * (pairs - 3),
        moved=field.size * 2,
    )
    return call(
        functools.partial(outer_kernel, *counts),
        shape((embed, pairs * lat // 2)),
        (field, *sides, upper_edge, lower_edge, *weights, inner),
        scratch=[pltpu.VMEM((4 * lat, wide), jnp.float32), pltpu.VMEM((2, lat, wide), jnp.bfloat16)],
        flops=work * 4,
        moved=field.size * 2,
    )


def sent_kernel(first, block, tokens_ref, mixing_ref, sent_ref):
    rows, width = sent_ref.shape
    step = STEP if width % STEP == 0 else width
    tokens = tokens_ref[pl.ds(block * rows, rows), :]
    for at in range(0, width, step):
        product = dot(tokens, mixing_ref[:, pl.ds(first + at, step)])
        sent_ref[:, pl.ds(at, step)] = product.astype(sent_ref.dtype)


def hop_kernel(first, blocks, arrived_ref, tokens_ref, mixing_ref, sent_ref, kept_ref):
    rows, width = sent_ref.shape
    step = STEP if width % STEP == 0 else width
    tokens = jnp.concatenate([tokens_ref[pl.ds(block * rows, rows), :] for block in blocks], axis=0)
    for at in range(0, width, step):
        product = dot(tokens, mixing_ref[:, pl.ds(first + at, step)])
        arrived = arrived_ref[:, pl.ds(at, step)].astype(jnp.float32)
        sent_ref[:, pl.ds(at, step)] = (arrived + product[:rows]).astype(sent_ref.dtype)
        kept_ref[:, pl.ds(at, step)] = product[rows:]


def last_kernel(first, arrived_ref, kept_ref, *refs):
    result_ref, held_ref, written = refs[-3:]
    rows, width = arrived_ref.shape
    part = width // written.shape[0]
    copies = []
    for at in range(written.shape[0]):
        here = pl.ds(at * part, part)
        own = kept_ref[kept_ref.shape[0] - rows :, at * part : (at + 1) * part]
        held_ref[:, here] = gelu(arrived_ref[:, here].astype(jnp.float32) + own).astype(held_ref.dtype)
        target = result_ref.at[:, pl.ds(first + at * part, part)]
        copies.append(pltpu.make_async_copy(held_ref.at[:, here], target, written.at[at]))
        copies[-1].start()
    for copy in copies:
        copy.wait()


def finish(first, arrived, kept, result, columns):
    rows, width = arrived.shape
    near, far = pl.BlockSpec(memory_space=pltpu.VMEM), pl.BlockSpec(memory_space=pl.ANY)
    earlier = [] if result is None else [result]
    return pl.pallas_call(
        functools.partial(last_kernel, first),
        out_shape=jax.ShapeDtypeStruct((rows, columns), jnp.bfloat16),
        in_specs=[near, near] + [far] * len(earlier),
        out_specs=far,
        input_output_aliases={2: 0} if earlier else {},
        scratch_shapes=[
            pltpu.VMEM((rows, width), jnp.bfloat16),
            pltpu.SemaphoreType.DMA((WRITES if width % (WRITES * LANES) == 0 else 1,)),
        ],
        compiler_params=pltpu.CompilerParams(vmem_limit_bytes=VMEM_BYTES),
        cost_estimate=pl.CostEstimate(flops=0, bytes_accessed=0, transcendentals=0),
    )(arrived, kept, *earlier)


def lift(tokens, token_mixing, pieces):
    count = lax.axis_size("tok")
    embed = tokens.shape[0]
    rows = embed // count
    width = token_mixing.shape[1] // pieces
    sent = jax.ShapeDtypeStruct((rows, width), jnp.bfloat16)
    ways = [1] * pieces
    blocks = [list(range(count - 2, -1, -1)) if way == 1 else list(range(count - 1)) for way in ways]
    travelling = [
        call(functools.partial(sent_kernel, piece * width, blocks[piece][0]), sent, (tokens, token_mixing))
        for piece in range(pieces)
    ]
    kept = [None] * pieces
    result = None
    for step in range(1, count):
        for piece in range(pieces):
            arrived = turned(travelling[piece], "tok", ways[piece])
            if step == 1:
                travelling[piece], kept[piece] = call(
                    functools.partial(hop_kernel, piece * width, blocks[piece][1:] + [count - 1]),
                    [sent, jax.ShapeDtypeStruct((embed - 2 * rows, width), jnp.float32)],
                    (arrived, tokens, token_mixing),
                )
            elif step < count - 1:
                at = (step - 2) * rows
                summed = arrived.astype(jnp.float32) + kept[piece][at : at + rows]
                travelling[piece] = summed.astype(jnp.bfloat16)
            else:
                result = finish(piece * width, arrived, kept[piece], result, pieces * width)
    return result


def local(weather, conv_first, conv_second, patch_embed, token_mixing):
    tokens = encode(weather, conv_first, conv_second, patch_embed)
    return lift(tokens, token_mixing, PIECES)


def solution(mesh):
    placed = (P("groups", "tok", ("ch", "sub")), P(), P(), P(), P("tok", ("ch", "sub")))
    return jax.shard_map(
        local,
        mesh=mesh,
        in_specs=placed,
        out_specs=P(("groups", "tok"), ("ch", "sub")),
        check_vma=False,
    )
```

```python
import functools

import jax
import jax.numpy as jnp
from jax import lax
from jax.experimental import pallas as pl
from jax.experimental.pallas import tpu as pltpu
from jax.sharding import PartitionSpec as P

PIECES = 4
STEP = 256
LANES = 128
PACK_COST = 20 * 10**9
WRITES = 4
VMEM_BYTES = 24 * 1024 * 1024
ROWS_AT_ONCE = 1024


def pack_kernel(field_ref, packed_ref, low_ref, high_ref):
    lon, lat, chans = field_ref.shape
    pairs = field_ref[...].reshape(lon // 2, 2, lat, chans)
    joined = jnp.concatenate([pairs[:, 0], pairs[:, 1]], axis=-1).astype(packed_ref.dtype)
    packed_ref[...] = joined
    low_ref[...] = joined[:1]
    high_ref[...] = joined[-1:]


def place(away, count_ch, count_sub, width):
    away_ch, away_sub = away // count_sub, away % count_sub
    at_ch = lax.rem(lax.axis_index("ch") + count_ch - away_ch, count_ch)
    at_sub = lax.rem(lax.axis_index("sub") + count_sub - away_sub, count_sub)
    return pl.ds(pl.multiple_of((at_ch * count_sub + at_sub) * width, width), width)


def join_kernel(count_ch, count_sub, *refs):
    blocks, field_ref = refs[:-1], refs[-1]
    width = field_ref.shape[1] // len(blocks)
    for away, block in enumerate(blocks):
        field_ref[:, place(away, count_ch, count_sub, width), :] = block[...]


def split_two(value):
    upper = value.astype(jnp.bfloat16)
    return upper, (value - upper.astype(jnp.float32)).astype(jnp.bfloat16)


def spread_taps(kernel_ref):
    chans = kernel_ref.shape[1]
    nothing = jnp.zeros((chans, kernel_ref.shape[2]), jnp.float32)
    rows = []
    for tap in range(3):
        taps = [kernel_ref[3 * turn + tap] for turn in range(3)]
        rows.append(jnp.concatenate([taps[1], taps[2], nothing, taps[0]], axis=-1))
        rows.append(jnp.concatenate([taps[0], taps[1], taps[2], nothing], axis=-1))
    return jnp.concatenate(rows, axis=0).T


def weights_kernel(first_ref, second_ref, embed_ref, taps_one_ref, taps_two_ref, embed_out_ref, scratch):
    for source, target in ((first_ref, taps_one_ref), (second_ref, taps_two_ref)):
        upper, lower = split_two(spread_taps(source))
        target[...] = jnp.concatenate([upper, lower], axis=1)
    chans = embed_ref.shape[0] // 4
    embed = embed_ref.shape[1]
    count = lax.axis_size("tok")
    turn = lax.rem(lax.axis_index("tok") + 1, count) * (embed // count)
    turned_embed = pltpu.roll(embed_ref[...].astype(jnp.float32), lax.rem(embed - turn, embed), axis=1)
    for first in range(0, embed, LANES):
        scratch[...] = turned_embed[:, first : first + LANES]
        ordered = [scratch[pl.ds(2 * a + b, chans, stride=4), :] for b in range(2) for a in range(2)]
        rows = jnp.concatenate(ordered, axis=0).T
        embed_out_ref[pl.ds(first, LANES), :] = rows.astype(embed_out_ref.dtype)


def pairs_at_once(pairs, lat):
    best = 1
    for size in range(1, pairs + 1):
        if pairs % size == 0 and size * lat <= ROWS_AT_ONCE:
            best = size
    return best


def window(pair_at, pairs):
    rows = []
    for pair in pairs:
        here = pair_at(pair)
        lane = lax.broadcasted_iota(jnp.int32, here.shape, 1)
        beside = jnp.where(lane < here.shape[1] // 2, pair_at(pair + 1), pair_at(pair - 1))
        rows.append(jnp.concatenate([here, beside], axis=-1))
    return jnp.concatenate(rows, axis=0)


def add_lat_taps(products, lat):
    wide = products.shape[1] // 3
    count = products.shape[0]
    row = lax.broadcasted_iota(jnp.int32, (1, lat, wide), 1)
    below = pltpu.roll(products[:, :wide], 1, axis=0).reshape(-1, lat, wide)
    above = pltpu.roll(products[:, 2 * wide :], count - 1, axis=0).reshape(-1, lat, wide)
    here = products[:, wide : 2 * wide].reshape(-1, lat, wide)
    return here + jnp.where(row == 0, 0.0, below) + jnp.where(row == lat - 1, 0.0, above)


def gelu(value):
    return 0.5 * value * (1.0 + lax.erf(value * (0.5**0.5)))


def dot(left, right):
    return jnp.dot(left, right, preferred_element_type=jnp.float32)


def dot_both(rows, taps_ref):
    both = dot(rows, taps_ref[...])
    half = both.shape[1] // 2
    return both[:, :half] + both[:, half:]


def first_conv(field_at, pairs, taps_ref, lat):
    products = dot_both(window(field_at, pairs), taps_ref)
    return split_two(gelu(add_lat_taps(products, lat)))


def second_conv(upper_at, lower_at, pairs, taps_ref, lat):
    upper, lower = window(upper_at, pairs), window(lower_at, pairs)
    products = dot_both(upper, taps_ref) + dot(lower, taps_ref[:, : taps_ref.shape[1] // 2])
    rounded = add_lat_taps(products, lat).astype(jnp.bfloat16).astype(jnp.float32)
    return rounded.reshape(-1, rounded.shape[2])


def embed_patches(two_ref, embed_ref):
    half = two_ref.shape[0] // 2
    patches = jnp.concatenate(
        [two_ref[pl.ds(b, half, stride=2), :].astype(jnp.bfloat16) for b in range(2)], axis=-1
    )
    return lax.dot_general(
        embed_ref[...], patches, (((1,), (1,)), ((), ())), preferred_element_type=jnp.float32
    ).astype(jnp.bfloat16)


def runs(first, last, lat):
    size = pairs_at_once(last - first, lat)
    return [list(range(at, at + size)) for at in range(first, last, size)]


def inner_kernel(
    field_ref, taps_one_ref, taps_two_ref, embed_ref, tokens_ref, upper_edge_ref, lower_edge_ref, upper_ref, lower_ref, two_ref
):
    pairs, lat, wide = field_ref.shape
    for run in runs(1, pairs - 1, lat):
        upper, lower = first_conv(lambda pair: field_ref[pair], run, taps_one_ref, lat)
        upper_ref[pl.ds(run[0], len(run))] = upper
        lower_ref[pl.ds(run[0], len(run))] = lower
    for inside, edge in ((upper_ref, upper_edge_ref), (lower_ref, lower_edge_ref)):
        edge[pl.ds(0, 2)] = inside[pl.ds(1, 2)]
        edge[pl.ds(2, 2)] = inside[pl.ds(pairs - 3, 2)]
    for run in runs(2, pairs - 2, lat):
        two = second_conv(lambda pair: upper_ref[pair], lambda pair: lower_ref[pair], run, taps_two_ref, lat)
        two_ref[pl.ds((run[0] - 2) * lat, len(run) * lat), :] = two
    tokens_ref[...] = embed_patches(two_ref, embed_ref)


def outer_kernel(count_ch, count_sub, field_ref, *refs):
    count = count_ch * count_sub
    sides, refs = refs[:count], refs[count:]
    upper_edge_ref, lower_edge_ref, taps_one_ref, taps_two_ref, embed_ref, inner_ref, tokens_ref, two_ref, sides_ref = refs
    pairs, lat, wide = field_ref.shape
    for away, block in enumerate(sides):
        sides_ref[:, place(away, count_ch, count_sub, lat // count), :] = block[...]

    def field_at(pair):
        if pair < 0:
            return sides_ref[0]
        if pair >= pairs:
            return sides_ref[1]
        return field_ref[pair]

    outermost = [-1, 0, pairs - 1, pairs]
    next_inside = [1, 2, pairs - 3, pairs - 2]
    upper, lower = first_conv(field_at, outermost, taps_one_ref, lat)

    def hidden_at(found, edge_ref):
        def at(pair):
            if pair in outermost:
                return found[outermost.index(pair)]
            return edge_ref[next_inside.index(pair)]

        return at

    two_ref[...] = second_conv(
        hidden_at(upper, upper_edge_ref), hidden_at(lower, lower_edge_ref), [0, 1, pairs - 2, pairs - 1], taps_two_ref, lat
    )
    outer = embed_patches(two_ref, embed_ref)
    inner = inner_ref.shape[1]
    tokens_ref[:, :lat] = outer[:, :lat]
    tokens_ref[:, pl.ds(lat, inner)] = inner_ref[...]
    tokens_ref[:, pl.ds(lat + inner, lat)] = outer[:, lat:]


def call(kernel, out_shape, inputs, scratch=(), flops=0, moved=0):
    return pl.pallas_call(
        kernel,
        out_shape=out_shape,
        in_specs=[pl.BlockSpec(memory_space=pltpu.VMEM)] * len(inputs),
        out_specs=jax.tree.map(lambda unused: pl.BlockSpec(memory_space=pltpu.VMEM), out_shape),
        scratch_shapes=list(scratch),
        compiler_params=pltpu.CompilerParams(vmem_limit_bytes=VMEM_BYTES),
        cost_estimate=pl.CostEstimate(flops=flops, bytes_accessed=moved, transcendentals=0),
    )(*inputs)


def turned(value, axis, away):
    count = lax.axis_size(axis)
    return lax.ppermute(value, axis, [(i, (i + away) % count) for i in range(count)])


def band_blocks(block):
    rows = [block] + [turned(block, "ch", away) for away in range(1, lax.axis_size("ch"))]
    blocks = []
    for row in rows:
        blocks.append(row)
        blocks.extend(turned(row, "sub", away) for away in range(1, lax.axis_size("sub")))
    return blocks


def direct_blocks(block):
    sizes = lax.axis_size("ch"), lax.axis_size("sub")
    devices = [(at_ch, at_sub) for at_ch in range(sizes[0]) for at_sub in range(sizes[1])]
    blocks = [block]
    for away in devices[1:]:
        targets = [tuple((at + step) % size for at, step, size in zip(device, away, sizes)) for device in devices]
        route = [(number, devices.index(target)) for number, target in enumerate(targets)]
        blocks.append(lax.ppermute(block, ("ch", "sub"), route))
    return blocks


def encode(weather, conv_first, conv_second, patch_embed):
    chans, lon, lat = weather.shape
    pairs, wide = lon // 2, 2 * chans
    embed = patch_embed.shape[1]
    shape = functools.partial(jax.ShapeDtypeStruct, dtype=jnp.bfloat16)
    edge = shape((1, lat, wide))
    packed, low, high = call(
        pack_kernel,
        (shape((pairs, lat, wide)), edge, edge),
        (jnp.transpose(weather, (1, 2, 0)),),
        moved=weather.size * 10,
        flops=PACK_COST,
    )
    before = turned(high, "tok", 1)
    after = turned(low, "tok", -1)
    blocks = band_blocks(packed)
    taps = shape((4 * chans, 12 * chans))
    weights = call(
        weights_kernel,
        (taps, taps, shape((embed, 4 * chans))),
        (conv_first, conv_second, patch_embed),
        scratch=[pltpu.VMEM((patch_embed.shape[0], LANES), jnp.float32)],
        moved=conv_first.size * 20,
    )
    sides = direct_blocks(jnp.concatenate([before, after], axis=0))
    counts = lax.axis_size("ch"), lax.axis_size("sub")
    lat = len(blocks) * lat
    field = call(
        functools.partial(join_kernel, *counts),
        shape((pairs, lat, wide)),
        blocks,
        moved=packed.size * 4 * len(blocks),
    )
    work = 2 * lat * 4 * chans * 6 * chans * 5
    held = shape((4, lat, wide))
    hidden = pltpu.VMEM((pairs, lat, wide), jnp.bfloat16)
    inner, upper_edge, lower_edge = call(
        inner_kernel,
        (shape((embed, (pairs - 4) * lat // 2)), held, held),
        (field, *weights),
        scratch=[hidden, hidden, pltpu.VMEM(((pairs - 4) * lat, wide), jnp.float32)],
        flops=work * (pairs - 3),
        moved=field.size * 2,
    )
    return call(
        functools.partial(outer_kernel, *counts),
        shape((embed, pairs * lat // 2)),
        (field, *sides, upper_edge, lower_edge, *weights, inner),
        scratch=[pltpu.VMEM((4 * lat, wide), jnp.float32), pltpu.VMEM((2, lat, wide), jnp.bfloat16)],
        flops=work * 4,
        moved=field.size * 2,
    )


def sent_kernel(first, block, tokens_ref, mixing_ref, sent_ref):
    rows, width = sent_ref.shape
    step = STEP if width % STEP == 0 else width
    tokens = tokens_ref[pl.ds(block * rows, rows), :]
    for at in range(0, width, step):
        product = dot(tokens, mixing_ref[:, pl.ds(first + at, step)])
        sent_ref[:, pl.ds(at, step)] = product.astype(sent_ref.dtype)


def hop_kernel(first, blocks, arrived_ref, tokens_ref, mixing_ref, sent_ref, kept_ref):
    rows, width = sent_ref.shape
    step = STEP if width % STEP == 0 else width
    tokens = jnp.concatenate([tokens_ref[pl.ds(block * rows, rows), :] for block in blocks], axis=0)
    for at in range(0, width, step):
        product = dot(tokens, mixing_ref[:, pl.ds(first + at, step)])
        arrived = arrived_ref[:, pl.ds(at, step)].astype(jnp.float32)
        sent_ref[:, pl.ds(at, step)] = (arrived + product[:rows]).astype(sent_ref.dtype)
        kept_ref[:, pl.ds(at, step)] = product[rows:]


def last_kernel(first, arrived_ref, kept_ref, *refs):
    result_ref, held_ref, written = refs[-3:]
    rows, width = arrived_ref.shape
    part = width // written.shape[0]
    copies = []
    for at in range(written.shape[0]):
        here = pl.ds(at * part, part)
        own = kept_ref[kept_ref.shape[0] - rows :, at * part : (at + 1) * part]
        held_ref[:, here] = gelu(arrived_ref[:, here].astype(jnp.float32) + own).astype(held_ref.dtype)
        target = result_ref.at[:, pl.ds(first + at * part, part)]
        copies.append(pltpu.make_async_copy(held_ref.at[:, here], target, written.at[at]))
        copies[-1].start()
    for copy in copies:
        copy.wait()


def finish(first, arrived, kept, result, columns):
    rows, width = arrived.shape
    near, far = pl.BlockSpec(memory_space=pltpu.VMEM), pl.BlockSpec(memory_space=pl.ANY)
    earlier = [] if result is None else [result]
    return pl.pallas_call(
        functools.partial(last_kernel, first),
        out_shape=jax.ShapeDtypeStruct((rows, columns), jnp.bfloat16),
        in_specs=[near, near] + [far] * len(earlier),
        out_specs=far,
        input_output_aliases={2: 0} if earlier else {},
        scratch_shapes=[
            pltpu.VMEM((rows, width), jnp.bfloat16),
            pltpu.SemaphoreType.DMA((WRITES if width % (WRITES * LANES) == 0 else 1,)),
        ],
        compiler_params=pltpu.CompilerParams(vmem_limit_bytes=VMEM_BYTES),
        cost_estimate=pl.CostEstimate(flops=0, bytes_accessed=0, transcendentals=0),
    )(arrived, kept, *earlier)


def lift(tokens, token_mixing, pieces):
    count = lax.axis_size("tok")
    embed = tokens.shape[0]
    rows = embed // count
    width = token_mixing.shape[1] // pieces
    sent = jax.ShapeDtypeStruct((rows, width), jnp.bfloat16)
    ways = [-1] * pieces
    blocks = [list(range(count - 2, -1, -1)) if way == 1 else list(range(count - 1)) for way in ways]
    travelling = [
        call(functools.partial(sent_kernel, piece * width, blocks[piece][0]), sent, (tokens, token_mixing))
        for piece in range(pieces)
    ]
    kept = [None] * pieces
    result = None
    for step in range(1, count):
        for piece in range(pieces):
            arrived = turned(travelling[piece], "tok", ways[piece])
            if step == 1:
                travelling[piece], kept[piece] = call(
                    functools.partial(hop_kernel, piece * width, blocks[piece][1:] + [count - 1]),
                    [sent, jax.ShapeDtypeStruct((embed - 2 * rows, width), jnp.float32)],
                    (arrived, tokens, token_mixing),
                )
            elif step < count - 1:
                at = (step - 2) * rows
                summed = arrived.astype(jnp.float32) + kept[piece][at : at + rows]
                travelling[piece] = summed.astype(jnp.bfloat16)
            else:
                result = finish(piece * width, arrived, kept[piece], result, pieces * width)
    return result


def local(weather, conv_first, conv_second, patch_embed, token_mixing):
    tokens = encode(weather, conv_first, conv_second, patch_embed)
    return lift(tokens, token_mixing, PIECES)


def solution(mesh):
    placed = (P("groups", "tok", ("ch", "sub")), P(), P(), P(), P("tok", ("ch", "sub")))
    return jax.shard_map(
        local,
        mesh=mesh,
        in_specs=placed,
        out_specs=P(("groups", "tok"), ("ch", "sub")),
        check_vma=False,
    )
```

```python
import functools

import jax
import jax.numpy as jnp
from jax import lax
from jax.experimental import pallas as pl
from jax.experimental.pallas import tpu as pltpu
from jax.sharding import PartitionSpec as P

PIECES = (2, 3, 3)
STEP = 256
LANES = 128
PACK_COST = 20 * 10**9
WRITES = 4
VMEM_BYTES = 24 * 1024 * 1024
ROWS_AT_ONCE = 1024


def pack_kernel(field_ref, packed_ref, low_ref, high_ref):
    lon, lat, chans = field_ref.shape
    pairs = field_ref[...].reshape(lon // 2, 2, lat, chans)
    joined = jnp.concatenate([pairs[:, 0], pairs[:, 1]], axis=-1).astype(packed_ref.dtype)
    packed_ref[...] = joined
    low_ref[...] = joined[:1]
    high_ref[...] = joined[-1:]


def place(away, count_ch, count_sub, width):
    away_ch, away_sub = away // count_sub, away % count_sub
    at_ch = lax.rem(lax.axis_index("ch") + count_ch - away_ch, count_ch)
    at_sub = lax.rem(lax.axis_index("sub") + count_sub - away_sub, count_sub)
    return pl.ds(pl.multiple_of((at_ch * count_sub + at_sub) * width, width), width)


def join_kernel(count_ch, count_sub, *refs):
    blocks, field_ref = refs[:-1], refs[-1]
    width = field_ref.shape[1] // len(blocks)
    for away, block in enumerate(blocks):
        field_ref[:, place(away, count_ch, count_sub, width), :] = block[...]


def split_two(value):
    upper = value.astype(jnp.bfloat16)
    return upper, (value - upper.astype(jnp.float32)).astype(jnp.bfloat16)


def spread_taps(kernel_ref):
    chans = kernel_ref.shape[1]
    nothing = jnp.zeros((chans, kernel_ref.shape[2]), jnp.float32)
    rows = []
    for tap in range(3):
        taps = [kernel_ref[3 * turn + tap] for turn in range(3)]
        rows.append(jnp.concatenate([taps[1], taps[2], nothing, taps[0]], axis=-1))
        rows.append(jnp.concatenate([taps[0], taps[1], taps[2], nothing], axis=-1))
    return jnp.concatenate(rows, axis=0).T


def weights_kernel(first_ref, second_ref, embed_ref, taps_one_ref, taps_two_ref, embed_out_ref, scratch):
    for source, target in ((first_ref, taps_one_ref), (second_ref, taps_two_ref)):
        upper, lower = split_two(spread_taps(source))
        target[...] = jnp.concatenate([upper, lower], axis=1)
    chans = embed_ref.shape[0] // 4
    embed = embed_ref.shape[1]
    count = lax.axis_size("tok")
    turn = lax.rem(lax.axis_index("tok") + 1, count) * (embed // count)
    turned_embed = pltpu.roll(embed_ref[...].astype(jnp.float32), lax.rem(embed - turn, embed), axis=1)
    for first in range(0, embed, LANES):
        scratch[...] = turned_embed[:, first : first + LANES]
        ordered = [scratch[pl.ds(2 * a + b, chans, stride=4), :] for b in range(2) for a in range(2)]
        rows = jnp.concatenate(ordered, axis=0).T
        embed_out_ref[pl.ds(first, LANES), :] = rows.astype(embed_out_ref.dtype)


def pairs_at_once(pairs, lat):
    best = 1
    for size in range(1, pairs + 1):
        if pairs % size == 0 and size * lat <= ROWS_AT_ONCE:
            best = size
    return best


def window(pair_at, pairs):
    rows = []
    for pair in pairs:
        here = pair_at(pair)
        lane = lax.broadcasted_iota(jnp.int32, here.shape, 1)
        beside = jnp.where(lane < here.shape[1] // 2, pair_at(pair + 1), pair_at(pair - 1))
        rows.append(jnp.concatenate([here, beside], axis=-1))
    return jnp.concatenate(rows, axis=0)


def add_lat_taps(products, lat):
    wide = products.shape[1] // 3
    count = products.shape[0]
    row = lax.broadcasted_iota(jnp.int32, (1, lat, wide), 1)
    below = pltpu.roll(products[:, :wide], 1, axis=0).reshape(-1, lat, wide)
    above = pltpu.roll(products[:, 2 * wide :], count - 1, axis=0).reshape(-1, lat, wide)
    here = products[:, wide : 2 * wide].reshape(-1, lat, wide)
    return here + jnp.where(row == 0, 0.0, below) + jnp.where(row == lat - 1, 0.0, above)


def gelu(value):
    return 0.5 * value * (1.0 + lax.erf(value * (0.5**0.5)))


def dot(left, right):
    return jnp.dot(left, right, preferred_element_type=jnp.float32)


def dot_both(rows, taps_ref):
    both = dot(rows, taps_ref[...])
    half = both.shape[1] // 2
    return both[:, :half] + both[:, half:]


def first_conv(field_at, pairs, taps_ref, lat):
    products = dot_both(window(field_at, pairs), taps_ref)
    return split_two(gelu(add_lat_taps(products, lat)))


def second_conv(upper_at, lower_at, pairs, taps_ref, lat):
    upper, lower = window(upper_at, pairs), window(lower_at, pairs)
    products = dot_both(upper, taps_ref) + dot(lower, taps_ref[:, : taps_ref.shape[1] // 2])
    rounded = add_lat_taps(products, lat).astype(jnp.bfloat16).astype(jnp.float32)
    return rounded.reshape(-1, rounded.shape[2])


def embed_patches(two_ref, embed_ref):
    half = two_ref.shape[0] // 2
    patches = jnp.concatenate(
        [two_ref[pl.ds(b, half, stride=2), :].astype(jnp.bfloat16) for b in range(2)], axis=-1
    )
    return lax.dot_general(
        embed_ref[...], patches, (((1,), (1,)), ((), ())), preferred_element_type=jnp.float32
    ).astype(jnp.bfloat16)


def runs(first, last, lat):
    size = pairs_at_once(last - first, lat)
    return [list(range(at, at + size)) for at in range(first, last, size)]


def inner_kernel(
    field_ref, taps_one_ref, taps_two_ref, embed_ref, tokens_ref, upper_edge_ref, lower_edge_ref, upper_ref, lower_ref, two_ref
):
    pairs, lat, wide = field_ref.shape
    for run in runs(1, pairs - 1, lat):
        upper, lower = first_conv(lambda pair: field_ref[pair], run, taps_one_ref, lat)
        upper_ref[pl.ds(run[0], len(run))] = upper
        lower_ref[pl.ds(run[0], len(run))] = lower
    for inside, edge in ((upper_ref, upper_edge_ref), (lower_ref, lower_edge_ref)):
        edge[pl.ds(0, 2)] = inside[pl.ds(1, 2)]
        edge[pl.ds(2, 2)] = inside[pl.ds(pairs - 3, 2)]
    for run in runs(2, pairs - 2, lat):
        two = second_conv(lambda pair: upper_ref[pair], lambda pair: lower_ref[pair], run, taps_two_ref, lat)
        two_ref[pl.ds((run[0] - 2) * lat, len(run) * lat), :] = two
    tokens_ref[...] = embed_patches(two_ref, embed_ref)


def outer_kernel(count_ch, count_sub, field_ref, *refs):
    count = count_ch * count_sub
    sides, refs = refs[:count], refs[count:]
    upper_edge_ref, lower_edge_ref, taps_one_ref, taps_two_ref, embed_ref, inner_ref, tokens_ref, two_ref, sides_ref = refs
    pairs, lat, wide = field_ref.shape
    for away, block in enumerate(sides):
        sides_ref[:, place(away, count_ch, count_sub, lat // count), :] = block[...]

    def field_at(pair):
        if pair < 0:
            return sides_ref[0]
        if pair >= pairs:
            return sides_ref[1]
        return field_ref[pair]

    outermost = [-1, 0, pairs - 1, pairs]
    next_inside = [1, 2, pairs - 3, pairs - 2]
    upper, lower = first_conv(field_at, outermost, taps_one_ref, lat)

    def hidden_at(found, edge_ref):
        def at(pair):
            if pair in outermost:
                return found[outermost.index(pair)]
            return edge_ref[next_inside.index(pair)]

        return at

    two_ref[...] = second_conv(
        hidden_at(upper, upper_edge_ref), hidden_at(lower, lower_edge_ref), [0, 1, pairs - 2, pairs - 1], taps_two_ref, lat
    )
    outer = embed_patches(two_ref, embed_ref)
    inner = inner_ref.shape[1]
    tokens_ref[:, :lat] = outer[:, :lat]
    tokens_ref[:, pl.ds(lat, inner)] = inner_ref[...]
    tokens_ref[:, pl.ds(lat + inner, lat)] = outer[:, lat:]


def call(kernel, out_shape, inputs, scratch=(), flops=0, moved=0):
    return pl.pallas_call(
        kernel,
        out_shape=out_shape,
        in_specs=[pl.BlockSpec(memory_space=pltpu.VMEM)] * len(inputs),
        out_specs=jax.tree.map(lambda unused: pl.BlockSpec(memory_space=pltpu.VMEM), out_shape),
        scratch_shapes=list(scratch),
        compiler_params=pltpu.CompilerParams(vmem_limit_bytes=VMEM_BYTES),
        cost_estimate=pl.CostEstimate(flops=flops, bytes_accessed=moved, transcendentals=0),
    )(*inputs)


def turned(value, axis, away):
    count = lax.axis_size(axis)
    return lax.ppermute(value, axis, [(i, (i + away) % count) for i in range(count)])


def band_blocks(block):
    rows = [block] + [turned(block, "ch", away) for away in range(1, lax.axis_size("ch"))]
    blocks = []
    for row in rows:
        blocks.append(row)
        blocks.extend(turned(row, "sub", away) for away in range(1, lax.axis_size("sub")))
    return blocks


def direct_blocks(block):
    sizes = lax.axis_size("ch"), lax.axis_size("sub")
    devices = [(at_ch, at_sub) for at_ch in range(sizes[0]) for at_sub in range(sizes[1])]
    blocks = [block]
    for away in devices[1:]:
        targets = [tuple((at + step) % size for at, step, size in zip(device, away, sizes)) for device in devices]
        route = [(number, devices.index(target)) for number, target in enumerate(targets)]
        blocks.append(lax.ppermute(block, ("ch", "sub"), route))
    return blocks


def encode(weather, conv_first, conv_second, patch_embed):
    chans, lon, lat = weather.shape
    pairs, wide = lon // 2, 2 * chans
    embed = patch_embed.shape[1]
    shape = functools.partial(jax.ShapeDtypeStruct, dtype=jnp.bfloat16)
    edge = shape((1, lat, wide))
    packed, low, high = call(
        pack_kernel,
        (shape((pairs, lat, wide)), edge, edge),
        (jnp.transpose(weather, (1, 2, 0)),),
        moved=weather.size * 10,
        flops=PACK_COST,
    )
    before = turned(high, "tok", 1)
    after = turned(low, "tok", -1)
    blocks = band_blocks(packed)
    taps = shape((4 * chans, 12 * chans))
    weights = call(
        weights_kernel,
        (taps, taps, shape((embed, 4 * chans))),
        (conv_first, conv_second, patch_embed),
        scratch=[pltpu.VMEM((patch_embed.shape[0], LANES), jnp.float32)],
        moved=conv_first.size * 20,
    )
    sides = direct_blocks(jnp.concatenate([before, after], axis=0))
    counts = lax.axis_size("ch"), lax.axis_size("sub")
    lat = len(blocks) * lat
    field = call(
        functools.partial(join_kernel, *counts),
        shape((pairs, lat, wide)),
        blocks,
        moved=packed.size * 4 * len(blocks),
    )
    work = 2 * lat * 4 * chans * 6 * chans * 5
    held = shape((4, lat, wide))
    hidden = pltpu.VMEM((pairs, lat, wide), jnp.bfloat16)
    inner, upper_edge, lower_edge = call(
        inner_kernel,
        (shape((embed, (pairs - 4) * lat // 2)), held, held),
        (field, *weights),
        scratch=[hidden, hidden, pltpu.VMEM(((pairs - 4) * lat, wide), jnp.float32)],
        flops=work * (pairs - 3),
        moved=field.size * 2,
    )
    return call(
        functools.partial(outer_kernel, *counts),
        shape((embed, pairs * lat // 2)),
        (field, *sides, upper_edge, lower_edge, *weights, inner),
        scratch=[pltpu.VMEM((4 * lat, wide), jnp.float32), pltpu.VMEM((2, lat, wide), jnp.bfloat16)],
        flops=work * 4,
        moved=field.size * 2,
    )


def sent_kernel(first, block, tokens_ref, mixing_ref, sent_ref):
    rows, width = sent_ref.shape
    step = STEP if width % STEP == 0 else width
    tokens = tokens_ref[pl.ds(block * rows, rows), :]
    for at in range(0, width, step):
        product = dot(tokens, mixing_ref[:, pl.ds(first + at, step)])
        sent_ref[:, pl.ds(at, step)] = product.astype(sent_ref.dtype)


def hop_kernel(first, blocks, arrived_ref, tokens_ref, mixing_ref, sent_ref, kept_ref):
    rows, width = sent_ref.shape
    step = STEP if width % STEP == 0 else width
    tokens = jnp.concatenate([tokens_ref[pl.ds(block * rows, rows), :] for block in blocks], axis=0)
    for at in range(0, width, step):
        product = dot(tokens, mixing_ref[:, pl.ds(first + at, step)])
        arrived = arrived_ref[:, pl.ds(at, step)].astype(jnp.float32)
        sent_ref[:, pl.ds(at, step)] = (arrived + product[:rows]).astype(sent_ref.dtype)
        kept_ref[:, pl.ds(at, step)] = product[rows:]


def last_kernel(first, arrived_ref, kept_ref, *refs):
    result_ref, held_ref, written = refs[-3:]
    rows, width = arrived_ref.shape
    part = width // written.shape[0]
    copies = []
    for at in range(written.shape[0]):
        here = pl.ds(at * part, part)
        own = kept_ref[kept_ref.shape[0] - rows :, at * part : (at + 1) * part]
        held_ref[:, here] = gelu(arrived_ref[:, here].astype(jnp.float32) + own).astype(held_ref.dtype)
        target = result_ref.at[:, pl.ds(first + at * part, part)]
        copies.append(pltpu.make_async_copy(held_ref.at[:, here], target, written.at[at]))
        copies[-1].start()
    for copy in copies:
        copy.wait()


def finish(first, arrived, kept, result, columns):
    rows, width = arrived.shape
    near, far = pl.BlockSpec(memory_space=pltpu.VMEM), pl.BlockSpec(memory_space=pl.ANY)
    earlier = [] if result is None else [result]
    return pl.pallas_call(
        functools.partial(last_kernel, first),
        out_shape=jax.ShapeDtypeStruct((rows, columns), jnp.bfloat16),
        in_specs=[near, near] + [far] * len(earlier),
        out_specs=far,
        input_output_aliases={2: 0} if earlier else {},
        scratch_shapes=[
            pltpu.VMEM((rows, width), jnp.bfloat16),
            pltpu.SemaphoreType.DMA((WRITES if width % (WRITES * LANES) == 0 else 1,)),
        ],
        compiler_params=pltpu.CompilerParams(vmem_limit_bytes=VMEM_BYTES),
        cost_estimate=pl.CostEstimate(flops=0, bytes_accessed=0, transcendentals=0),
    )(arrived, kept, *earlier)


def lift(tokens, token_mixing, shares):
    count = lax.axis_size("tok")
    embed, columns = tokens.shape[0], token_mixing.shape[1]
    rows = embed // count
    cuts = [columns * sum(shares[:at]) // sum(shares) for at in range(len(shares) + 1)]
    widths = [last - first for first, last in zip(cuts[:-1], cuts[1:])]
    pieces = len(widths)
    sent = [jax.ShapeDtypeStruct((rows, width), jnp.bfloat16) for width in widths]
    travelling = [
        call(functools.partial(sent_kernel, cuts[piece], 0), sent[piece], (tokens, token_mixing)) for piece in range(pieces)
    ]
    kept = [None] * pieces
    result = None
    for step in range(1, count):
        for piece in range(pieces):
            arrived = turned(travelling[piece], "tok", -1)
            if step == 1:
                travelling[piece], kept[piece] = call(
                    functools.partial(hop_kernel, cuts[piece], list(range(1, count))),
                    [sent[piece], jax.ShapeDtypeStruct((embed - 2 * rows, widths[piece]), jnp.float32)],
                    (arrived, tokens, token_mixing),
                )
            elif step < count - 1:
                at = (step - 2) * rows
                summed = arrived.astype(jnp.float32) + kept[piece][at : at + rows]
                travelling[piece] = summed.astype(jnp.bfloat16)
            else:
                result = finish(cuts[piece], arrived, kept[piece], result, columns)
    return result


def local(weather, conv_first, conv_second, patch_embed, token_mixing):
    tokens = encode(weather, conv_first, conv_second, patch_embed)
    return lift(tokens, token_mixing, PIECES)


def solution(mesh):
    placed = (P("groups", "tok", ("ch", "sub")), P(), P(), P(), P("tok", ("ch", "sub")))
    return jax.shard_map(
        local,
        mesh=mesh,
        in_specs=placed,
        out_specs=P(("groups", "tok"), ("ch", "sub")),
        check_vma=False,
    )
```

```python
import functools

import jax
import jax.numpy as jnp
from jax import lax
from jax.experimental import pallas as pl
from jax.experimental.pallas import tpu as pltpu
from jax.sharding import PartitionSpec as P

PIECES = (1, 1)
STEP = 256
LANES = 128
PACK_COST = 20 * 10**9
WRITES = 4
VMEM_BYTES = 24 * 1024 * 1024
ROWS_AT_ONCE = 1024


def pack_kernel(field_ref, packed_ref, low_ref, high_ref):
    lon, lat, chans = field_ref.shape
    pairs = field_ref[...].reshape(lon // 2, 2, lat, chans)
    joined = jnp.concatenate([pairs[:, 0], pairs[:, 1]], axis=-1).astype(packed_ref.dtype)
    packed_ref[...] = joined
    low_ref[...] = joined[:1]
    high_ref[...] = joined[-1:]


def place(away, count_ch, count_sub, width):
    away_ch, away_sub = away // count_sub, away % count_sub
    at_ch = lax.rem(lax.axis_index("ch") + count_ch - away_ch, count_ch)
    at_sub = lax.rem(lax.axis_index("sub") + count_sub - away_sub, count_sub)
    return pl.ds(pl.multiple_of((at_ch * count_sub + at_sub) * width, width), width)


def join_kernel(count_ch, count_sub, *refs):
    blocks, field_ref = refs[:-1], refs[-1]
    width = field_ref.shape[1] // len(blocks)
    for away, block in enumerate(blocks):
        field_ref[:, place(away, count_ch, count_sub, width), :] = block[...]


def split_two(value):
    upper = value.astype(jnp.bfloat16)
    return upper, (value - upper.astype(jnp.float32)).astype(jnp.bfloat16)


def spread_taps(kernel_ref):
    chans = kernel_ref.shape[1]
    nothing = jnp.zeros((chans, kernel_ref.shape[2]), jnp.float32)
    rows = []
    for tap in range(3):
        taps = [kernel_ref[3 * turn + tap] for turn in range(3)]
        rows.append(jnp.concatenate([taps[1], taps[2], nothing, taps[0]], axis=-1))
        rows.append(jnp.concatenate([taps[0], taps[1], taps[2], nothing], axis=-1))
    return jnp.concatenate(rows, axis=0).T


def weights_kernel(first_ref, second_ref, embed_ref, taps_one_ref, taps_two_ref, embed_out_ref, scratch):
    for source, target in ((first_ref, taps_one_ref), (second_ref, taps_two_ref)):
        upper, lower = split_two(spread_taps(source))
        target[...] = jnp.concatenate([upper, lower], axis=1)
    chans = embed_ref.shape[0] // 4
    embed = embed_ref.shape[1]
    count = lax.axis_size("tok")
    turn = lax.rem(lax.axis_index("tok") + 1, count) * (embed // count)
    turned_embed = pltpu.roll(embed_ref[...].astype(jnp.float32), lax.rem(embed - turn, embed), axis=1)
    for first in range(0, embed, LANES):
        scratch[...] = turned_embed[:, first : first + LANES]
        ordered = [scratch[pl.ds(2 * a + b, chans, stride=4), :] for b in range(2) for a in range(2)]
        rows = jnp.concatenate(ordered, axis=0).T
        embed_out_ref[pl.ds(first, LANES), :] = rows.astype(embed_out_ref.dtype)


def pairs_at_once(pairs, lat):
    best = 1
    for size in range(1, pairs + 1):
        if pairs % size == 0 and size * lat <= ROWS_AT_ONCE:
            best = size
    return best


def window(pair_at, pairs):
    rows = []
    for pair in pairs:
        here = pair_at(pair)
        lane = lax.broadcasted_iota(jnp.int32, here.shape, 1)
        beside = jnp.where(lane < here.shape[1] // 2, pair_at(pair + 1), pair_at(pair - 1))
        rows.append(jnp.concatenate([here, beside], axis=-1))
    return jnp.concatenate(rows, axis=0)


def add_lat_taps(products, lat):
    wide = products.shape[1] // 3
    count = products.shape[0]
    row = lax.broadcasted_iota(jnp.int32, (1, lat, wide), 1)
    below = pltpu.roll(products[:, :wide], 1, axis=0).reshape(-1, lat, wide)
    above = pltpu.roll(products[:, 2 * wide :], count - 1, axis=0).reshape(-1, lat, wide)
    here = products[:, wide : 2 * wide].reshape(-1, lat, wide)
    return here + jnp.where(row == 0, 0.0, below) + jnp.where(row == lat - 1, 0.0, above)


def gelu(value):
    return 0.5 * value * (1.0 + lax.erf(value * (0.5**0.5)))


def dot(left, right):
    return jnp.dot(left, right, preferred_element_type=jnp.float32)


def dot_both(rows, taps_ref):
    both = dot(rows, taps_ref[...])
    half = both.shape[1] // 2
    return both[:, :half] + both[:, half:]


def first_conv(field_at, pairs, taps_ref, lat):
    products = dot_both(window(field_at, pairs), taps_ref)
    return split_two(gelu(add_lat_taps(products, lat)))


def second_conv(upper_at, lower_at, pairs, taps_ref, lat):
    upper, lower = window(upper_at, pairs), window(lower_at, pairs)
    products = dot_both(upper, taps_ref) + dot(lower, taps_ref[:, : taps_ref.shape[1] // 2])
    rounded = add_lat_taps(products, lat).astype(jnp.bfloat16).astype(jnp.float32)
    return rounded.reshape(-1, rounded.shape[2])


def embed_patches(two_ref, embed_ref):
    half = two_ref.shape[0] // 2
    patches = jnp.concatenate(
        [two_ref[pl.ds(b, half, stride=2), :].astype(jnp.bfloat16) for b in range(2)], axis=-1
    )
    return lax.dot_general(
        embed_ref[...], patches, (((1,), (1,)), ((), ())), preferred_element_type=jnp.float32
    ).astype(jnp.bfloat16)


def runs(first, last, lat):
    size = pairs_at_once(last - first, lat)
    return [list(range(at, at + size)) for at in range(first, last, size)]


def inner_kernel(
    field_ref, taps_one_ref, taps_two_ref, embed_ref, tokens_ref, upper_edge_ref, lower_edge_ref, upper_ref, lower_ref, two_ref
):
    pairs, lat, wide = field_ref.shape
    for run in runs(1, pairs - 1, lat):
        upper, lower = first_conv(lambda pair: field_ref[pair], run, taps_one_ref, lat)
        upper_ref[pl.ds(run[0], len(run))] = upper
        lower_ref[pl.ds(run[0], len(run))] = lower
    for inside, edge in ((upper_ref, upper_edge_ref), (lower_ref, lower_edge_ref)):
        edge[pl.ds(0, 2)] = inside[pl.ds(1, 2)]
        edge[pl.ds(2, 2)] = inside[pl.ds(pairs - 3, 2)]
    for run in runs(2, pairs - 2, lat):
        two = second_conv(lambda pair: upper_ref[pair], lambda pair: lower_ref[pair], run, taps_two_ref, lat)
        two_ref[pl.ds((run[0] - 2) * lat, len(run) * lat), :] = two
    tokens_ref[...] = embed_patches(two_ref, embed_ref)


def outer_kernel(count_ch, count_sub, field_ref, *refs):
    count = count_ch * count_sub
    sides, refs = refs[:count], refs[count:]
    upper_edge_ref, lower_edge_ref, taps_one_ref, taps_two_ref, embed_ref, inner_ref, tokens_ref, two_ref, sides_ref = refs
    pairs, lat, wide = field_ref.shape
    for away, block in enumerate(sides):
        sides_ref[:, place(away, count_ch, count_sub, lat // count), :] = block[...]

    def field_at(pair):
        if pair < 0:
            return sides_ref[0]
        if pair >= pairs:
            return sides_ref[1]
        return field_ref[pair]

    outermost = [-1, 0, pairs - 1, pairs]
    next_inside = [1, 2, pairs - 3, pairs - 2]
    upper, lower = first_conv(field_at, outermost, taps_one_ref, lat)

    def hidden_at(found, edge_ref):
        def at(pair):
            if pair in outermost:
                return found[outermost.index(pair)]
            return edge_ref[next_inside.index(pair)]

        return at

    two_ref[...] = second_conv(
        hidden_at(upper, upper_edge_ref), hidden_at(lower, lower_edge_ref), [0, 1, pairs - 2, pairs - 1], taps_two_ref, lat
    )
    outer = embed_patches(two_ref, embed_ref)
    inner = inner_ref.shape[1]
    tokens_ref[:, :lat] = outer[:, :lat]
    tokens_ref[:, pl.ds(lat, inner)] = inner_ref[...]
    tokens_ref[:, pl.ds(lat + inner, lat)] = outer[:, lat:]


def call(kernel, out_shape, inputs, scratch=(), flops=0, moved=0):
    return pl.pallas_call(
        kernel,
        out_shape=out_shape,
        in_specs=[pl.BlockSpec(memory_space=pltpu.VMEM)] * len(inputs),
        out_specs=jax.tree.map(lambda unused: pl.BlockSpec(memory_space=pltpu.VMEM), out_shape),
        scratch_shapes=list(scratch),
        compiler_params=pltpu.CompilerParams(vmem_limit_bytes=VMEM_BYTES),
        cost_estimate=pl.CostEstimate(flops=flops, bytes_accessed=moved, transcendentals=0),
    )(*inputs)


def turned(value, axis, away):
    count = lax.axis_size(axis)
    return lax.ppermute(value, axis, [(i, (i + away) % count) for i in range(count)])


def band_blocks(block):
    rows = [block] + [turned(block, "ch", away) for away in range(1, lax.axis_size("ch"))]
    blocks = []
    for row in rows:
        blocks.append(row)
        blocks.extend(turned(row, "sub", away) for away in range(1, lax.axis_size("sub")))
    return blocks


def direct_blocks(block):
    sizes = lax.axis_size("ch"), lax.axis_size("sub")
    devices = [(at_ch, at_sub) for at_ch in range(sizes[0]) for at_sub in range(sizes[1])]
    blocks = [block]
    for away in devices[1:]:
        targets = [tuple((at + step) % size for at, step, size in zip(device, away, sizes)) for device in devices]
        route = [(number, devices.index(target)) for number, target in enumerate(targets)]
        blocks.append(lax.ppermute(block, ("ch", "sub"), route))
    return blocks


def encode(weather, conv_first, conv_second, patch_embed):
    chans, lon, lat = weather.shape
    pairs, wide = lon // 2, 2 * chans
    embed = patch_embed.shape[1]
    shape = functools.partial(jax.ShapeDtypeStruct, dtype=jnp.bfloat16)
    edge = shape((1, lat, wide))
    packed, low, high = call(
        pack_kernel,
        (shape((pairs, lat, wide)), edge, edge),
        (jnp.transpose(weather, (1, 2, 0)),),
        moved=weather.size * 10,
        flops=PACK_COST,
    )
    before = turned(high, "tok", 1)
    after = turned(low, "tok", -1)
    blocks = band_blocks(packed)
    taps = shape((4 * chans, 12 * chans))
    weights = call(
        weights_kernel,
        (taps, taps, shape((embed, 4 * chans))),
        (conv_first, conv_second, patch_embed),
        scratch=[pltpu.VMEM((patch_embed.shape[0], LANES), jnp.float32)],
        moved=conv_first.size * 20,
    )
    sides = direct_blocks(jnp.concatenate([before, after], axis=0))
    counts = lax.axis_size("ch"), lax.axis_size("sub")
    lat = len(blocks) * lat
    field = call(
        functools.partial(join_kernel, *counts),
        shape((pairs, lat, wide)),
        blocks,
        moved=packed.size * 4 * len(blocks),
    )
    work = 2 * lat * 4 * chans * 6 * chans * 5
    held = shape((4, lat, wide))
    hidden = pltpu.VMEM((pairs, lat, wide), jnp.bfloat16)
    inner, upper_edge, lower_edge = call(
        inner_kernel,
        (shape((embed, (pairs - 4) * lat // 2)), held, held),
        (field, *weights),
        scratch=[hidden, hidden, pltpu.VMEM(((pairs - 4) * lat, wide), jnp.float32)],
        flops=work * (pairs - 3),
        moved=field.size * 2,
    )
    return call(
        functools.partial(outer_kernel, *counts),
        shape((embed, pairs * lat // 2)),
        (field, *sides, upper_edge, lower_edge, *weights, inner),
        scratch=[pltpu.VMEM((4 * lat, wide), jnp.float32), pltpu.VMEM((2, lat, wide), jnp.bfloat16)],
        flops=work * 4,
        moved=field.size * 2,
    )


def sent_kernel(first, block, tokens_ref, mixing_ref, sent_ref):
    rows, width = sent_ref.shape
    step = STEP if width % STEP == 0 else width
    tokens = tokens_ref[pl.ds(block * rows, rows), :]
    for at in range(0, width, step):
        product = dot(tokens, mixing_ref[:, pl.ds(first + at, step)])
        sent_ref[:, pl.ds(at, step)] = product.astype(sent_ref.dtype)


def hop_kernel(first, blocks, arrived_ref, tokens_ref, mixing_ref, sent_ref, kept_ref):
    rows, width = sent_ref.shape
    step = STEP if width % STEP == 0 else width
    tokens = jnp.concatenate([tokens_ref[pl.ds(block * rows, rows), :] for block in blocks], axis=0)
    for at in range(0, width, step):
        product = dot(tokens, mixing_ref[:, pl.ds(first + at, step)])
        arrived = arrived_ref[:, pl.ds(at, step)].astype(jnp.float32)
        sent_ref[:, pl.ds(at, step)] = (arrived + product[:rows]).astype(sent_ref.dtype)
        kept_ref[:, pl.ds(at, step)] = product[rows:]


def last_kernel(first, arrived_ref, kept_ref, *refs):
    result_ref, held_ref, written = refs[-3:]
    rows, width = arrived_ref.shape
    part = width // written.shape[0]
    copies = []
    for at in range(written.shape[0]):
        here = pl.ds(at * part, part)
        own = kept_ref[kept_ref.shape[0] - rows :, at * part : (at + 1) * part]
        held_ref[:, here] = gelu(arrived_ref[:, here].astype(jnp.float32) + own).astype(held_ref.dtype)
        target = result_ref.at[:, pl.ds(first + at * part, part)]
        copies.append(pltpu.make_async_copy(held_ref.at[:, here], target, written.at[at]))
        copies[-1].start()
    for copy in copies:
        copy.wait()


def finish(first, arrived, kept, result, columns):
    rows, width = arrived.shape
    near, far = pl.BlockSpec(memory_space=pltpu.VMEM), pl.BlockSpec(memory_space=pl.ANY)
    earlier = [] if result is None else [result]
    return pl.pallas_call(
        functools.partial(last_kernel, first),
        out_shape=jax.ShapeDtypeStruct((rows, columns), jnp.bfloat16),
        in_specs=[near, near] + [far] * len(earlier),
        out_specs=far,
        input_output_aliases={2: 0} if earlier else {},
        scratch_shapes=[
            pltpu.VMEM((rows, width), jnp.bfloat16),
            pltpu.SemaphoreType.DMA((WRITES if width % (WRITES * LANES) == 0 else 1,)),
        ],
        compiler_params=pltpu.CompilerParams(vmem_limit_bytes=VMEM_BYTES),
        cost_estimate=pl.CostEstimate(flops=0, bytes_accessed=0, transcendentals=0),
    )(arrived, kept, *earlier)


def lift(tokens, token_mixing, shares):
    count = lax.axis_size("tok")
    embed, columns = tokens.shape[0], token_mixing.shape[1]
    rows = embed // count
    cuts = [columns * sum(shares[:at]) // sum(shares) for at in range(len(shares) + 1)]
    widths = [last - first for first, last in zip(cuts[:-1], cuts[1:])]
    pieces = len(widths)
    sent = [jax.ShapeDtypeStruct((rows, width), jnp.bfloat16) for width in widths]
    travelling = [
        call(functools.partial(sent_kernel, cuts[piece], 0), sent[piece], (tokens, token_mixing)) for piece in range(pieces)
    ]
    kept = [None] * pieces
    result = None
    for step in range(1, count):
        for piece in range(pieces):
            arrived = turned(travelling[piece], "tok", -1)
            if step == 1:
                travelling[piece], kept[piece] = call(
                    functools.partial(hop_kernel, cuts[piece], list(range(1, count))),
                    [sent[piece], jax.ShapeDtypeStruct((embed - 2 * rows, widths[piece]), jnp.float32)],
                    (arrived, tokens, token_mixing),
                )
            elif step < count - 1:
                at = (step - 2) * rows
                summed = arrived.astype(jnp.float32) + kept[piece][at : at + rows]
                travelling[piece] = summed.astype(jnp.bfloat16)
            else:
                result = finish(cuts[piece], arrived, kept[piece], result, columns)
    return result


def local(weather, conv_first, conv_second, patch_embed, token_mixing):
    tokens = encode(weather, conv_first, conv_second, patch_embed)
    return lift(tokens, token_mixing, PIECES)


def solution(mesh):
    placed = (P("groups", "tok", ("ch", "sub")), P(), P(), P(), P("tok", ("ch", "sub")))
    return jax.shard_map(
        local,
        mesh=mesh,
        in_specs=placed,
        out_specs=P(("groups", "tok"), ("ch", "sub")),
        check_vma=False,
    )
```

```python
import functools

import jax
import jax.numpy as jnp
from jax import lax
from jax.experimental import pallas as pl
from jax.experimental.pallas import tpu as pltpu
from jax.sharding import PartitionSpec as P

PIECES = 4
STEP = 256
LANES = 128
PACK_COST = 20 * 10**9
WRITES = 4
VMEM_BYTES = 24 * 1024 * 1024
ROWS_AT_ONCE = 2048


def pack_kernel(field_ref, packed_ref, low_ref, high_ref):
    lon, lat, chans = field_ref.shape
    pairs = field_ref[...].reshape(lon // 2, 2, lat, chans)
    joined = jnp.concatenate([pairs[:, 0], pairs[:, 1]], axis=-1).astype(packed_ref.dtype)
    packed_ref[...] = joined
    low_ref[...] = joined[:1]
    high_ref[...] = joined[-1:]


def place(away, count_ch, count_sub, width):
    away_ch, away_sub = away // count_sub, away % count_sub
    at_ch = lax.rem(lax.axis_index("ch") + count_ch - away_ch, count_ch)
    at_sub = lax.rem(lax.axis_index("sub") + count_sub - away_sub, count_sub)
    return pl.ds(pl.multiple_of((at_ch * count_sub + at_sub) * width, width), width)


def join_kernel(count_ch, count_sub, *refs):
    blocks, field_ref = refs[:-1], refs[-1]
    width = field_ref.shape[1] // len(blocks)
    for away, block in enumerate(blocks):
        field_ref[:, place(away, count_ch, count_sub, width), :] = block[...]


def split_two(value):
    upper = value.astype(jnp.bfloat16)
    return upper, (value - upper.astype(jnp.float32)).astype(jnp.bfloat16)


def spread_taps(kernel_ref):
    chans = kernel_ref.shape[1]
    nothing = jnp.zeros((chans, kernel_ref.shape[2]), jnp.float32)
    rows = []
    for tap in range(3):
        taps = [kernel_ref[3 * turn + tap] for turn in range(3)]
        rows.append(jnp.concatenate([taps[1], taps[2], nothing, taps[0]], axis=-1))
        rows.append(jnp.concatenate([taps[0], taps[1], taps[2], nothing], axis=-1))
    return jnp.concatenate(rows, axis=0).T


def weights_kernel(first_ref, second_ref, embed_ref, taps_one_ref, taps_two_ref, embed_out_ref, scratch):
    for source, target in ((first_ref, taps_one_ref), (second_ref, taps_two_ref)):
        upper, lower = split_two(spread_taps(source))
        target[...] = jnp.concatenate([upper, lower], axis=1)
    chans = embed_ref.shape[0] // 4
    embed = embed_ref.shape[1]
    count = lax.axis_size("tok")
    turn = lax.rem(lax.axis_index("tok") + 1, count) * (embed // count)
    turned_embed = pltpu.roll(embed_ref[...].astype(jnp.float32), lax.rem(embed - turn, embed), axis=1)
    for first in range(0, embed, LANES):
        scratch[...] = turned_embed[:, first : first + LANES]
        ordered = [scratch[pl.ds(2 * a + b, chans, stride=4), :] for b in range(2) for a in range(2)]
        rows = jnp.concatenate(ordered, axis=0).T
        embed_out_ref[pl.ds(first, LANES), :] = rows.astype(embed_out_ref.dtype)


def pairs_at_once(pairs, lat):
    best = 1
    for size in range(1, pairs + 1):
        if pairs % size == 0 and size * lat <= ROWS_AT_ONCE:
            best = size
    return best


def window(pair_at, pairs):
    rows = []
    for pair in pairs:
        here = pair_at(pair)
        lane = lax.broadcasted_iota(jnp.int32, here.shape, 1)
        beside = jnp.where(lane < here.shape[1] // 2, pair_at(pair + 1), pair_at(pair - 1))
        rows.append(jnp.concatenate([here, beside], axis=-1))
    return jnp.concatenate(rows, axis=0)


def add_lat_taps(products, lat):
    wide = products.shape[1] // 3
    count = products.shape[0]
    row = lax.broadcasted_iota(jnp.int32, (1, lat, wide), 1)
    below = pltpu.roll(products[:, :wide], 1, axis=0).reshape(-1, lat, wide)
    above = pltpu.roll(products[:, 2 * wide :], count - 1, axis=0).reshape(-1, lat, wide)
    here = products[:, wide : 2 * wide].reshape(-1, lat, wide)
    return here + jnp.where(row == 0, 0.0, below) + jnp.where(row == lat - 1, 0.0, above)


def gelu(value):
    return 0.5 * value * (1.0 + lax.erf(value * (0.5**0.5)))


def dot(left, right):
    return jnp.dot(left, right, preferred_element_type=jnp.float32)


def dot_both(rows, taps_ref):
    both = dot(rows, taps_ref[...])
    half = both.shape[1] // 2
    return both[:, :half] + both[:, half:]


def first_conv(field_at, pairs, taps_ref, lat):
    products = dot_both(window(field_at, pairs), taps_ref)
    return split_two(gelu(add_lat_taps(products, lat)))


def second_conv(upper_at, lower_at, pairs, taps_ref, lat):
    upper, lower = window(upper_at, pairs), window(lower_at, pairs)
    products = dot_both(upper, taps_ref) + dot(lower, taps_ref[:, : taps_ref.shape[1] // 2])
    rounded = add_lat_taps(products, lat).astype(jnp.bfloat16).astype(jnp.float32)
    return rounded.reshape(-1, rounded.shape[2])


def embed_patches(two_ref, embed_ref):
    half = two_ref.shape[0] // 2
    patches = jnp.concatenate(
        [two_ref[pl.ds(b, half, stride=2), :].astype(jnp.bfloat16) for b in range(2)], axis=-1
    )
    return lax.dot_general(
        embed_ref[...], patches, (((1,), (1,)), ((), ())), preferred_element_type=jnp.float32
    ).astype(jnp.bfloat16)


def runs(first, last, lat):
    size = pairs_at_once(last - first, lat)
    return [list(range(at, at + size)) for at in range(first, last, size)]


def inner_kernel(
    field_ref, taps_one_ref, taps_two_ref, embed_ref, tokens_ref, upper_edge_ref, lower_edge_ref, upper_ref, lower_ref, two_ref
):
    pairs, lat, wide = field_ref.shape
    for run in runs(1, pairs - 1, lat):
        upper, lower = first_conv(lambda pair: field_ref[pair], run, taps_one_ref, lat)
        upper_ref[pl.ds(run[0], len(run))] = upper
        lower_ref[pl.ds(run[0], len(run))] = lower
    for inside, edge in ((upper_ref, upper_edge_ref), (lower_ref, lower_edge_ref)):
        edge[pl.ds(0, 2)] = inside[pl.ds(1, 2)]
        edge[pl.ds(2, 2)] = inside[pl.ds(pairs - 3, 2)]
    for run in runs(2, pairs - 2, lat):
        two = second_conv(lambda pair: upper_ref[pair], lambda pair: lower_ref[pair], run, taps_two_ref, lat)
        two_ref[pl.ds((run[0] - 2) * lat, len(run) * lat), :] = two
    tokens_ref[...] = embed_patches(two_ref, embed_ref)


def outer_kernel(count_ch, count_sub, field_ref, *refs):
    count = count_ch * count_sub
    sides, refs = refs[:count], refs[count:]
    upper_edge_ref, lower_edge_ref, taps_one_ref, taps_two_ref, embed_ref, inner_ref, tokens_ref, two_ref, sides_ref = refs
    pairs, lat, wide = field_ref.shape
    for away, block in enumerate(sides):
        sides_ref[:, place(away, count_ch, count_sub, lat // count), :] = block[...]

    def field_at(pair):
        if pair < 0:
            return sides_ref[0]
        if pair >= pairs:
            return sides_ref[1]
        return field_ref[pair]

    outermost = [-1, 0, pairs - 1, pairs]
    next_inside = [1, 2, pairs - 3, pairs - 2]
    upper, lower = first_conv(field_at, outermost, taps_one_ref, lat)

    def hidden_at(found, edge_ref):
        def at(pair):
            if pair in outermost:
                return found[outermost.index(pair)]
            return edge_ref[next_inside.index(pair)]

        return at

    two_ref[...] = second_conv(
        hidden_at(upper, upper_edge_ref), hidden_at(lower, lower_edge_ref), [0, 1, pairs - 2, pairs - 1], taps_two_ref, lat
    )
    outer = embed_patches(two_ref, embed_ref)
    inner = inner_ref.shape[1]
    tokens_ref[:, :lat] = outer[:, :lat]
    tokens_ref[:, pl.ds(lat, inner)] = inner_ref[...]
    tokens_ref[:, pl.ds(lat + inner, lat)] = outer[:, lat:]


def call(kernel, out_shape, inputs, scratch=(), flops=0, moved=0):
    return pl.pallas_call(
        kernel,
        out_shape=out_shape,
        in_specs=[pl.BlockSpec(memory_space=pltpu.VMEM)] * len(inputs),
        out_specs=jax.tree.map(lambda unused: pl.BlockSpec(memory_space=pltpu.VMEM), out_shape),
        scratch_shapes=list(scratch),
        compiler_params=pltpu.CompilerParams(vmem_limit_bytes=VMEM_BYTES),
        cost_estimate=pl.CostEstimate(flops=flops, bytes_accessed=moved, transcendentals=0),
    )(*inputs)


def turned(value, axis, away):
    count = lax.axis_size(axis)
    return lax.ppermute(value, axis, [(i, (i + away) % count) for i in range(count)])


def band_blocks(block):
    rows = [block] + [turned(block, "ch", away) for away in range(1, lax.axis_size("ch"))]
    blocks = []
    for row in rows:
        blocks.append(row)
        blocks.extend(turned(row, "sub", away) for away in range(1, lax.axis_size("sub")))
    return blocks


def direct_blocks(block):
    sizes = lax.axis_size("ch"), lax.axis_size("sub")
    devices = [(at_ch, at_sub) for at_ch in range(sizes[0]) for at_sub in range(sizes[1])]
    blocks = [block]
    for away in devices[1:]:
        targets = [tuple((at + step) % size for at, step, size in zip(device, away, sizes)) for device in devices]
        route = [(number, devices.index(target)) for number, target in enumerate(targets)]
        blocks.append(lax.ppermute(block, ("ch", "sub"), route))
    return blocks


def encode(weather, conv_first, conv_second, patch_embed):
    chans, lon, lat = weather.shape
    pairs, wide = lon // 2, 2 * chans
    embed = patch_embed.shape[1]
    shape = functools.partial(jax.ShapeDtypeStruct, dtype=jnp.bfloat16)
    edge = shape((1, lat, wide))
    packed, low, high = call(
        pack_kernel,
        (shape((pairs, lat, wide)), edge, edge),
        (jnp.transpose(weather, (1, 2, 0)),),
        moved=weather.size * 10,
        flops=PACK_COST,
    )
    before = turned(high, "tok", 1)
    after = turned(low, "tok", -1)
    blocks = band_blocks(packed)
    taps = shape((4 * chans, 12 * chans))
    weights = call(
        weights_kernel,
        (taps, taps, shape((embed, 4 * chans))),
        (conv_first, conv_second, patch_embed),
        scratch=[pltpu.VMEM((patch_embed.shape[0], LANES), jnp.float32)],
        moved=conv_first.size * 20,
    )
    sides = direct_blocks(jnp.concatenate([before, after], axis=0))
    counts = lax.axis_size("ch"), lax.axis_size("sub")
    lat = len(blocks) * lat
    field = call(
        functools.partial(join_kernel, *counts),
        shape((pairs, lat, wide)),
        blocks,
        moved=packed.size * 4 * len(blocks),
    )
    work = 2 * lat * 4 * chans * 6 * chans * 5
    held = shape((4, lat, wide))
    hidden = pltpu.VMEM((pairs, lat, wide), jnp.bfloat16)
    inner, upper_edge, lower_edge = call(
        inner_kernel,
        (shape((embed, (pairs - 4) * lat // 2)), held, held),
        (field, *weights),
        scratch=[hidden, hidden, pltpu.VMEM(((pairs - 4) * lat, wide), jnp.float32)],
        flops=work * (pairs - 3),
        moved=field.size * 2,
    )
    return call(
        functools.partial(outer_kernel, *counts),
        shape((embed, pairs * lat // 2)),
        (field, *sides, upper_edge, lower_edge, *weights, inner),
        scratch=[pltpu.VMEM((4 * lat, wide), jnp.float32), pltpu.VMEM((2, lat, wide), jnp.bfloat16)],
        flops=work * 4,
        moved=field.size * 2,
    )


def sent_kernel(first, block, tokens_ref, mixing_ref, sent_ref):
    rows, width = sent_ref.shape
    step = STEP if width % STEP == 0 else width
    tokens = tokens_ref[pl.ds(block * rows, rows), :]
    for at in range(0, width, step):
        product = dot(tokens, mixing_ref[:, pl.ds(first + at, step)])
        sent_ref[:, pl.ds(at, step)] = product.astype(sent_ref.dtype)


def hop_kernel(first, blocks, arrived_ref, tokens_ref, mixing_ref, sent_ref, kept_ref):
    rows, width = sent_ref.shape
    step = STEP if width % STEP == 0 else width
    tokens = jnp.concatenate([tokens_ref[pl.ds(block * rows, rows), :] for block in blocks], axis=0)
    for at in range(0, width, step):
        product = dot(tokens, mixing_ref[:, pl.ds(first + at, step)])
        arrived = arrived_ref[:, pl.ds(at, step)].astype(jnp.float32)
        sent_ref[:, pl.ds(at, step)] = (arrived + product[:rows]).astype(sent_ref.dtype)
        kept_ref[:, pl.ds(at, step)] = product[rows:]


def last_kernel(first, arrived_ref, kept_ref, *refs):
    result_ref, held_ref, written = refs[-3:]
    rows, width = arrived_ref.shape
    part = width // written.shape[0]
    copies = []
    for at in range(written.shape[0]):
        here = pl.ds(at * part, part)
        own = kept_ref[kept_ref.shape[0] - rows :, at * part : (at + 1) * part]
        held_ref[:, here] = gelu(arrived_ref[:, here].astype(jnp.float32) + own).astype(held_ref.dtype)
        target = result_ref.at[:, pl.ds(first + at * part, part)]
        copies.append(pltpu.make_async_copy(held_ref.at[:, here], target, written.at[at]))
        copies[-1].start()
    for copy in copies:
        copy.wait()


def finish(first, arrived, kept, result, columns):
    rows, width = arrived.shape
    near, far = pl.BlockSpec(memory_space=pltpu.VMEM), pl.BlockSpec(memory_space=pl.ANY)
    earlier = [] if result is None else [result]
    return pl.pallas_call(
        functools.partial(last_kernel, first),
        out_shape=jax.ShapeDtypeStruct((rows, columns), jnp.bfloat16),
        in_specs=[near, near] + [far] * len(earlier),
        out_specs=far,
        input_output_aliases={2: 0} if earlier else {},
        scratch_shapes=[
            pltpu.VMEM((rows, width), jnp.bfloat16),
            pltpu.SemaphoreType.DMA((WRITES if width % (WRITES * LANES) == 0 else 1,)),
        ],
        compiler_params=pltpu.CompilerParams(vmem_limit_bytes=VMEM_BYTES),
        cost_estimate=pl.CostEstimate(flops=0, bytes_accessed=0, transcendentals=0),
    )(arrived, kept, *earlier)


def lift(tokens, token_mixing, pieces):
    count = lax.axis_size("tok")
    embed = tokens.shape[0]
    rows = embed // count
    width = token_mixing.shape[1] // pieces
    sent = jax.ShapeDtypeStruct((rows, width), jnp.bfloat16)
    ways = [-1] * pieces
    blocks = [list(range(count - 2, -1, -1)) if way == 1 else list(range(count - 1)) for way in ways]
    travelling = [
        call(functools.partial(sent_kernel, piece * width, blocks[piece][0]), sent, (tokens, token_mixing))
        for piece in range(pieces)
    ]
    kept = [None] * pieces
    result = None
    for step in range(1, count):
        for piece in range(pieces):
            arrived = turned(travelling[piece], "tok", ways[piece])
            if step == 1:
                travelling[piece], kept[piece] = call(
                    functools.partial(hop_kernel, piece * width, blocks[piece][1:] + [count - 1]),
                    [sent, jax.ShapeDtypeStruct((embed - 2 * rows, width), jnp.float32)],
                    (arrived, tokens, token_mixing),
                )
            elif step < count - 1:
                at = (step - 2) * rows
                summed = arrived.astype(jnp.float32) + kept[piece][at : at + rows]
                travelling[piece] = summed.astype(jnp.bfloat16)
            else:
                result = finish(piece * width, arrived, kept[piece], result, pieces * width)
    return result


def local(weather, conv_first, conv_second, patch_embed, token_mixing):
    tokens = encode(weather, conv_first, conv_second, patch_embed)
    return lift(tokens, token_mixing, PIECES)


def solution(mesh):
    placed = (P("groups", "tok", ("ch", "sub")), P(), P(), P(), P("tok", ("ch", "sub")))
    return jax.shard_map(
        local,
        mesh=mesh,
        in_specs=placed,
        out_specs=P(("groups", "tok"), ("ch", "sub")),
        check_vma=False,
    )
```

```python
import functools

import jax
import jax.numpy as jnp
from jax import lax
from jax.experimental import pallas as pl
from jax.experimental.pallas import tpu as pltpu
from jax.sharding import PartitionSpec as P

PIECES = 4
STEP = 256
LANES = 128
PACK_COST = 20 * 10**9
WRITES = 4
VMEM_BYTES = 24 * 1024 * 1024
ROWS_AT_ONCE = 640


def pack_kernel(field_ref, packed_ref, low_ref, high_ref):
    lon, lat, chans = field_ref.shape
    pairs = field_ref[...].reshape(lon // 2, 2, lat, chans)
    joined = jnp.concatenate([pairs[:, 0], pairs[:, 1]], axis=-1).astype(packed_ref.dtype)
    packed_ref[...] = joined
    low_ref[...] = joined[:1]
    high_ref[...] = joined[-1:]


def place(away, count_ch, count_sub, width):
    away_ch, away_sub = away // count_sub, away % count_sub
    at_ch = lax.rem(lax.axis_index("ch") + count_ch - away_ch, count_ch)
    at_sub = lax.rem(lax.axis_index("sub") + count_sub - away_sub, count_sub)
    return pl.ds(pl.multiple_of((at_ch * count_sub + at_sub) * width, width), width)


def join_kernel(count_ch, count_sub, *refs):
    blocks, field_ref = refs[:-1], refs[-1]
    width = field_ref.shape[1] // len(blocks)
    for away, block in enumerate(blocks):
        field_ref[:, place(away, count_ch, count_sub, width), :] = block[...]


def split_two(value):
    upper = value.astype(jnp.bfloat16)
    return upper, (value - upper.astype(jnp.float32)).astype(jnp.bfloat16)


def spread_taps(kernel_ref):
    chans = kernel_ref.shape[1]
    nothing = jnp.zeros((chans, kernel_ref.shape[2]), jnp.float32)
    rows = []
    for tap in range(3):
        taps = [kernel_ref[3 * turn + tap] for turn in range(3)]
        rows.append(jnp.concatenate([taps[1], taps[2], nothing, taps[0]], axis=-1))
        rows.append(jnp.concatenate([taps[0], taps[1], taps[2], nothing], axis=-1))
    return jnp.concatenate(rows, axis=0).T


def weights_kernel(first_ref, second_ref, embed_ref, taps_one_ref, taps_two_ref, embed_out_ref, scratch):
    for source, target in ((first_ref, taps_one_ref), (second_ref, taps_two_ref)):
        upper, lower = split_two(spread_taps(source))
        target[...] = jnp.concatenate([upper, lower], axis=1)
    chans = embed_ref.shape[0] // 4
    embed = embed_ref.shape[1]
    count = lax.axis_size("tok")
    turn = lax.rem(lax.axis_index("tok") + 1, count) * (embed // count)
    turned_embed = pltpu.roll(embed_ref[...].astype(jnp.float32), lax.rem(embed - turn, embed), axis=1)
    for first in range(0, embed, LANES):
        scratch[...] = turned_embed[:, first : first + LANES]
        ordered = [scratch[pl.ds(2 * a + b, chans, stride=4), :] for b in range(2) for a in range(2)]
        rows = jnp.concatenate(ordered, axis=0).T
        embed_out_ref[pl.ds(first, LANES), :] = rows.astype(embed_out_ref.dtype)


def window(pair_at, pairs):
    rows = []
    for pair in pairs:
        here = pair_at(pair)
        lane = lax.broadcasted_iota(jnp.int32, here.shape, 1)
        beside = jnp.where(lane < here.shape[1] // 2, pair_at(pair + 1), pair_at(pair - 1))
        rows.append(jnp.concatenate([here, beside], axis=-1))
    return jnp.concatenate(rows, axis=0)


def add_lat_taps(products, lat):
    wide = products.shape[1] // 3
    count = products.shape[0]
    row = lax.broadcasted_iota(jnp.int32, (1, lat, wide), 1)
    below = pltpu.roll(products[:, :wide], 1, axis=0).reshape(-1, lat, wide)
    above = pltpu.roll(products[:, 2 * wide :], count - 1, axis=0).reshape(-1, lat, wide)
    here = products[:, wide : 2 * wide].reshape(-1, lat, wide)
    return here + jnp.where(row == 0, 0.0, below) + jnp.where(row == lat - 1, 0.0, above)


def gelu(value):
    return 0.5 * value * (1.0 + lax.erf(value * (0.5**0.5)))


def dot(left, right):
    return jnp.dot(left, right, preferred_element_type=jnp.float32)


def dot_both(rows, taps_ref):
    both = dot(rows, taps_ref[...])
    half = both.shape[1] // 2
    return both[:, :half] + both[:, half:]


def first_conv(field_at, pairs, taps_ref, lat):
    products = dot_both(window(field_at, pairs), taps_ref)
    return split_two(gelu(add_lat_taps(products, lat)))


def second_conv(upper_at, lower_at, pairs, taps_ref, lat):
    upper, lower = window(upper_at, pairs), window(lower_at, pairs)
    products = dot_both(upper, taps_ref) + dot(lower, taps_ref[:, : taps_ref.shape[1] // 2])
    rounded = add_lat_taps(products, lat).astype(jnp.bfloat16).astype(jnp.float32)
    return rounded.reshape(-1, rounded.shape[2])


def embed_patches(two_ref, embed_ref):
    half = two_ref.shape[0] // 2
    patches = jnp.concatenate(
        [two_ref[pl.ds(b, half, stride=2), :].astype(jnp.bfloat16) for b in range(2)], axis=-1
    )
    return lax.dot_general(
        embed_ref[...], patches, (((1,), (1,)), ((), ())), preferred_element_type=jnp.float32
    ).astype(jnp.bfloat16)


def runs(first, last, lat):
    count = -(-(last - first) * lat // max(ROWS_AT_ONCE, lat))
    cuts = [first + (last - first) * at // count for at in range(count + 1)]
    return [list(range(*cut)) for cut in zip(cuts[:-1], cuts[1:])]


def inner_kernel(
    field_ref, taps_one_ref, taps_two_ref, embed_ref, tokens_ref, upper_edge_ref, lower_edge_ref, upper_ref, lower_ref, two_ref
):
    pairs, lat, wide = field_ref.shape
    for run in runs(1, pairs - 1, lat):
        upper, lower = first_conv(lambda pair: field_ref[pair], run, taps_one_ref, lat)
        upper_ref[pl.ds(run[0], len(run))] = upper
        lower_ref[pl.ds(run[0], len(run))] = lower
    for inside, edge in ((upper_ref, upper_edge_ref), (lower_ref, lower_edge_ref)):
        edge[pl.ds(0, 2)] = inside[pl.ds(1, 2)]
        edge[pl.ds(2, 2)] = inside[pl.ds(pairs - 3, 2)]
    for run in runs(2, pairs - 2, lat):
        two = second_conv(lambda pair: upper_ref[pair], lambda pair: lower_ref[pair], run, taps_two_ref, lat)
        two_ref[pl.ds((run[0] - 2) * lat, len(run) * lat), :] = two
    tokens_ref[...] = embed_patches(two_ref, embed_ref)


def outer_kernel(count_ch, count_sub, field_ref, *refs):
    count = count_ch * count_sub
    sides, refs = refs[:count], refs[count:]
    upper_edge_ref, lower_edge_ref, taps_one_ref, taps_two_ref, embed_ref, inner_ref, tokens_ref, two_ref, sides_ref = refs
    pairs, lat, wide = field_ref.shape
    for away, block in enumerate(sides):
        sides_ref[:, place(away, count_ch, count_sub, lat // count), :] = block[...]

    def field_at(pair):
        if pair < 0:
            return sides_ref[0]
        if pair >= pairs:
            return sides_ref[1]
        return field_ref[pair]

    outermost = [-1, 0, pairs - 1, pairs]
    next_inside = [1, 2, pairs - 3, pairs - 2]
    upper, lower = first_conv(field_at, outermost, taps_one_ref, lat)

    def hidden_at(found, edge_ref):
        def at(pair):
            if pair in outermost:
                return found[outermost.index(pair)]
            return edge_ref[next_inside.index(pair)]

        return at

    two_ref[...] = second_conv(
        hidden_at(upper, upper_edge_ref), hidden_at(lower, lower_edge_ref), [0, 1, pairs - 2, pairs - 1], taps_two_ref, lat
    )
    outer = embed_patches(two_ref, embed_ref)
    inner = inner_ref.shape[1]
    tokens_ref[:, :lat] = outer[:, :lat]
    tokens_ref[:, pl.ds(lat, inner)] = inner_ref[...]
    tokens_ref[:, pl.ds(lat + inner, lat)] = outer[:, lat:]


def call(kernel, out_shape, inputs, scratch=(), flops=0, moved=0):
    return pl.pallas_call(
        kernel,
        out_shape=out_shape,
        in_specs=[pl.BlockSpec(memory_space=pltpu.VMEM)] * len(inputs),
        out_specs=jax.tree.map(lambda unused: pl.BlockSpec(memory_space=pltpu.VMEM), out_shape),
        scratch_shapes=list(scratch),
        compiler_params=pltpu.CompilerParams(vmem_limit_bytes=VMEM_BYTES),
        cost_estimate=pl.CostEstimate(flops=flops, bytes_accessed=moved, transcendentals=0),
    )(*inputs)


def turned(value, axis, away):
    count = lax.axis_size(axis)
    return lax.ppermute(value, axis, [(i, (i + away) % count) for i in range(count)])


def band_blocks(block):
    rows = [block] + [turned(block, "ch", away) for away in range(1, lax.axis_size("ch"))]
    blocks = []
    for row in rows:
        blocks.append(row)
        blocks.extend(turned(row, "sub", away) for away in range(1, lax.axis_size("sub")))
    return blocks


def direct_blocks(block):
    sizes = lax.axis_size("ch"), lax.axis_size("sub")
    devices = [(at_ch, at_sub) for at_ch in range(sizes[0]) for at_sub in range(sizes[1])]
    blocks = [block]
    for away in devices[1:]:
        targets = [tuple((at + step) % size for at, step, size in zip(device, away, sizes)) for device in devices]
        route = [(number, devices.index(target)) for number, target in enumerate(targets)]
        blocks.append(lax.ppermute(block, ("ch", "sub"), route))
    return blocks


def encode(weather, conv_first, conv_second, patch_embed):
    chans, lon, lat = weather.shape
    pairs, wide = lon // 2, 2 * chans
    embed = patch_embed.shape[1]
    shape = functools.partial(jax.ShapeDtypeStruct, dtype=jnp.bfloat16)
    edge = shape((1, lat, wide))
    packed, low, high = call(
        pack_kernel,
        (shape((pairs, lat, wide)), edge, edge),
        (jnp.transpose(weather, (1, 2, 0)),),
        moved=weather.size * 10,
        flops=PACK_COST,
    )
    before = turned(high, "tok", 1)
    after = turned(low, "tok", -1)
    blocks = band_blocks(packed)
    taps = shape((4 * chans, 12 * chans))
    weights = call(
        weights_kernel,
        (taps, taps, shape((embed, 4 * chans))),
        (conv_first, conv_second, patch_embed),
        scratch=[pltpu.VMEM((patch_embed.shape[0], LANES), jnp.float32)],
        moved=conv_first.size * 20,
    )
    sides = direct_blocks(jnp.concatenate([before, after], axis=0))
    counts = lax.axis_size("ch"), lax.axis_size("sub")
    lat = len(blocks) * lat
    field = call(
        functools.partial(join_kernel, *counts),
        shape((pairs, lat, wide)),
        blocks,
        moved=packed.size * 4 * len(blocks),
    )
    work = 2 * lat * 4 * chans * 6 * chans * 5
    held = shape((4, lat, wide))
    hidden = pltpu.VMEM((pairs, lat, wide), jnp.bfloat16)
    inner, upper_edge, lower_edge = call(
        inner_kernel,
        (shape((embed, (pairs - 4) * lat // 2)), held, held),
        (field, *weights),
        scratch=[hidden, hidden, pltpu.VMEM(((pairs - 4) * lat, wide), jnp.float32)],
        flops=work * (pairs - 3),
        moved=field.size * 2,
    )
    return call(
        functools.partial(outer_kernel, *counts),
        shape((embed, pairs * lat // 2)),
        (field, *sides, upper_edge, lower_edge, *weights, inner),
        scratch=[pltpu.VMEM((4 * lat, wide), jnp.float32), pltpu.VMEM((2, lat, wide), jnp.bfloat16)],
        flops=work * 4,
        moved=field.size * 2,
    )


def sent_kernel(first, block, tokens_ref, mixing_ref, sent_ref):
    rows, width = sent_ref.shape
    step = STEP if width % STEP == 0 else width
    tokens = tokens_ref[pl.ds(block * rows, rows), :]
    for at in range(0, width, step):
        product = dot(tokens, mixing_ref[:, pl.ds(first + at, step)])
        sent_ref[:, pl.ds(at, step)] = product.astype(sent_ref.dtype)


def hop_kernel(first, blocks, arrived_ref, tokens_ref, mixing_ref, sent_ref, kept_ref):
    rows, width = sent_ref.shape
    step = STEP if width % STEP == 0 else width
    tokens = jnp.concatenate([tokens_ref[pl.ds(block * rows, rows), :] for block in blocks], axis=0)
    for at in range(0, width, step):
        product = dot(tokens, mixing_ref[:, pl.ds(first + at, step)])
        arrived = arrived_ref[:, pl.ds(at, step)].astype(jnp.float32)
        sent_ref[:, pl.ds(at, step)] = (arrived + product[:rows]).astype(sent_ref.dtype)
        kept_ref[:, pl.ds(at, step)] = product[rows:]


def last_kernel(first, arrived_ref, kept_ref, *refs):
    result_ref, held_ref, written = refs[-3:]
    rows, width = arrived_ref.shape
    part = width // written.shape[0]
    copies = []
    for at in range(written.shape[0]):
        here = pl.ds(at * part, part)
        own = kept_ref[kept_ref.shape[0] - rows :, at * part : (at + 1) * part]
        held_ref[:, here] = gelu(arrived_ref[:, here].astype(jnp.float32) + own).astype(held_ref.dtype)
        target = result_ref.at[:, pl.ds(first + at * part, part)]
        copies.append(pltpu.make_async_copy(held_ref.at[:, here], target, written.at[at]))
        copies[-1].start()
    for copy in copies:
        copy.wait()


def finish(first, arrived, kept, result, columns):
    rows, width = arrived.shape
    near, far = pl.BlockSpec(memory_space=pltpu.VMEM), pl.BlockSpec(memory_space=pl.ANY)
    earlier = [] if result is None else [result]
    return pl.pallas_call(
        functools.partial(last_kernel, first),
        out_shape=jax.ShapeDtypeStruct((rows, columns), jnp.bfloat16),
        in_specs=[near, near] + [far] * len(earlier),
        out_specs=far,
        input_output_aliases={2: 0} if earlier else {},
        scratch_shapes=[
            pltpu.VMEM((rows, width), jnp.bfloat16),
            pltpu.SemaphoreType.DMA((WRITES if width % (WRITES * LANES) == 0 else 1,)),
        ],
        compiler_params=pltpu.CompilerParams(vmem_limit_bytes=VMEM_BYTES),
        cost_estimate=pl.CostEstimate(flops=0, bytes_accessed=0, transcendentals=0),
    )(arrived, kept, *earlier)


def lift(tokens, token_mixing, pieces):
    count = lax.axis_size("tok")
    embed = tokens.shape[0]
    rows = embed // count
    width = token_mixing.shape[1] // pieces
    sent = jax.ShapeDtypeStruct((rows, width), jnp.bfloat16)
    ways = [-1] * pieces
    blocks = [list(range(count - 2, -1, -1)) if way == 1 else list(range(count - 1)) for way in ways]
    travelling = [
        call(functools.partial(sent_kernel, piece * width, blocks[piece][0]), sent, (tokens, token_mixing))
        for piece in range(pieces)
    ]
    kept = [None] * pieces
    result = None
    for step in range(1, count):
        for piece in range(pieces):
            arrived = turned(travelling[piece], "tok", ways[piece])
            if step == 1:
                travelling[piece], kept[piece] = call(
                    functools.partial(hop_kernel, piece * width, blocks[piece][1:] + [count - 1]),
                    [sent, jax.ShapeDtypeStruct((embed - 2 * rows, width), jnp.float32)],
                    (arrived, tokens, token_mixing),
                )
            elif step < count - 1:
                at = (step - 2) * rows
                summed = arrived.astype(jnp.float32) + kept[piece][at : at + rows]
                travelling[piece] = summed.astype(jnp.bfloat16)
            else:
                result = finish(piece * width, arrived, kept[piece], result, pieces * width)
    return result


def local(weather, conv_first, conv_second, patch_embed, token_mixing):
    tokens = encode(weather, conv_first, conv_second, patch_embed)
    return lift(tokens, token_mixing, PIECES)


def solution(mesh):
    placed = (P("groups", "tok", ("ch", "sub")), P(), P(), P(), P("tok", ("ch", "sub")))
    return jax.shard_map(
        local,
        mesh=mesh,
        in_specs=placed,
        out_specs=P(("groups", "tok"), ("ch", "sub")),
        check_vma=False,
    )
```

```python
import functools

import jax
import jax.numpy as jnp
from jax import lax
from jax.experimental import pallas as pl
from jax.experimental.pallas import tpu as pltpu
from jax.sharding import PartitionSpec as P

PIECES = 4
STEP = 256
LANES = 128
PACK_COST = 20 * 10**9
WRITES = 4
VMEM_BYTES = 24 * 1024 * 1024
ROWS_AT_ONCE = 640


def pack_kernel(field_ref, packed_ref, low_ref, high_ref):
    lon, lat, chans = field_ref.shape
    pairs = field_ref[...].reshape(lon // 2, 2, lat, chans)
    joined = jnp.concatenate([pairs[:, 0], pairs[:, 1]], axis=-1).astype(packed_ref.dtype)
    packed_ref[...] = joined
    low_ref[...] = joined[:1]
    high_ref[...] = joined[-1:]


def place(away, count_ch, count_sub, width):
    away_ch, away_sub = away // count_sub, away % count_sub
    at_ch = lax.rem(lax.axis_index("ch") + count_ch - away_ch, count_ch)
    at_sub = lax.rem(lax.axis_index("sub") + count_sub - away_sub, count_sub)
    return pl.ds(pl.multiple_of((at_ch * count_sub + at_sub) * width, width), width)


def join_kernel(count_ch, count_sub, *refs):
    blocks, field_ref = refs[:-1], refs[-1]
    width = field_ref.shape[1] // len(blocks)
    for away, block in enumerate(blocks):
        field_ref[:, place(away, count_ch, count_sub, width), :] = block[...]


def split_two(value):
    upper = value.astype(jnp.bfloat16)
    return upper, (value - upper.astype(jnp.float32)).astype(jnp.bfloat16)


def spread_taps(kernel_ref):
    chans = kernel_ref.shape[1]
    nothing = jnp.zeros((chans, kernel_ref.shape[2]), jnp.float32)
    rows = []
    for tap in range(3):
        taps = [kernel_ref[3 * turn + tap] for turn in range(3)]
        rows.append(jnp.concatenate([taps[1], taps[2], nothing, taps[0]], axis=-1))
        rows.append(jnp.concatenate([taps[0], taps[1], taps[2], nothing], axis=-1))
    return jnp.concatenate(rows, axis=0).T


def weights_kernel(first_ref, second_ref, embed_ref, taps_one_ref, taps_two_ref, embed_out_ref, scratch):
    for source, target in ((first_ref, taps_one_ref), (second_ref, taps_two_ref)):
        upper, lower = split_two(spread_taps(source))
        target[...] = jnp.concatenate([upper, lower], axis=1)
    chans = embed_ref.shape[0] // 4
    embed = embed_ref.shape[1]
    count = lax.axis_size("tok")
    turn = lax.rem(lax.axis_index("tok") + 1, count) * (embed // count)
    turned_embed = pltpu.roll(embed_ref[...].astype(jnp.float32), lax.rem(embed - turn, embed), axis=1)
    for first in range(0, embed, LANES):
        scratch[...] = turned_embed[:, first : first + LANES]
        ordered = [scratch[pl.ds(2 * a + b, chans, stride=4), :] for b in range(2) for a in range(2)]
        rows = jnp.concatenate(ordered, axis=0).T
        embed_out_ref[pl.ds(first, LANES), :] = rows.astype(embed_out_ref.dtype)


def window(pair_at, pairs):
    rows = []
    for pair in pairs:
        here = pair_at(pair)
        lane = lax.broadcasted_iota(jnp.int32, here.shape, 1)
        beside = jnp.where(lane < here.shape[1] // 2, pair_at(pair + 1), pair_at(pair - 1))
        rows.append(jnp.concatenate([here, beside], axis=-1))
    return jnp.concatenate(rows, axis=0)


def add_lat_taps(products, lat):
    wide = products.shape[1] // 3
    count = products.shape[0]
    row = lax.broadcasted_iota(jnp.int32, (1, lat, wide), 1)
    below = pltpu.roll(products[:, :wide], 1, axis=0).reshape(-1, lat, wide)
    above = pltpu.roll(products[:, 2 * wide :], count - 1, axis=0).reshape(-1, lat, wide)
    here = products[:, wide : 2 * wide].reshape(-1, lat, wide)
    return here + jnp.where(row == 0, 0.0, below) + jnp.where(row == lat - 1, 0.0, above)


def gelu(value):
    return 0.5 * value * (1.0 + lax.erf(value * (0.5**0.5)))


def dot(left, right):
    return jnp.dot(left, right, preferred_element_type=jnp.float32)


def dot_both(rows, taps_ref):
    both = dot(rows, taps_ref[...])
    half = both.shape[1] // 2
    return both[:, :half] + both[:, half:]


def first_conv(field_at, pairs, taps_ref, lat):
    products = dot_both(window(field_at, pairs), taps_ref)
    return split_two(gelu(add_lat_taps(products, lat)))


def second_conv(upper_at, lower_at, pairs, taps_ref, lat):
    upper, lower = window(upper_at, pairs), window(lower_at, pairs)
    products = dot_both(upper, taps_ref) + dot(lower, taps_ref[:, : taps_ref.shape[1] // 2])
    rounded = add_lat_taps(products, lat).astype(jnp.bfloat16).astype(jnp.float32)
    return rounded.reshape(-1, rounded.shape[2])


def embed_patches(two_ref, embed_ref):
    half = two_ref.shape[0] // 2
    patches = jnp.concatenate(
        [two_ref[pl.ds(b, half, stride=2), :].astype(jnp.bfloat16) for b in range(2)], axis=-1
    )
    return lax.dot_general(
        embed_ref[...], patches, (((1,), (1,)), ((), ())), preferred_element_type=jnp.float32
    ).astype(jnp.bfloat16)


def runs(first, last, lat):
    count = -(-(last - first) * lat // max(ROWS_AT_ONCE, lat))
    cuts = [first + (last - first) * at // count for at in range(count + 1)]
    return [list(range(*cut)) for cut in zip(cuts[:-1], cuts[1:])]


def inner_kernel(
    field_ref, taps_one_ref, taps_two_ref, embed_ref, tokens_ref, upper_edge_ref, lower_edge_ref, upper_ref, lower_ref, two_ref
):
    pairs, lat, wide = field_ref.shape
    for run in runs(1, pairs - 1, lat):
        upper, lower = first_conv(lambda pair: field_ref[pair], run, taps_one_ref, lat)
        upper_ref[pl.ds(run[0], len(run))] = upper
        lower_ref[pl.ds(run[0], len(run))] = lower
    for inside, edge in ((upper_ref, upper_edge_ref), (lower_ref, lower_edge_ref)):
        edge[pl.ds(0, 2)] = inside[pl.ds(1, 2)]
        edge[pl.ds(2, 2)] = inside[pl.ds(pairs - 3, 2)]
    for run in runs(2, pairs - 2, lat):
        two = second_conv(lambda pair: upper_ref[pair], lambda pair: lower_ref[pair], run, taps_two_ref, lat)
        two_ref[pl.ds((run[0] - 2) * lat, len(run) * lat), :] = two
    tokens_ref[...] = embed_patches(two_ref, embed_ref)


def outer_kernel(count_ch, count_sub, field_ref, *refs):
    count = count_ch * count_sub
    sides, refs = refs[:count], refs[count:]
    upper_edge_ref, lower_edge_ref, taps_one_ref, taps_two_ref, embed_ref, inner_ref, tokens_ref, two_ref, sides_ref = refs
    pairs, lat, wide = field_ref.shape
    for away, block in enumerate(sides):
        sides_ref[:, place(away, count_ch, count_sub, lat // count), :] = block[...]

    def field_at(pair):
        if pair < 0:
            return sides_ref[0]
        if pair >= pairs:
            return sides_ref[1]
        return field_ref[pair]

    outermost = [[-1, 0], [pairs - 1, pairs]]
    next_inside = [1, 2, pairs - 3, pairs - 2]
    found = [first_conv(field_at, side, taps_one_ref, lat) for side in outermost]

    def hidden_at(side, part, edge_ref):
        def at(pair):
            if pair in outermost[side]:
                return found[side][part][outermost[side].index(pair)]
            return edge_ref[next_inside.index(pair)]

        return at

    for side, ends in enumerate(([0, 1], [pairs - 2, pairs - 1])):
        upper_at, lower_at = hidden_at(side, 0, upper_edge_ref), hidden_at(side, 1, lower_edge_ref)
        two = second_conv(upper_at, lower_at, ends, taps_two_ref, lat)
        two_ref[pl.ds(side * 2 * lat, 2 * lat), :] = two
    outer = embed_patches(two_ref, embed_ref)
    inner = inner_ref.shape[1]
    tokens_ref[:, :lat] = outer[:, :lat]
    tokens_ref[:, pl.ds(lat, inner)] = inner_ref[...]
    tokens_ref[:, pl.ds(lat + inner, lat)] = outer[:, lat:]


def call(kernel, out_shape, inputs, scratch=(), flops=0, moved=0):
    return pl.pallas_call(
        kernel,
        out_shape=out_shape,
        in_specs=[pl.BlockSpec(memory_space=pltpu.VMEM)] * len(inputs),
        out_specs=jax.tree.map(lambda unused: pl.BlockSpec(memory_space=pltpu.VMEM), out_shape),
        scratch_shapes=list(scratch),
        compiler_params=pltpu.CompilerParams(vmem_limit_bytes=VMEM_BYTES),
        cost_estimate=pl.CostEstimate(flops=flops, bytes_accessed=moved, transcendentals=0),
    )(*inputs)


def turned(value, axis, away):
    count = lax.axis_size(axis)
    return lax.ppermute(value, axis, [(i, (i + away) % count) for i in range(count)])


def band_blocks(block):
    rows = [block] + [turned(block, "ch", away) for away in range(1, lax.axis_size("ch"))]
    blocks = []
    for row in rows:
        blocks.append(row)
        blocks.extend(turned(row, "sub", away) for away in range(1, lax.axis_size("sub")))
    return blocks


def direct_blocks(block):
    sizes = lax.axis_size("ch"), lax.axis_size("sub")
    devices = [(at_ch, at_sub) for at_ch in range(sizes[0]) for at_sub in range(sizes[1])]
    blocks = [block]
    for away in devices[1:]:
        targets = [tuple((at + step) % size for at, step, size in zip(device, away, sizes)) for device in devices]
        route = [(number, devices.index(target)) for number, target in enumerate(targets)]
        blocks.append(lax.ppermute(block, ("ch", "sub"), route))
    return blocks


def encode(weather, conv_first, conv_second, patch_embed):
    chans, lon, lat = weather.shape
    pairs, wide = lon // 2, 2 * chans
    embed = patch_embed.shape[1]
    shape = functools.partial(jax.ShapeDtypeStruct, dtype=jnp.bfloat16)
    edge = shape((1, lat, wide))
    packed, low, high = call(
        pack_kernel,
        (shape((pairs, lat, wide)), edge, edge),
        (jnp.transpose(weather, (1, 2, 0)),),
        moved=weather.size * 10,
        flops=PACK_COST,
    )
    before = turned(high, "tok", 1)
    after = turned(low, "tok", -1)
    blocks = band_blocks(packed)
    taps = shape((4 * chans, 12 * chans))
    weights = call(
        weights_kernel,
        (taps, taps, shape((embed, 4 * chans))),
        (conv_first, conv_second, patch_embed),
        scratch=[pltpu.VMEM((patch_embed.shape[0], LANES), jnp.float32)],
        moved=conv_first.size * 20,
    )
    sides = direct_blocks(jnp.concatenate([before, after], axis=0))
    counts = lax.axis_size("ch"), lax.axis_size("sub")
    lat = len(blocks) * lat
    field = call(
        functools.partial(join_kernel, *counts),
        shape((pairs, lat, wide)),
        blocks,
        moved=packed.size * 4 * len(blocks),
    )
    work = 2 * lat * 4 * chans * 6 * chans * 5
    held = shape((4, lat, wide))
    hidden = pltpu.VMEM((pairs, lat, wide), jnp.bfloat16)
    inner, upper_edge, lower_edge = call(
        inner_kernel,
        (shape((embed, (pairs - 4) * lat // 2)), held, held),
        (field, *weights),
        scratch=[hidden, hidden, pltpu.VMEM(((pairs - 4) * lat, wide), jnp.float32)],
        flops=work * (pairs - 3),
        moved=field.size * 2,
    )
    return call(
        functools.partial(outer_kernel, *counts),
        shape((embed, pairs * lat // 2)),
        (field, *sides, upper_edge, lower_edge, *weights, inner),
        scratch=[pltpu.VMEM((4 * lat, wide), jnp.float32), pltpu.VMEM((2, lat, wide), jnp.bfloat16)],
        flops=work * 4,
        moved=field.size * 2,
    )


def sent_kernel(first, block, tokens_ref, mixing_ref, sent_ref):
    rows, width = sent_ref.shape
    step = STEP if width % STEP == 0 else width
    tokens = tokens_ref[pl.ds(block * rows, rows), :]
    for at in range(0, width, step):
        product = dot(tokens, mixing_ref[:, pl.ds(first + at, step)])
        sent_ref[:, pl.ds(at, step)] = product.astype(sent_ref.dtype)


def hop_kernel(first, blocks, arrived_ref, tokens_ref, mixing_ref, sent_ref, kept_ref):
    rows, width = sent_ref.shape
    step = STEP if width % STEP == 0 else width
    tokens = jnp.concatenate([tokens_ref[pl.ds(block * rows, rows), :] for block in blocks], axis=0)
    for at in range(0, width, step):
        product = dot(tokens, mixing_ref[:, pl.ds(first + at, step)])
        arrived = arrived_ref[:, pl.ds(at, step)].astype(jnp.float32)
        sent_ref[:, pl.ds(at, step)] = (arrived + product[:rows]).astype(sent_ref.dtype)
        kept_ref[:, pl.ds(at, step)] = product[rows:]


def last_kernel(first, arrived_ref, kept_ref, *refs):
    result_ref, held_ref, written = refs[-3:]
    rows, width = arrived_ref.shape
    part = width // written.shape[0]
    copies = []
    for at in range(written.shape[0]):
        here = pl.ds(at * part, part)
        own = kept_ref[kept_ref.shape[0] - rows :, at * part : (at + 1) * part]
        held_ref[:, here] = gelu(arrived_ref[:, here].astype(jnp.float32) + own).astype(held_ref.dtype)
        target = result_ref.at[:, pl.ds(first + at * part, part)]
        copies.append(pltpu.make_async_copy(held_ref.at[:, here], target, written.at[at]))
        copies[-1].start()
    for copy in copies:
        copy.wait()


def finish(first, arrived, kept, result, columns):
    rows, width = arrived.shape
    near, far = pl.BlockSpec(memory_space=pltpu.VMEM), pl.BlockSpec(memory_space=pl.ANY)
    earlier = [] if result is None else [result]
    return pl.pallas_call(
        functools.partial(last_kernel, first),
        out_shape=jax.ShapeDtypeStruct((rows, columns), jnp.bfloat16),
        in_specs=[near, near] + [far] * len(earlier),
        out_specs=far,
        input_output_aliases={2: 0} if earlier else {},
        scratch_shapes=[
            pltpu.VMEM((rows, width), jnp.bfloat16),
            pltpu.SemaphoreType.DMA((WRITES if width % (WRITES * LANES) == 0 else 1,)),
        ],
        compiler_params=pltpu.CompilerParams(vmem_limit_bytes=VMEM_BYTES),
        cost_estimate=pl.CostEstimate(flops=0, bytes_accessed=0, transcendentals=0),
    )(arrived, kept, *earlier)


def lift(tokens, token_mixing, pieces):
    count = lax.axis_size("tok")
    embed = tokens.shape[0]
    rows = embed // count
    width = token_mixing.shape[1] // pieces
    sent = jax.ShapeDtypeStruct((rows, width), jnp.bfloat16)
    ways = [-1] * pieces
    blocks = [list(range(count - 2, -1, -1)) if way == 1 else list(range(count - 1)) for way in ways]
    travelling = [
        call(functools.partial(sent_kernel, piece * width, blocks[piece][0]), sent, (tokens, token_mixing))
        for piece in range(pieces)
    ]
    kept = [None] * pieces
    result = None
    for step in range(1, count):
        for piece in range(pieces):
            arrived = turned(travelling[piece], "tok", ways[piece])
            if step == 1:
                travelling[piece], kept[piece] = call(
                    functools.partial(hop_kernel, piece * width, blocks[piece][1:] + [count - 1]),
                    [sent, jax.ShapeDtypeStruct((embed - 2 * rows, width), jnp.float32)],
                    (arrived, tokens, token_mixing),
                )
            elif step < count - 1:
                at = (step - 2) * rows
                summed = arrived.astype(jnp.float32) + kept[piece][at : at + rows]
                travelling[piece] = summed.astype(jnp.bfloat16)
            else:
                result = finish(piece * width, arrived, kept[piece], result, pieces * width)
    return result


def local(weather, conv_first, conv_second, patch_embed, token_mixing):
    tokens = encode(weather, conv_first, conv_second, patch_embed)
    return lift(tokens, token_mixing, PIECES)


def solution(mesh):
    placed = (P("groups", "tok", ("ch", "sub")), P(), P(), P(), P("tok", ("ch", "sub")))
    return jax.shard_map(
        local,
        mesh=mesh,
        in_specs=placed,
        out_specs=P(("groups", "tok"), ("ch", "sub")),
        check_vma=False,
    )
```

```python
import functools

import jax
import jax.numpy as jnp
from jax import lax
from jax.experimental import pallas as pl
from jax.experimental.pallas import tpu as pltpu
from jax.sharding import PartitionSpec as P

PIECES = 4
STEP = 256
LANES = 128
PACK_COST = 20 * 10**9
WRITES = 4
VMEM_BYTES = 24 * 1024 * 1024
ROWS_AT_ONCE = 640


def pack_kernel(field_ref, packed_ref, low_ref, high_ref):
    lon, lat, chans = field_ref.shape
    pairs = field_ref[...].reshape(lon // 2, 2, lat, chans)
    joined = jnp.concatenate([pairs[:, 0], pairs[:, 1]], axis=-1).astype(packed_ref.dtype)
    packed_ref[...] = joined
    low_ref[...] = joined[:1]
    high_ref[...] = joined[-1:]


def place(away, count_ch, count_sub, width):
    away_ch, away_sub = away // count_sub, away % count_sub
    at_ch = lax.rem(lax.axis_index("ch") + count_ch - away_ch, count_ch)
    at_sub = lax.rem(lax.axis_index("sub") + count_sub - away_sub, count_sub)
    return pl.ds(pl.multiple_of((at_ch * count_sub + at_sub) * width, width), width)


def join_kernel(count_ch, count_sub, *refs):
    blocks, field_ref = refs[:-1], refs[-1]
    width = field_ref.shape[1] // len(blocks)
    for away, block in enumerate(blocks):
        field_ref[:, place(away, count_ch, count_sub, width), :] = block[...]


def split_two(value):
    upper = value.astype(jnp.bfloat16)
    return upper, (value - upper.astype(jnp.float32)).astype(jnp.bfloat16)


def spread_taps(kernel_ref):
    chans = kernel_ref.shape[1]
    nothing = jnp.zeros((chans, kernel_ref.shape[2]), jnp.float32)
    rows = []
    for tap in range(3):
        taps = [kernel_ref[3 * turn + tap] for turn in range(3)]
        rows.append(jnp.concatenate([taps[1], taps[2], nothing, taps[0]], axis=-1))
        rows.append(jnp.concatenate([taps[0], taps[1], taps[2], nothing], axis=-1))
    return jnp.concatenate(rows, axis=0).T


def weights_kernel(first_ref, second_ref, embed_ref, taps_one_ref, taps_two_ref, embed_out_ref, scratch):
    for source, target in ((first_ref, taps_one_ref), (second_ref, taps_two_ref)):
        upper, lower = split_two(spread_taps(source))
        target[...] = jnp.concatenate([upper, lower], axis=1)
    chans = embed_ref.shape[0] // 4
    embed = embed_ref.shape[1]
    count = lax.axis_size("tok")
    turn = lax.rem(lax.axis_index("tok") + 1, count) * (embed // count)
    turned_embed = pltpu.roll(embed_ref[...].astype(jnp.float32), lax.rem(embed - turn, embed), axis=1)
    for first in range(0, embed, LANES):
        scratch[...] = turned_embed[:, first : first + LANES]
        ordered = [scratch[pl.ds(2 * a + b, chans, stride=4), :] for b in range(2) for a in range(2)]
        rows = jnp.concatenate(ordered, axis=0).T
        embed_out_ref[pl.ds(first, LANES), :] = rows.astype(embed_out_ref.dtype)


def window(pair_at, pairs):
    rows = []
    for pair in pairs:
        here = pair_at(pair)
        lane = lax.broadcasted_iota(jnp.int32, here.shape, 1)
        beside = jnp.where(lane < here.shape[1] // 2, pair_at(pair + 1), pair_at(pair - 1))
        rows.append(jnp.concatenate([here, beside], axis=-1))
    return jnp.concatenate(rows, axis=0)


def add_lat_taps(products, lat):
    wide = products.shape[1] // 3
    count = products.shape[0]
    row = lax.broadcasted_iota(jnp.int32, (1, lat, wide), 1)
    below = pltpu.roll(products[:, :wide], 1, axis=0).reshape(-1, lat, wide)
    above = pltpu.roll(products[:, 2 * wide :], count - 1, axis=0).reshape(-1, lat, wide)
    here = products[:, wide : 2 * wide].reshape(-1, lat, wide)
    return here + jnp.where(row == 0, 0.0, below) + jnp.where(row == lat - 1, 0.0, above)


def gelu(value):
    return 0.5 * value * (1.0 + lax.erf(value * (0.5**0.5)))


def dot(left, right):
    return jnp.dot(left, right, preferred_element_type=jnp.float32)


def dot_both(rows, taps_ref):
    both = dot(rows, taps_ref[...])
    half = both.shape[1] // 2
    return both[:, :half] + both[:, half:]


def first_conv(field_at, pairs, taps_ref, lat):
    products = dot_both(window(field_at, pairs), taps_ref)
    return split_two(gelu(add_lat_taps(products, lat)))


def second_conv(upper_at, lower_at, pairs, taps_ref, lat):
    upper, lower = window(upper_at, pairs), window(lower_at, pairs)
    products = dot_both(upper, taps_ref) + dot(lower, taps_ref[:, : taps_ref.shape[1] // 2])
    rounded = add_lat_taps(products, lat).astype(jnp.bfloat16).astype(jnp.float32)
    return rounded.reshape(-1, rounded.shape[2])


def embed_patches(two_ref, embed_ref):
    half = two_ref.shape[0] // 2
    patches = jnp.concatenate(
        [two_ref[pl.ds(b, half, stride=2), :].astype(jnp.bfloat16) for b in range(2)], axis=-1
    )
    return lax.dot_general(
        embed_ref[...], patches, (((1,), (1,)), ((), ())), preferred_element_type=jnp.float32
    ).astype(jnp.bfloat16)


def runs(first, last, lat):
    count = -(-(last - first) * lat // max(ROWS_AT_ONCE, lat))
    cuts = [first + (last - first) * at // count for at in range(count + 1)]
    return [list(range(*cut)) for cut in zip(cuts[:-1], cuts[1:])]


def inner_kernel(
    field_ref, taps_one_ref, taps_two_ref, embed_ref, tokens_ref, upper_edge_ref, lower_edge_ref, upper_ref, lower_ref, two_ref
):
    pairs, lat, wide = field_ref.shape
    for run in runs(1, pairs - 1, lat):
        upper, lower = first_conv(lambda pair: field_ref[pair], run, taps_one_ref, lat)
        upper_ref[pl.ds(run[0], len(run))] = upper
        lower_ref[pl.ds(run[0], len(run))] = lower
    for inside, edge in ((upper_ref, upper_edge_ref), (lower_ref, lower_edge_ref)):
        edge[pl.ds(0, 2)] = inside[pl.ds(1, 2)]
        edge[pl.ds(2, 2)] = inside[pl.ds(pairs - 3, 2)]
    for run in runs(2, pairs - 2, lat):
        two = second_conv(lambda pair: upper_ref[pair], lambda pair: lower_ref[pair], run, taps_two_ref, lat)
        two_ref[pl.ds((run[0] - 2) * lat, len(run) * lat), :] = two
    tokens_ref[...] = embed_patches(two_ref, embed_ref)


def outer_kernel(count_ch, count_sub, field_ref, *refs):
    count = count_ch * count_sub
    sides, refs = refs[:count], refs[count:]
    upper_edge_ref, lower_edge_ref, taps_one_ref, taps_two_ref, embed_ref, inner_ref, mixing_ref = refs[:7]
    tokens_ref, sent_ref, two_ref, sides_ref, product_ref = refs[7:]
    pairs, lat, wide = field_ref.shape
    for away, block in enumerate(sides):
        sides_ref[:, place(away, count_ch, count_sub, lat // count), :] = block[...]

    def field_at(pair):
        if pair < 0:
            return sides_ref[0]
        if pair >= pairs:
            return sides_ref[1]
        return field_ref[pair]

    outermost = [[-1, 0], [pairs - 1, pairs]]
    next_inside = [1, 2, pairs - 3, pairs - 2]
    found = [first_conv(field_at, side, taps_one_ref, lat) for side in outermost]
    inner = inner_ref.shape[1]
    rows, width = sent_ref.shape
    step = STEP if width % STEP == 0 else width
    for at in range(0, width, step):
        product_ref[:, pl.ds(at, step)] = dot(inner_ref[:rows], mixing_ref[pl.ds(lat, inner), pl.ds(at, step)])

    def hidden_at(side, part, edge_ref):
        def at(pair):
            if pair in outermost[side]:
                return found[side][part][outermost[side].index(pair)]
            return edge_ref[next_inside.index(pair)]

        return at

    for side, ends in enumerate(([0, 1], [pairs - 2, pairs - 1])):
        upper_at, lower_at = hidden_at(side, 0, upper_edge_ref), hidden_at(side, 1, lower_edge_ref)
        two = second_conv(upper_at, lower_at, ends, taps_two_ref, lat)
        two_ref[pl.ds(side * 2 * lat, 2 * lat), :] = two
    outer = embed_patches(two_ref, embed_ref)
    for at in range(0, width, step):
        here = pl.ds(at, step)
        product = dot(outer[:rows, :lat], mixing_ref[pl.ds(0, lat), here])
        product = product + dot(outer[:rows, lat:], mixing_ref[pl.ds(lat + inner, lat), here])
        sent_ref[:, here] = (product_ref[:, here] + product).astype(sent_ref.dtype)
    tokens_ref[:, :lat] = outer[:, :lat]
    tokens_ref[:, pl.ds(lat, inner)] = inner_ref[...]
    tokens_ref[:, pl.ds(lat + inner, lat)] = outer[:, lat:]


def call(kernel, out_shape, inputs, scratch=(), flops=0, moved=0):
    return pl.pallas_call(
        kernel,
        out_shape=out_shape,
        in_specs=[pl.BlockSpec(memory_space=pltpu.VMEM)] * len(inputs),
        out_specs=jax.tree.map(lambda unused: pl.BlockSpec(memory_space=pltpu.VMEM), out_shape),
        scratch_shapes=list(scratch),
        compiler_params=pltpu.CompilerParams(vmem_limit_bytes=VMEM_BYTES),
        cost_estimate=pl.CostEstimate(flops=flops, bytes_accessed=moved, transcendentals=0),
    )(*inputs)


def turned(value, axis, away):
    count = lax.axis_size(axis)
    return lax.ppermute(value, axis, [(i, (i + away) % count) for i in range(count)])


def band_blocks(block):
    rows = [block] + [turned(block, "ch", away) for away in range(1, lax.axis_size("ch"))]
    blocks = []
    for row in rows:
        blocks.append(row)
        blocks.extend(turned(row, "sub", away) for away in range(1, lax.axis_size("sub")))
    return blocks


def direct_blocks(block):
    sizes = lax.axis_size("ch"), lax.axis_size("sub")
    devices = [(at_ch, at_sub) for at_ch in range(sizes[0]) for at_sub in range(sizes[1])]
    blocks = [block]
    for away in devices[1:]:
        targets = [tuple((at + step) % size for at, step, size in zip(device, away, sizes)) for device in devices]
        route = [(number, devices.index(target)) for number, target in enumerate(targets)]
        blocks.append(lax.ppermute(block, ("ch", "sub"), route))
    return blocks


def encode(weather, conv_first, conv_second, patch_embed, token_mixing):
    chans, lon, lat = weather.shape
    pairs, wide = lon // 2, 2 * chans
    embed = patch_embed.shape[1]
    shape = functools.partial(jax.ShapeDtypeStruct, dtype=jnp.bfloat16)
    edge = shape((1, lat, wide))
    packed, low, high = call(
        pack_kernel,
        (shape((pairs, lat, wide)), edge, edge),
        (jnp.transpose(weather, (1, 2, 0)),),
        moved=weather.size * 10,
        flops=PACK_COST,
    )
    before = turned(high, "tok", 1)
    after = turned(low, "tok", -1)
    blocks = band_blocks(packed)
    taps = shape((4 * chans, 12 * chans))
    weights = call(
        weights_kernel,
        (taps, taps, shape((embed, 4 * chans))),
        (conv_first, conv_second, patch_embed),
        scratch=[pltpu.VMEM((patch_embed.shape[0], LANES), jnp.float32)],
        moved=conv_first.size * 20,
    )
    sides = direct_blocks(jnp.concatenate([before, after], axis=0))
    counts = lax.axis_size("ch"), lax.axis_size("sub")
    lat = len(blocks) * lat
    field = call(
        functools.partial(join_kernel, *counts),
        shape((pairs, lat, wide)),
        blocks,
        moved=packed.size * 4 * len(blocks),
    )
    work = 2 * lat * 4 * chans * 6 * chans * 5
    held = shape((4, lat, wide))
    hidden = pltpu.VMEM((pairs, lat, wide), jnp.bfloat16)
    inner, upper_edge, lower_edge = call(
        inner_kernel,
        (shape((embed, (pairs - 4) * lat // 2)), held, held),
        (field, *weights),
        scratch=[hidden, hidden, pltpu.VMEM(((pairs - 4) * lat, wide), jnp.float32)],
        flops=work * (pairs - 3),
        moved=field.size * 2,
    )
    sent = (embed // lax.axis_size("tok"), token_mixing.shape[1] // PIECES)
    return call(
        functools.partial(outer_kernel, *counts),
        (shape((embed, pairs * lat // 2)), shape(sent)),
        (field, *sides, upper_edge, lower_edge, *weights, inner, token_mixing),
        scratch=[
            pltpu.VMEM((4 * lat, wide), jnp.float32),
            pltpu.VMEM((2, lat, wide), jnp.bfloat16),
            pltpu.VMEM(sent, jnp.float32),
        ],
        flops=work * 4,
        moved=field.size * 2,
    )


def sent_kernel(first, block, tokens_ref, mixing_ref, sent_ref):
    rows, width = sent_ref.shape
    step = STEP if width % STEP == 0 else width
    tokens = tokens_ref[pl.ds(block * rows, rows), :]
    for at in range(0, width, step):
        product = dot(tokens, mixing_ref[:, pl.ds(first + at, step)])
        sent_ref[:, pl.ds(at, step)] = product.astype(sent_ref.dtype)


def hop_kernel(first, blocks, arrived_ref, tokens_ref, mixing_ref, sent_ref, kept_ref):
    rows, width = sent_ref.shape
    step = STEP if width % STEP == 0 else width
    tokens = jnp.concatenate([tokens_ref[pl.ds(block * rows, rows), :] for block in blocks], axis=0)
    for at in range(0, width, step):
        product = dot(tokens, mixing_ref[:, pl.ds(first + at, step)])
        arrived = arrived_ref[:, pl.ds(at, step)].astype(jnp.float32)
        sent_ref[:, pl.ds(at, step)] = (arrived + product[:rows]).astype(sent_ref.dtype)
        kept_ref[:, pl.ds(at, step)] = product[rows:]


def last_kernel(first, arrived_ref, kept_ref, *refs):
    result_ref, held_ref, written = refs[-3:]
    rows, width = arrived_ref.shape
    part = width // written.shape[0]
    copies = []
    for at in range(written.shape[0]):
        here = pl.ds(at * part, part)
        own = kept_ref[kept_ref.shape[0] - rows :, at * part : (at + 1) * part]
        held_ref[:, here] = gelu(arrived_ref[:, here].astype(jnp.float32) + own).astype(held_ref.dtype)
        target = result_ref.at[:, pl.ds(first + at * part, part)]
        copies.append(pltpu.make_async_copy(held_ref.at[:, here], target, written.at[at]))
        copies[-1].start()
    for copy in copies:
        copy.wait()


def finish(first, arrived, kept, result, columns):
    rows, width = arrived.shape
    near, far = pl.BlockSpec(memory_space=pltpu.VMEM), pl.BlockSpec(memory_space=pl.ANY)
    earlier = [] if result is None else [result]
    return pl.pallas_call(
        functools.partial(last_kernel, first),
        out_shape=jax.ShapeDtypeStruct((rows, columns), jnp.bfloat16),
        in_specs=[near, near] + [far] * len(earlier),
        out_specs=far,
        input_output_aliases={2: 0} if earlier else {},
        scratch_shapes=[
            pltpu.VMEM((rows, width), jnp.bfloat16),
            pltpu.SemaphoreType.DMA((WRITES if width % (WRITES * LANES) == 0 else 1,)),
        ],
        compiler_params=pltpu.CompilerParams(vmem_limit_bytes=VMEM_BYTES),
        cost_estimate=pl.CostEstimate(flops=0, bytes_accessed=0, transcendentals=0),
    )(arrived, kept, *earlier)


def lift(tokens, first_sent, token_mixing, pieces):
    count = lax.axis_size("tok")
    embed = tokens.shape[0]
    rows = embed // count
    width = token_mixing.shape[1] // pieces
    sent = jax.ShapeDtypeStruct((rows, width), jnp.bfloat16)
    ways = [-1] * pieces
    blocks = [list(range(count - 2, -1, -1)) if way == 1 else list(range(count - 1)) for way in ways]
    travelling = [first_sent] + [
        call(functools.partial(sent_kernel, piece * width, blocks[piece][0]), sent, (tokens, token_mixing))
        for piece in range(1, pieces)
    ]
    kept = [None] * pieces
    result = None
    for step in range(1, count):
        for piece in range(pieces):
            arrived = turned(travelling[piece], "tok", ways[piece])
            if step == 1:
                travelling[piece], kept[piece] = call(
                    functools.partial(hop_kernel, piece * width, blocks[piece][1:] + [count - 1]),
                    [sent, jax.ShapeDtypeStruct((embed - 2 * rows, width), jnp.float32)],
                    (arrived, tokens, token_mixing),
                )
            elif step < count - 1:
                at = (step - 2) * rows
                summed = arrived.astype(jnp.float32) + kept[piece][at : at + rows]
                travelling[piece] = summed.astype(jnp.bfloat16)
            else:
                result = finish(piece * width, arrived, kept[piece], result, pieces * width)
    return result


def local(weather, conv_first, conv_second, patch_embed, token_mixing):
    tokens, first_sent = encode(weather, conv_first, conv_second, patch_embed, token_mixing)
    return lift(tokens, first_sent, token_mixing, PIECES)


def solution(mesh):
    placed = (P("groups", "tok", ("ch", "sub")), P(), P(), P(), P("tok", ("ch", "sub")))
    return jax.shard_map(
        local,
        mesh=mesh,
        in_specs=placed,
        out_specs=P(("groups", "tok"), ("ch", "sub")),
        check_vma=False,
    )
```

```python
import functools

import jax
import jax.numpy as jnp
from jax import lax
from jax.experimental import pallas as pl
from jax.experimental.pallas import tpu as pltpu
from jax.sharding import PartitionSpec as P

PIECES = 4
STEP = 256
LANES = 128
PACK_COST = 20 * 10**9
WRITES = 4
VMEM_BYTES = 24 * 1024 * 1024
ROWS_AT_ONCE = 640


def pack_kernel(field_ref, packed_ref, low_ref, high_ref):
    lon, lat, chans = field_ref.shape
    pairs = field_ref[...].reshape(lon // 2, 2, lat, chans)
    joined = jnp.concatenate([pairs[:, 0], pairs[:, 1]], axis=-1).astype(packed_ref.dtype)
    packed_ref[...] = joined
    low_ref[...] = joined[:1]
    high_ref[...] = joined[-1:]


def place(away, count_ch, count_sub, width):
    away_ch, away_sub = away // count_sub, away % count_sub
    at_ch = lax.rem(lax.axis_index("ch") + count_ch - away_ch, count_ch)
    at_sub = lax.rem(lax.axis_index("sub") + count_sub - away_sub, count_sub)
    return pl.ds(pl.multiple_of((at_ch * count_sub + at_sub) * width, width), width)


def join_kernel(count_ch, count_sub, *refs):
    blocks, field_ref = refs[:-1], refs[-1]
    width = field_ref.shape[1] // len(blocks)
    for away, block in enumerate(blocks):
        field_ref[:, place(away, count_ch, count_sub, width), :] = block[...]


def split_two(value):
    upper = value.astype(jnp.bfloat16)
    return upper, (value - upper.astype(jnp.float32)).astype(jnp.bfloat16)


def spread_taps(kernel_ref):
    chans = kernel_ref.shape[1]
    nothing = jnp.zeros((chans, kernel_ref.shape[2]), jnp.float32)
    rows = []
    for tap in range(3):
        taps = [kernel_ref[3 * turn + tap] for turn in range(3)]
        rows.append(jnp.concatenate([taps[1], taps[2], nothing, taps[0]], axis=-1))
        rows.append(jnp.concatenate([taps[0], taps[1], taps[2], nothing], axis=-1))
    return jnp.concatenate(rows, axis=0).T


def weights_kernel(first_ref, second_ref, embed_ref, taps_one_ref, taps_two_ref, embed_out_ref, scratch):
    for source, target in ((first_ref, taps_one_ref), (second_ref, taps_two_ref)):
        upper, lower = split_two(spread_taps(source))
        target[...] = jnp.concatenate([upper, lower], axis=1)
    chans = embed_ref.shape[0] // 4
    embed = embed_ref.shape[1]
    count = lax.axis_size("tok")
    turn = lax.rem(lax.axis_index("tok") + 1, count) * (embed // count)
    turned_embed = pltpu.roll(embed_ref[...].astype(jnp.float32), lax.rem(embed - turn, embed), axis=1)
    for first in range(0, embed, LANES):
        scratch[...] = turned_embed[:, first : first + LANES]
        ordered = [scratch[pl.ds(2 * a + b, chans, stride=4), :] for b in range(2) for a in range(2)]
        rows = jnp.concatenate(ordered, axis=0).T
        embed_out_ref[pl.ds(first, LANES), :] = rows.astype(embed_out_ref.dtype)


def window(pair_at, pairs):
    rows = []
    for pair in pairs:
        here = pair_at(pair)
        lane = lax.broadcasted_iota(jnp.int32, here.shape, 1)
        beside = jnp.where(lane < here.shape[1] // 2, pair_at(pair + 1), pair_at(pair - 1))
        rows.append(jnp.concatenate([here, beside], axis=-1))
    return jnp.concatenate(rows, axis=0)


def add_lat_taps(products, lat):
    wide = products.shape[1] // 3
    count = products.shape[0]
    row = lax.broadcasted_iota(jnp.int32, (1, lat, wide), 1)
    below = pltpu.roll(products[:, :wide], 1, axis=0).reshape(-1, lat, wide)
    above = pltpu.roll(products[:, 2 * wide :], count - 1, axis=0).reshape(-1, lat, wide)
    here = products[:, wide : 2 * wide].reshape(-1, lat, wide)
    return here + jnp.where(row == 0, 0.0, below) + jnp.where(row == lat - 1, 0.0, above)


def gelu(value):
    return 0.5 * value * (1.0 + lax.erf(value * (0.5**0.5)))


def dot(left, right):
    return jnp.dot(left, right, preferred_element_type=jnp.float32)


def dot_both(rows, taps_ref):
    both = dot(rows, taps_ref[...])
    half = both.shape[1] // 2
    return both[:, :half] + both[:, half:]


def first_conv(field_at, pairs, taps_ref, lat):
    products = dot_both(window(field_at, pairs), taps_ref)
    return split_two(gelu(add_lat_taps(products, lat)))


def second_conv(upper_at, lower_at, pairs, taps_ref, lat):
    upper, lower = window(upper_at, pairs), window(lower_at, pairs)
    products = dot_both(upper, taps_ref) + dot(lower, taps_ref[:, : taps_ref.shape[1] // 2])
    rounded = add_lat_taps(products, lat).astype(jnp.bfloat16).astype(jnp.float32)
    return rounded.reshape(-1, rounded.shape[2])


def embed_patches(two_ref, embed_ref):
    half = two_ref.shape[0] // 2
    patches = jnp.concatenate(
        [two_ref[pl.ds(b, half, stride=2), :].astype(jnp.bfloat16) for b in range(2)], axis=-1
    )
    return lax.dot_general(
        embed_ref[...], patches, (((1,), (1,)), ((), ())), preferred_element_type=jnp.float32
    ).astype(jnp.bfloat16)


def runs(first, last, lat):
    count = -(-(last - first) * lat // max(ROWS_AT_ONCE, lat))
    cuts = [first + (last - first) * at // count for at in range(count + 1)]
    return [list(range(*cut)) for cut in zip(cuts[:-1], cuts[1:])]


def inner_kernel(
    field_ref, taps_one_ref, taps_two_ref, embed_ref, tokens_ref, upper_edge_ref, lower_edge_ref, upper_ref, lower_ref, two_ref
):
    pairs, lat, wide = field_ref.shape
    for run in runs(1, pairs - 1, lat):
        upper, lower = first_conv(lambda pair: field_ref[pair], run, taps_one_ref, lat)
        upper_ref[pl.ds(run[0], len(run))] = upper
        lower_ref[pl.ds(run[0], len(run))] = lower
    for inside, edge in ((upper_ref, upper_edge_ref), (lower_ref, lower_edge_ref)):
        edge[pl.ds(0, 2)] = inside[pl.ds(1, 2)]
        edge[pl.ds(2, 2)] = inside[pl.ds(pairs - 3, 2)]
    for run in runs(2, pairs - 2, lat):
        two = second_conv(lambda pair: upper_ref[pair], lambda pair: lower_ref[pair], run, taps_two_ref, lat)
        two_ref[pl.ds((run[0] - 2) * lat, len(run) * lat), :] = two
    tokens_ref[...] = embed_patches(two_ref, embed_ref)


def outer_kernel(count_ch, count_sub, field_ref, *refs):
    count = count_ch * count_sub
    sides, refs = refs[:count], refs[count:]
    upper_edge_ref, lower_edge_ref, taps_one_ref, taps_two_ref, embed_ref, inner_ref, mixing_ref = refs[:7]
    tokens_ref, sent_ref, two_ref, sides_ref, product_ref = refs[7:]
    pairs, lat, wide = field_ref.shape
    for away, block in enumerate(sides):
        sides_ref[:, place(away, count_ch, count_sub, lat // count), :] = block[...]

    def field_at(pair):
        if pair < 0:
            return sides_ref[0]
        if pair >= pairs:
            return sides_ref[1]
        return field_ref[pair]

    outermost = [[-1, 0], [pairs - 1, pairs]]
    next_inside = [1, 2, pairs - 3, pairs - 2]
    found = [first_conv(field_at, side, taps_one_ref, lat) for side in outermost]
    inner = inner_ref.shape[1]
    rows, width = sent_ref.shape
    step = STEP if width % STEP == 0 else width
    for at in range(0, width, step):
        product_ref[:, pl.ds(at, step)] = dot(inner_ref[:rows], mixing_ref[pl.ds(lat, inner), pl.ds(at, step)])

    def hidden_at(side, part, edge_ref):
        def at(pair):
            if pair in outermost[side]:
                return found[side][part][outermost[side].index(pair)]
            return edge_ref[next_inside.index(pair)]

        return at

    for side, ends in enumerate(([0, 1], [pairs - 2, pairs - 1])):
        upper_at, lower_at = hidden_at(side, 0, upper_edge_ref), hidden_at(side, 1, lower_edge_ref)
        two = second_conv(upper_at, lower_at, ends, taps_two_ref, lat)
        two_ref[pl.ds(side * 2 * lat, 2 * lat), :] = two
    outer = embed_patches(two_ref, embed_ref)
    for at in range(0, width, step):
        here = pl.ds(at, step)
        product = dot(outer[:rows, :lat], mixing_ref[pl.ds(0, lat), here])
        product = product + dot(outer[:rows, lat:], mixing_ref[pl.ds(lat + inner, lat), here])
        sent_ref[:, here] = (product_ref[:, here] + product).astype(sent_ref.dtype)
    tokens_ref[:, :lat] = outer[:, :lat]
    tokens_ref[:, pl.ds(lat, inner)] = inner_ref[...]
    tokens_ref[:, pl.ds(lat + inner, lat)] = outer[:, lat:]


def call(kernel, out_shape, inputs, scratch=(), flops=0, moved=0):
    return pl.pallas_call(
        kernel,
        out_shape=out_shape,
        in_specs=[pl.BlockSpec(memory_space=pltpu.VMEM)] * len(inputs),
        out_specs=jax.tree.map(lambda unused: pl.BlockSpec(memory_space=pltpu.VMEM), out_shape),
        scratch_shapes=list(scratch),
        compiler_params=pltpu.CompilerParams(vmem_limit_bytes=VMEM_BYTES),
        cost_estimate=pl.CostEstimate(flops=flops, bytes_accessed=moved, transcendentals=0),
    )(*inputs)


def turned(value, axis, away):
    count = lax.axis_size(axis)
    return lax.ppermute(value, axis, [(i, (i + away) % count) for i in range(count)])


def band_blocks(block):
    rows = [block] + [turned(block, "ch", away) for away in range(1, lax.axis_size("ch"))]
    blocks = []
    for row in rows:
        blocks.append(row)
        blocks.extend(turned(row, "sub", away) for away in range(1, lax.axis_size("sub")))
    return blocks


def direct_blocks(block):
    sizes = lax.axis_size("ch"), lax.axis_size("sub")
    devices = [(at_ch, at_sub) for at_ch in range(sizes[0]) for at_sub in range(sizes[1])]
    blocks = [block]
    for away in devices[1:]:
        targets = [tuple((at + step) % size for at, step, size in zip(device, away, sizes)) for device in devices]
        route = [(number, devices.index(target)) for number, target in enumerate(targets)]
        blocks.append(lax.ppermute(block, ("ch", "sub"), route))
    return blocks


def encode(weather, conv_first, conv_second, patch_embed, token_mixing):
    chans, lon, lat = weather.shape
    pairs, wide = lon // 2, 2 * chans
    embed = patch_embed.shape[1]
    shape = functools.partial(jax.ShapeDtypeStruct, dtype=jnp.bfloat16)
    edge = shape((1, lat, wide))
    packed, low, high = call(
        pack_kernel,
        (shape((pairs, lat, wide)), edge, edge),
        (jnp.transpose(weather, (1, 2, 0)),),
        moved=weather.size * 10,
        flops=PACK_COST,
    )
    before = turned(high, "tok", 1)
    after = turned(low, "tok", -1)
    blocks = band_blocks(packed)
    taps = shape((4 * chans, 12 * chans))
    weights = call(
        weights_kernel,
        (taps, taps, shape((embed, 4 * chans))),
        (conv_first, conv_second, patch_embed),
        scratch=[pltpu.VMEM((patch_embed.shape[0], LANES), jnp.float32)],
        moved=conv_first.size * 20,
    )
    sides = direct_blocks(jnp.concatenate([before, after], axis=0))
    counts = lax.axis_size("ch"), lax.axis_size("sub")
    lat = len(blocks) * lat
    field = call(
        functools.partial(join_kernel, *counts),
        shape((pairs, lat, wide)),
        blocks,
        moved=packed.size * 4 * len(blocks),
    )
    work = 2 * lat * 4 * chans * 6 * chans * 5
    held = shape((4, lat, wide))
    hidden = pltpu.VMEM((pairs, lat, wide), jnp.bfloat16)
    inner, upper_edge, lower_edge = call(
        inner_kernel,
        (shape((embed, (pairs - 4) * lat // 2)), held, held),
        (field, *weights),
        scratch=[hidden, hidden, pltpu.VMEM(((pairs - 4) * lat, wide), jnp.float32)],
        flops=work * (pairs - 3),
        moved=field.size * 2,
    )
    sent = (embed // lax.axis_size("tok"), token_mixing.shape[1] // PIECES)
    return call(
        functools.partial(outer_kernel, *counts),
        (shape((embed, pairs * lat // 2)), shape(sent)),
        (field, *sides, upper_edge, lower_edge, *weights, inner, token_mixing),
        scratch=[
            pltpu.VMEM((4 * lat, wide), jnp.float32),
            pltpu.VMEM((2, lat, wide), jnp.bfloat16),
            pltpu.VMEM(sent, jnp.float32),
        ],
        flops=work * 4,
        moved=field.size * 2,
    )


def sent_kernel(first, block, tokens_ref, mixing_ref, sent_ref):
    rows, width = sent_ref.shape
    step = STEP if width % STEP == 0 else width
    tokens = tokens_ref[pl.ds(block * rows, rows), :]
    for at in range(0, width, step):
        product = dot(tokens, mixing_ref[:, pl.ds(first + at, step)])
        sent_ref[:, pl.ds(at, step)] = product.astype(sent_ref.dtype)


def hop_kernel(first, blocks, arrived_ref, tokens_ref, mixing_ref, sent_ref, kept_ref):
    rows, width = sent_ref.shape
    step = STEP if width % STEP == 0 else width
    tokens = jnp.concatenate([tokens_ref[pl.ds(block * rows, rows), :] for block in blocks], axis=0)
    for at in range(0, width, step):
        product = dot(tokens, mixing_ref[:, pl.ds(first + at, step)])
        arrived = arrived_ref[:, pl.ds(at, step)].astype(jnp.float32)
        sent_ref[:, pl.ds(at, step)] = (arrived + product[:rows]).astype(sent_ref.dtype)
        kept_ref[:, pl.ds(at, step)] = product[rows:]


def last_kernel(first, arrived_ref, kept_ref, *refs):
    result_ref, held_ref, written = refs[-3:]
    rows, width = arrived_ref.shape
    part = width // written.shape[0]
    copies = []
    for at in range(written.shape[0]):
        here = pl.ds(at * part, part)
        own = kept_ref[kept_ref.shape[0] - rows :, at * part : (at + 1) * part]
        held_ref[:, here] = gelu(arrived_ref[:, here].astype(jnp.float32) + own).astype(held_ref.dtype)
        target = result_ref.at[:, pl.ds(first + at * part, part)]
        copies.append(pltpu.make_async_copy(held_ref.at[:, here], target, written.at[at]))
        copies[-1].start()
    for copy in copies:
        copy.wait()


def finish(first, arrived, kept, result, columns):
    rows, width = arrived.shape
    near, far = pl.BlockSpec(memory_space=pltpu.VMEM), pl.BlockSpec(memory_space=pl.ANY)
    earlier = [] if result is None else [result]
    return pl.pallas_call(
        functools.partial(last_kernel, first),
        out_shape=jax.ShapeDtypeStruct((rows, columns), jnp.bfloat16),
        in_specs=[near, near] + [far] * len(earlier),
        out_specs=far,
        input_output_aliases={2: 0} if earlier else {},
        scratch_shapes=[
            pltpu.VMEM((rows, width), jnp.bfloat16),
            pltpu.SemaphoreType.DMA((WRITES if width % (WRITES * LANES) == 0 else 1,)),
        ],
        compiler_params=pltpu.CompilerParams(vmem_limit_bytes=VMEM_BYTES),
        cost_estimate=pl.CostEstimate(flops=0, bytes_accessed=0, transcendentals=0),
    )(arrived, kept, *earlier)


def lift(tokens, first_sent, token_mixing, pieces):
    count = lax.axis_size("tok")
    embed = tokens.shape[0]
    rows = embed // count
    width = token_mixing.shape[1] // pieces
    sent = jax.ShapeDtypeStruct((rows, width), jnp.bfloat16)
    ways = [-1 if piece % 2 == 0 else 1 for piece in range(pieces)]
    blocks = [list(range(count - 2, -1, -1)) if way == 1 else list(range(count - 1)) for way in ways]
    travelling = [first_sent] + [
        call(functools.partial(sent_kernel, piece * width, blocks[piece][0]), sent, (tokens, token_mixing))
        for piece in range(1, pieces)
    ]
    kept = [None] * pieces
    result = None
    for step in range(1, count):
        for piece in range(pieces):
            arrived = turned(travelling[piece], "tok", ways[piece])
            if step == 1:
                travelling[piece], kept[piece] = call(
                    functools.partial(hop_kernel, piece * width, blocks[piece][1:] + [count - 1]),
                    [sent, jax.ShapeDtypeStruct((embed - 2 * rows, width), jnp.float32)],
                    (arrived, tokens, token_mixing),
                )
            elif step < count - 1:
                at = (step - 2) * rows
                summed = arrived.astype(jnp.float32) + kept[piece][at : at + rows]
                travelling[piece] = summed.astype(jnp.bfloat16)
            else:
                result = finish(piece * width, arrived, kept[piece], result, pieces * width)
    return result


def local(weather, conv_first, conv_second, patch_embed, token_mixing):
    tokens, first_sent = encode(weather, conv_first, conv_second, patch_embed, token_mixing)
    return lift(tokens, first_sent, token_mixing, PIECES)


def solution(mesh):
    placed = (P("groups", "tok", ("ch", "sub")), P(), P(), P(), P("tok", ("ch", "sub")))
    return jax.shard_map(
        local,
        mesh=mesh,
        in_specs=placed,
        out_specs=P(("groups", "tok"), ("ch", "sub")),
        check_vma=False,
    )
```

```python
import functools

import jax
import jax.numpy as jnp
from jax import lax
from jax.experimental import pallas as pl
from jax.experimental.pallas import tpu as pltpu
from jax.sharding import PartitionSpec as P

PIECES = 2
STEP = 256
LANES = 128
PACK_COST = 20 * 10**9
WRITES = 4
VMEM_BYTES = 24 * 1024 * 1024
ROWS_AT_ONCE = 640


def pack_kernel(field_ref, packed_ref, low_ref, high_ref):
    lon, lat, chans = field_ref.shape
    pairs = field_ref[...].reshape(lon // 2, 2, lat, chans)
    joined = jnp.concatenate([pairs[:, 0], pairs[:, 1]], axis=-1).astype(packed_ref.dtype)
    packed_ref[...] = joined
    low_ref[...] = joined[:1]
    high_ref[...] = joined[-1:]


def place(away, count_ch, count_sub, width):
    away_ch, away_sub = away // count_sub, away % count_sub
    at_ch = lax.rem(lax.axis_index("ch") + count_ch - away_ch, count_ch)
    at_sub = lax.rem(lax.axis_index("sub") + count_sub - away_sub, count_sub)
    return pl.ds(pl.multiple_of((at_ch * count_sub + at_sub) * width, width), width)


def join_kernel(count_ch, count_sub, *refs):
    blocks, field_ref = refs[:-1], refs[-1]
    width = field_ref.shape[1] // len(blocks)
    for away, block in enumerate(blocks):
        field_ref[:, place(away, count_ch, count_sub, width), :] = block[...]


def split_two(value):
    upper = value.astype(jnp.bfloat16)
    return upper, (value - upper.astype(jnp.float32)).astype(jnp.bfloat16)


def spread_taps(kernel_ref):
    chans = kernel_ref.shape[1]
    nothing = jnp.zeros((chans, kernel_ref.shape[2]), jnp.float32)
    rows = []
    for tap in range(3):
        taps = [kernel_ref[3 * turn + tap] for turn in range(3)]
        rows.append(jnp.concatenate([taps[1], taps[2], nothing, taps[0]], axis=-1))
        rows.append(jnp.concatenate([taps[0], taps[1], taps[2], nothing], axis=-1))
    return jnp.concatenate(rows, axis=0).T


def weights_kernel(first_ref, second_ref, embed_ref, taps_one_ref, taps_two_ref, embed_out_ref, scratch):
    for source, target in ((first_ref, taps_one_ref), (second_ref, taps_two_ref)):
        upper, lower = split_two(spread_taps(source))
        target[...] = jnp.concatenate([upper, lower], axis=1)
    chans = embed_ref.shape[0] // 4
    embed = embed_ref.shape[1]
    count = lax.axis_size("tok")
    turn = lax.rem(lax.axis_index("tok") + 1, count) * (embed // count)
    turned_embed = pltpu.roll(embed_ref[...].astype(jnp.float32), lax.rem(embed - turn, embed), axis=1)
    for first in range(0, embed, LANES):
        scratch[...] = turned_embed[:, first : first + LANES]
        ordered = [scratch[pl.ds(2 * a + b, chans, stride=4), :] for b in range(2) for a in range(2)]
        rows = jnp.concatenate(ordered, axis=0).T
        embed_out_ref[pl.ds(first, LANES), :] = rows.astype(embed_out_ref.dtype)


def window(pair_at, pairs):
    rows = []
    for pair in pairs:
        here = pair_at(pair)
        lane = lax.broadcasted_iota(jnp.int32, here.shape, 1)
        beside = jnp.where(lane < here.shape[1] // 2, pair_at(pair + 1), pair_at(pair - 1))
        rows.append(jnp.concatenate([here, beside], axis=-1))
    return jnp.concatenate(rows, axis=0)


def add_lat_taps(products, lat):
    wide = products.shape[1] // 3
    count = products.shape[0]
    row = lax.broadcasted_iota(jnp.int32, (1, lat, wide), 1)
    below = pltpu.roll(products[:, :wide], 1, axis=0).reshape(-1, lat, wide)
    above = pltpu.roll(products[:, 2 * wide :], count - 1, axis=0).reshape(-1, lat, wide)
    here = products[:, wide : 2 * wide].reshape(-1, lat, wide)
    return here + jnp.where(row == 0, 0.0, below) + jnp.where(row == lat - 1, 0.0, above)


def gelu(value):
    return 0.5 * value * (1.0 + lax.erf(value * (0.5**0.5)))


def dot(left, right):
    return jnp.dot(left, right, preferred_element_type=jnp.float32)


def dot_both(rows, taps_ref):
    both = dot(rows, taps_ref[...])
    half = both.shape[1] // 2
    return both[:, :half] + both[:, half:]


def first_conv(field_at, pairs, taps_ref, lat):
    products = dot_both(window(field_at, pairs), taps_ref)
    return split_two(gelu(add_lat_taps(products, lat)))


def second_conv(upper_at, lower_at, pairs, taps_ref, lat):
    upper, lower = window(upper_at, pairs), window(lower_at, pairs)
    products = dot_both(upper, taps_ref) + dot(lower, taps_ref[:, : taps_ref.shape[1] // 2])
    rounded = add_lat_taps(products, lat).astype(jnp.bfloat16).astype(jnp.float32)
    return rounded.reshape(-1, rounded.shape[2])


def embed_patches(two_ref, embed_ref):
    half = two_ref.shape[0] // 2
    patches = jnp.concatenate(
        [two_ref[pl.ds(b, half, stride=2), :].astype(jnp.bfloat16) for b in range(2)], axis=-1
    )
    return lax.dot_general(
        embed_ref[...], patches, (((1,), (1,)), ((), ())), preferred_element_type=jnp.float32
    ).astype(jnp.bfloat16)


def runs(first, last, lat):
    count = -(-(last - first) * lat // max(ROWS_AT_ONCE, lat))
    cuts = [first + (last - first) * at // count for at in range(count + 1)]
    return [list(range(*cut)) for cut in zip(cuts[:-1], cuts[1:])]


def inner_kernel(
    field_ref, taps_one_ref, taps_two_ref, embed_ref, tokens_ref, upper_edge_ref, lower_edge_ref, upper_ref, lower_ref, two_ref
):
    pairs, lat, wide = field_ref.shape
    for run in runs(1, pairs - 1, lat):
        upper, lower = first_conv(lambda pair: field_ref[pair], run, taps_one_ref, lat)
        upper_ref[pl.ds(run[0], len(run))] = upper
        lower_ref[pl.ds(run[0], len(run))] = lower
    for inside, edge in ((upper_ref, upper_edge_ref), (lower_ref, lower_edge_ref)):
        edge[pl.ds(0, 2)] = inside[pl.ds(1, 2)]
        edge[pl.ds(2, 2)] = inside[pl.ds(pairs - 3, 2)]
    for run in runs(2, pairs - 2, lat):
        two = second_conv(lambda pair: upper_ref[pair], lambda pair: lower_ref[pair], run, taps_two_ref, lat)
        two_ref[pl.ds((run[0] - 2) * lat, len(run) * lat), :] = two
    tokens_ref[...] = embed_patches(two_ref, embed_ref)


def outer_kernel(count_ch, count_sub, field_ref, *refs):
    count = count_ch * count_sub
    sides, refs = refs[:count], refs[count:]
    upper_edge_ref, lower_edge_ref, taps_one_ref, taps_two_ref, embed_ref, inner_ref, mixing_ref = refs[:7]
    tokens_ref, sent_ref, two_ref, sides_ref, product_ref = refs[7:]
    pairs, lat, wide = field_ref.shape
    for away, block in enumerate(sides):
        sides_ref[:, place(away, count_ch, count_sub, lat // count), :] = block[...]

    def field_at(pair):
        if pair < 0:
            return sides_ref[0]
        if pair >= pairs:
            return sides_ref[1]
        return field_ref[pair]

    outermost = [[-1, 0], [pairs - 1, pairs]]
    next_inside = [1, 2, pairs - 3, pairs - 2]
    found = [first_conv(field_at, side, taps_one_ref, lat) for side in outermost]
    inner = inner_ref.shape[1]
    rows, width = sent_ref.shape
    step = STEP if width % STEP == 0 else width
    for at in range(0, width, step):
        product_ref[:, pl.ds(at, step)] = dot(inner_ref[:rows], mixing_ref[pl.ds(lat, inner), pl.ds(at, step)])

    def hidden_at(side, part, edge_ref):
        def at(pair):
            if pair in outermost[side]:
                return found[side][part][outermost[side].index(pair)]
            return edge_ref[next_inside.index(pair)]

        return at

    for side, ends in enumerate(([0, 1], [pairs - 2, pairs - 1])):
        upper_at, lower_at = hidden_at(side, 0, upper_edge_ref), hidden_at(side, 1, lower_edge_ref)
        two = second_conv(upper_at, lower_at, ends, taps_two_ref, lat)
        two_ref[pl.ds(side * 2 * lat, 2 * lat), :] = two
    outer = embed_patches(two_ref, embed_ref)
    for at in range(0, width, step):
        here = pl.ds(at, step)
        product = dot(outer[:rows, :lat], mixing_ref[pl.ds(0, lat), here])
        product = product + dot(outer[:rows, lat:], mixing_ref[pl.ds(lat + inner, lat), here])
        sent_ref[:, here] = (product_ref[:, here] + product).astype(sent_ref.dtype)
    tokens_ref[:, :lat] = outer[:, :lat]
    tokens_ref[:, pl.ds(lat, inner)] = inner_ref[...]
    tokens_ref[:, pl.ds(lat + inner, lat)] = outer[:, lat:]


def call(kernel, out_shape, inputs, scratch=(), flops=0, moved=0):
    return pl.pallas_call(
        kernel,
        out_shape=out_shape,
        in_specs=[pl.BlockSpec(memory_space=pltpu.VMEM)] * len(inputs),
        out_specs=jax.tree.map(lambda unused: pl.BlockSpec(memory_space=pltpu.VMEM), out_shape),
        scratch_shapes=list(scratch),
        compiler_params=pltpu.CompilerParams(vmem_limit_bytes=VMEM_BYTES),
        cost_estimate=pl.CostEstimate(flops=flops, bytes_accessed=moved, transcendentals=0),
    )(*inputs)


def turned(value, axis, away):
    count = lax.axis_size(axis)
    return lax.ppermute(value, axis, [(i, (i + away) % count) for i in range(count)])


def band_blocks(block):
    rows = [block] + [turned(block, "ch", away) for away in range(1, lax.axis_size("ch"))]
    blocks = []
    for row in rows:
        blocks.append(row)
        blocks.extend(turned(row, "sub", away) for away in range(1, lax.axis_size("sub")))
    return blocks


def direct_blocks(block):
    sizes = lax.axis_size("ch"), lax.axis_size("sub")
    devices = [(at_ch, at_sub) for at_ch in range(sizes[0]) for at_sub in range(sizes[1])]
    blocks = [block]
    for away in devices[1:]:
        targets = [tuple((at + step) % size for at, step, size in zip(device, away, sizes)) for device in devices]
        route = [(number, devices.index(target)) for number, target in enumerate(targets)]
        blocks.append(lax.ppermute(block, ("ch", "sub"), route))
    return blocks


def encode(weather, conv_first, conv_second, patch_embed, token_mixing):
    chans, lon, lat = weather.shape
    pairs, wide = lon // 2, 2 * chans
    embed = patch_embed.shape[1]
    shape = functools.partial(jax.ShapeDtypeStruct, dtype=jnp.bfloat16)
    edge = shape((1, lat, wide))
    packed, low, high = call(
        pack_kernel,
        (shape((pairs, lat, wide)), edge, edge),
        (jnp.transpose(weather, (1, 2, 0)),),
        moved=weather.size * 10,
        flops=PACK_COST,
    )
    before = turned(high, "tok", 1)
    after = turned(low, "tok", -1)
    blocks = band_blocks(packed)
    taps = shape((4 * chans, 12 * chans))
    weights = call(
        weights_kernel,
        (taps, taps, shape((embed, 4 * chans))),
        (conv_first, conv_second, patch_embed),
        scratch=[pltpu.VMEM((patch_embed.shape[0], LANES), jnp.float32)],
        moved=conv_first.size * 20,
    )
    sides = direct_blocks(jnp.concatenate([before, after], axis=0))
    counts = lax.axis_size("ch"), lax.axis_size("sub")
    lat = len(blocks) * lat
    field = call(
        functools.partial(join_kernel, *counts),
        shape((pairs, lat, wide)),
        blocks,
        moved=packed.size * 4 * len(blocks),
    )
    work = 2 * lat * 4 * chans * 6 * chans * 5
    held = shape((4, lat, wide))
    hidden = pltpu.VMEM((pairs, lat, wide), jnp.bfloat16)
    inner, upper_edge, lower_edge = call(
        inner_kernel,
        (shape((embed, (pairs - 4) * lat // 2)), held, held),
        (field, *weights),
        scratch=[hidden, hidden, pltpu.VMEM(((pairs - 4) * lat, wide), jnp.float32)],
        flops=work * (pairs - 3),
        moved=field.size * 2,
    )
    sent = (embed // lax.axis_size("tok"), token_mixing.shape[1] // PIECES)
    return call(
        functools.partial(outer_kernel, *counts),
        (shape((embed, pairs * lat // 2)), shape(sent)),
        (field, *sides, upper_edge, lower_edge, *weights, inner, token_mixing),
        scratch=[
            pltpu.VMEM((4 * lat, wide), jnp.float32),
            pltpu.VMEM((2, lat, wide), jnp.bfloat16),
            pltpu.VMEM(sent, jnp.float32),
        ],
        flops=work * 4,
        moved=field.size * 2,
    )


def sent_kernel(first, block, tokens_ref, mixing_ref, sent_ref):
    rows, width = sent_ref.shape
    step = STEP if width % STEP == 0 else width
    tokens = tokens_ref[pl.ds(block * rows, rows), :]
    for at in range(0, width, step):
        product = dot(tokens, mixing_ref[:, pl.ds(first + at, step)])
        sent_ref[:, pl.ds(at, step)] = product.astype(sent_ref.dtype)


def hop_kernel(first, blocks, arrived_ref, tokens_ref, mixing_ref, sent_ref, kept_ref):
    rows, width = sent_ref.shape
    step = STEP if width % STEP == 0 else width
    tokens = jnp.concatenate([tokens_ref[pl.ds(block * rows, rows), :] for block in blocks], axis=0)
    for at in range(0, width, step):
        product = dot(tokens, mixing_ref[:, pl.ds(first + at, step)])
        arrived = arrived_ref[:, pl.ds(at, step)].astype(jnp.float32)
        sent_ref[:, pl.ds(at, step)] = (arrived + product[:rows]).astype(sent_ref.dtype)
        kept_ref[:, pl.ds(at, step)] = product[rows:]


def last_kernel(first, arrived_ref, kept_ref, *refs):
    result_ref, held_ref, written = refs[-3:]
    rows, width = arrived_ref.shape
    part = width // written.shape[0]
    copies = []
    for at in range(written.shape[0]):
        here = pl.ds(at * part, part)
        own = kept_ref[kept_ref.shape[0] - rows :, at * part : (at + 1) * part]
        held_ref[:, here] = gelu(arrived_ref[:, here].astype(jnp.float32) + own).astype(held_ref.dtype)
        target = result_ref.at[:, pl.ds(first + at * part, part)]
        copies.append(pltpu.make_async_copy(held_ref.at[:, here], target, written.at[at]))
        copies[-1].start()
    for copy in copies:
        copy.wait()


def finish(first, arrived, kept, result, columns):
    rows, width = arrived.shape
    near, far = pl.BlockSpec(memory_space=pltpu.VMEM), pl.BlockSpec(memory_space=pl.ANY)
    earlier = [] if result is None else [result]
    return pl.pallas_call(
        functools.partial(last_kernel, first),
        out_shape=jax.ShapeDtypeStruct((rows, columns), jnp.bfloat16),
        in_specs=[near, near] + [far] * len(earlier),
        out_specs=far,
        input_output_aliases={2: 0} if earlier else {},
        scratch_shapes=[
            pltpu.VMEM((rows, width), jnp.bfloat16),
            pltpu.SemaphoreType.DMA((WRITES if width % (WRITES * LANES) == 0 else 1,)),
        ],
        compiler_params=pltpu.CompilerParams(vmem_limit_bytes=VMEM_BYTES),
        cost_estimate=pl.CostEstimate(flops=0, bytes_accessed=0, transcendentals=0),
    )(arrived, kept, *earlier)


def lift(tokens, first_sent, token_mixing, pieces):
    count = lax.axis_size("tok")
    embed = tokens.shape[0]
    rows = embed // count
    width = token_mixing.shape[1] // pieces
    sent = jax.ShapeDtypeStruct((rows, width), jnp.bfloat16)
    ways = [-1] * pieces
    blocks = [list(range(count - 2, -1, -1)) if way == 1 else list(range(count - 1)) for way in ways]
    travelling = [first_sent] + [
        call(functools.partial(sent_kernel, piece * width, blocks[piece][0]), sent, (tokens, token_mixing))
        for piece in range(1, pieces)
    ]
    kept = [None] * pieces
    result = None
    for step in range(1, count):
        for piece in range(pieces):
            arrived = turned(travelling[piece], "tok", ways[piece])
            if step == 1:
                travelling[piece], kept[piece] = call(
                    functools.partial(hop_kernel, piece * width, blocks[piece][1:] + [count - 1]),
                    [sent, jax.ShapeDtypeStruct((embed - 2 * rows, width), jnp.float32)],
                    (arrived, tokens, token_mixing),
                )
            elif step < count - 1:
                at = (step - 2) * rows
                summed = arrived.astype(jnp.float32) + kept[piece][at : at + rows]
                travelling[piece] = summed.astype(jnp.bfloat16)
            else:
                result = finish(piece * width, arrived, kept[piece], result, pieces * width)
    return result


def local(weather, conv_first, conv_second, patch_embed, token_mixing):
    tokens, first_sent = encode(weather, conv_first, conv_second, patch_embed, token_mixing)
    return lift(tokens, first_sent, token_mixing, PIECES)


def solution(mesh):
    placed = (P("groups", "tok", ("ch", "sub")), P(), P(), P(), P("tok", ("ch", "sub")))
    return jax.shard_map(
        local,
        mesh=mesh,
        in_specs=placed,
        out_specs=P(("groups", "tok"), ("ch", "sub")),
        check_vma=False,
    )
```

```python
import functools

import jax
import jax.numpy as jnp
from jax import lax
from jax.experimental import pallas as pl
from jax.experimental.pallas import tpu as pltpu
from jax.sharding import PartitionSpec as P

PIECES = 4
STEP = 256
LANES = 128
PACK_COST = 20 * 10**9
WRITES = 4
VMEM_BYTES = 24 * 1024 * 1024
ROWS_AT_ONCE = 512


def pack_kernel(field_ref, packed_ref, low_ref, high_ref):
    lon, lat, chans = field_ref.shape
    pairs = field_ref[...].reshape(lon // 2, 2, lat, chans)
    joined = jnp.concatenate([pairs[:, 0], pairs[:, 1]], axis=-1).astype(packed_ref.dtype)
    packed_ref[...] = joined
    low_ref[...] = joined[:1]
    high_ref[...] = joined[-1:]


def place(away, count_ch, count_sub, width):
    away_ch, away_sub = away // count_sub, away % count_sub
    at_ch = lax.rem(lax.axis_index("ch") + count_ch - away_ch, count_ch)
    at_sub = lax.rem(lax.axis_index("sub") + count_sub - away_sub, count_sub)
    return pl.ds(pl.multiple_of((at_ch * count_sub + at_sub) * width, width), width)


def join_kernel(count_ch, count_sub, *refs):
    blocks, field_ref = refs[:-1], refs[-1]
    width = field_ref.shape[1] // len(blocks)
    for away, block in enumerate(blocks):
        field_ref[:, place(away, count_ch, count_sub, width), :] = block[...]


def split_two(value):
    upper = value.astype(jnp.bfloat16)
    return upper, (value - upper.astype(jnp.float32)).astype(jnp.bfloat16)


def spread_taps(kernel_ref):
    chans = kernel_ref.shape[1]
    nothing = jnp.zeros((chans, kernel_ref.shape[2]), jnp.float32)
    rows = []
    for tap in range(3):
        taps = [kernel_ref[3 * turn + tap] for turn in range(3)]
        rows.append(jnp.concatenate([taps[1], taps[2], nothing, taps[0]], axis=-1))
        rows.append(jnp.concatenate([taps[0], taps[1], taps[2], nothing], axis=-1))
    return jnp.concatenate(rows, axis=0).T


def weights_kernel(first_ref, second_ref, embed_ref, taps_one_ref, taps_two_ref, embed_out_ref, scratch):
    for source, target in ((first_ref, taps_one_ref), (second_ref, taps_two_ref)):
        upper, lower = split_two(spread_taps(source))
        target[...] = jnp.concatenate([upper, lower], axis=1)
    chans = embed_ref.shape[0] // 4
    embed = embed_ref.shape[1]
    count = lax.axis_size("tok")
    turn = lax.rem(lax.axis_index("tok") + 1, count) * (embed // count)
    turned_embed = pltpu.roll(embed_ref[...].astype(jnp.float32), lax.rem(embed - turn, embed), axis=1)
    for first in range(0, embed, LANES):
        scratch[...] = turned_embed[:, first : first + LANES]
        ordered = [scratch[pl.ds(2 * a + b, chans, stride=4), :] for b in range(2) for a in range(2)]
        rows = jnp.concatenate(ordered, axis=0).T
        embed_out_ref[pl.ds(first, LANES), :] = rows.astype(embed_out_ref.dtype)


def window(pair_at, pairs):
    rows = []
    for pair in pairs:
        here = pair_at(pair)
        lane = lax.broadcasted_iota(jnp.int32, here.shape, 1)
        beside = jnp.where(lane < here.shape[1] // 2, pair_at(pair + 1), pair_at(pair - 1))
        rows.append(jnp.concatenate([here, beside], axis=-1))
    return jnp.concatenate(rows, axis=0)


def add_lat_taps(products, lat):
    wide = products.shape[1] // 3
    count = products.shape[0]
    row = lax.broadcasted_iota(jnp.int32, (1, lat, wide), 1)
    below = pltpu.roll(products[:, :wide], 1, axis=0).reshape(-1, lat, wide)
    above = pltpu.roll(products[:, 2 * wide :], count - 1, axis=0).reshape(-1, lat, wide)
    here = products[:, wide : 2 * wide].reshape(-1, lat, wide)
    return here + jnp.where(row == 0, 0.0, below) + jnp.where(row == lat - 1, 0.0, above)


def gelu(value):
    return 0.5 * value * (1.0 + lax.erf(value * (0.5**0.5)))


def dot(left, right):
    return jnp.dot(left, right, preferred_element_type=jnp.float32)


def dot_both(rows, taps_ref):
    both = dot(rows, taps_ref[...])
    half = both.shape[1] // 2
    return both[:, :half] + both[:, half:]


def first_conv(field_at, pairs, taps_ref, lat):
    products = dot_both(window(field_at, pairs), taps_ref)
    return split_two(gelu(add_lat_taps(products, lat)))


def second_conv(upper_at, lower_at, pairs, taps_ref, lat):
    upper, lower = window(upper_at, pairs), window(lower_at, pairs)
    products = dot_both(upper, taps_ref) + dot(lower, taps_ref[:, : taps_ref.shape[1] // 2])
    rounded = add_lat_taps(products, lat).astype(jnp.bfloat16).astype(jnp.float32)
    return rounded.reshape(-1, rounded.shape[2])


def embed_patches(two_ref, embed_ref):
    half = two_ref.shape[0] // 2
    patches = jnp.concatenate(
        [two_ref[pl.ds(b, half, stride=2), :].astype(jnp.bfloat16) for b in range(2)], axis=-1
    )
    return lax.dot_general(
        embed_ref[...], patches, (((1,), (1,)), ((), ())), preferred_element_type=jnp.float32
    ).astype(jnp.bfloat16)


def runs(first, last, lat):
    count = -(-(last - first) * lat // max(ROWS_AT_ONCE, lat))
    cuts = [first + (last - first) * at // count for at in range(count + 1)]
    return [list(range(*cut)) for cut in zip(cuts[:-1], cuts[1:])]


def inner_kernel(
    field_ref, taps_one_ref, taps_two_ref, embed_ref, tokens_ref, upper_edge_ref, lower_edge_ref, upper_ref, lower_ref, two_ref
):
    pairs, lat, wide = field_ref.shape
    for run in runs(1, pairs - 1, lat):
        upper, lower = first_conv(lambda pair: field_ref[pair], run, taps_one_ref, lat)
        upper_ref[pl.ds(run[0], len(run))] = upper
        lower_ref[pl.ds(run[0], len(run))] = lower
    for inside, edge in ((upper_ref, upper_edge_ref), (lower_ref, lower_edge_ref)):
        edge[pl.ds(0, 2)] = inside[pl.ds(1, 2)]
        edge[pl.ds(2, 2)] = inside[pl.ds(pairs - 3, 2)]
    for run in runs(2, pairs - 2, lat):
        two = second_conv(lambda pair: upper_ref[pair], lambda pair: lower_ref[pair], run, taps_two_ref, lat)
        two_ref[pl.ds((run[0] - 2) * lat, len(run) * lat), :] = two
    tokens_ref[...] = embed_patches(two_ref, embed_ref)


def outer_kernel(count_ch, count_sub, field_ref, *refs):
    count = count_ch * count_sub
    sides, refs = refs[:count], refs[count:]
    upper_edge_ref, lower_edge_ref, taps_one_ref, taps_two_ref, embed_ref, inner_ref, mixing_ref = refs[:7]
    tokens_ref, sent_ref, two_ref, sides_ref, product_ref = refs[7:]
    pairs, lat, wide = field_ref.shape
    for away, block in enumerate(sides):
        sides_ref[:, place(away, count_ch, count_sub, lat // count), :] = block[...]

    def field_at(pair):
        if pair < 0:
            return sides_ref[0]
        if pair >= pairs:
            return sides_ref[1]
        return field_ref[pair]

    outermost = [[-1, 0], [pairs - 1, pairs]]
    next_inside = [1, 2, pairs - 3, pairs - 2]
    found = [first_conv(field_at, side, taps_one_ref, lat) for side in outermost]
    inner = inner_ref.shape[1]
    rows, width = sent_ref.shape
    step = STEP if width % STEP == 0 else width
    for at in range(0, width, step):
        product_ref[:, pl.ds(at, step)] = dot(inner_ref[:rows], mixing_ref[pl.ds(lat, inner), pl.ds(at, step)])

    def hidden_at(side, part, edge_ref):
        def at(pair):
            if pair in outermost[side]:
                return found[side][part][outermost[side].index(pair)]
            return edge_ref[next_inside.index(pair)]

        return at

    for side, ends in enumerate(([0, 1], [pairs - 2, pairs - 1])):
        upper_at, lower_at = hidden_at(side, 0, upper_edge_ref), hidden_at(side, 1, lower_edge_ref)
        two = second_conv(upper_at, lower_at, ends, taps_two_ref, lat)
        two_ref[pl.ds(side * 2 * lat, 2 * lat), :] = two
    outer = embed_patches(two_ref, embed_ref)
    for at in range(0, width, step):
        here = pl.ds(at, step)
        product = dot(outer[:rows, :lat], mixing_ref[pl.ds(0, lat), here])
        product = product + dot(outer[:rows, lat:], mixing_ref[pl.ds(lat + inner, lat), here])
        sent_ref[:, here] = (product_ref[:, here] + product).astype(sent_ref.dtype)
    tokens_ref[:, :lat] = outer[:, :lat]
    tokens_ref[:, pl.ds(lat, inner)] = inner_ref[...]
    tokens_ref[:, pl.ds(lat + inner, lat)] = outer[:, lat:]


def call(kernel, out_shape, inputs, scratch=(), flops=0, moved=0):
    return pl.pallas_call(
        kernel,
        out_shape=out_shape,
        in_specs=[pl.BlockSpec(memory_space=pltpu.VMEM)] * len(inputs),
        out_specs=jax.tree.map(lambda unused: pl.BlockSpec(memory_space=pltpu.VMEM), out_shape),
        scratch_shapes=list(scratch),
        compiler_params=pltpu.CompilerParams(vmem_limit_bytes=VMEM_BYTES),
        cost_estimate=pl.CostEstimate(flops=flops, bytes_accessed=moved, transcendentals=0),
    )(*inputs)


def turned(value, axis, away):
    count = lax.axis_size(axis)
    return lax.ppermute(value, axis, [(i, (i + away) % count) for i in range(count)])


def band_blocks(block):
    rows = [block] + [turned(block, "ch", away) for away in range(1, lax.axis_size("ch"))]
    blocks = []
    for row in rows:
        blocks.append(row)
        blocks.extend(turned(row, "sub", away) for away in range(1, lax.axis_size("sub")))
    return blocks


def direct_blocks(block):
    sizes = lax.axis_size("ch"), lax.axis_size("sub")
    devices = [(at_ch, at_sub) for at_ch in range(sizes[0]) for at_sub in range(sizes[1])]
    blocks = [block]
    for away in devices[1:]:
        targets = [tuple((at + step) % size for at, step, size in zip(device, away, sizes)) for device in devices]
        route = [(number, devices.index(target)) for number, target in enumerate(targets)]
        blocks.append(lax.ppermute(block, ("ch", "sub"), route))
    return blocks


def encode(weather, conv_first, conv_second, patch_embed, token_mixing):
    chans, lon, lat = weather.shape
    pairs, wide = lon // 2, 2 * chans
    embed = patch_embed.shape[1]
    shape = functools.partial(jax.ShapeDtypeStruct, dtype=jnp.bfloat16)
    edge = shape((1, lat, wide))
    packed, low, high = call(
        pack_kernel,
        (shape((pairs, lat, wide)), edge, edge),
        (jnp.transpose(weather, (1, 2, 0)),),
        moved=weather.size * 10,
        flops=PACK_COST,
    )
    before = turned(high, "tok", 1)
    after = turned(low, "tok", -1)
    blocks = band_blocks(packed)
    taps = shape((4 * chans, 12 * chans))
    weights = call(
        weights_kernel,
        (taps, taps, shape((embed, 4 * chans))),
        (conv_first, conv_second, patch_embed),
        scratch=[pltpu.VMEM((patch_embed.shape[0], LANES), jnp.float32)],
        moved=conv_first.size * 20,
    )
    sides = direct_blocks(jnp.concatenate([before, after], axis=0))
    counts = lax.axis_size("ch"), lax.axis_size("sub")
    lat = len(blocks) * lat
    field = call(
        functools.partial(join_kernel, *counts),
        shape((pairs, lat, wide)),
        blocks,
        moved=packed.size * 4 * len(blocks),
    )
    work = 2 * lat * 4 * chans * 6 * chans * 5
    held = shape((4, lat, wide))
    hidden = pltpu.VMEM((pairs, lat, wide), jnp.bfloat16)
    inner, upper_edge, lower_edge = call(
        inner_kernel,
        (shape((embed, (pairs - 4) * lat // 2)), held, held),
        (field, *weights),
        scratch=[hidden, hidden, pltpu.VMEM(((pairs - 4) * lat, wide), jnp.float32)],
        flops=work * (pairs - 3),
        moved=field.size * 2,
    )
    sent = (embed // lax.axis_size("tok"), token_mixing.shape[1] // PIECES)
    return call(
        functools.partial(outer_kernel, *counts),
        (shape((embed, pairs * lat // 2)), shape(sent)),
        (field, *sides, upper_edge, lower_edge, *weights, inner, token_mixing),
        scratch=[
            pltpu.VMEM((4 * lat, wide), jnp.float32),
            pltpu.VMEM((2, lat, wide), jnp.bfloat16),
            pltpu.VMEM(sent, jnp.float32),
        ],
        flops=work * 4,
        moved=field.size * 2,
    )


def sent_kernel(first, block, tokens_ref, mixing_ref, sent_ref):
    rows, width = sent_ref.shape
    step = STEP if width % STEP == 0 else width
    tokens = tokens_ref[pl.ds(block * rows, rows), :]
    for at in range(0, width, step):
        product = dot(tokens, mixing_ref[:, pl.ds(first + at, step)])
        sent_ref[:, pl.ds(at, step)] = product.astype(sent_ref.dtype)


def hop_kernel(first, blocks, arrived_ref, tokens_ref, mixing_ref, sent_ref, kept_ref):
    rows, width = sent_ref.shape
    step = STEP if width % STEP == 0 else width
    tokens = jnp.concatenate([tokens_ref[pl.ds(block * rows, rows), :] for block in blocks], axis=0)
    for at in range(0, width, step):
        product = dot(tokens, mixing_ref[:, pl.ds(first + at, step)])
        arrived = arrived_ref[:, pl.ds(at, step)].astype(jnp.float32)
        sent_ref[:, pl.ds(at, step)] = (arrived + product[:rows]).astype(sent_ref.dtype)
        kept_ref[:, pl.ds(at, step)] = product[rows:]


def last_kernel(first, arrived_ref, kept_ref, *refs):
    result_ref, held_ref, written = refs[-3:]
    rows, width = arrived_ref.shape
    part = width // written.shape[0]
    copies = []
    for at in range(written.shape[0]):
        here = pl.ds(at * part, part)
        own = kept_ref[kept_ref.shape[0] - rows :, at * part : (at + 1) * part]
        held_ref[:, here] = gelu(arrived_ref[:, here].astype(jnp.float32) + own).astype(held_ref.dtype)
        target = result_ref.at[:, pl.ds(first + at * part, part)]
        copies.append(pltpu.make_async_copy(held_ref.at[:, here], target, written.at[at]))
        copies[-1].start()
    for copy in copies:
        copy.wait()


def finish(first, arrived, kept, result, columns):
    rows, width = arrived.shape
    near, far = pl.BlockSpec(memory_space=pltpu.VMEM), pl.BlockSpec(memory_space=pl.ANY)
    earlier = [] if result is None else [result]
    return pl.pallas_call(
        functools.partial(last_kernel, first),
        out_shape=jax.ShapeDtypeStruct((rows, columns), jnp.bfloat16),
        in_specs=[near, near] + [far] * len(earlier),
        out_specs=far,
        input_output_aliases={2: 0} if earlier else {},
        scratch_shapes=[
            pltpu.VMEM((rows, width), jnp.bfloat16),
            pltpu.SemaphoreType.DMA((WRITES if width % (WRITES * LANES) == 0 else 1,)),
        ],
        compiler_params=pltpu.CompilerParams(vmem_limit_bytes=VMEM_BYTES),
        cost_estimate=pl.CostEstimate(flops=0, bytes_accessed=0, transcendentals=0),
    )(arrived, kept, *earlier)


def lift(tokens, first_sent, token_mixing, pieces):
    count = lax.axis_size("tok")
    embed = tokens.shape[0]
    rows = embed // count
    width = token_mixing.shape[1] // pieces
    sent = jax.ShapeDtypeStruct((rows, width), jnp.bfloat16)
    ways = [-1] * pieces
    blocks = [list(range(count - 2, -1, -1)) if way == 1 else list(range(count - 1)) for way in ways]
    travelling = [first_sent] + [
        call(functools.partial(sent_kernel, piece * width, blocks[piece][0]), sent, (tokens, token_mixing))
        for piece in range(1, pieces)
    ]
    kept = [None] * pieces
    result = None
    for step in range(1, count):
        for piece in range(pieces):
            arrived = turned(travelling[piece], "tok", ways[piece])
            if step == 1:
                travelling[piece], kept[piece] = call(
                    functools.partial(hop_kernel, piece * width, blocks[piece][1:] + [count - 1]),
                    [sent, jax.ShapeDtypeStruct((embed - 2 * rows, width), jnp.float32)],
                    (arrived, tokens, token_mixing),
                )
            elif step < count - 1:
                at = (step - 2) * rows
                summed = arrived.astype(jnp.float32) + kept[piece][at : at + rows]
                travelling[piece] = summed.astype(jnp.bfloat16)
            else:
                result = finish(piece * width, arrived, kept[piece], result, pieces * width)
    return result


def local(weather, conv_first, conv_second, patch_embed, token_mixing):
    tokens, first_sent = encode(weather, conv_first, conv_second, patch_embed, token_mixing)
    return lift(tokens, first_sent, token_mixing, PIECES)


def solution(mesh):
    placed = (P("groups", "tok", ("ch", "sub")), P(), P(), P(), P("tok", ("ch", "sub")))
    return jax.shard_map(
        local,
        mesh=mesh,
        in_specs=placed,
        out_specs=P(("groups", "tok"), ("ch", "sub")),
        check_vma=False,
    )
```
